128 devices in a mesh: dp: 4 (over y), seq: 16 (over x, z), tensor: 2 (over core).
Axes of the slice: x: 4, y: 4, z: 4, core: 2. Of those that a mesh axis runs over, the one named last changes fastest.
Arguments:
- tokens: float32 [10240, 2560], P(('dp', 'seq')), may hold values from -6 to 6
- cotangent: float32 [10240, 2560], P(('dp', 'seq')), may hold values from -6 to 6
- w_query: float32 [2560, 2560], P(('dp', 'seq'), 'tensor'), may hold values from -0.125 to 0.125
- w_keyvalue: float32 [2560, 2, 256], P(('dp', 'seq')), may hold values from -0.125 to 0.125
- w_out: float32 [2560, 2560], P('tensor', ('dp', 'seq')), may hold values from -2.5 to 2.5
- w_gateup: float32 [2560, 2, 7680], P(('dp', 'seq'), None, 'tensor'), may hold values from -0.125 to 0.125
- w_down: float32 [7680, 2560], P('tensor', ('dp', 'seq')), may hold values from -0.09375 to 0.09375
- norm_scales: float32 [2, 2560], P(None, ('dp', 'seq')), may hold values from -0.8 to 0.8
- first_query: float32 [2560, 2560], P(('dp', 'seq'), 'tensor'), may hold values from -96 to 96
- first_keyvalue: float32 [2560, 2, 256], P(('dp', 'seq')), may hold values from -192 to 192
- first_out: float32 [2560, 2560], P('tensor', ('dp', 'seq')), may hold values from -5 to 5
- first_gateup: float32 [2560, 2, 7680], P(('dp', 'seq'), None, 'tensor'), may hold values from -32 to 32
- first_down: float32 [7680, 2560], P('tensor', ('dp', 'seq')), may hold values from -40 to 40
- first_scales: float32 [2, 2560], P(None, ('dp', 'seq')), may hold values from -112 to 112
- second_query: float32 [2560, 2560], P(('dp', 'seq'), 'tensor'), may hold values from 1228.8 to 4812.8
- second_keyvalue: float32 [2560, 2, 256], P(('dp', 'seq')), may hold values from 4812.8 to 19456
- second_out: float32 [2560, 2560], P('tensor', ('dp', 'seq')), may hold values from 2.5 to 10
- second_gateup: float32 [2560, 2, 7680], P(('dp', 'seq'), None, 'tensor'), may hold values from 133.12 to 542.72
- second_down: float32 [7680, 2560], P('tensor', ('dp', 'seq')), may hold values from 225.28 to 901.12
- second_scales: float32 [2, 2560], P(None, ('dp', 'seq')), may hold values from 1331.2 to 5427.2
Outputs:
- output: float32 [10240, 2560], P(('dp', 'seq'))
- grad_tokens: float32 [10240, 2560], P(('dp', 'seq'))
- new_query: float32 [2560, 2560], P(('dp', 'seq'), 'tensor')
- new_keyvalue: float32 [2560, 2, 256], P(('dp', 'seq'))
- new_out: float32 [2560, 2560], P('tensor', ('dp', 'seq'))
- new_gateup: float32 [2560, 2, 7680], P(('dp', 'seq'), None, 'tensor')
- new_down: float32 [7680, 2560], P('tensor', ('dp', 'seq'))
- new_scales: float32 [2, 2560], P(None, ('dp', 'seq'))
- new_first_query: float32 [2560, 2560], P(('dp', 'seq'), 'tensor')
- new_first_keyvalue: float32 [2560, 2, 256], P(('dp', 'seq'))
- new_first_out: float32 [2560, 2560], P('tensor', ('dp', 'seq'))
- new_first_gateup: float32 [2560, 2, 7680], P(('dp', 'seq'), None, 'tensor')
- new_first_down: float32 [7680, 2560], P('tensor', ('dp', 'seq'))
- new_first_scales: float32 [2, 2560], P(None, ('dp', 'seq'))
- new_second_query: float32 [2560, 2560], P(('dp', 'seq'), 'tensor')
- new_second_keyvalue: float32 [2560, 2, 256], P(('dp', 'seq'))
- new_second_out: float32 [2560, 2560], P('tensor', ('dp', 'seq'))
- new_second_gateup: float32 [2560, 2, 7680], P(('dp', 'seq'), None, 'tensor')
- new_second_down: float32 [7680, 2560], P('tensor', ('dp', 'seq'))
- new_second_scales: float32 [2, 2560], P(None, ('dp', 'seq'))
The draws below stay inside these ranges and needn't reach their ends.
All inputs are finite; a program needn't handle non-finite values.
Results may differ from the reference program's by a relative error of at most 0.02.
Values may be sent and summed in bfloat16 or wider, within the bound.
A program may use at most 384 MiB of HBM per device.

```python
import math
import jax
import jax.numpy as jnp
from jax import lax

D = 2560
H = 10
HD = 256
FF = 7680
WINDOW = 2048
STEP = 10
LENGTH = 2560
TOKENS = 10240
N_DP = 4


def shard_levels(own_key, shape, cuts, smallest, largest):
    def one(position, parts):
        heights = jax.random.uniform(jax.random.fold_in(jax.random.fold_in(own_key, 6), position), (parts,), jnp.float32, smallest / len(cuts), largest / len(cuts))
        return jnp.repeat(jnp.exp(heights), shape[position] // parts).reshape((-1,) + (1,) * (len(shape) - position - 1))

    gain = one(*cuts[0])
    for cut in cuts[1:]:
        gain = gain * one(*cut)
    return gain


def bell_draw(own_key, dims, deviation, reach, split=(), kind=jnp.bfloat16):
    loudness = shard_levels(own_key, dims, split, -0.22, 0.18) if split else 1.0
    result = jax.random.normal(own_key, dims, jnp.float32) * deviation * loudness
    return jnp.minimum(jnp.maximum(result, -reach), reach).astype(kind)


def setup_inputs(seed: int = 0) -> dict:
    keys = jax.random.split(jax.random.key(seed), 21)
    tokens = bell_draw(keys[0], (TOKENS, D), 1.0, 6.0, ((0, 64),), jnp.float32)
    cotangent = bell_draw(keys[1], (TOKENS, D), 1.0, 6.0, ((0, 64),), jnp.float32)
    w_query = bell_draw(keys[2], (D, H * HD), D ** -0.5, 0.125, ((0, 64), (1, 2)), jnp.float32)
    w_keyvalue = bell_draw(keys[3], (D, 2, HD), D ** -0.5, 0.125, ((0, 64),), jnp.float32)
    w_out = bell_draw(keys[4], (H * HD, D), (max(1, H * HD * 4 // min(WINDOW, LENGTH))) ** -0.5, 2.5, ((0, 2), (1, 64)), jnp.float32)
    w_gateup = bell_draw(keys[5], (D, 2, FF), D ** -0.5, 0.125, ((0, 64), (2, 2)), jnp.float32)
    w_down = bell_draw(keys[6], (FF, D), (FF // 2) ** -0.5, 0.09375, ((0, 2), (1, 64)), jnp.float32)
    norm_scales = bell_draw(keys[7], (2, D), 0.2, 0.8, ((1, 64),), jnp.float32)
    first_query = bell_draw(keys[8], (D, H * HD), (0.17 * TOKENS ** 0.5), 96.0, ((0, 64), (1, 2)), jnp.float32)
    first_keyvalue = bell_draw(keys[9], (D, 2, HD), (0.33 * TOKENS ** 0.5), 192.0, ((0, 64),), jnp.float32)
    first_out = bell_draw(keys[10], (H * HD, D), (0.35 * (TOKENS * min(WINDOW, LENGTH) ** -1) ** 0.5), 5.0, ((0, 2), (1, 64)), jnp.float32)
    first_gateup = bell_draw(keys[11], (D, 2, FF), (0.056 * TOKENS ** 0.5), 32.0, ((0, 64), (2, 2)), jnp.float32)
    first_down = bell_draw(keys[12], (FF, D), (0.072 * TOKENS ** 0.5), 40.0, ((0, 2), (1, 64)), jnp.float32)
    first_scales = bell_draw(keys[13], (2, D), (0.18 * TOKENS ** 0.5), 112.0, ((1, 64),), jnp.float32)
    second_query = jnp.clip(jnp.exp(math.log(4812.8) - 1.36524087 * jax.random.uniform(keys[14], (D, H * HD), jnp.float32) ** shard_levels(keys[14], (D, H * HD), ((0, 64), (1, 2)), -0.2, 0.2)), 1228.8, 4812.8)
    second_keyvalue = jnp.clip(jnp.exp(math.log(19456.0) - 1.3968765 * jax.random.uniform(keys[15], (D, 2, HD), jnp.float32) ** shard_levels(keys[15], (D, 2, HD), ((0, 64),), -0.2, 0.2)), 4812.8, 19456.0)
    second_out = jnp.clip(jnp.exp(math.log(10.0) - 1.3862944 * jax.random.uniform(keys[16], (H * HD, D), jnp.float32) ** shard_levels(keys[16], (H * HD, D), ((0, 2), (1, 64)), -0.2, 0.2)), 2.5, 10.0)
    second_gateup = jnp.clip(jnp.exp(math.log(542.72) - 1.40534254 * jax.random.uniform(keys[17], (D, 2, FF), jnp.float32) ** shard_levels(keys[17], (D, 2, FF), ((0, 64), (2, 2)), -0.2, 0.2)), 133.12, 542.72)
    second_down = jnp.clip(jnp.exp(math.log(901.12) - 1.3862944 * jax.random.uniform(keys[18], (FF, D), jnp.float32) ** shard_levels(keys[18], (FF, D), ((0, 2), (1, 64)), -0.2, 0.2)), 225.28, 901.12)
    second_scales = jnp.clip(jnp.exp(math.log(5427.2) - 1.4053426 * jax.random.uniform(keys[19], (2, D), jnp.float32) ** shard_levels(keys[19], (2, D), ((1, 64),), -0.2, 0.2)), 1331.2, 5427.2)
    return {"tokens": tokens, "cotangent": cotangent, "w_query": w_query, "w_keyvalue": w_keyvalue, "w_out": w_out, "w_gateup": w_gateup, "w_down": w_down, "norm_scales": norm_scales, "first_query": first_query, "first_keyvalue": first_keyvalue, "first_out": first_out, "first_gateup": first_gateup, "first_down": first_down, "first_scales": first_scales, "second_query": second_query, "second_keyvalue": second_keyvalue, "second_out": second_out, "second_gateup": second_gateup, "second_down": second_down, "second_scales": second_scales}


@jax.custom_vjp
def low(v):
    return lax.optimization_barrier(v.astype(jnp.bfloat16)).astype(jnp.float32)

@jax.custom_vjp
def low_back(v):
    return v

def low_keep(v):
    return (low(v), None)

def low_pass(kept, grad):
    return (grad,)

def back_keep(v):
    return (v, None)

def back_low(kept, grad):
    return (low(grad),)
low.defvjp(low_keep, low_pass)
low_back.defvjp(back_keep, back_low)
highest = lax.Precision.HIGHEST
eps_norm = 1e-06
masked_fill = -1e+30
first_decay = 0.9
second_decay = 0.95
adam_eps = 1e-08
weight_decay = 0.1
gain_rate = 0.2

def rotate(values, positions, direction):
    quarter = values.shape[-1] // 4
    frequency = 10000.0 ** (-jnp.arange(quarter, dtype=jnp.float32) / quarter)
    angles = positions.astype(jnp.float32)[:, None] * frequency[None, :]
    table_shape = (angles.shape[0],) + (1,) * (values.ndim - 2) + (quarter,)
    cos_table = jnp.cos(angles).reshape(table_shape)
    sin_table = direction * jnp.sin(angles).reshape(table_shape)
    lower_part = values[..., :quarter]
    upper_part = values[..., quarter:2 * quarter]
    kept_part = values[..., 2 * quarter:]
    return jnp.concatenate([lower_part * cos_table - upper_part * sin_table, upper_part * cos_table + lower_part * sin_table, kept_part], axis=-1)

def rms_norm(values, offset):
    inverse = lax.rsqrt(lax.optimization_barrier(jnp.mean(values * values, axis=-1, keepdims=True)) + eps_norm)
    return values * inverse * (1.0 + offset)

def adam_update(weight, gradient, first_moment, second_moment, learn_rate, decay_rate):
    first_moment = first_decay * first_moment + (1.0 - first_decay) * gradient
    second_moment = second_decay * second_moment + (1.0 - second_decay) * gradient * gradient
    corrected = first_moment / (1.0 - first_decay ** STEP) / (jnp.sqrt(second_moment / (1.0 - second_decay ** STEP)) + adam_eps)
    return (weight - learn_rate * (corrected + decay_rate * weight), first_moment, second_moment)

def out_fan_in(seq_length):
    return max(1, H * HD * 4 // min(WINDOW, seq_length))

def attend_block(query_block, key_rows, value_rows, start):
    block_len = query_block.shape[0]
    scores = low_back(jnp.einsum('qhd,kd->hqk', query_block, key_rows, precision=highest))
    query_pos = start + jnp.arange(block_len, dtype=jnp.int32)
    key_pos = jnp.arange(key_rows.shape[0], dtype=jnp.int32)
    distance = query_pos[:, None] - key_pos[None, :]
    visible = (distance >= 0) & (distance < WINDOW)
    scores = jnp.where(visible[None], scores, masked_fill)
    maximum = lax.optimization_barrier(jnp.max(scores, axis=-1, keepdims=True))
    exponent = jnp.exp(scores - maximum)
    prob_low = low(exponent / lax.optimization_barrier(jnp.sum(exponent, axis=-1, keepdims=True)))
    return jnp.einsum('hqk,kd->qhd', prob_low, value_rows, precision=highest)

def sequence_attention(triple):
    queries, key_rows, value_rows = triple
    seq_length = queries.shape[0]
    block_len = math.gcd(seq_length, 512)
    block_count = seq_length // block_len
    blocks = queries.reshape(block_count, block_len, queries.shape[1], queries.shape[2])
    starts = jnp.arange(block_count, dtype=jnp.int32) * block_len

    def one_block(pieces):
        return attend_block(pieces[0], key_rows, value_rows, pieces[1])
    results = lax.map(jax.checkpoint(one_block), (blocks, starts))
    return results.reshape(queries.shape)

def forward_block(tokens, w_query, w_keyvalue, w_out, w_gateup, w_down, norm_scales):
    scales_low = low(norm_scales)
    positions = jnp.tile(jnp.arange(LENGTH, dtype=jnp.int32), N_DP)
    normed_one = low(rms_norm(tokens, scales_low[0]))
    query_raw = jnp.dot(normed_one, low(w_query), precision=highest).reshape(TOKENS, H, HD)
    queries = low(rotate(low_back(query_raw), positions, 1.0) * HD ** (-0.5))
    keyvalue = low_back(jnp.einsum('td,dgh->tgh', normed_one, low(w_keyvalue), precision=highest))
    key_rows = low(rotate(keyvalue[:, 0], positions, 1.0))
    value_rows = low(keyvalue[:, 1])
    attended = lax.map(sequence_attention, (queries.reshape(N_DP, LENGTH, H, HD), key_rows.reshape(N_DP, LENGTH, HD), value_rows.reshape(N_DP, LENGTH, HD)))
    attended = low(low_back(attended.reshape(TOKENS, H * HD)))
    residual = tokens + low_back(jnp.dot(attended, low(w_out), precision=highest))
    normed_two = low(rms_norm(residual, scales_low[1]))
    gateup = low_back(jnp.einsum('td,dgf->tgf', normed_two, low(w_gateup), precision=highest))
    hidden = low(jax.nn.gelu(gateup[:, 0], approximate=True) * gateup[:, 1])
    return residual + low_back(jnp.dot(hidden, low(w_down), precision=highest))

def reference(tokens, cotangent, w_query, w_keyvalue, w_out, w_gateup, w_down, norm_scales, first_query, first_keyvalue, first_out, first_gateup, first_down, first_scales, second_query, second_keyvalue, second_out, second_gateup, second_down, second_scales):
    output, pull_back = jax.vjp(forward_block, tokens, w_query, w_keyvalue, w_out, w_gateup, w_down, norm_scales)
    gradients = pull_back(cotangent)
    matrix_rate = 2.0 * D ** (-0.5)
    new_query, new_first_query, new_second_query = adam_update(w_query, gradients[1], first_query, second_query, matrix_rate, weight_decay)
    new_keyvalue, new_first_keyvalue, new_second_keyvalue = adam_update(w_keyvalue, gradients[2], first_keyvalue, second_keyvalue, matrix_rate, weight_decay)
    new_out, new_first_out, new_second_out = adam_update(w_out, gradients[3], first_out, second_out, 2.0 * out_fan_in(LENGTH) ** (-0.5), weight_decay)
    new_gateup, new_first_gateup, new_second_gateup = adam_update(w_gateup, gradients[4], first_gateup, second_gateup, matrix_rate, weight_decay)
    new_down, new_first_down, new_second_down = adam_update(w_down, gradients[5], first_down, second_down, 2.0 * (FF // 2) ** (-0.5), weight_decay)
    new_scales, new_first_scales, new_second_scales = adam_update(norm_scales, gradients[6], first_scales, second_scales, gain_rate, 0.0)
    return (output, gradients[0], new_query, new_keyvalue, new_out, new_gateup, new_down, new_scales, new_first_query, new_first_keyvalue, new_first_out, new_first_gateup, new_first_down, new_first_scales, new_second_query, new_second_keyvalue, new_second_out, new_second_gateup, new_second_down, new_second_scales)
```

```python
import functools

import jax
import jax.numpy as jnp
from jax import lax
from jax.experimental import pallas as pl
from jax.experimental.pallas import tpu as pltpu
from jax.sharding import Mesh
from jax.sharding import PartitionSpec as P

D = 2560
H = 10
HD = 256
FF = 7680
WINDOW = 2048
STEP = 10

eps_norm = 1e-06
masked_fill = -1e30
first_decay = 0.9
second_decay = 0.95
adam_eps = 1e-08
weight_decay = 0.1
gain_rate = 0.2

MESH = pl.DeviceIdType.MESH
LOW = jnp.bfloat16
F32 = jnp.float32
RING = 4
BLOCK = 160
HALF = BLOCK // 2
PART = 48
OWN = 40
PAD = 48
MAIN = 896
TAIL = 64


def step(axis, distance):
    return lax.rem(lax.axis_index(axis) + (RING + distance), RING)


def sibling():
    return {"tensor": 1 - lax.axis_index("tensor")}


def greet(peers):
    barrier = pltpu.get_barrier_semaphore()
    for peer in peers:
        pl.semaphore_signal(barrier, inc=1, device_id=peer, device_id_type=MESH)
    pl.semaphore_wait(barrier, len(peers))


class Sender:
    def __init__(self, send_sem, recv_sem):
        self.send_sem, self.recv_sem, self.count = send_sem, recv_sem, 0

    def copy(self, src, dst, peer):
        one = pltpu.make_async_remote_copy(
            src_ref=src,
            dst_ref=dst,
            send_sem=self.send_sem.at[self.count],
            recv_sem=self.recv_sem.at[self.count],
            device_id=peer,
            device_id_type=MESH,
        )
        self.count += 1
        one.start()
        return one


def comm_call(kernel, ident, copies, out_shape, out_spaces, scratch, *operands, in_spaces=None):
    in_spaces = in_spaces or [pl.ANY] * len(operands)
    return pl.pallas_call(
        kernel,
        out_shape=out_shape,
        in_specs=[pl.BlockSpec(memory_space=space) for space in in_spaces],
        out_specs=jax.tree.map(lambda space: pl.BlockSpec(memory_space=space), out_spaces),
        scratch_shapes=[
            pltpu.SemaphoreType.DMA((copies,)),
            pltpu.SemaphoreType.DMA((copies,)),
            pltpu.SemaphoreType.DMA((2,)),
            *scratch,
        ],
        compiler_params=pltpu.CompilerParams(
            collective_id=ident, has_side_effects=True, vmem_limit_bytes=48 * 1024 * 1024
        ),
    )(*operands)


def exchange_kernel(x_ref, o_ref, send_sem, recv_sem, local_sem):
    me = lax.axis_index("z")
    greet([{"z": step("z", d)} for d in (1, 2, 3)])
    sender = Sender(send_sem, recv_sem)
    copies = [
        sender.copy(x_ref.at[step("z", d)], o_ref.at[me], {"z": step("z", d)}) for d in (2, 1, 3)
    ]
    own = pltpu.make_async_copy(x_ref.at[me], o_ref.at[me], local_sem.at[0])
    own.start()
    own.wait()
    for copy in copies:
        copy.wait()


def exchange_z(x, ident):
    return comm_call(
        exchange_kernel, ident, 3, jax.ShapeDtypeStruct(x.shape, x.dtype), pl.ANY, [], x
    )


def swap_kernel(x_ref, o_ref, send_sem, recv_sem, local_sem):
    greet([sibling()])
    Sender(send_sem, recv_sem).copy(x_ref, o_ref, sibling()).wait()


def swap_cores(x, ident):
    return comm_call(swap_kernel, ident, 1, jax.ShapeDtypeStruct(x.shape, x.dtype), pl.ANY, [], x)


def gather_kernel(x_ref, o_ref, send_sem, recv_sem, local_sem):
    me, left, right, far = (step("z", d) for d in (0, -1, 1, 2))
    base = pl.multiple_of(lax.axis_index("tensor") * HALF, 16)
    half = pl.ds(base, HALF)
    first = pl.ds(base, PART)
    last = pl.ds(pl.multiple_of(base + PART, 16), HALF - PART)
    greet([{"z": left}, {"z": right}, sibling()])
    sender = Sender(send_sem, recv_sem)
    to_right = sender.copy(x_ref.at[half], o_ref.at[me, half], {"z": right})
    to_left = sender.copy(x_ref.at[half], o_ref.at[me, half], {"z": left})
    own = pltpu.make_async_copy(x_ref, o_ref.at[me], local_sem.at[0])
    own.start()
    to_right.wait_recv()
    on_right = sender.copy(o_ref.at[left, first], o_ref.at[left, first], {"z": right})
    share_left = sender.copy(o_ref.at[left, half], o_ref.at[left, half], sibling())
    to_left.wait_recv()
    on_left = sender.copy(o_ref.at[right, last], o_ref.at[right, last], {"z": left})
    share_right = sender.copy(o_ref.at[right, half], o_ref.at[right, half], sibling())
    on_right.wait_recv()
    on_left.wait_recv()
    share_far = sender.copy(o_ref.at[far, half], o_ref.at[far, half], sibling())
    own.wait()
    for copy in (share_left, share_right, share_far):
        copy.wait()
    for copy in (to_right, to_left, on_right, on_left):
        copy.wait_send()


def gather_z(x, ident):
    shape = jax.ShapeDtypeStruct((RING,) + x.shape, x.dtype)
    return comm_call(gather_kernel, ident, 7, shape, pl.ANY, [], x).reshape(-1, x.shape[1])


def reduce_kernel(
    p_ref, o_ref, send_sem, recv_sem, local_sem, other, total, part_a, part_b, from_left, from_right
):
    me, left, right, far = (step("z", d) for d in (0, -1, 1, 2))
    core = lax.axis_index("tensor")
    mine = pl.ds(pl.multiple_of(core * HALF, 16), HALF)
    theirs = pl.ds(pl.multiple_of((1 - core) * HALF, 16), HALF)
    greet([{"z": left}, {"z": right}, sibling()])
    sender = Sender(send_sem, recv_sem)
    shares = [
        sender.copy(p_ref.at[block, theirs], other.at[slot], sibling())
        for slot, block in enumerate((far, right, left, me))
    ]

    def both(slot, block):
        return p_ref[block, mine].astype(F32) + other[slot].astype(F32)

    shares[0].wait_recv()
    total[0] = both(0, far).astype(LOW)
    far_right = sender.copy(total.at[0, pl.ds(0, PART)], part_a, {"z": right})
    far_left = sender.copy(total.at[0, pl.ds(PART, HALF - PART)], part_b, {"z": left})
    shares[1].wait_recv()
    summed = both(1, right)
    far_right.wait_recv()
    total[1, :PART] = (summed[:PART] + part_a[...].astype(F32)).astype(LOW)
    total[1, PART:] = summed[PART:].astype(LOW)
    to_right = sender.copy(total.at[1], from_left, {"z": right})
    shares[2].wait_recv()
    summed = both(2, left)
    far_left.wait_recv()
    total[2, :PART] = summed[:PART].astype(LOW)
    total[2, PART:] = (summed[PART:] + part_b[...].astype(F32)).astype(LOW)
    to_left = sender.copy(total.at[2], from_right, {"z": left})
    shares[3].wait_recv()
    to_right.wait_recv()
    to_left.wait_recv()
    o_ref[mine, :] = both(3, me) + from_left[...].astype(F32) + from_right[...].astype(F32)
    share = sender.copy(o_ref.at[mine], o_ref.at[mine], sibling())
    share.wait()
    for copy in (*shares, far_right, far_left, to_right, to_left):
        copy.wait_send()


def reduce_z(x, ident):
    columns = x.shape[1]
    return comm_call(
        reduce_kernel,
        ident,
        9,
        jax.ShapeDtypeStruct((BLOCK, columns), F32),
        pltpu.VMEM,
        [
            pltpu.VMEM((4, HALF, columns), LOW),
            pltpu.VMEM((3, HALF, columns), LOW),
            pltpu.VMEM((PART, columns), LOW),
            pltpu.VMEM((HALF - PART, columns), LOW),
            pltpu.VMEM((HALF, columns), LOW),
            pltpu.VMEM((HALF, columns), LOW),
        ],
        x.reshape(RING, BLOCK, columns),
        in_spaces=[pltpu.VMEM],
    )


def plane_peers(axes):
    return [{axis: step(axis, d)} for axis in axes for d in (-1, 1)]


def plane_gather_kernel(axes, share, x_ref, o_ref, send_sem, recv_sem, local_sem):
    out = o_ref.at[lax.axis_index("tensor")] if share else o_ref
    a, b = (lax.axis_index(axis) for axis in axes)
    greet(plane_peers(axes) + ([sibling()] if share else []))
    sender = Sender(send_sem, recv_sem)
    own = pltpu.make_async_copy(x_ref, out.at[a, b], local_sem.at[0])
    own.start()
    waits = []
    state = []
    for which, axis in enumerate(axes):
        rows = pl.ds(which * HALF, HALF)
        place = (lambda i, r: out.at[i, b, r]) if which == 0 else (lambda i, r: out.at[a, i, r])
        me = (a, b)[which]
        to_right = sender.copy(x_ref.at[rows], place(me, rows), {axis: step(axis, 1)})
        to_left = sender.copy(x_ref.at[rows], place(me, rows), {axis: step(axis, -1)})
        state.append((axis, which, place, to_right, to_left))
        waits += [to_right, to_left]
    passed = []
    for axis, which, place, to_right, to_left in state:
        first = pl.ds(which * HALF, PART)
        last = pl.ds(which * HALF + PART, HALF - PART)
        left, right = step(axis, -1), step(axis, 1)
        to_right.wait_recv()
        on_right = sender.copy(place(left, first), place(left, first), {axis: right})
        to_left.wait_recv()
        on_left = sender.copy(place(right, last), place(right, last), {axis: left})
        passed.append((on_right, on_left))
        waits += [on_right, on_left]
    own.wait()
    state = []
    for which, axis in enumerate(axes):
        other = axes[1 - which]
        rows = pl.ds(which * HALF, HALF)
        if which == 0:
            place = lambda i, lo, n, rows=rows: out.at[pl.ds(lo, n), i, rows]
        else:
            place = lambda i, lo, n, rows=rows: out.at[i, pl.ds(lo, n), rows]
        me = (b, a)[which]
        for copy in passed[which]:
            copy.wait_recv()
        to_right = sender.copy(place(me, 0, 4), place(me, 0, 4), {other: step(other, 1)})
        to_left = sender.copy(place(me, 0, 4), place(me, 0, 4), {other: step(other, -1)})
        state.append((other, place, to_right, to_left))
        waits += [to_right, to_left]
    ends = []
    for other, place, to_right, to_left in state:
        left, right = step(other, -1), step(other, 1)
        to_right.wait_recv()
        on_right = sender.copy(place(left, 0, 2), place(left, 0, 2), {other: right})
        to_left.wait_recv()
        on_left = sender.copy(place(right, 2, 2), place(right, 2, 2), {other: left})
        ends += [on_right, on_left]
    for copy in ends:
        copy.wait_recv()
    if share:
        last = sender.copy(out, out, sibling())
        last.wait()
    for copy in waits + ends:
        copy.wait_send()


def gather_plane(x, axes, ident, share=False):
    shape = ((2,) if share else ()) + (RING, RING) + x.shape
    return comm_call(
        functools.partial(plane_gather_kernel, axes, share),
        ident,
        17,
        jax.ShapeDtypeStruct(shape, x.dtype),
        pl.ANY,
        [],
        x,
    )


def plane_reduce_kernel(
    axes, g_ref, o_ref, send_sem, recv_sem, local_sem, far_one, side_one, sum_one, far_two, side_two
):
    place_a, place_b = (lax.axis_index(axis) for axis in axes)
    greet(plane_peers(axes))
    sender = Sender(send_sem, recv_sem)
    copies = []

    def start(*args):
        copies.append(sender.copy(*args))
        return copies[-1]

    def block(which, i, lo, n):
        rows = pl.ds(which * HALF, HALF)
        return g_ref.at[i, pl.ds(lo, n), rows] if which == 0 else g_ref.at[pl.ds(lo, n), i, rows]

    first = []
    for which, axis in enumerate(axes):
        far, right, left = step(axis, 2), {axis: step(axis, 1)}, {axis: step(axis, -1)}
        first.append(
            (
                start(block(which, far, 0, 2), far_one.at[which, 0], right),
                start(block(which, far, 2, 2), far_one.at[which, 1], left),
            )
        )
    sides = []
    for which, axis in enumerate(axes):
        right, left = step(axis, 1), step(axis, -1)
        plain_right = start(block(which, right, 2, 2), side_one.at[which, 0, pl.ds(2, 2)], {axis: right})
        plain_left = start(block(which, left, 0, 2), side_one.at[which, 1, pl.ds(0, 2)], {axis: left})
        sides.append([plain_right, plain_left])
    for which, axis in enumerate(axes):
        right, left = step(axis, 1), step(axis, -1)
        first[which][0].wait_recv()
        sum_one[which, 0] = (
            block(which, right, 0, 2)[...].astype(F32) + far_one[which, 0].astype(F32)
        ).astype(LOW)
        sides[which].append(
            start(sum_one.at[which, 0], side_one.at[which, 0, pl.ds(0, 2)], {axis: right})
        )
        first[which][1].wait_recv()
        sum_one[which, 1] = (
            block(which, left, 2, 2)[...].astype(F32) + far_one[which, 1].astype(F32)
        ).astype(LOW)
        sides[which].append(
            start(sum_one.at[which, 1], side_one.at[which, 1, pl.ds(2, 2)], {axis: left})
        )
    second = []
    own = []

    def summed(which, i):
        me = (place_a, place_b)[which]
        rows = pl.ds(which * HALF, HALF)
        ref = g_ref.at[me, i, rows] if which == 0 else g_ref.at[i, me, rows]
        return (
            ref[...].astype(F32)
            + side_one[which, 0, i].astype(F32)
            + side_one[which, 1, i].astype(F32)
        )

    for which, axis in enumerate(axes):
        other = axes[1 - which]
        right, left = {other: step(other, 1)}, {other: step(other, -1)}
        for copy in sides[which]:
            copy.wait_recv()
        far_two[which, 0] = summed(which, step(other, 2)).astype(LOW)
        second.append(
            (
                start(far_two.at[which, 0, pl.ds(0, PART)], far_two.at[which, 1, pl.ds(0, PART)], right),
                start(
                    far_two.at[which, 0, pl.ds(PART, HALF - PART)],
                    far_two.at[which, 1, pl.ds(PART, HALF - PART)],
                    left,
                ),
            )
        )
    last = []
    for which, axis in enumerate(axes):
        other = axes[1 - which]
        right, left = step(other, 1), step(other, -1)
        total = summed(which, right)
        second[which][0].wait_recv()
        side_two[which, 0, :PART] = (
            total[:PART] + far_two[which, 1, :PART].astype(F32)
        ).astype(LOW)
        side_two[which, 0, PART:] = total[PART:].astype(LOW)
        last.append(start(side_two.at[which, 0], side_two.at[which, 2], {other: right}))
        total = summed(which, left)
        second[which][1].wait_recv()
        side_two[which, 1, :PART] = total[:PART].astype(LOW)
        side_two[which, 1, PART:] = (
            total[PART:] + far_two[which, 1, PART:].astype(F32)
        ).astype(LOW)
        last.append(start(side_two.at[which, 1], side_two.at[which, 3], {other: left}))
    for which, axis in enumerate(axes):
        other = axes[1 - which]
        last[2 * which].wait_recv()
        last[2 * which + 1].wait_recv()
        o_ref[which * HALF : (which + 1) * HALF] = (
            summed(which, lax.axis_index(other))
            + side_two[which, 2].astype(F32)
            + side_two[which, 3].astype(F32)
        )
    for copy in copies:
        copy.wait_send()


def reduce_plane(x, axes, ident):
    columns = x.shape[1]
    return comm_call(
        functools.partial(plane_reduce_kernel, axes),
        ident,
        20,
        jax.ShapeDtypeStruct((BLOCK, columns), F32),
        pltpu.VMEM,
        [
            pltpu.VMEM((2, 2, 2, HALF, columns), LOW),
            pltpu.VMEM((2, 2, 4, HALF, columns), LOW),
            pltpu.VMEM((2, 2, 2, HALF, columns), LOW),
            pltpu.VMEM((2, 2, HALF, columns), LOW),
            pltpu.VMEM((2, 4, HALF, columns), LOW),
        ],
        x.reshape(RING, RING, BLOCK, columns),
        in_spaces=[pltpu.VMEM],
    )


def rotate(values, positions, direction):
    quarter = values.shape[-1] // 4
    frequency = 10000.0 ** (-jnp.arange(quarter, dtype=F32) / quarter)
    angles = positions.astype(F32)[:, None] * frequency[None, :]
    table_shape = (angles.shape[0],) + (1,) * (values.ndim - 2) + (quarter,)
    cos_table = jnp.cos(angles).reshape(table_shape)
    sin_table = direction * jnp.sin(angles).reshape(table_shape)
    lower_part = values[..., :quarter]
    upper_part = values[..., quarter : 2 * quarter]
    kept_part = values[..., 2 * quarter :]
    return jnp.concatenate(
        [
            lower_part * cos_table - upper_part * sin_table,
            upper_part * cos_table + lower_part * sin_table,
            kept_part,
        ],
        axis=-1,
    )


def inverse_rms(values):
    return lax.rsqrt(jnp.mean(values * values, axis=-1, keepdims=True) + eps_norm)


def rms_back(grad, gain, unit, inverse):
    scaled = grad * gain
    return inverse * (scaled - unit * jnp.mean(scaled * unit, axis=-1, keepdims=True))


def adam_update(weight, gradient, first_moment, second_moment, learn_rate, decay_rate):
    first_moment = first_decay * first_moment + (1.0 - first_decay) * gradient
    second_moment = second_decay * second_moment + (1.0 - second_decay) * gradient * gradient
    corrected = (
        first_moment
        / (1.0 - first_decay**STEP)
        / (jnp.sqrt(second_moment / (1.0 - second_decay**STEP)) + adam_eps)
    )
    return (weight - learn_rate * (corrected + decay_rate * weight), first_moment, second_moment)


def out_fan_in(seq_length):
    return max(1, H * HD * 4 // min(WINDOW, seq_length))


def dot(left_side, right_side, contract):
    return lax.dot_general(
        left_side, right_side, ((contract[:1], contract[1:]), ((), ())), preferred_element_type=F32
    )


def activate(gate_part, upper_part):
    return jax.nn.gelu(gate_part, approximate=True) * upper_part


def quarters(rows):
    return rows.reshape(OWN, RING, -1).transpose(1, 0, 2)


def whole(slices):
    return slices.transpose(1, 0, 2).reshape(slices.shape[1], -1)


def pad_to(x, axis, size):
    widths = [(0, 0)] * x.ndim
    widths[axis] = (0, size - x.shape[axis])
    return jnp.pad(x, widths)


def per_device(
    tokens,
    cotangent,
    w_query,
    w_keyvalue,
    w_out,
    w_gateup,
    w_down,
    norm_scales,
    first_query,
    first_keyvalue,
    first_out,
    first_gateup,
    first_down,
    first_scales,
    second_query,
    second_keyvalue,
    second_out,
    second_gateup,
    second_down,
    second_scales,
):
    core = lax.axis_index("tensor")
    seq_index = lax.axis_index("x") * RING + lax.axis_index("z")
    positions = seq_index * BLOCK + jnp.arange(BLOCK, dtype=jnp.int32)
    seq_length = BLOCK * RING * RING
    head_count = H // 2

    keyvalue_part = lax.dynamic_index_in_dim(w_keyvalue, core, 1, keepdims=False)
    scale_columns = jnp.broadcast_to(norm_scales.T[None], (RING, OWN, 2))
    attn_rows = jnp.concatenate(
        [quarters(w_query), quarters(keyvalue_part), quarters(w_out.T), scale_columns], axis=2
    ).astype(LOW)
    attn_rows = pad_to(pad_to(attn_rows, 2, 768), 1, PAD)
    gateup = w_gateup.astype(LOW).reshape(OWN, 2, RING, MAIN + TAIL).transpose(2, 0, 1, 3)
    feed_rows = jnp.concatenate(
        [
            gateup[..., :MAIN].reshape(RING, OWN, 2 * MAIN),
            gateup[..., MAIN:].reshape(RING, OWN, 2 * TAIL),
            quarters(w_down.T).astype(LOW),
        ],
        axis=2,
    )
    feed_rows = pad_to(pad_to(feed_rows, 2, 2944), 1, PAD)
    attn_mine = exchange_z(attn_rows, 1)[:, :OWN].reshape(BLOCK, 768)
    feed_mine = exchange_z(feed_rows, 2)[:, :OWN].reshape(BLOCK, 2944)
    feed_full = lax.all_gather(feed_mine, ("dp", "x"), axis=0, tiled=True)
    attn_full = gather_plane(attn_mine, ("dp", "x"), 3).reshape(D, 768)
    gateup_full = feed_full[:, : 2 * (MAIN + TAIL)]
    down_full = feed_full[:, 2 * (MAIN + TAIL) : 3 * (MAIN + TAIL)]
    qkv_full = attn_full[:, :384]
    out_full = attn_full[:, 384:704]
    gains = 1.0 + attn_full[:, 704:706].astype(F32).T
    gain_one, gain_two = gains[0], gains[1]

    inverse_one = inverse_rms(tokens)
    unit_one = tokens * inverse_one
    unit_all = gather_z(unit_one.astype(LOW), 4)
    dy_all = gather_z(cotangent.astype(LOW), 5)
    normed_one = (unit_all.astype(F32) * gain_one).astype(LOW)
    qkv_slice = dot(normed_one, qkv_full, (1, 0)).astype(LOW).reshape(RING, BLOCK, 384)
    qkv = exchange_z(qkv_slice, 6).astype(F32)
    query_raw = whole(qkv[..., :320]).reshape(BLOCK, head_count, HD)
    query_low = (rotate(query_raw, positions, 1.0) * HD ** (-0.5)).astype(LOW)
    keyvalue_raw = whole(qkv[..., 320:])
    keyvalue_low = jnp.where(
        core == 0, rotate(keyvalue_raw, positions, 1.0), keyvalue_raw
    ).astype(LOW)
    keyvalue_all = gather_plane(keyvalue_low, ("x", "z"), 7, share=True).reshape(2, seq_length, HD)
    key_rows, value_rows = keyvalue_all[0], keyvalue_all[1]
    key_pos = jnp.arange(seq_length, dtype=jnp.int32)
    distance = positions[:, None] - key_pos[None, :]
    visible = (distance >= 0) & (distance < WINDOW)
    scores = jnp.einsum("chd,kd->hck", query_low, key_rows, preferred_element_type=F32)
    scores = jnp.where(visible[None], scores, masked_fill)
    maximum = jnp.max(scores, axis=-1, keepdims=True)
    exponent = jnp.exp(scores - maximum)
    row_total = jnp.sum(exponent, axis=-1, keepdims=True)
    log_total = maximum + jnp.log(row_total)
    prob_low = (exponent / row_total).astype(LOW)
    attended = jnp.einsum("hck,kd->chd", prob_low, value_rows, preferred_element_type=F32)
    attended_low = attended.reshape(BLOCK, RING, 320).astype(LOW).transpose(1, 0, 2)
    attended_slice = exchange_z(attended_low, 8).reshape(-1, 320)
    out_part = dot(attended_slice, out_full, (1, 1)).astype(LOW)
    residual = tokens + reduce_z(out_part, 9)
    inverse_two = inverse_rms(residual)
    unit_two = residual * inverse_two
    normed_two = gather_z((unit_two * gain_two).astype(LOW), 10)

    gateup = dot(normed_two, gateup_full, (1, 0))
    gate = jnp.concatenate([gateup[:, :MAIN], gateup[:, 2 * MAIN : 2 * MAIN + TAIL]], axis=1)
    upper = jnp.concatenate([gateup[:, MAIN : 2 * MAIN], gateup[:, 2 * MAIN + TAIL :]], axis=1)
    hidden, activate_back = jax.vjp(activate, gate, upper)
    hidden_low = hidden.astype(LOW)
    grad_down = dot(dy_all, hidden_low, (0, 0)).astype(LOW)
    down_sum = lax.psum_scatter(grad_down, ("dp", "x"), scatter_dimension=0, tiled=True)
    grad_hidden = dot(dy_all, down_full, (1, 0))
    grad_gate, grad_upper = activate_back(grad_hidden)
    grad_gateup_low = jnp.concatenate(
        [grad_gate[:, :MAIN], grad_upper[:, :MAIN], grad_gate[:, MAIN:], grad_upper[:, MAIN:]], axis=1
    ).astype(LOW)
    norm_part_two = dot(grad_gateup_low, gateup_full, (1, 1)).astype(LOW)
    grad_gateup = dot(normed_two, grad_gateup_low, (0, 0)).astype(LOW)
    gateup_sum = lax.psum_scatter(grad_gateup, ("dp", "x"), scatter_dimension=0, tiled=True)
    normed_grad_two = reduce_z(norm_part_two, 11)
    feed_part = dot(hidden_low, down_full, (1, 1)).astype(LOW)
    output = residual + reduce_z(feed_part, 12)
    grad_scale_two = jnp.sum(normed_grad_two * unit_two, axis=0)
    grad_residual = cotangent + rms_back(normed_grad_two, gain_two, unit_two, inverse_two)

    grad_attn = gather_z(grad_residual.astype(LOW), 13)
    grad_out = dot(grad_attn, attended_slice, (0, 0)).astype(LOW)
    grad_att_slice = dot(grad_attn, out_full, (1, 0)).astype(LOW).reshape(RING, BLOCK, 320)
    grad_att_low = whole(exchange_z(grad_att_slice, 14)).reshape(BLOCK, head_count, HD)
    scores = jnp.einsum("chd,kd->hck", query_low, key_rows, preferred_element_type=F32)
    probs = jnp.where(visible[None], jnp.exp(scores - log_total), 0.0)
    prob_low = probs.astype(LOW)
    grad_probs = jnp.einsum("chd,kd->hck", grad_att_low, value_rows, preferred_element_type=F32)
    delta = jnp.sum(probs * grad_probs, axis=-1, keepdims=True)
    grad_scores_low = (probs * (grad_probs - delta)).astype(LOW)
    grad_query = jnp.einsum("hck,kd->chd", grad_scores_low, key_rows, preferred_element_type=F32)
    grad_keys = jnp.einsum("hck,chd->kd", grad_scores_low, query_low, preferred_element_type=F32)
    grad_values = jnp.einsum("hck,chd->kd", prob_low, grad_att_low, preferred_element_type=F32)
    pair = jnp.stack([grad_keys, grad_values]).astype(LOW)
    mine = lax.dynamic_index_in_dim(pair, core, 0, keepdims=False)
    theirs = swap_cores(lax.dynamic_index_in_dim(pair, 1 - core, 0, keepdims=False), 15)
    both = (mine.astype(F32) + theirs.astype(F32)).astype(LOW)
    grad_kv = reduce_plane(both, ("x", "z"), 16)
    grad_kv_low = jnp.where(core == 0, rotate(grad_kv, positions, -1.0), grad_kv).astype(LOW)
    grad_query_low = rotate(grad_query * HD ** (-0.5), positions, -1.0).astype(LOW)
    grad_qkv = jnp.concatenate(
        [grad_query_low.reshape(BLOCK, RING, 320), grad_kv_low.reshape(BLOCK, RING, 64)], axis=2
    ).transpose(1, 0, 2)
    grad_qkv_slice = exchange_z(grad_qkv, 17).reshape(-1, 384)
    norm_part_one = dot(grad_qkv_slice, qkv_full, (1, 1)).astype(LOW)
    normed_grad_one = reduce_z(norm_part_one, 18)
    grad_qkv_w = dot(normed_one, grad_qkv_slice, (0, 0)).astype(LOW)
    grad_scale_one = jnp.sum(normed_grad_one * unit_one, axis=0)
    grad_tokens = grad_residual + rms_back(normed_grad_one, gain_one, unit_one, inverse_one)

    grad_scales = jnp.stack([grad_scale_one, grad_scale_two], axis=1).astype(LOW)
    attn_grads = jnp.concatenate([grad_qkv_w, grad_out, pad_to(grad_scales, 1, 64)], axis=1)
    attn_sum = reduce_plane(attn_grads, ("dp", "x"), 19).astype(LOW)

    def to_owners(rows, ident):
        rows = pad_to(rows.reshape(RING, OWN, -1), 1, PAD)
        return exchange_z(rows, ident)[:, :OWN].astype(F32)

    down_shard = whole(to_owners(down_sum, 20)).T
    gateup_shard = to_owners(gateup_sum, 21)
    gateup_shard = jnp.concatenate(
        [
            gateup_shard[..., : 2 * MAIN].reshape(RING, OWN, 2, MAIN),
            gateup_shard[..., 2 * MAIN :].reshape(RING, OWN, 2, TAIL),
        ],
        axis=3,
    ).transpose(1, 2, 0, 3).reshape(OWN, 2, -1)
    attn_shard = to_owners(attn_sum, 22)
    query_shard = whole(attn_shard[..., :320])
    kv_half = whole(attn_shard[..., 320:384])
    out_shard = whole(attn_shard[..., 384:704]).T
    scale_grads = jnp.sum(attn_shard[..., 704:706], axis=0).T
    kv_other = swap_cores(pad_to(kv_half, 0, PAD).astype(LOW), 23)[:OWN].astype(F32)
    keyvalue_shard = jnp.stack(
        [jnp.where(core == 0, kv_half, kv_other), jnp.where(core == 0, kv_other, kv_half)], axis=1
    )

    matrix_rate = 2.0 * D ** (-0.5)
    out_rate = 2.0 * out_fan_in(seq_length) ** (-0.5)
    down_rate = 2.0 * (FF // 2) ** (-0.5)
    triples = [
        adam_update(w_query, query_shard, first_query, second_query, matrix_rate, weight_decay),
        adam_update(
            w_keyvalue, keyvalue_shard, first_keyvalue, second_keyvalue, matrix_rate, weight_decay
        ),
        adam_update(w_out, out_shard, first_out, second_out, out_rate, weight_decay),
        adam_update(w_gateup, gateup_shard, first_gateup, second_gateup, matrix_rate, weight_decay),
        adam_update(w_down, down_shard, first_down, second_down, down_rate, weight_decay),
        adam_update(norm_scales, scale_grads, first_scales, second_scales, gain_rate, 0.0),
    ]
    return (output, grad_tokens, *(triple[i] for i in range(3) for triple in triples))


def solution(mesh):
    split = Mesh(
        mesh.devices.reshape(RING, RING, RING, 2), ("dp", "x", "z", "tensor")
    )
    rows = ("dp", "x", "z")
    matrices = (
        P(rows, "tensor"),
        P(rows, None, None),
        P("tensor", rows),
        P(rows, None, "tensor"),
        P("tensor", rows),
        P(None, rows),
    )
    in_specs = (P(rows, None), P(rows, None), *matrices, *matrices, *matrices)
    out_specs = in_specs
    return jax.shard_map(
        per_device, mesh=split, in_specs=in_specs, out_specs=out_specs, check_vma=False
    )
```

```python
import functools

import jax
import jax.numpy as jnp
from jax import lax
from jax.experimental import pallas as pl
from jax.experimental.pallas import tpu as pltpu
from jax.sharding import Mesh
from jax.sharding import PartitionSpec as P

D = 2560
H = 10
HD = 256
FF = 7680
WINDOW = 2048
STEP = 10

eps_norm = 1e-06
masked_fill = -1e30
first_decay = 0.9
second_decay = 0.95
adam_eps = 1e-08
weight_decay = 0.1
gain_rate = 0.2

MESH = pl.DeviceIdType.MESH
LOW = jnp.bfloat16
F32 = jnp.float32
RING = 4
BLOCK = 160
HALF = BLOCK // 2
PART = 48
OWN = 40
PAD = 48
MAIN = 896
TAIL = 64


def step(axis, distance):
    return lax.rem(lax.axis_index(axis) + (RING + distance), RING)


def sibling():
    return {"tensor": 1 - lax.axis_index("tensor")}


def greet(peers):
    barrier = pltpu.get_barrier_semaphore()
    for peer in peers:
        pl.semaphore_signal(barrier, inc=1, device_id=peer, device_id_type=MESH)
    pl.semaphore_wait(barrier, len(peers))


def dot(left_side, right_side, contract):
    return lax.dot_general(
        left_side, right_side, ((contract[:1], contract[1:]), ((), ())), preferred_element_type=F32
    )


class Sender:
    def __init__(self, send_sem, recv_sem):
        self.send_sem, self.recv_sem, self.count = send_sem, recv_sem, 0

    def copy(self, src, dst, peer):
        one = pltpu.make_async_remote_copy(
            src_ref=src,
            dst_ref=dst,
            send_sem=self.send_sem.at[self.count],
            recv_sem=self.recv_sem.at[self.count],
            device_id=peer,
            device_id_type=MESH,
        )
        self.count += 1
        one.start()
        return one


def comm_call(kernel, ident, copies, out_shape, out_spaces, scratch, *operands, in_spaces=None):
    in_spaces = in_spaces or [pl.ANY] * len(operands)
    return pl.pallas_call(
        kernel,
        out_shape=out_shape,
        in_specs=[pl.BlockSpec(memory_space=space) for space in in_spaces],
        out_specs=jax.tree.map(lambda space: pl.BlockSpec(memory_space=space), out_spaces),
        scratch_shapes=[
            pltpu.SemaphoreType.DMA((copies,)),
            pltpu.SemaphoreType.DMA((copies,)),
            pltpu.SemaphoreType.DMA((2,)),
            *scratch,
        ],
        compiler_params=pltpu.CompilerParams(
            collective_id=ident, has_side_effects=True, vmem_limit_bytes=48 * 1024 * 1024
        ),
    )(*operands)


def exchange_kernel(x_ref, o_ref, send_sem, recv_sem, local_sem):
    me = lax.axis_index("z")
    greet([{"z": step("z", d)} for d in (1, 2, 3)])
    sender = Sender(send_sem, recv_sem)
    copies = [
        sender.copy(x_ref.at[step("z", d)], o_ref.at[me], {"z": step("z", d)}) for d in (2, 1, 3)
    ]
    own = pltpu.make_async_copy(x_ref.at[me], o_ref.at[me], local_sem.at[0])
    own.start()
    own.wait()
    for copy in copies:
        copy.wait()


def exchange_z(x, ident):
    return comm_call(
        exchange_kernel, ident, 3, jax.ShapeDtypeStruct(x.shape, x.dtype), pl.ANY, [], x
    )


def swap_kernel(x_ref, o_ref, send_sem, recv_sem, local_sem):
    greet([sibling()])
    Sender(send_sem, recv_sem).copy(x_ref, o_ref, sibling()).wait()


def swap_cores(x, ident):
    return comm_call(swap_kernel, ident, 1, jax.ShapeDtypeStruct(x.shape, x.dtype), pl.ANY, [], x)


def gather_kernel(x_ref, o_ref, send_sem, recv_sem, local_sem):
    me, left, right, far = (step("z", d) for d in (0, -1, 1, 2))
    base = pl.multiple_of(lax.axis_index("tensor") * HALF, 16)
    half = pl.ds(base, HALF)
    first = pl.ds(base, PART)
    last = pl.ds(pl.multiple_of(base + PART, 16), HALF - PART)
    greet([{"z": left}, {"z": right}, sibling()])
    sender = Sender(send_sem, recv_sem)
    to_right = sender.copy(x_ref.at[half], o_ref.at[me, half], {"z": right})
    to_left = sender.copy(x_ref.at[half], o_ref.at[me, half], {"z": left})
    own = pltpu.make_async_copy(x_ref, o_ref.at[me], local_sem.at[0])
    own.start()
    to_right.wait_recv()
    on_right = sender.copy(o_ref.at[left, first], o_ref.at[left, first], {"z": right})
    share_left = sender.copy(o_ref.at[left, half], o_ref.at[left, half], sibling())
    to_left.wait_recv()
    on_left = sender.copy(o_ref.at[right, last], o_ref.at[right, last], {"z": left})
    share_right = sender.copy(o_ref.at[right, half], o_ref.at[right, half], sibling())
    on_right.wait_recv()
    on_left.wait_recv()
    share_far = sender.copy(o_ref.at[far, half], o_ref.at[far, half], sibling())
    own.wait()
    for copy in (share_left, share_right, share_far):
        copy.wait()
    for copy in (to_right, to_left, on_right, on_left):
        copy.wait_send()


def gather_z(x, ident):
    shape = jax.ShapeDtypeStruct((RING,) + x.shape, x.dtype)
    return comm_call(gather_kernel, ident, 7, shape, pl.ANY, [], x).reshape(-1, x.shape[1])


def reduce_kernel(
    p_ref, o_ref, send_sem, recv_sem, local_sem, other, total, part_a, part_b, from_left, from_right
):
    me, left, right, far = (step("z", d) for d in (0, -1, 1, 2))
    core = lax.axis_index("tensor")
    mine = pl.ds(pl.multiple_of(core * HALF, 16), HALF)
    theirs = pl.ds(pl.multiple_of((1 - core) * HALF, 16), HALF)
    greet([{"z": left}, {"z": right}, sibling()])
    sender = Sender(send_sem, recv_sem)
    shares = [
        sender.copy(p_ref.at[block, theirs], other.at[slot], sibling())
        for slot, block in enumerate((far, right, left, me))
    ]

    def both(slot, block):
        return p_ref[block, mine].astype(F32) + other[slot].astype(F32)

    shares[0].wait_recv()
    total[0] = both(0, far).astype(LOW)
    far_right = sender.copy(total.at[0, pl.ds(0, PART)], part_a, {"z": right})
    far_left = sender.copy(total.at[0, pl.ds(PART, HALF - PART)], part_b, {"z": left})
    shares[1].wait_recv()
    summed = both(1, right)
    far_right.wait_recv()
    total[1, :PART] = (summed[:PART] + part_a[...].astype(F32)).astype(LOW)
    total[1, PART:] = summed[PART:].astype(LOW)
    to_right = sender.copy(total.at[1], from_left, {"z": right})
    shares[2].wait_recv()
    summed = both(2, left)
    far_left.wait_recv()
    total[2, :PART] = summed[:PART].astype(LOW)
    total[2, PART:] = (summed[PART:] + part_b[...].astype(F32)).astype(LOW)
    to_left = sender.copy(total.at[2], from_right, {"z": left})
    shares[3].wait_recv()
    to_right.wait_recv()
    to_left.wait_recv()
    o_ref[mine, :] = both(3, me) + from_left[...].astype(F32) + from_right[...].astype(F32)
    share = sender.copy(o_ref.at[mine], o_ref.at[mine], sibling())
    share.wait()
    for copy in (*shares, far_right, far_left, to_right, to_left):
        copy.wait_send()


def reduce_z(x, ident):
    columns = x.shape[1]
    return comm_call(
        reduce_kernel,
        ident,
        9,
        jax.ShapeDtypeStruct((BLOCK, columns), F32),
        pltpu.VMEM,
        [
            pltpu.VMEM((4, HALF, columns), LOW),
            pltpu.VMEM((3, HALF, columns), LOW),
            pltpu.VMEM((PART, columns), LOW),
            pltpu.VMEM((HALF - PART, columns), LOW),
            pltpu.VMEM((HALF, columns), LOW),
            pltpu.VMEM((HALF, columns), LOW),
        ],
        x.reshape(RING, BLOCK, columns),
        in_spaces=[pltpu.VMEM],
    )


def plane_peers(axes):
    return [{axis: step(axis, d)} for axis in axes for d in (-1, 1)]


def plane_gather_kernel(axes, share, x_ref, o_ref, send_sem, recv_sem, local_sem):
    out = o_ref.at[lax.axis_index("tensor")] if share else o_ref
    a, b = (lax.axis_index(axis) for axis in axes)
    greet(plane_peers(axes) + ([sibling()] if share else []))
    sender = Sender(send_sem, recv_sem)
    own = pltpu.make_async_copy(x_ref, out.at[a, b], local_sem.at[0])
    own.start()
    waits = []
    state = []
    for which, axis in enumerate(axes):
        rows = pl.ds(which * HALF, HALF)
        place = (lambda i, r: out.at[i, b, r]) if which == 0 else (lambda i, r: out.at[a, i, r])
        me = (a, b)[which]
        to_right = sender.copy(x_ref.at[rows], place(me, rows), {axis: step(axis, 1)})
        to_left = sender.copy(x_ref.at[rows], place(me, rows), {axis: step(axis, -1)})
        state.append((axis, which, place, to_right, to_left))
        waits += [to_right, to_left]
    passed = []
    for axis, which, place, to_right, to_left in state:
        first = pl.ds(which * HALF, PART)
        last = pl.ds(which * HALF + PART, HALF - PART)
        left, right = step(axis, -1), step(axis, 1)
        to_right.wait_recv()
        on_right = sender.copy(place(left, first), place(left, first), {axis: right})
        to_left.wait_recv()
        on_left = sender.copy(place(right, last), place(right, last), {axis: left})
        passed.append((on_right, on_left))
        waits += [on_right, on_left]
    own.wait()
    state = []
    for which, axis in enumerate(axes):
        other = axes[1 - which]
        rows = pl.ds(which * HALF, HALF)
        if which == 0:
            place = lambda i, lo, n, rows=rows: out.at[pl.ds(lo, n), i, rows]
        else:
            place = lambda i, lo, n, rows=rows: out.at[i, pl.ds(lo, n), rows]
        me = (b, a)[which]
        for copy in passed[which]:
            copy.wait_recv()
        to_right = sender.copy(place(me, 0, 4), place(me, 0, 4), {other: step(other, 1)})
        to_left = sender.copy(place(me, 0, 4), place(me, 0, 4), {other: step(other, -1)})
        state.append((other, place, to_right, to_left))
        waits += [to_right, to_left]
    ends = []
    for other, place, to_right, to_left in state:
        left, right = step(other, -1), step(other, 1)
        to_right.wait_recv()
        on_right = sender.copy(place(left, 0, 2), place(left, 0, 2), {other: right})
        to_left.wait_recv()
        on_left = sender.copy(place(right, 2, 2), place(right, 2, 2), {other: left})
        ends += [on_right, on_left]
    for copy in ends:
        copy.wait_recv()
    if share:
        last = sender.copy(out, out, sibling())
        last.wait()
    for copy in waits + ends:
        copy.wait_send()


def gather_plane(x, axes, ident, share=False):
    shape = ((2,) if share else ()) + (RING, RING) + x.shape
    return comm_call(
        functools.partial(plane_gather_kernel, axes, share),
        ident,
        17,
        jax.ShapeDtypeStruct(shape, x.dtype),
        pl.ANY,
        [],
        x,
    )


def plane_reduce_kernel(
    axes, g_ref, o_ref, send_sem, recv_sem, local_sem, far_one, side_one, sum_one, far_two, side_two
):
    place_a, place_b = (lax.axis_index(axis) for axis in axes)
    greet(plane_peers(axes))
    sender = Sender(send_sem, recv_sem)
    copies = []

    def start(*args):
        copies.append(sender.copy(*args))
        return copies[-1]

    def block(which, i, lo, n):
        rows = pl.ds(which * HALF, HALF)
        return g_ref.at[i, pl.ds(lo, n), rows] if which == 0 else g_ref.at[pl.ds(lo, n), i, rows]

    first = []
    for which, axis in enumerate(axes):
        far, right, left = step(axis, 2), {axis: step(axis, 1)}, {axis: step(axis, -1)}
        first.append(
            (
                start(block(which, far, 0, 2), far_one.at[which, 0], right),
                start(block(which, far, 2, 2), far_one.at[which, 1], left),
            )
        )
    sides = []
    for which, axis in enumerate(axes):
        right, left = step(axis, 1), step(axis, -1)
        plain_right = start(block(which, right, 2, 2), side_one.at[which, 0, pl.ds(2, 2)], {axis: right})
        plain_left = start(block(which, left, 0, 2), side_one.at[which, 1, pl.ds(0, 2)], {axis: left})
        sides.append([plain_right, plain_left])
    for which, axis in enumerate(axes):
        right, left = step(axis, 1), step(axis, -1)
        first[which][0].wait_recv()
        sum_one[which, 0] = (
            block(which, right, 0, 2)[...].astype(F32) + far_one[which, 0].astype(F32)
        ).astype(LOW)
        sides[which].append(
            start(sum_one.at[which, 0], side_one.at[which, 0, pl.ds(0, 2)], {axis: right})
        )
        first[which][1].wait_recv()
        sum_one[which, 1] = (
            block(which, left, 2, 2)[...].astype(F32) + far_one[which, 1].astype(F32)
        ).astype(LOW)
        sides[which].append(
            start(sum_one.at[which, 1], side_one.at[which, 1, pl.ds(2, 2)], {axis: left})
        )
    second = []
    own = []

    def summed(which, i):
        me = (place_a, place_b)[which]
        rows = pl.ds(which * HALF, HALF)
        ref = g_ref.at[me, i, rows] if which == 0 else g_ref.at[i, me, rows]
        return (
            ref[...].astype(F32)
            + side_one[which, 0, i].astype(F32)
            + side_one[which, 1, i].astype(F32)
        )

    for which, axis in enumerate(axes):
        other = axes[1 - which]
        right, left = {other: step(other, 1)}, {other: step(other, -1)}
        for copy in sides[which]:
            copy.wait_recv()
        far_two[which, 0] = summed(which, step(other, 2)).astype(LOW)
        second.append(
            (
                start(far_two.at[which, 0, pl.ds(0, PART)], far_two.at[which, 1, pl.ds(0, PART)], right),
                start(
                    far_two.at[which, 0, pl.ds(PART, HALF - PART)],
                    far_two.at[which, 1, pl.ds(PART, HALF - PART)],
                    left,
                ),
            )
        )
    last = []
    for which, axis in enumerate(axes):
        other = axes[1 - which]
        right, left = step(other, 1), step(other, -1)
        total = summed(which, right)
        second[which][0].wait_recv()
        side_two[which, 0, :PART] = (
            total[:PART] + far_two[which, 1, :PART].astype(F32)
        ).astype(LOW)
        side_two[which, 0, PART:] = total[PART:].astype(LOW)
        last.append(start(side_two.at[which, 0], side_two.at[which, 2], {other: right}))
        total = summed(which, left)
        second[which][1].wait_recv()
        side_two[which, 1, :PART] = total[:PART].astype(LOW)
        side_two[which, 1, PART:] = (
            total[PART:] + far_two[which, 1, PART:].astype(F32)
        ).astype(LOW)
        last.append(start(side_two.at[which, 1], side_two.at[which, 3], {other: left}))
    for which, axis in enumerate(axes):
        other = axes[1 - which]
        last[2 * which].wait_recv()
        last[2 * which + 1].wait_recv()
        o_ref[which * HALF : (which + 1) * HALF] = (
            summed(which, lax.axis_index(other))
            + side_two[which, 2].astype(F32)
            + side_two[which, 3].astype(F32)
        )
    for copy in copies:
        copy.wait_send()


def reduce_plane(x, axes, ident):
    columns = x.shape[1]
    return comm_call(
        functools.partial(plane_reduce_kernel, axes),
        ident,
        20,
        jax.ShapeDtypeStruct((BLOCK, columns), F32),
        pltpu.VMEM,
        [
            pltpu.VMEM((2, 2, 2, HALF, columns), LOW),
            pltpu.VMEM((2, 2, 4, HALF, columns), LOW),
            pltpu.VMEM((2, 2, 2, HALF, columns), LOW),
            pltpu.VMEM((2, 2, HALF, columns), LOW),
            pltpu.VMEM((2, 4, HALF, columns), LOW),
        ],
        x.reshape(RING, RING, BLOCK, columns),
        in_spaces=[pltpu.VMEM],
    )


class Mover:
    def __init__(self, send_sem, recv_sem):
        self.send_sem, self.recv_sem, self.pending = send_sem, recv_sem, []

    def copy(self, src, dst, peer):
        index = len(self.pending)
        one = pltpu.make_async_remote_copy(
            src_ref=src,
            dst_ref=dst,
            send_sem=self.send_sem.at[index],
            recv_sem=self.recv_sem.at[index],
            device_id=peer,
            device_id_type=MESH,
        )
        one.start()
        self.pending.append(one)
        return one

    def finish(self):
        for one in self.pending:
            one.wait_send()


def advance(steps):
    next(steps, None)


def exchange_steps(mover, src, dst):
    me = lax.axis_index("z")
    copies = [
        mover.copy(src.at[step("z", d)], dst.at[me], {"z": step("z", d)}) for d in (2, 1, 3)
    ]
    yield
    for copy in copies:
        copy.wait_recv()


def core_rows():
    base = pl.multiple_of(lax.axis_index("tensor") * HALF, 16)
    return (
        pl.ds(base, HALF),
        pl.ds(base, PART),
        pl.ds(pl.multiple_of(base + PART, 16), HALF - PART),
        pl.ds(pl.multiple_of(HALF - base, 16), HALF),
    )


def gather_steps(mover, x, out):
    me, left, right, far = (step("z", d) for d in (0, -1, 1, 2))
    half, first, last, _ = core_rows()
    to_right = mover.copy(x.at[half], out.at[me, half], {"z": right})
    to_left = mover.copy(x.at[half], out.at[me, half], {"z": left})
    yield
    to_right.wait_recv()
    on_right = mover.copy(out.at[left, first], out.at[left, first], {"z": right})
    shares = [mover.copy(out.at[left, half], out.at[left, half], sibling())]
    to_left.wait_recv()
    on_left = mover.copy(out.at[right, last], out.at[right, last], {"z": left})
    shares.append(mover.copy(out.at[right, half], out.at[right, half], sibling()))
    yield
    on_right.wait_recv()
    on_left.wait_recv()
    shares.append(mover.copy(out.at[far, half], out.at[far, half], sibling()))
    yield
    for copy in shares:
        copy.wait_recv()


def cut_rows(which, cut):
    base, size = (0, cut) if which == 0 else (cut, BLOCK - cut)
    part = -(-size // 32) * 16
    return pl.ds(base, size), pl.ds(base, part), pl.ds(base + part, size - part)


def plane_gather_steps(mover, axes, x, out, cut=HALF, order=(0, 1), share=False):
    a, b = (lax.axis_index(axis) for axis in axes)
    state = {}
    for which, axis in enumerate(axes):
        rows = cut_rows(which, cut)[0]
        place = (lambda i, r: out.at[i, b, r]) if which == 0 else (lambda i, r: out.at[a, i, r])
        me = (a, b)[which]
        to_right = mover.copy(x.at[rows], place(me, rows), {axis: step(axis, 1)})
        to_left = mover.copy(x.at[rows], place(me, rows), {axis: step(axis, -1)})
        state[which] = (axis, place, to_right, to_left)
    yield
    passed = {}
    for which in order:
        axis, place, to_right, to_left = state[which]
        _, first, last = cut_rows(which, cut)
        left, right = step(axis, -1), step(axis, 1)
        to_right.wait_recv()
        on_right = mover.copy(place(left, first), place(left, first), {axis: right})
        to_left.wait_recv()
        on_left = mover.copy(place(right, last), place(right, last), {axis: left})
        passed[which] = (on_right, on_left)
    yield
    state = {}
    shares = []

    def give(piece):
        if share:
            shares.append(mover.copy(piece, piece, sibling()))

    for which in order:
        axis, other = axes[which], axes[1 - which]
        rows = cut_rows(which, cut)[0]
        if which == 0:
            place = lambda i, lo, n, rows=rows: out.at[pl.ds(lo, n), i, rows]
        else:
            place = lambda i, lo, n, rows=rows: out.at[i, pl.ds(lo, n), rows]
        me = (b, a)[which]
        for copy in passed[which]:
            copy.wait_recv()
        to_right = mover.copy(place(me, 0, 4), place(me, 0, 4), {other: step(other, 1)})
        to_left = mover.copy(place(me, 0, 4), place(me, 0, 4), {other: step(other, -1)})
        give(place(me, 0, 4))
        state[which] = (other, place, to_right, to_left)
        yield
    ends = []
    for which in order:
        other, place, to_right, to_left = state[which]
        left, right = step(other, -1), step(other, 1)
        to_right.wait_recv()
        ends.append(mover.copy(place(left, 0, 2), place(left, 0, 2), {other: right}))
        give(place(left, 0, 4))
        to_left.wait_recv()
        ends.append(mover.copy(place(right, 2, 2), place(right, 2, 2), {other: left}))
        give(place(right, 0, 4))
        yield
    for copy in ends:
        copy.wait_recv()
    for which in order:
        other, place, _, _ = state[which]
        give(place(step(other, 2), 0, 4))
    for copy in shares:
        copy.wait_recv()


def lanes(shape):
    return lax.broadcasted_iota(jnp.int32, shape, len(shape) - 1)


def turn(values, cos, sin):
    return values * cos + pltpu.roll(values, 64, 1) * sin


def whole_rows(blocks, stage, dst):
    for i in range(RING):
        stage[i * OWN : (i + 1) * OWN] = blocks[i].astype(F32)[:OWN]
    dst[...] = stage[...].astype(LOW)


def first_kernel(
    attn_rows,
    feed_rows,
    tokens,
    dy,
    cos_ref,
    sin_ref,
    cos_kv,
    sin_kv,
    feed_full,
    attn_full,
    normed_one,
    dy_all,
    query,
    keyvalue,
    log_total,
    att_slice,
    residual,
    normed_two,
    send_sem,
    recv_sem,
    local_sem,
    attn_got,
    attn_mine,
    attn_stage,
    feed_got,
    feed_mine,
    feed_stage,
    unit_low,
    unit_all,
    gain_ref,
    qkv_send,
    qkv_got,
    kv_own,
    scores,
    attended,
    att_send,
    part,
    other,
    total,
    part_a,
    part_b,
    from_left,
    from_right,
    normed_low,
):
    z, x, y, core = (lax.axis_index(axis) for axis in ("z", "x", "dp", "tensor"))
    left, right, far = (step("z", d) for d in (-1, 1, 2))
    half, _, _, their_half = core_rows()
    plane = ("dp", "x")
    greet(
        [{"z": step("z", d)} for d in (1, 2, 3)] + plane_peers(("dp", "x")) + [sibling()]
    )
    mover = Mover(send_sem, recv_sem)

    attn_swap = exchange_steps(mover, attn_rows, attn_got)
    advance(attn_swap)
    values = tokens[...]
    unit = values * lax.rsqrt(jnp.mean(values * values, axis=-1, keepdims=True) + eps_norm)
    unit_low[...] = unit.astype(LOW)
    unit_gather = gather_steps(mover, unit_low, unit_all)
    advance(unit_gather)
    feed_swap = exchange_steps(mover, feed_rows, feed_got)
    advance(feed_swap)
    unit_all[z] = unit_low[...]
    attn_got[z] = attn_rows[z]
    advance(attn_swap)
    whole_rows(attn_got, attn_stage, attn_mine)
    attn_gather = plane_gather_steps(mover, plane, attn_mine, attn_full)
    advance(attn_gather)
    attn_full[y, x] = attn_mine[...]
    advance(unit_gather)
    advance(attn_gather)
    advance(attn_gather)
    advance(attn_gather)
    feed_got[z] = feed_rows[z]
    advance(unit_gather)
    advance(feed_swap)
    whole_rows(feed_got, feed_stage, feed_mine)
    feed_own = pltpu.make_async_copy(feed_mine, feed_full.at[y, x], local_sem.at[0])
    feed_own.start()
    advance(attn_gather)
    advance(attn_gather)
    feed_gather = plane_gather_steps(mover, plane, feed_mine, feed_full, cut=64, order=(1, 0))
    advance(feed_gather)
    dy_gather = gather_steps(mover, dy, dy_all)
    advance(dy_gather)
    dy_own = pltpu.make_async_copy(dy, dy_all.at[z], local_sem.at[1])
    dy_own.start()
    advance(unit_gather)
    advance(attn_gather)

    scale_cols = attn_full[:, :, :, 640:768].reshape(D, 128)
    pick = (lanes((8, 128)) == 64 + lax.broadcasted_iota(jnp.int32, (8, 128), 0)).astype(LOW)
    gain_ref[...] = 1.0 + dot(pick, scale_cols, (1, 1))
    qkv_weight = attn_full[:, :, :, :384].reshape(D, 384)
    copies = []
    for d in (2, 1, 3, 0):
        block = step("z", d)
        normed = (unit_all[block].astype(F32) * gain_ref[0:1, :]).astype(LOW)
        normed_one[block] = normed
        qkv_send[block] = dot(normed, qkv_weight, (1, 0)).astype(LOW)
        if d:
            copies.append(mover.copy(qkv_send.at[block], qkv_got.at[z], {"z": block}))
    qkv_got[z] = qkv_send[z]
    advance(feed_gather)
    feed_own.wait()
    for copy in copies:
        copy.wait_recv()
    low_lanes = lanes((BLOCK, 128)) < TAIL
    cos, sin = cos_ref[...], sin_ref[...]

    def joined(i, offset):
        one, two = (qkv_got[i + k, :, 256:384].astype(F32) for k in (0, 1))
        if offset == 0:
            return jnp.where(low_lanes, one, pltpu.roll(two, TAIL, 1))
        return jnp.where(low_lanes, pltpu.roll(one, TAIL, 1), two)

    kv_own[:, :128] = turn(joined(0, 1), cos_kv[...], sin_kv[...]).astype(LOW)
    kv_own[:, 128:] = joined(2, 1).astype(LOW)
    kv_mine = keyvalue.at[core]
    kv_gather = plane_gather_steps(mover, ("x", "z"), kv_own, kv_mine, share=True)
    advance(kv_gather)
    keyvalue[core, x, z] = kv_own[...]
    scale = HD ** (-0.5)
    for h in range(4):
        first = qkv_got[h, :, :128].astype(F32)
        query[h, :, :128] = (turn(first, cos, sin) * scale).astype(LOW)
        query[h, :, 128:] = (qkv_got[h, :, 128:256].astype(F32) * scale).astype(LOW)
    query[4, :, :128] = (turn(joined(0, 0), cos, sin) * scale).astype(LOW)
    query[4, :, 128:] = (joined(2, 0) * scale).astype(LOW)
    advance(kv_gather)
    advance(feed_gather)
    advance(kv_gather)
    advance(kv_gather)
    advance(kv_gather)
    advance(kv_gather)
    advance(feed_gather)
    advance(dy_gather)
    advance(kv_gather)

    start = (x * RING + z) * BLOCK
    chunk = RING * BLOCK

    def one_head(h, carry):
        queries = query[h]
        top = jnp.full((BLOCK, 1), masked_fill, F32)
        for k in range(RING):
            rows = keyvalue[0, k].reshape(chunk, HD)
            tile = dot(queries, rows, (1, 1))
            gap = (start - k * chunk) + (
                lax.broadcasted_iota(jnp.int32, tile.shape, 0) - lanes(tile.shape)
            )
            tile = jnp.where((gap >= 0) & (gap < WINDOW), tile, masked_fill)
            scores[:, k * chunk : (k + 1) * chunk] = tile
            top = jnp.maximum(top, jnp.max(tile, axis=-1, keepdims=True))
        sums = jnp.zeros((BLOCK, 1), F32)
        for k in range(RING):
            tile = jnp.exp(scores[:, k * chunk : (k + 1) * chunk] - top)
            scores[:, k * chunk : (k + 1) * chunk] = tile
            sums = sums + jnp.sum(tile, axis=-1, keepdims=True)
        inverse = 1.0 / sums
        result = jnp.zeros((BLOCK, HD), F32)
        for k in range(RING):
            low = (scores[:, k * chunk : (k + 1) * chunk] * inverse).astype(LOW)
            result = result + dot(low, keyvalue[1, k].reshape(chunk, HD), (1, 0))
        attended[h] = result
        log_total[h] = jnp.broadcast_to(top + jnp.log(sums), (BLOCK, 128))
        return carry

    lax.fori_loop(0, 5, one_head, 0)
    for j in range(RING):
        att_send[j, :, :256] = attended[j].astype(LOW)
        tile = attended[4, :, (j // 2) * 128 : (j // 2 + 1) * 128]
        tile = pltpu.roll(tile, TAIL, 1) if j % 2 else tile
        att_send[j, :, 256:] = jnp.where(low_lanes, tile, 0.0).astype(LOW)
    att_swap = exchange_steps(mover, att_send, att_slice)
    advance(att_swap)
    att_slice[z] = att_send[z]
    advance(dy_gather)
    advance(att_swap)

    out_weight = attn_full[:, :, :, 384:].reshape(D, 384)
    blocks = (far, right, left, z)
    shares = []
    for slot, block in enumerate(blocks):
        part[block] = dot(att_slice[block], out_weight, (1, 1)).astype(LOW)
        shares.append(mover.copy(part.at[block, their_half], other.at[slot], sibling()))

    def both(slot):
        return part[blocks[slot], half].astype(F32) + other[slot].astype(F32)

    shares[0].wait_recv()
    total[0] = both(0).astype(LOW)
    far_right = mover.copy(total.at[0, pl.ds(0, PART)], part_a, {"z": right})
    far_left = mover.copy(total.at[0, pl.ds(PART, HALF - PART)], part_b, {"z": left})
    shares[1].wait_recv()
    shares[2].wait_recv()
    far_right.wait_recv()
    summed = both(1)
    total[1, :PART] = (summed[:PART] + part_a[...].astype(F32)).astype(LOW)
    total[1, PART:] = summed[PART:].astype(LOW)
    to_right = mover.copy(total.at[1], from_left, {"z": right})
    far_left.wait_recv()
    summed = both(2)
    total[2, :PART] = summed[:PART].astype(LOW)
    total[2, PART:] = (summed[PART:] + part_b[...].astype(F32)).astype(LOW)
    to_left = mover.copy(total.at[2], from_right, {"z": left})
    shares[3].wait_recv()
    to_right.wait_recv()
    to_left.wait_recv()
    rows = tokens[half, :] + (
        both(3) + from_left[...].astype(F32) + from_right[...].astype(F32)
    )
    residual[half, :] = rows
    res_share = mover.copy(residual.at[half], residual.at[half], sibling())

    def normed_rows(rows):
        unit = rows * lax.rsqrt(jnp.mean(rows * rows, axis=-1, keepdims=True) + eps_norm)
        return (unit * gain_ref[1:2, :]).astype(LOW)

    normed_low[half, :] = normed_rows(rows)
    normed_gather = gather_steps(mover, normed_low, normed_two)
    advance(normed_gather)
    res_share.wait_recv()
    normed_low[their_half, :] = normed_rows(residual[their_half, :])
    normed_two[z] = normed_low[...]
    advance(normed_gather)
    advance(feed_gather)
    advance(normed_gather)
    advance(feed_gather)
    advance(dy_gather)
    advance(normed_gather)
    advance(feed_gather)
    dy_own.wait()
    mover.finish()


def run_first(*operands):
    out = {
        "feed_full": ((RING, RING, BLOCK, 2944), LOW, pl.ANY),
        "attn_full": ((RING, RING, BLOCK, 768), LOW, pltpu.VMEM),
        "normed_one": ((RING, BLOCK, D), LOW, pltpu.VMEM),
        "dy_all": ((RING, BLOCK, D), LOW, pl.ANY),
        "query": ((5, BLOCK, HD), LOW, pltpu.VMEM),
        "keyvalue": ((2, RING, RING, BLOCK, HD), LOW, pltpu.VMEM),
        "log_total": ((5, BLOCK, 128), F32, pltpu.VMEM),
        "att_slice": ((RING, BLOCK, 384), LOW, pltpu.VMEM),
        "residual": ((BLOCK, D), F32, pltpu.VMEM),
        "normed_two": ((RING, BLOCK, D), LOW, pltpu.VMEM),
    }
    spaces = [pltpu.VMEM, pltpu.VMEM, pltpu.VMEM, pl.ANY] + [pltpu.VMEM] * 4
    copies = 120
    results = pl.pallas_call(
        first_kernel,
        out_shape=[jax.ShapeDtypeStruct(shape, kind) for shape, kind, _ in out.values()],
        in_specs=[pl.BlockSpec(memory_space=space) for space in spaces],
        out_specs=[pl.BlockSpec(memory_space=space) for _, _, space in out.values()],
        scratch_shapes=[
            pltpu.SemaphoreType.DMA((copies,)),
            pltpu.SemaphoreType.DMA((copies,)),
            pltpu.SemaphoreType.DMA((2,)),
            pltpu.VMEM((RING, PAD, 768), LOW),
            pltpu.VMEM((BLOCK, 768), LOW),
            pltpu.VMEM((BLOCK, 768), F32),
            pltpu.VMEM((RING, PAD, 2944), LOW),
            pltpu.VMEM((BLOCK, 2944), LOW),
            pltpu.VMEM((BLOCK, 2944), F32),
            pltpu.VMEM((BLOCK, D), LOW),
            pltpu.VMEM((RING, BLOCK, D), LOW),
            pltpu.VMEM((8, D), F32),
            pltpu.VMEM((RING, BLOCK, 384), LOW),
            pltpu.VMEM((RING, BLOCK, 384), LOW),
            pltpu.VMEM((BLOCK, HD), LOW),
            pltpu.VMEM((BLOCK, RING * RING * BLOCK), F32),
            pltpu.VMEM((5, BLOCK, HD), F32),
            pltpu.VMEM((RING, BLOCK, 384), LOW),
            pltpu.VMEM((RING, BLOCK, D), LOW),
            pltpu.VMEM((4, HALF, D), LOW),
            pltpu.VMEM((3, HALF, D), LOW),
            pltpu.VMEM((PART, D), LOW),
            pltpu.VMEM((HALF - PART, D), LOW),
            pltpu.VMEM((HALF, D), LOW),
            pltpu.VMEM((HALF, D), LOW),
            pltpu.VMEM((BLOCK, D), LOW),
        ],
        compiler_params=pltpu.CompilerParams(
            collective_id=1, has_side_effects=True, vmem_limit_bytes=60 * 1024 * 1024
        ),
    )(*operands)
    return dict(zip(out, results, strict=True))


def rotate(values, positions, direction):
    quarter = values.shape[-1] // 4
    frequency = 10000.0 ** (-jnp.arange(quarter, dtype=F32) / quarter)
    angles = positions.astype(F32)[:, None] * frequency[None, :]
    table_shape = (angles.shape[0],) + (1,) * (values.ndim - 2) + (quarter,)
    cos_table = jnp.cos(angles).reshape(table_shape)
    sin_table = direction * jnp.sin(angles).reshape(table_shape)
    lower_part = values[..., :quarter]
    upper_part = values[..., quarter : 2 * quarter]
    kept_part = values[..., 2 * quarter :]
    return jnp.concatenate(
        [
            lower_part * cos_table - upper_part * sin_table,
            upper_part * cos_table + lower_part * sin_table,
            kept_part,
        ],
        axis=-1,
    )


def inverse_rms(values):
    return lax.rsqrt(jnp.mean(values * values, axis=-1, keepdims=True) + eps_norm)


def rms_back(grad, gain, unit, inverse):
    scaled = grad * gain
    return inverse * (scaled - unit * jnp.mean(scaled * unit, axis=-1, keepdims=True))


def adam_update(weight, gradient, first_moment, second_moment, learn_rate, decay_rate):
    first_moment = first_decay * first_moment + (1.0 - first_decay) * gradient
    second_moment = second_decay * second_moment + (1.0 - second_decay) * gradient * gradient
    corrected = (
        first_moment
        / (1.0 - first_decay**STEP)
        / (jnp.sqrt(second_moment / (1.0 - second_decay**STEP)) + adam_eps)
    )
    return (weight - learn_rate * (corrected + decay_rate * weight), first_moment, second_moment)


def out_fan_in(seq_length):
    return max(1, H * HD * 4 // min(WINDOW, seq_length))


def activate(gate_part, upper_part):
    return jax.nn.gelu(gate_part, approximate=True) * upper_part


def quarters(rows):
    return rows.reshape(OWN, RING, -1).transpose(1, 0, 2)


def head_quarters(rows):
    split = rows.reshape(rows.shape[0], 5, HD)
    last = split[:, 4].reshape(-1, RING, TAIL)
    return jnp.concatenate([split[:, :4], last], axis=2).transpose(1, 0, 2)


def whole_heads(slices):
    slices = slices.transpose(1, 0, 2)
    rows = slices.shape[0]
    return jnp.concatenate(
        [slices[..., :HD].reshape(rows, -1), slices[..., HD:].reshape(rows, -1)], axis=1
    )


def whole(slices):
    return slices.transpose(1, 0, 2).reshape(slices.shape[1], -1)


def pad_to(x, axis, size):
    widths = [(0, 0)] * x.ndim
    widths[axis] = (0, size - x.shape[axis])
    return jnp.pad(x, widths)


def per_device(
    tokens,
    cotangent,
    w_query,
    w_keyvalue,
    w_out,
    w_gateup,
    w_down,
    norm_scales,
    first_query,
    first_keyvalue,
    first_out,
    first_gateup,
    first_down,
    first_scales,
    second_query,
    second_keyvalue,
    second_out,
    second_gateup,
    second_down,
    second_scales,
):
    core = lax.axis_index("tensor")
    seq_index = lax.axis_index("x") * RING + lax.axis_index("z")
    positions = seq_index * BLOCK + jnp.arange(BLOCK, dtype=jnp.int32)
    seq_length = BLOCK * RING * RING
    head_count = H // 2

    keyvalue_part = lax.dynamic_index_in_dim(w_keyvalue, core, 1, keepdims=False)
    scale_columns = jnp.broadcast_to(norm_scales.T[None], (RING, OWN, 2))
    attn_rows = jnp.concatenate(
        [head_quarters(w_query), quarters(keyvalue_part), head_quarters(w_out.T), scale_columns],
        axis=2,
    ).astype(LOW)
    attn_rows = pad_to(pad_to(attn_rows, 2, 768), 1, PAD)
    gateup = w_gateup.astype(LOW).reshape(OWN, 2, RING, MAIN + TAIL).transpose(2, 0, 1, 3)
    feed_rows = jnp.concatenate(
        [
            gateup[..., :MAIN].reshape(RING, OWN, 2 * MAIN),
            gateup[..., MAIN:].reshape(RING, OWN, 2 * TAIL),
            quarters(w_down.T).astype(LOW),
        ],
        axis=2,
    )
    feed_rows = pad_to(pad_to(feed_rows, 2, 2944), 1, PAD)
    frequency = 10000.0 ** (-jnp.arange(TAIL, dtype=F32) / TAIL)
    angles = positions.astype(F32)[:, None] * frequency[None, :]
    cos_table = jnp.tile(jnp.cos(angles), (1, 2))
    sin_table = jnp.concatenate([-jnp.sin(angles), jnp.sin(angles)], axis=1)
    cos_kv = jnp.where(core == 0, cos_table, 1.0)
    sin_kv = jnp.where(core == 0, sin_table, 0.0)
    first = run_first(
        attn_rows, feed_rows, tokens, cotangent.astype(LOW), cos_table, sin_table, cos_kv, sin_kv
    )
    feed_full = first["feed_full"].reshape(D, 2944)
    attn_full = first["attn_full"].reshape(D, 768)
    gateup_full = feed_full[:, : 2 * (MAIN + TAIL)]
    down_full = feed_full[:, 2 * (MAIN + TAIL) : 3 * (MAIN + TAIL)]
    qkv_full = attn_full[:, :384]
    out_full = attn_full[:, 384:704]
    gains = 1.0 + attn_full[:, 704:706].astype(F32).T
    gain_one, gain_two = gains[0], gains[1]
    inverse_one = inverse_rms(tokens)
    unit_one = tokens * inverse_one
    dy_all = first["dy_all"].reshape(-1, D)
    normed_one = first["normed_one"].reshape(-1, D)
    query_low = first["query"]
    key_rows, value_rows = first["keyvalue"].reshape(2, seq_length, HD)
    log_total = first["log_total"][:, :, :1]
    attended_slice = first["att_slice"].reshape(-1, 384)[:, :320]
    residual = first["residual"]
    normed_two = first["normed_two"].reshape(-1, D)
    key_pos = jnp.arange(seq_length, dtype=jnp.int32)
    distance = positions[:, None] - key_pos[None, :]
    visible = (distance >= 0) & (distance < WINDOW)
    inverse_two = inverse_rms(residual)
    unit_two = residual * inverse_two

    gateup = dot(normed_two, gateup_full, (1, 0))
    gate = jnp.concatenate([gateup[:, :MAIN], gateup[:, 2 * MAIN : 2 * MAIN + TAIL]], axis=1)
    upper = jnp.concatenate([gateup[:, MAIN : 2 * MAIN], gateup[:, 2 * MAIN + TAIL :]], axis=1)
    hidden, activate_back = jax.vjp(activate, gate, upper)
    hidden_low = hidden.astype(LOW)
    grad_down = dot(dy_all, hidden_low, (0, 0)).astype(LOW)
    down_sum = lax.psum_scatter(grad_down, ("dp", "x"), scatter_dimension=0, tiled=True)
    grad_hidden = dot(dy_all, down_full, (1, 0))
    grad_gate, grad_upper = activate_back(grad_hidden)
    grad_gateup_low = jnp.concatenate(
        [grad_gate[:, :MAIN], grad_upper[:, :MAIN], grad_gate[:, MAIN:], grad_upper[:, MAIN:]], axis=1
    ).astype(LOW)
    norm_part_two = dot(grad_gateup_low, gateup_full, (1, 1)).astype(LOW)
    grad_gateup = dot(normed_two, grad_gateup_low, (0, 0)).astype(LOW)
    gateup_sum = lax.psum_scatter(grad_gateup, ("dp", "x"), scatter_dimension=0, tiled=True)
    normed_grad_two = reduce_z(norm_part_two, 11)
    feed_part = dot(hidden_low, down_full, (1, 1)).astype(LOW)
    output = residual + reduce_z(feed_part, 12)
    grad_scale_two = jnp.sum(normed_grad_two * unit_two, axis=0)
    grad_residual = cotangent + rms_back(normed_grad_two, gain_two, unit_two, inverse_two)

    grad_attn = gather_z(grad_residual.astype(LOW), 13)
    grad_out = dot(grad_attn, attended_slice, (0, 0)).astype(LOW)
    grad_att_slice = dot(grad_attn, out_full, (1, 0)).astype(LOW).reshape(RING, BLOCK, 320)
    grad_att_low = whole_heads(exchange_z(grad_att_slice, 14)).reshape(BLOCK, head_count, HD)
    scores = jnp.einsum("hcd,kd->hck", query_low, key_rows, preferred_element_type=F32)
    probs = jnp.where(visible[None], jnp.exp(scores - log_total), 0.0)
    prob_low = probs.astype(LOW)
    grad_probs = jnp.einsum("chd,kd->hck", grad_att_low, value_rows, preferred_element_type=F32)
    delta = jnp.sum(probs * grad_probs, axis=-1, keepdims=True)
    grad_scores_low = (probs * (grad_probs - delta)).astype(LOW)
    grad_query = jnp.einsum("hck,kd->chd", grad_scores_low, key_rows, preferred_element_type=F32)
    grad_keys = jnp.einsum("hck,hcd->kd", grad_scores_low, query_low, preferred_element_type=F32)
    grad_values = jnp.einsum("hck,chd->kd", prob_low, grad_att_low, preferred_element_type=F32)
    pair = jnp.stack([grad_keys, grad_values]).astype(LOW)
    mine = lax.dynamic_index_in_dim(pair, core, 0, keepdims=False)
    theirs = swap_cores(lax.dynamic_index_in_dim(pair, 1 - core, 0, keepdims=False), 15)
    both = (mine.astype(F32) + theirs.astype(F32)).astype(LOW)
    grad_kv = reduce_plane(both, ("x", "z"), 16)
    grad_kv_low = jnp.where(core == 0, rotate(grad_kv, positions, -1.0), grad_kv).astype(LOW)
    grad_query_low = rotate(grad_query * HD ** (-0.5), positions, -1.0).astype(LOW)
    grad_qkv = jnp.concatenate(
        [head_quarters(grad_query_low.reshape(BLOCK, -1)), grad_kv_low.reshape(BLOCK, RING, TAIL).transpose(1, 0, 2)],
        axis=2,
    )
    grad_qkv_slice = exchange_z(grad_qkv, 17).reshape(-1, 384)
    norm_part_one = dot(grad_qkv_slice, qkv_full, (1, 1)).astype(LOW)
    normed_grad_one = reduce_z(norm_part_one, 18)
    grad_qkv_w = dot(normed_one, grad_qkv_slice, (0, 0)).astype(LOW)
    grad_scale_one = jnp.sum(normed_grad_one * unit_one, axis=0)
    grad_tokens = grad_residual + rms_back(normed_grad_one, gain_one, unit_one, inverse_one)

    grad_scales = jnp.stack([grad_scale_one, grad_scale_two], axis=1).astype(LOW)
    attn_grads = jnp.concatenate([grad_qkv_w, grad_out, pad_to(grad_scales, 1, 64)], axis=1)
    attn_sum = reduce_plane(attn_grads, ("dp", "x"), 19).astype(LOW)

    def to_owners(rows, ident):
        rows = pad_to(rows.reshape(RING, OWN, -1), 1, PAD)
        return exchange_z(rows, ident)[:, :OWN].astype(F32)

    down_shard = whole(to_owners(down_sum, 20)).T
    gateup_shard = to_owners(gateup_sum, 21)
    gateup_shard = jnp.concatenate(
        [
            gateup_shard[..., : 2 * MAIN].reshape(RING, OWN, 2, MAIN),
            gateup_shard[..., 2 * MAIN :].reshape(RING, OWN, 2, TAIL),
        ],
        axis=3,
    ).transpose(1, 2, 0, 3).reshape(OWN, 2, -1)
    attn_shard = to_owners(attn_sum, 22)
    query_shard = whole_heads(attn_shard[..., :320])
    kv_half = whole(attn_shard[..., 320:384])
    out_shard = whole_heads(attn_shard[..., 384:704]).T
    scale_grads = jnp.sum(attn_shard[..., 704:706], axis=0).T
    kv_other = swap_cores(pad_to(kv_half, 0, PAD).astype(LOW), 23)[:OWN].astype(F32)
    keyvalue_shard = jnp.stack(
        [jnp.where(core == 0, kv_half, kv_other), jnp.where(core == 0, kv_other, kv_half)], axis=1
    )

    matrix_rate = 2.0 * D ** (-0.5)
    out_rate = 2.0 * out_fan_in(seq_length) ** (-0.5)
    down_rate = 2.0 * (FF // 2) ** (-0.5)
    triples = [
        adam_update(w_query, query_shard, first_query, second_query, matrix_rate, weight_decay),
        adam_update(
            w_keyvalue, keyvalue_shard, first_keyvalue, second_keyvalue, matrix_rate, weight_decay
        ),
        adam_update(w_out, out_shard, first_out, second_out, out_rate, weight_decay),
        adam_update(w_gateup, gateup_shard, first_gateup, second_gateup, matrix_rate, weight_decay),
        adam_update(w_down, down_shard, first_down, second_down, down_rate, weight_decay),
        adam_update(norm_scales, scale_grads, first_scales, second_scales, gain_rate, 0.0),
    ]
    return (output, grad_tokens, *(triple[i] for i in range(3) for triple in triples))


def solution(mesh):
    split = Mesh(
        mesh.devices.reshape(RING, RING, RING, 2), ("dp", "x", "z", "tensor")
    )
    rows = ("dp", "x", "z")
    matrices = (
        P(rows, "tensor"),
        P(rows, None, None),
        P("tensor", rows),
        P(rows, None, "tensor"),
        P("tensor", rows),
        P(None, rows),
    )
    in_specs = (P(rows, None), P(rows, None), *matrices, *matrices, *matrices)
    out_specs = in_specs
    return jax.shard_map(
        per_device, mesh=split, in_specs=in_specs, out_specs=out_specs, check_vma=False
    )
```

```python
import jax
import jax.numpy as jnp
from jax import lax
from jax.experimental import pallas as pl
from jax.experimental.pallas import tpu as pltpu
from jax.sharding import Mesh
from jax.sharding import PartitionSpec as P

D = 2560
H = 10
HD = 256
FF = 7680
WINDOW = 2048
STEP = 10

eps_norm = 1e-06
masked_fill = -1e30
first_decay = 0.9
second_decay = 0.95
adam_eps = 1e-08
weight_decay = 0.1
gain_rate = 0.2

MESH = pl.DeviceIdType.MESH
LOW = jnp.bfloat16
F32 = jnp.float32
RING = 4
BLOCK = 160
HALF = BLOCK // 2
PART = 48
OWN = 40
PAD = 48
MAIN = 896
TAIL = 64


def step(axis, distance):
    return lax.rem(lax.axis_index(axis) + (RING + distance), RING)


def sibling():
    return {"tensor": 1 - lax.axis_index("tensor")}


def greet(peers):
    barrier = pltpu.get_barrier_semaphore()
    for peer in peers:
        pl.semaphore_signal(barrier, inc=1, device_id=peer, device_id_type=MESH)
    pl.semaphore_wait(barrier, len(peers))


def dot(left_side, right_side, contract):
    return lax.dot_general(
        left_side, right_side, ((contract[:1], contract[1:]), ((), ())), preferred_element_type=F32
    )


class Mover:
    def __init__(self, send_sem, recv_sem):
        self.send_sem, self.recv_sem, self.pending = send_sem, recv_sem, []

    def copy(self, src, dst, peer):
        index = len(self.pending)
        one = pltpu.make_async_remote_copy(
            src_ref=src,
            dst_ref=dst,
            send_sem=self.send_sem.at[index],
            recv_sem=self.recv_sem.at[index],
            device_id=peer,
            device_id_type=MESH,
        )
        one.start()
        self.pending.append(one)
        return one

    def finish(self):
        for one in self.pending:
            one.wait_send()


def advance(steps):
    next(steps, None)


def plane_peers(axes):
    return [{axis: step(axis, d)} for axis in axes for d in (-1, 1)]


def swap_kernel(x_ref, o_ref, send_sem, recv_sem):
    greet([sibling()])
    mover = Mover(send_sem, recv_sem)
    mover.copy(x_ref, o_ref, sibling()).wait_recv()
    mover.finish()


def swap_cores(x, ident):
    return pl.pallas_call(
        swap_kernel,
        out_shape=jax.ShapeDtypeStruct(x.shape, x.dtype),
        in_specs=[pl.BlockSpec(memory_space=pltpu.VMEM)],
        out_specs=pl.BlockSpec(memory_space=pltpu.VMEM),
        scratch_shapes=[pltpu.SemaphoreType.DMA((1,)), pltpu.SemaphoreType.DMA((1,))],
        compiler_params=pltpu.CompilerParams(collective_id=ident, has_side_effects=True),
    )(x)


def exchange_steps(mover, src, dst):
    me = lax.axis_index("z")
    copies = [
        mover.copy(src.at[step("z", d)], dst.at[me], {"z": step("z", d)}) for d in (2, 1, 3)
    ]
    yield
    for copy in copies:
        copy.wait_recv()


def core_rows():
    base = pl.multiple_of(lax.axis_index("tensor") * HALF, 16)
    return (
        pl.ds(base, HALF),
        pl.ds(base, PART),
        pl.ds(pl.multiple_of(base + PART, 16), HALF - PART),
        pl.ds(pl.multiple_of(HALF - base, 16), HALF),
    )


def gather_steps(mover, x, out):
    me, left, right, far = (step("z", d) for d in (0, -1, 1, 2))
    half, first, last, _ = core_rows()
    to_right = mover.copy(x.at[half], out.at[me, half], {"z": right})
    to_left = mover.copy(x.at[half], out.at[me, half], {"z": left})
    yield
    to_right.wait_recv()
    on_right = mover.copy(out.at[left, first], out.at[left, first], {"z": right})
    shares = [mover.copy(out.at[left, half], out.at[left, half], sibling())]
    to_left.wait_recv()
    on_left = mover.copy(out.at[right, last], out.at[right, last], {"z": left})
    shares.append(mover.copy(out.at[right, half], out.at[right, half], sibling()))
    yield
    on_right.wait_recv()
    on_left.wait_recv()
    shares.append(mover.copy(out.at[far, half], out.at[far, half], sibling()))
    yield
    for copy in shares:
        copy.wait_recv()


def cut_rows(which, cut):
    base, size = (0, cut) if which == 0 else (cut, BLOCK - cut)
    part = -(-size // 32) * 16
    return pl.ds(base, size), pl.ds(base, part), pl.ds(base + part, size - part)


def plane_gather_steps(mover, axes, x, out, cut=HALF, order=(0, 1), share=False):
    a, b = (lax.axis_index(axis) for axis in axes)
    state = {}
    for which, axis in enumerate(axes):
        rows = cut_rows(which, cut)[0]
        place = (lambda i, r: out.at[i, b, r]) if which == 0 else (lambda i, r: out.at[a, i, r])
        me = (a, b)[which]
        to_right = mover.copy(x.at[rows], place(me, rows), {axis: step(axis, 1)})
        to_left = mover.copy(x.at[rows], place(me, rows), {axis: step(axis, -1)})
        state[which] = (axis, place, to_right, to_left)
    yield
    passed = {}
    for which in order:
        axis, place, to_right, to_left = state[which]
        _, first, last = cut_rows(which, cut)
        left, right = step(axis, -1), step(axis, 1)
        to_right.wait_recv()
        on_right = mover.copy(place(left, first), place(left, first), {axis: right})
        to_left.wait_recv()
        on_left = mover.copy(place(right, last), place(right, last), {axis: left})
        passed[which] = (on_right, on_left)
    yield
    state = {}
    shares = []

    def give(piece):
        if share:
            shares.append(mover.copy(piece, piece, sibling()))

    for which in order:
        axis, other = axes[which], axes[1 - which]
        rows = cut_rows(which, cut)[0]
        if which == 0:
            place = lambda i, lo, n, rows=rows: out.at[pl.ds(lo, n), i, rows]
        else:
            place = lambda i, lo, n, rows=rows: out.at[i, pl.ds(lo, n), rows]
        me = (b, a)[which]
        for copy in passed[which]:
            copy.wait_recv()
        to_right = mover.copy(place(me, 0, 4), place(me, 0, 4), {other: step(other, 1)})
        to_left = mover.copy(place(me, 0, 4), place(me, 0, 4), {other: step(other, -1)})
        give(place(me, 0, 4))
        state[which] = (other, place, to_right, to_left)
        yield
    ends = []
    for which in order:
        other, place, to_right, to_left = state[which]
        left, right = step(other, -1), step(other, 1)
        to_right.wait_recv()
        ends.append(mover.copy(place(left, 0, 2), place(left, 0, 2), {other: right}))
        give(place(left, 0, 4))
        to_left.wait_recv()
        ends.append(mover.copy(place(right, 2, 2), place(right, 2, 2), {other: left}))
        give(place(right, 0, 4))
        yield
    for copy in ends:
        copy.wait_recv()
    for which in order:
        other, place, _, _ = state[which]
        give(place(step(other, 2), 0, 4))
    for copy in shares:
        copy.wait_recv()


def lanes(shape):
    return lax.broadcasted_iota(jnp.int32, shape, len(shape) - 1)


def turn(values, cos, sin):
    return values * cos + pltpu.roll(values, 64, 1) * sin


def whole_rows(blocks, stage, dst):
    for i in range(RING):
        stage[i * OWN : (i + 1) * OWN] = blocks[i].astype(F32)[:OWN]
    dst[...] = stage[...].astype(LOW)


def first_kernel(
    attn_rows,
    feed_rows,
    tokens,
    dy,
    cos_ref,
    sin_ref,
    cos_kv,
    sin_kv,
    feed_full,
    attn_full,
    normed_one,
    dy_all,
    query,
    keyvalue,
    log_total,
    att_slice,
    residual,
    normed_two,
    attended,
    gain_ref,
    send_sem,
    recv_sem,
    local_sem,
    attn_got,
    attn_mine,
    attn_stage,
    feed_got,
    feed_mine,
    feed_stage,
    unit_low,
    unit_all,
    qkv_send,
    qkv_got,
    kv_own,
    scores,
    att_send,
    part,
    other,
    total,
    part_a,
    part_b,
    from_left,
    from_right,
    normed_low,
):
    z, x, y, core = (lax.axis_index(axis) for axis in ("z", "x", "dp", "tensor"))
    left, right, far = (step("z", d) for d in (-1, 1, 2))
    half, _, _, their_half = core_rows()
    plane = ("dp", "x")
    greet(
        [{"z": step("z", d)} for d in (1, 2, 3)] + plane_peers(("dp", "x")) + [sibling()]
    )
    mover = Mover(send_sem, recv_sem)

    attn_swap = exchange_steps(mover, attn_rows, attn_got)
    advance(attn_swap)
    values = tokens[...]
    unit = values * lax.rsqrt(jnp.mean(values * values, axis=-1, keepdims=True) + eps_norm)
    unit_low[...] = unit.astype(LOW)
    unit_gather = gather_steps(mover, unit_low, unit_all)
    advance(unit_gather)
    feed_swap = exchange_steps(mover, feed_rows, feed_got)
    advance(feed_swap)
    unit_all[z] = unit_low[...]
    attn_got[z] = attn_rows[z]
    advance(attn_swap)
    whole_rows(attn_got, attn_stage, attn_mine)
    attn_gather = plane_gather_steps(mover, plane, attn_mine, attn_full)
    advance(attn_gather)
    attn_full[y, x] = attn_mine[...]
    advance(unit_gather)
    advance(attn_gather)
    advance(attn_gather)
    advance(attn_gather)
    feed_got[z] = feed_rows[z]
    advance(unit_gather)
    advance(feed_swap)
    whole_rows(feed_got, feed_stage, feed_mine)
    feed_own = pltpu.make_async_copy(feed_mine, feed_full.at[y, x], local_sem.at[0])
    feed_own.start()
    advance(attn_gather)
    advance(attn_gather)
    feed_gather = plane_gather_steps(mover, plane, feed_mine, feed_full, cut=64, order=(1, 0))
    advance(feed_gather)
    dy_gather = gather_steps(mover, dy, dy_all)
    advance(dy_gather)
    dy_own = pltpu.make_async_copy(dy, dy_all.at[z], local_sem.at[1])
    dy_own.start()
    advance(unit_gather)
    advance(attn_gather)

    scale_cols = attn_full[:, :, :, 640:768].reshape(D, 128)
    pick = (lanes((8, 128)) == 64 + lax.broadcasted_iota(jnp.int32, (8, 128), 0)).astype(LOW)
    gain_ref[...] = 1.0 + dot(pick, scale_cols, (1, 1))
    qkv_weight = attn_full[:, :, :, :384].reshape(D, 384)
    copies = []
    for d in (2, 1, 3, 0):
        block = step("z", d)
        normed = (unit_all[block].astype(F32) * gain_ref[0:1, :]).astype(LOW)
        normed_one[block] = normed
        qkv_send[block] = dot(normed, qkv_weight, (1, 0)).astype(LOW)
        if d:
            copies.append(mover.copy(qkv_send.at[block], qkv_got.at[z], {"z": block}))
    qkv_got[z] = qkv_send[z]
    advance(feed_gather)
    feed_own.wait()
    for copy in copies:
        copy.wait_recv()
    low_lanes = lanes((BLOCK, 128)) < TAIL
    cos, sin = cos_ref[...], sin_ref[...]

    def joined(i, offset):
        one, two = (qkv_got[i + k, :, 256:384].astype(F32) for k in (0, 1))
        if offset == 0:
            return jnp.where(low_lanes, one, pltpu.roll(two, TAIL, 1))
        return jnp.where(low_lanes, pltpu.roll(one, TAIL, 1), two)

    kv_own[:, :128] = turn(joined(0, 1), cos_kv[...], sin_kv[...]).astype(LOW)
    kv_own[:, 128:] = joined(2, 1).astype(LOW)
    kv_mine = keyvalue.at[core]
    kv_gather = plane_gather_steps(mover, ("x", "z"), kv_own, kv_mine, share=True)
    advance(kv_gather)
    keyvalue[core, x, z] = kv_own[...]
    scale = HD ** (-0.5)
    for h in range(4):
        first = qkv_got[h, :, :128].astype(F32)
        query[h, :, :128] = (turn(first, cos, sin) * scale).astype(LOW)
        query[h, :, 128:] = (qkv_got[h, :, 128:256].astype(F32) * scale).astype(LOW)
    query[4, :, :128] = (turn(joined(0, 0), cos, sin) * scale).astype(LOW)
    query[4, :, 128:] = (joined(2, 0) * scale).astype(LOW)
    advance(kv_gather)
    advance(feed_gather)
    advance(kv_gather)
    advance(kv_gather)
    advance(kv_gather)
    advance(kv_gather)
    advance(feed_gather)
    advance(dy_gather)
    advance(kv_gather)

    start = (x * RING + z) * BLOCK
    chunk = RING * BLOCK

    def one_head(h, carry):
        queries = query[h]
        top = jnp.full((BLOCK, 1), masked_fill, F32)
        for k in range(RING):
            rows = keyvalue[0, k].reshape(chunk, HD)
            tile = dot(queries, rows, (1, 1))
            gap = (start - k * chunk) + (
                lax.broadcasted_iota(jnp.int32, tile.shape, 0) - lanes(tile.shape)
            )
            tile = jnp.where((gap >= 0) & (gap < WINDOW), tile, masked_fill)
            scores[:, k * chunk : (k + 1) * chunk] = tile
            top = jnp.maximum(top, jnp.max(tile, axis=-1, keepdims=True))
        sums = jnp.zeros((BLOCK, 1), F32)
        for k in range(RING):
            tile = jnp.exp(scores[:, k * chunk : (k + 1) * chunk] - top)
            scores[:, k * chunk : (k + 1) * chunk] = tile
            sums = sums + jnp.sum(tile, axis=-1, keepdims=True)
        inverse = 1.0 / sums
        result = jnp.zeros((BLOCK, HD), F32)
        for k in range(RING):
            low = (scores[:, k * chunk : (k + 1) * chunk] * inverse).astype(LOW)
            result = result + dot(low, keyvalue[1, k].reshape(chunk, HD), (1, 0))
        attended[h] = result
        log_total[h] = jnp.broadcast_to(top + jnp.log(sums), (BLOCK, 128))
        return carry

    lax.fori_loop(0, 5, one_head, 0)
    for j in range(RING):
        att_send[j, :, :256] = attended[j].astype(LOW)
        tile = attended[4, :, (j // 2) * 128 : (j // 2 + 1) * 128]
        tile = pltpu.roll(tile, TAIL, 1) if j % 2 else tile
        att_send[j, :, 256:] = jnp.where(low_lanes, tile, 0.0).astype(LOW)
    att_swap = exchange_steps(mover, att_send, att_slice)
    advance(att_swap)
    att_slice[z] = att_send[z]
    advance(dy_gather)
    advance(att_swap)

    out_weight = attn_full[:, :, :, 384:].reshape(D, 384)
    blocks = (far, right, left, z)
    shares = []
    for slot, block in enumerate(blocks):
        part[block] = dot(att_slice[block], out_weight, (1, 1)).astype(LOW)
        shares.append(mover.copy(part.at[block, their_half], other.at[slot], sibling()))

    def both(slot):
        return part[blocks[slot], half].astype(F32) + other[slot].astype(F32)

    shares[0].wait_recv()
    total[0] = both(0).astype(LOW)
    far_right = mover.copy(total.at[0, pl.ds(0, PART)], part_a, {"z": right})
    far_left = mover.copy(total.at[0, pl.ds(PART, HALF - PART)], part_b, {"z": left})
    shares[1].wait_recv()
    shares[2].wait_recv()
    far_right.wait_recv()
    summed = both(1)
    total[1, :PART] = (summed[:PART] + part_a[...].astype(F32)).astype(LOW)
    total[1, PART:] = summed[PART:].astype(LOW)
    to_right = mover.copy(total.at[1], from_left, {"z": right})
    far_left.wait_recv()
    summed = both(2)
    total[2, :PART] = summed[:PART].astype(LOW)
    total[2, PART:] = (summed[PART:] + part_b[...].astype(F32)).astype(LOW)
    to_left = mover.copy(total.at[2], from_right, {"z": left})
    shares[3].wait_recv()
    to_right.wait_recv()
    to_left.wait_recv()
    rows = tokens[half, :] + (
        both(3) + from_left[...].astype(F32) + from_right[...].astype(F32)
    )
    residual[half, :] = rows
    res_share = mover.copy(residual.at[half], residual.at[half], sibling())

    def normed_rows(rows):
        unit = rows * lax.rsqrt(jnp.mean(rows * rows, axis=-1, keepdims=True) + eps_norm)
        return (unit * gain_ref[1:2, :]).astype(LOW)

    normed_low[half, :] = normed_rows(rows)
    normed_gather = gather_steps(mover, normed_low, normed_two)
    advance(normed_gather)
    res_share.wait_recv()
    normed_low[their_half, :] = normed_rows(residual[their_half, :])
    normed_two[z] = normed_low[...]
    advance(normed_gather)
    advance(feed_gather)
    advance(normed_gather)
    advance(feed_gather)
    advance(dy_gather)
    advance(normed_gather)
    advance(feed_gather)
    dy_own.wait()
    mover.finish()


def run_first(*operands):
    out = {
        "feed_full": ((RING, RING, BLOCK, 2944), LOW, pl.ANY),
        "attn_full": ((RING, RING, BLOCK, 768), LOW, pltpu.VMEM),
        "normed_one": ((RING, BLOCK, D), LOW, pltpu.VMEM),
        "dy_all": ((RING, BLOCK, D), LOW, pl.ANY),
        "query": ((5, BLOCK, HD), LOW, pltpu.VMEM),
        "keyvalue": ((2, RING, RING, BLOCK, HD), LOW, pltpu.VMEM),
        "log_total": ((5, BLOCK, 128), F32, pltpu.VMEM),
        "att_slice": ((RING, BLOCK, 384), LOW, pltpu.VMEM),
        "residual": ((BLOCK, D), F32, pltpu.VMEM),
        "normed_two": ((RING, BLOCK, D), LOW, pltpu.VMEM),
        "attended": ((5, BLOCK, HD), F32, pltpu.VMEM),
        "gains": ((8, D), F32, pltpu.VMEM),
    }
    spaces = [pltpu.VMEM, pltpu.VMEM, pltpu.VMEM, pl.ANY] + [pltpu.VMEM] * 4
    copies = 120
    results = pl.pallas_call(
        first_kernel,
        out_shape=[jax.ShapeDtypeStruct(shape, kind) for shape, kind, _ in out.values()],
        in_specs=[pl.BlockSpec(memory_space=space) for space in spaces],
        out_specs=[pl.BlockSpec(memory_space=space) for _, _, space in out.values()],
        scratch_shapes=[
            pltpu.SemaphoreType.DMA((copies,)),
            pltpu.SemaphoreType.DMA((copies,)),
            pltpu.SemaphoreType.DMA((2,)),
            pltpu.VMEM((RING, PAD, 768), LOW),
            pltpu.VMEM((BLOCK, 768), LOW),
            pltpu.VMEM((BLOCK, 768), F32),
            pltpu.VMEM((RING, PAD, 2944), LOW),
            pltpu.VMEM((BLOCK, 2944), LOW),
            pltpu.VMEM((BLOCK, 2944), F32),
            pltpu.VMEM((BLOCK, D), LOW),
            pltpu.VMEM((RING, BLOCK, D), LOW),
            pltpu.VMEM((RING, BLOCK, 384), LOW),
            pltpu.VMEM((RING, BLOCK, 384), LOW),
            pltpu.VMEM((BLOCK, HD), LOW),
            pltpu.VMEM((BLOCK, RING * RING * BLOCK), F32),
            pltpu.VMEM((RING, BLOCK, 384), LOW),
            pltpu.VMEM((RING, BLOCK, D), LOW),
            pltpu.VMEM((4, HALF, D), LOW),
            pltpu.VMEM((3, HALF, D), LOW),
            pltpu.VMEM((PART, D), LOW),
            pltpu.VMEM((HALF - PART, D), LOW),
            pltpu.VMEM((HALF, D), LOW),
            pltpu.VMEM((HALF, D), LOW),
            pltpu.VMEM((BLOCK, D), LOW),
        ],
        compiler_params=pltpu.CompilerParams(
            collective_id=1, has_side_effects=True, vmem_limit_bytes=60 * 1024 * 1024
        ),
    )(*operands)
    return dict(zip(out, results, strict=True))


def plane_reduce_steps(mover, axes, g, bufs, res, loads=None):
    far, side, near, far_two, side_two = bufs
    places = [lax.axis_index(axis) for axis in axes]

    def block(which, i, lo, n):
        rows = pl.ds(which * HALF, HALF)
        return g.at[i, pl.ds(lo, n), rows] if which == 0 else g.at[pl.ds(lo, n), i, rows]

    locals_ = []

    def load(src, dst):
        locals_.append(pltpu.make_async_copy(src, dst, loads.at[len(locals_)]))
        locals_[-1].start()
        return locals_[-1]

    first, sides, wanted = [], [], []
    for which, axis in enumerate(axes):
        right, left = step(axis, 1), step(axis, -1)
        far_place = step(axis, 2)
        first.append(
            (
                mover.copy(block(which, far_place, 0, 2), far.at[which, pl.ds(0, 2)], {axis: right}),
                mover.copy(block(which, far_place, 2, 2), far.at[which, pl.ds(2, 2)], {axis: left}),
            )
        )
        if loads is not None:
            wanted.append(
                (
                    load(block(which, right, 0, 2), near.at[which, 0]),
                    load(block(which, left, 2, 2), near.at[which, 1]),
                )
            )
    for which, axis in enumerate(axes):
        right, left = step(axis, 1), step(axis, -1)
        sides.append(
            [
                mover.copy(block(which, right, 2, 2), side.at[which, 0, pl.ds(2, 2)], {axis: right}),
                mover.copy(block(which, left, 0, 2), side.at[which, 1, pl.ds(0, 2)], {axis: left}),
            ]
        )
    yield
    owned = []
    for which, axis in enumerate(axes):
        for k, (d, lo) in enumerate(((1, 0), (-1, 2))):
            first[which][k].wait_recv()
            if loads is not None:
                wanted[which][k].wait()
                term = near[which, k]
            else:
                term = block(which, step(axis, d), lo, 2)[...]
            near[which, k] = (term.astype(F32) + far[which, lo : lo + 2].astype(F32)).astype(LOW)
            sides[which].append(
                mover.copy(near.at[which, k], side.at[which, k, pl.ds(lo, 2)], {axis: step(axis, d)})
            )
        if loads is not None:
            owned.append(load(block(which, places[which], 0, 4), far.at[which]))
    yield

    def summed(which, i):
        if loads is not None:
            term = far[which, i]
        else:
            rows = pl.ds(which * HALF, HALF)
            me = places[which]
            term = (g[me, i, rows] if which == 0 else g[i, me, rows])
        return (
            term.astype(F32) + side[which, 0, i].astype(F32) + side[which, 1, i].astype(F32)
        )

    second = []
    for which, axis in enumerate(axes):
        other = axes[1 - which]
        right, left = {other: step(other, 1)}, {other: step(other, -1)}
        for copy in sides[which]:
            copy.wait_recv()
        if loads is not None:
            owned[which].wait()
        far_two[which, 0] = summed(which, step(other, 2)).astype(LOW)
        upper, lower = pl.ds(0, PART), pl.ds(PART, HALF - PART)
        second.append(
            (
                mover.copy(far_two.at[which, 0, upper], far_two.at[which, 1, upper], right),
                mover.copy(far_two.at[which, 0, lower], far_two.at[which, 1, lower], left),
            )
        )
    yield
    last = []
    for which, axis in enumerate(axes):
        other = axes[1 - which]
        right, left = step(other, 1), step(other, -1)
        total = summed(which, right)
        second[which][0].wait_recv()
        side_two[which, 0, :PART] = (
            total[:PART] + far_two[which, 1, :PART].astype(F32)
        ).astype(LOW)
        side_two[which, 0, PART:] = total[PART:].astype(LOW)
        last.append(mover.copy(side_two.at[which, 0], side_two.at[which, 2], {other: right}))
        total = summed(which, left)
        second[which][1].wait_recv()
        side_two[which, 1, :PART] = total[:PART].astype(LOW)
        side_two[which, 1, PART:] = (
            total[PART:] + far_two[which, 1, PART:].astype(F32)
        ).astype(LOW)
        last.append(mover.copy(side_two.at[which, 1], side_two.at[which, 3], {other: left}))
    yield
    for which, axis in enumerate(axes):
        other = axes[1 - which]
        last[2 * which].wait_recv()
        last[2 * which + 1].wait_recv()
        res[which * HALF : (which + 1) * HALF] = (
            summed(which, lax.axis_index(other))
            + side_two[which, 2].astype(F32)
            + side_two[which, 3].astype(F32)
        )


def plane_reduce_scratch(columns):
    return [
        pltpu.VMEM((2, 4, HALF, columns), LOW),
        pltpu.VMEM((2, 2, 4, HALF, columns), LOW),
        pltpu.VMEM((2, 2, 2, HALF, columns), LOW),
        pltpu.VMEM((2, 2, HALF, columns), LOW),
        pltpu.VMEM((2, 4, HALF, columns), LOW),
        pltpu.VMEM((BLOCK, columns), F32),
    ]


def reduce_steps(mover, part, mine, bufs, out, make=None):
    other, total, part_a, part_b, from_left, from_right = bufs
    _, _, _, their_half = core_rows()
    me, left, right, far = (step("z", d) for d in (0, -1, 1, 2))
    blocks = (far, right, left, me)
    shares = []
    for slot, block in enumerate(blocks):
        if make is not None:
            make(block)
        shares.append(mover.copy(part.at[block, their_half], other.at[slot], sibling()))
    yield

    def both(slot):
        return mine(blocks[slot]).astype(F32) + other[slot].astype(F32)

    shares[0].wait_recv()
    total[0] = both(0).astype(LOW)
    far_right = mover.copy(total.at[0, pl.ds(0, PART)], part_a, {"z": right})
    far_left = mover.copy(total.at[0, pl.ds(PART, HALF - PART)], part_b, {"z": left})
    yield
    shares[1].wait_recv()
    shares[2].wait_recv()
    far_right.wait_recv()
    summed = both(1)
    total[1, :PART] = (summed[:PART] + part_a[...].astype(F32)).astype(LOW)
    total[1, PART:] = summed[PART:].astype(LOW)
    to_right = mover.copy(total.at[1], from_left, {"z": right})
    far_left.wait_recv()
    summed = both(2)
    total[2, :PART] = summed[:PART].astype(LOW)
    total[2, PART:] = (summed[PART:] + part_b[...].astype(F32)).astype(LOW)
    to_left = mover.copy(total.at[2], from_right, {"z": left})
    yield
    shares[3].wait_recv()
    to_right.wait_recv()
    to_left.wait_recv()
    out[...] = both(3) + from_left[...].astype(F32) + from_right[...].astype(F32)


def reduce_scratch():
    return [
        pltpu.VMEM((4, HALF, D), LOW),
        pltpu.VMEM((3, HALF, D), LOW),
        pltpu.VMEM((PART, D), LOW),
        pltpu.VMEM((HALF - PART, D), LOW),
        pltpu.VMEM((HALF, D), LOW),
        pltpu.VMEM((HALF, D), LOW),
    ]


def spread_rows(res, dst):
    for i in range(RING):
        rows = res[i * OWN : (i + 1) * OWN]
        dst[i] = jnp.concatenate([rows, jnp.zeros((PAD - OWN, rows.shape[1]), F32)]).astype(LOW)


def third_kernel(
    norm_part,
    feed_part,
    gateup_grads,
    cotangent,
    residual,
    gain_ref,
    attn_full,
    att_slice,
    query,
    keyvalue,
    log_total,
    attended,
    cos_ref,
    sin_ref,
    grad_rows,
    grad_out,
    grad_query,
    grad_kv,
    gateup_rows,
    output,
    send_sem,
    recv_sem,
    local_sem,
    norm_mine,
    feed_mine,
    grad_half,
    out_half,
    da_low,
    da_all,
    datt_send,
    datt_got,
    datt,
    delta,
    ds_all,
    p_all,
    dq,
    kv_pair,
    kv_in,
    *bufs,
):
    z, core = lax.axis_index("z"), lax.axis_index("tensor")
    x = lax.axis_index("x")
    half, _, _, their_half = core_rows()
    norm_bufs, out_bufs, rows_bufs = bufs[:6], bufs[6:12], bufs[12:17]
    rows_res = bufs[17]
    greet([{"z": step("z", d)} for d in (1, 2, 3)] + plane_peers(("dp", "x")) + [sibling()])
    mover = Mover(send_sem, recv_sem)
    norm_load = pltpu.make_async_copy(norm_part.at[:, half], norm_mine, local_sem.at[8])
    norm_load.start()
    feed_load = pltpu.make_async_copy(feed_part.at[:, half], feed_mine, local_sem.at[9])
    feed_load.start()
    norm_sum = reduce_steps(mover, norm_part, lambda i: norm_mine[i], norm_bufs, grad_half)
    advance(norm_sum)
    rows_sum = plane_reduce_steps(
        mover, ("dp", "x"), gateup_grads, rows_bufs, rows_res, loads=local_sem
    )
    advance(rows_sum)
    norm_load.wait()
    advance(norm_sum)
    advance(norm_sum)
    advance(norm_sum)

    rows = residual[half, :]
    inverse = lax.rsqrt(jnp.mean(rows * rows, axis=-1, keepdims=True) + eps_norm)
    unit = rows * inverse
    scaled = grad_half[...] * gain_ref[1:2, :]
    grad = cotangent[half, :] + inverse * (
        scaled - unit * jnp.mean(scaled * unit, axis=-1, keepdims=True)
    )
    grad_rows[...] = grad
    da_low[half, :] = grad.astype(LOW)
    da_share = mover.copy(da_low.at[half], da_low.at[half], sibling())
    da_gather = gather_steps(mover, da_low, da_all)
    advance(da_gather)
    feed_sum = reduce_steps(mover, feed_part, lambda i: feed_mine[i], out_bufs, out_half)
    da_share.wait_recv()
    da_all[z] = da_low[...]
    out_weight = attn_full[:, :, :, 384:].reshape(D, 384)
    datt_got[z] = dot(da_all[z], out_weight, (1, 0)).astype(LOW)
    advance(da_gather)
    advance(rows_sum)
    advance(da_gather)
    advance(da_gather)
    copies = []
    for d in (2, 1, 3):
        block = step("z", d)
        datt_send[block] = dot(da_all[block], out_weight, (1, 0)).astype(LOW)
        copies.append(mover.copy(datt_send.at[block], datt_got.at[z], {"z": block}))
    advance(feed_sum)
    slices = att_slice[...].reshape(RING * BLOCK, 384)
    wide = RING * BLOCK
    for i in range(RING):
        left_side = da_all[:, :, i * wide : (i + 1) * wide].reshape(wide, wide)
        grad_out[i] = dot(left_side, slices, (0, 0)).astype(LOW).reshape(RING, BLOCK, 384)
    for copy in copies:
        copy.wait_recv()
    feed_load.wait()
    advance(feed_sum)

    low_lanes = lanes((BLOCK, 128)) < TAIL
    for h in range(4):
        datt[h] = datt_got[h, :, :HD]
    for k in range(2):
        one, two = (datt_got[2 * k + i, :, HD:].astype(F32) for i in range(2))
        datt[4, :, k * 128 : (k + 1) * 128] = jnp.where(
            low_lanes, one, pltpu.roll(two, TAIL, 1)
        ).astype(LOW)
    for h in range(5):
        delta[h] = jnp.broadcast_to(
            jnp.sum(datt[h].astype(F32) * attended[h], axis=-1, keepdims=True), (BLOCK, 128)
        )
        dq[h] = jnp.zeros((BLOCK, HD), F32)
    start = (x * RING + z) * BLOCK
    chunk = RING * BLOCK

    def one_chunk(k, carry):
        keys = keyvalue[0, k].reshape(chunk, HD)
        values = keyvalue[1, k].reshape(chunk, HD)
        shape = (BLOCK, chunk)
        gap = (start - k * chunk) + (lax.broadcasted_iota(jnp.int32, shape, 0) - lanes(shape))
        visible = (gap >= 0) & (gap < WINDOW)

        def one_head(h, carry):
            scores = dot(query[h], keys, (1, 1))
            probs = jnp.where(visible, jnp.exp(scores - log_total[h, :, :1]), 0.0)
            grads = dot(datt[h], values, (1, 1))
            low = (probs * (grads - delta[h, :, :1])).astype(LOW)
            ds_all[h] = low
            p_all[h] = probs.astype(LOW)
            dq[h] = dq[h] + dot(low, keys, (1, 0))
            return carry

        lax.fori_loop(0, 5, one_head, 0)
        queries = query[...].reshape(5 * BLOCK, HD)
        outer = datt[...].reshape(5 * BLOCK, HD)
        kv_pair[0, k] = dot(ds_all[...].reshape(5 * BLOCK, chunk), queries, (0, 0)).astype(LOW).reshape(RING, BLOCK, HD)
        kv_pair[1, k] = dot(p_all[...].reshape(5 * BLOCK, chunk), outer, (0, 0)).astype(LOW).reshape(RING, BLOCK, HD)
        return carry

    lax.fori_loop(0, RING, one_chunk, 0)
    kv_swap = mover.copy(kv_pair.at[1 - core], kv_in, sibling())
    advance(feed_sum)
    advance(rows_sum)
    cos, sin = cos_ref[...], sin_ref[...]
    scale = HD ** (-0.5)
    for h in range(5):
        grad_query[h, :, :128] = turn(dq[h, :, :128] * scale, cos, -sin).astype(LOW)
        grad_query[h, :, 128:] = (dq[h, :, 128:] * scale).astype(LOW)
    kv_swap.wait_recv()
    grad_kv[...] = (kv_pair[core].astype(F32) + kv_in[...].astype(F32)).astype(LOW)
    advance(rows_sum)
    advance(feed_sum)
    output[half, :] = residual[half, :] + out_half[...]
    out_share = mover.copy(output.at[half], output.at[half], sibling())
    advance(rows_sum)
    spread_rows(rows_res, gateup_rows)
    out_share.wait_recv()
    mover.finish()


def fourth_kernel(
    grad_kv,
    grad_query,
    gateup_rows,
    down_grads,
    grad_out,
    attn_full,
    normed_one,
    grad_rows,
    tokens,
    gain_ref,
    cos_kv,
    sin_kv,
    grad_tokens,
    gateup_got,
    down_got,
    out_got,
    qkv_got,
    send_sem,
    recv_sem,
    local_sem,
    grad_send,
    grad_got,
    kv_low,
    part,
    grad_half,
    grad_qkv,
    down_send,
    out_send,
    qkv_send,
    *bufs,
):
    z = lax.axis_index("z")
    half, _, _, _ = core_rows()
    plane = ("dp", "x")
    sum_bufs = bufs[:6]
    kv_bufs, down_bufs, out_bufs, qkv_bufs = (bufs[6 + 6 * i : 12 + 6 * i] for i in range(4))
    greet([{"z": step("z", d)} for d in (1, 2, 3)] + plane_peers(plane) + [sibling()])
    mover = Mover(send_sem, recv_sem)
    kv_sum = plane_reduce_steps(mover, ("x", "z"), grad_kv, kv_bufs[:5], kv_bufs[5])
    advance(kv_sum)
    out_sum = plane_reduce_steps(mover, plane, grad_out, out_bufs[:5], out_bufs[5])
    down_sum = plane_reduce_steps(
        mover, plane, down_grads, down_bufs[:5], down_bufs[5], loads=local_sem
    )
    for k in range(5):
        grad_send_block(k, grad_query, grad_send)
    advance(kv_sum)
    advance(out_sum)
    advance(kv_sum)
    advance(out_sum)
    advance(kv_sum)
    advance(kv_sum)
    kv_rows = kv_bufs[5]
    kv_low[:, :128] = turn(kv_rows[:, :128], cos_kv[...], -sin_kv[...])
    kv_low[:, 128:] = kv_rows[:, 128:]
    low_lanes = lanes((BLOCK, 128)) < TAIL
    for j in range(RING):
        place = slice((j // 2) * 128, (j // 2 + 1) * 128)
        one = grad_query[4, :, place].astype(F32)
        two = kv_low[:, place]
        if j % 2:
            one = pltpu.roll(one, TAIL, 1)
        else:
            two = pltpu.roll(two, TAIL, 1)
        grad_send[j, :, HD:] = jnp.where(low_lanes, one, two).astype(LOW)
    swap = exchange_steps(mover, grad_send, grad_got)
    advance(swap)
    grad_got[z] = grad_send[z]
    advance(down_sum)
    advance(out_sum)
    gateup_swap = exchange_steps(mover, gateup_rows, gateup_got)
    advance(swap)

    qkv_weight = attn_full[:, :, :, :384].reshape(D, 384)

    def make(block):
        part[block] = dot(grad_got[block], qkv_weight, (1, 1)).astype(LOW)

    norm_sum = reduce_steps(mover, part, lambda i: part[i, half], sum_bufs, grad_half, make)
    advance(norm_sum)
    slices = grad_got[...].reshape(RING * BLOCK, 384)
    wide = RING * BLOCK
    for i in range(RING):
        left_side = normed_one[:, :, i * wide : (i + 1) * wide].reshape(wide, wide)
        grad_qkv[i] = dot(left_side, slices, (0, 0)).astype(LOW).reshape(RING, BLOCK, 384)
        if i == 0:
            advance(norm_sum)
    qkv_sum = plane_reduce_steps(mover, plane, grad_qkv, qkv_bufs[:5], qkv_bufs[5])
    advance(qkv_sum)
    advance(norm_sum)
    advance(out_sum)
    advance(down_sum)
    advance(gateup_swap)
    gateup_got[z] = gateup_rows[z]
    advance(qkv_sum)
    advance(out_sum)
    spread_rows(out_bufs[5], out_send)
    out_swap = exchange_steps(mover, out_send, out_got)
    advance(out_swap)
    out_got[z] = out_send[z]
    advance(down_sum)
    advance(qkv_sum)
    advance(norm_sum)
    rows = tokens[half, :]
    inverse = lax.rsqrt(jnp.mean(rows * rows, axis=-1, keepdims=True) + eps_norm)
    unit = rows * inverse
    scaled = grad_half[...] * gain_ref[0:1, :]
    grad_tokens[half, :] = grad_rows[...] + inverse * (
        scaled - unit * jnp.mean(scaled * unit, axis=-1, keepdims=True)
    )
    share = mover.copy(grad_tokens.at[half], grad_tokens.at[half], sibling())
    advance(qkv_sum)
    advance(down_sum)
    advance(qkv_sum)
    spread_rows(qkv_bufs[5], qkv_send)
    qkv_swap = exchange_steps(mover, qkv_send, qkv_got)
    advance(qkv_swap)
    qkv_got[z] = qkv_send[z]
    advance(down_sum)
    spread_rows(down_bufs[5], down_send)
    down_swap = exchange_steps(mover, down_send, down_got)
    advance(down_swap)
    down_got[z] = down_send[z]
    for steps in (gateup_swap, out_swap, qkv_swap, down_swap):
        advance(steps)
    share.wait_recv()
    mover.finish()


def grad_send_block(h, grad_query, grad_send):
    if h < 4:
        grad_send[h, :, :HD] = grad_query[h]


def call(kernel, ident, copies, out, scratch, operands, spaces):
    results = pl.pallas_call(
        kernel,
        out_shape=[jax.ShapeDtypeStruct(shape, kind) for shape, kind in out.values()],
        in_specs=[pl.BlockSpec(memory_space=space) for space in spaces],
        out_specs=[pl.BlockSpec(memory_space=pltpu.VMEM) for _ in out],
        scratch_shapes=[
            pltpu.SemaphoreType.DMA((copies,)),
            pltpu.SemaphoreType.DMA((copies,)),
            pltpu.SemaphoreType.DMA((10,)),
            *scratch,
        ],
        compiler_params=pltpu.CompilerParams(
            collective_id=ident, has_side_effects=True, vmem_limit_bytes=60 * 1024 * 1024
        ),
    )(*operands)
    return dict(zip(out, results, strict=True))


def run_third(*operands):
    out = {
        "grad_rows": ((HALF, D), F32),
        "grad_out": ((RING, RING, BLOCK, 384), LOW),
        "grad_query": ((5, BLOCK, HD), LOW),
        "grad_kv": ((RING, RING, BLOCK, HD), LOW),
        "gateup_rows": ((RING, PAD, 2 * (MAIN + TAIL)), LOW),
        "output": ((BLOCK, D), F32),
    }
    scratch = [
        pltpu.VMEM((RING, HALF, D), LOW),
        pltpu.VMEM((RING, HALF, D), LOW),
        pltpu.VMEM((HALF, D), F32),
        pltpu.VMEM((HALF, D), F32),
        pltpu.VMEM((BLOCK, D), LOW),
        pltpu.VMEM((RING, BLOCK, D), LOW),
        pltpu.VMEM((RING, BLOCK, 384), LOW),
        pltpu.VMEM((RING, BLOCK, 384), LOW),
        pltpu.VMEM((5, BLOCK, HD), LOW),
        pltpu.VMEM((5, BLOCK, 128), F32),
        pltpu.VMEM((5, BLOCK, RING * BLOCK), LOW),
        pltpu.VMEM((5, BLOCK, RING * BLOCK), LOW),
        pltpu.VMEM((5, BLOCK, HD), F32),
        pltpu.VMEM((2, RING, RING, BLOCK, HD), LOW),
        pltpu.VMEM((RING, RING, BLOCK, HD), LOW),
        *reduce_scratch(),
        *reduce_scratch(),
        *plane_reduce_scratch(2 * (MAIN + TAIL)),
    ]
    spaces = [pl.ANY] * 3 + [pltpu.VMEM] * 11
    return call(third_kernel, 2, 90, out, scratch, operands, spaces)


def run_fourth(*operands):
    out = {
        "grad_tokens": ((BLOCK, D), F32),
        "gateup_got": ((RING, PAD, 2 * (MAIN + TAIL)), LOW),
        "down_got": ((RING, PAD, 1024), LOW),
        "out_got": ((RING, PAD, 384), LOW),
        "qkv_got": ((RING, PAD, 384), LOW),
    }
    scratch = [
        pltpu.VMEM((RING, BLOCK, 384), LOW),
        pltpu.VMEM((RING, BLOCK, 384), LOW),
        pltpu.VMEM((BLOCK, HD), F32),
        pltpu.VMEM((RING, BLOCK, D), LOW),
        pltpu.VMEM((HALF, D), F32),
        pltpu.VMEM((RING, RING, BLOCK, 384), LOW),
        pltpu.VMEM((RING, PAD, 1024), LOW),
        pltpu.VMEM((RING, PAD, 384), LOW),
        pltpu.VMEM((RING, PAD, 384), LOW),
        *reduce_scratch(),
        *plane_reduce_scratch(HD),
        *plane_reduce_scratch(1024),
        *plane_reduce_scratch(384),
        *plane_reduce_scratch(384),
    ]
    spaces = [pltpu.VMEM] * 3 + [pl.ANY] + [pltpu.VMEM] * 8
    return call(fourth_kernel, 3, 130, out, scratch, operands, spaces)


def adam_update(weight, gradient, first_moment, second_moment, learn_rate, decay_rate):
    first_moment = first_decay * first_moment + (1.0 - first_decay) * gradient
    second_moment = second_decay * second_moment + (1.0 - second_decay) * gradient * gradient
    corrected = (
        first_moment
        / (1.0 - first_decay**STEP)
        / (jnp.sqrt(second_moment / (1.0 - second_decay**STEP)) + adam_eps)
    )
    return (weight - learn_rate * (corrected + decay_rate * weight), first_moment, second_moment)


def out_fan_in(seq_length):
    return max(1, H * HD * 4 // min(WINDOW, seq_length))


def activate(gate_part, upper_part):
    return jax.nn.gelu(gate_part, approximate=True) * upper_part


def quarters(rows):
    return rows.reshape(OWN, RING, -1).transpose(1, 0, 2)


def head_quarters(rows):
    split = rows.reshape(rows.shape[0], 5, HD)
    last = split[:, 4].reshape(-1, RING, TAIL)
    return jnp.concatenate([split[:, :4], last], axis=2).transpose(1, 0, 2)


def whole_heads(slices):
    slices = slices.transpose(1, 0, 2)
    rows = slices.shape[0]
    return jnp.concatenate(
        [slices[..., :HD].reshape(rows, -1), slices[..., HD:].reshape(rows, -1)], axis=1
    )


def whole(slices):
    return slices.transpose(1, 0, 2).reshape(slices.shape[1], -1)


def pad_to(x, axis, size):
    widths = [(0, 0)] * x.ndim
    widths[axis] = (0, size - x.shape[axis])
    return jnp.pad(x, widths)


def per_device(
    tokens,
    cotangent,
    w_query,
    w_keyvalue,
    w_out,
    w_gateup,
    w_down,
    norm_scales,
    first_query,
    first_keyvalue,
    first_out,
    first_gateup,
    first_down,
    first_scales,
    second_query,
    second_keyvalue,
    second_out,
    second_gateup,
    second_down,
    second_scales,
):
    core = lax.axis_index("tensor")
    seq_index = lax.axis_index("x") * RING + lax.axis_index("z")
    positions = seq_index * BLOCK + jnp.arange(BLOCK, dtype=jnp.int32)
    seq_length = BLOCK * RING * RING

    keyvalue_part = lax.dynamic_index_in_dim(w_keyvalue, core, 1, keepdims=False)
    scale_columns = jnp.broadcast_to(norm_scales.T[None], (RING, OWN, 2))
    attn_rows = jnp.concatenate(
        [head_quarters(w_query), quarters(keyvalue_part), head_quarters(w_out.T), scale_columns],
        axis=2,
    ).astype(LOW)
    attn_rows = pad_to(pad_to(attn_rows, 2, 768), 1, PAD)
    gateup = w_gateup.astype(LOW).reshape(OWN, 2, RING, MAIN + TAIL).transpose(2, 0, 1, 3)
    feed_rows = jnp.concatenate(
        [
            gateup[..., :MAIN].reshape(RING, OWN, 2 * MAIN),
            gateup[..., MAIN:].reshape(RING, OWN, 2 * TAIL),
            quarters(w_down.T).astype(LOW),
        ],
        axis=2,
    )
    feed_rows = pad_to(pad_to(feed_rows, 2, 2944), 1, PAD)
    frequency = 10000.0 ** (-jnp.arange(TAIL, dtype=F32) / TAIL)
    angles = positions.astype(F32)[:, None] * frequency[None, :]
    cos_table = jnp.tile(jnp.cos(angles), (1, 2))
    sin_table = jnp.concatenate([-jnp.sin(angles), jnp.sin(angles)], axis=1)
    cos_kv = jnp.where(core == 0, cos_table, 1.0)
    sin_kv = jnp.where(core == 0, sin_table, 0.0)
    first = run_first(
        attn_rows, feed_rows, tokens, cotangent.astype(LOW), cos_table, sin_table, cos_kv, sin_kv
    )
    feed_full = first["feed_full"].reshape(D, 2944)
    gateup_full = feed_full[:, : 2 * (MAIN + TAIL)]
    down_full = feed_full[:, 2 * (MAIN + TAIL) :]
    dy_all = first["dy_all"].reshape(-1, D)
    normed_two = first["normed_two"].reshape(-1, D)

    gateup = dot(normed_two, gateup_full, (1, 0))
    gate = jnp.concatenate([gateup[:, :MAIN], gateup[:, 2 * MAIN : 2 * MAIN + TAIL]], axis=1)
    upper = jnp.concatenate([gateup[:, MAIN : 2 * MAIN], gateup[:, 2 * MAIN + TAIL :]], axis=1)
    hidden, activate_back = jax.vjp(activate, gate, upper)
    hidden_low = pad_to(hidden.astype(LOW), 1, 1024)
    grad_hidden = dot(dy_all, down_full, (1, 0))[:, : MAIN + TAIL]
    grad_gate, grad_upper = activate_back(grad_hidden)
    grad_gateup_low = jnp.concatenate(
        [grad_gate[:, :MAIN], grad_upper[:, :MAIN], grad_gate[:, MAIN:], grad_upper[:, MAIN:]], axis=1
    ).astype(LOW)
    norm_part = dot(grad_gateup_low, gateup_full, (1, 1)).astype(LOW).reshape(RING, BLOCK, D)
    feed_part = dot(hidden_low, down_full, (1, 1)).astype(LOW).reshape(RING, BLOCK, D)
    gateup_grads = dot(normed_two, grad_gateup_low, (0, 0)).astype(LOW)
    down_grads = dot(dy_all, hidden_low, (0, 0)).astype(LOW)
    third = run_third(
        norm_part,
        feed_part,
        gateup_grads.reshape(RING, RING, BLOCK, -1),
        cotangent,
        first["residual"],
        first["gains"],
        first["attn_full"],
        first["att_slice"],
        first["query"],
        first["keyvalue"],
        first["log_total"],
        first["attended"],
        cos_table,
        sin_table,
    )
    fourth = run_fourth(
        third["grad_kv"],
        third["grad_query"],
        third["gateup_rows"],
        down_grads.reshape(RING, RING, BLOCK, -1),
        third["grad_out"],
        first["attn_full"],
        first["normed_one"],
        third["grad_rows"],
        tokens,
        first["gains"],
        cos_kv,
        sin_kv,
    )
    output, grad_tokens = third["output"], fourth["grad_tokens"]

    gateup_shard = fourth["gateup_got"][:, :OWN].astype(F32)
    gateup_shard = jnp.concatenate(
        [
            gateup_shard[..., : 2 * MAIN].reshape(RING, OWN, 2, MAIN),
            gateup_shard[..., 2 * MAIN :].reshape(RING, OWN, 2, TAIL),
        ],
        axis=3,
    ).transpose(1, 2, 0, 3).reshape(OWN, 2, -1)
    down_shard = whole(fourth["down_got"][:, :OWN, : MAIN + TAIL].astype(F32)).T
    out_shard = whole_heads(fourth["out_got"][:, :OWN, :320].astype(F32)).T
    qkv_shard = fourth["qkv_got"][:, :OWN].astype(F32)
    query_shard = whole_heads(qkv_shard[..., :320])
    kv_half = whole(qkv_shard[..., 320:])
    gain_rows = 1.0 + norm_scales.astype(LOW).astype(F32)

    def with_weight(weight, grads):
        return jnp.sum((weight.astype(LOW).astype(F32) * grads).reshape(OWN, -1), axis=1)

    scale_parts = jnp.stack(
        [
            with_weight(w_query, query_shard) + with_weight(keyvalue_part, kv_half),
            with_weight(w_gateup, gateup_shard),
        ],
        axis=1,
    )
    packed = pad_to(jnp.concatenate([kv_half, pad_to(scale_parts, 1, 128)], axis=1), 0, PAD)
    theirs = swap_cores(packed, 4)[:OWN]
    kv_other = theirs[:, :HD]
    scale_grads = (scale_parts + theirs[:, HD : HD + 2]).T / gain_rows
    keyvalue_shard = jnp.stack(
        [jnp.where(core == 0, kv_half, kv_other), jnp.where(core == 0, kv_other, kv_half)], axis=1
    )

    matrix_rate = 2.0 * D ** (-0.5)
    out_rate = 2.0 * out_fan_in(seq_length) ** (-0.5)
    down_rate = 2.0 * (FF // 2) ** (-0.5)
    triples = [
        adam_update(w_query, query_shard, first_query, second_query, matrix_rate, weight_decay),
        adam_update(
            w_keyvalue, keyvalue_shard, first_keyvalue, second_keyvalue, matrix_rate, weight_decay
        ),
        adam_update(w_out, out_shard, first_out, second_out, out_rate, weight_decay),
        adam_update(w_gateup, gateup_shard, first_gateup, second_gateup, matrix_rate, weight_decay),
        adam_update(w_down, down_shard, first_down, second_down, down_rate, weight_decay),
        adam_update(norm_scales, scale_grads, first_scales, second_scales, gain_rate, 0.0),
    ]
    return (output, grad_tokens, *(triple[i] for i in range(3) for triple in triples))


def solution(mesh):
    split = Mesh(
        mesh.devices.reshape(RING, RING, RING, 2), ("dp", "x", "z", "tensor")
    )
    rows = ("dp", "x", "z")
    matrices = (
        P(rows, "tensor"),
        P(rows, None, None),
        P("tensor", rows),
        P(rows, None, "tensor"),
        P("tensor", rows),
        P(None, rows),
    )
    in_specs = (P(rows, None), P(rows, None), *matrices, *matrices, *matrices)
    out_specs = in_specs
    return jax.shard_map(
        per_device, mesh=split, in_specs=in_specs, out_specs=out_specs, check_vma=False
    )
```

```python
import jax
import jax.numpy as jnp
from jax import lax
from jax.experimental import pallas as pl
from jax.experimental.pallas import tpu as pltpu
from jax.sharding import Mesh
from jax.sharding import PartitionSpec as P

D = 2560
H = 10
HD = 256
FF = 7680
WINDOW = 2048
STEP = 10

eps_norm = 1e-06
masked_fill = -1e30
first_decay = 0.9
second_decay = 0.95
adam_eps = 1e-08
weight_decay = 0.1
gain_rate = 0.2
GELU_SCALE = (2.0 / 3.141592653589793) ** 0.5
GELU_CUBE = 0.044715

MESH = pl.DeviceIdType.MESH
LOW = jnp.bfloat16
F32 = jnp.float32
RING = 4
BLOCK = 160
HALF = BLOCK // 2
PART = 48
OWN = 40
PAD = 48
MAIN = 896
TAIL = 64


def step(axis, distance):
    return lax.rem(lax.axis_index(axis) + (RING + distance), RING)


def sibling():
    return {"tensor": 1 - lax.axis_index("tensor")}


def greet(peers):
    barrier = pltpu.get_barrier_semaphore()
    for peer in peers:
        pl.semaphore_signal(barrier, inc=1, device_id=peer, device_id_type=MESH)
    pl.semaphore_wait(barrier, len(peers))


def dot(left_side, right_side, contract):
    return lax.dot_general(
        left_side, right_side, ((contract[:1], contract[1:]), ((), ())), preferred_element_type=F32
    )


class Mover:
    def __init__(self, send_sem, recv_sem):
        self.send_sem, self.recv_sem, self.pending = send_sem, recv_sem, []

    def copy(self, src, dst, peer):
        index = len(self.pending)
        one = pltpu.make_async_remote_copy(
            src_ref=src,
            dst_ref=dst,
            send_sem=self.send_sem.at[index],
            recv_sem=self.recv_sem.at[index],
            device_id=peer,
            device_id_type=MESH,
        )
        one.start()
        self.pending.append(one)
        return one

    def finish(self):
        for one in self.pending:
            one.wait_send()


def advance(steps):
    next(steps, None)


def plane_peers(axes):
    return [{axis: step(axis, d)} for axis in axes for d in (-1, 1)]


def swap_kernel(x_ref, o_ref, send_sem, recv_sem):
    greet([sibling()])
    mover = Mover(send_sem, recv_sem)
    mover.copy(x_ref, o_ref, sibling()).wait_recv()
    mover.finish()


def swap_cores(x, ident):
    return pl.pallas_call(
        swap_kernel,
        out_shape=jax.ShapeDtypeStruct(x.shape, x.dtype),
        in_specs=[pl.BlockSpec(memory_space=pltpu.VMEM)],
        out_specs=pl.BlockSpec(memory_space=pltpu.VMEM),
        scratch_shapes=[pltpu.SemaphoreType.DMA((1,)), pltpu.SemaphoreType.DMA((1,))],
        compiler_params=pltpu.CompilerParams(collective_id=ident, has_side_effects=True),
    )(x)


def exchange_steps(mover, src, dst):
    me = lax.axis_index("z")
    copies = [
        mover.copy(src.at[step("z", d)], dst.at[me], {"z": step("z", d)}) for d in (2, 1, 3)
    ]
    yield
    for copy in copies:
        copy.wait_recv()


def core_rows():
    base = pl.multiple_of(lax.axis_index("tensor") * HALF, 16)
    return (
        pl.ds(base, HALF),
        pl.ds(base, PART),
        pl.ds(pl.multiple_of(base + PART, 16), HALF - PART),
        pl.ds(pl.multiple_of(HALF - base, 16), HALF),
    )


def gather_steps(mover, x, out):
    me, left, right, far = (step("z", d) for d in (0, -1, 1, 2))
    half, first, last, _ = core_rows()
    to_right = mover.copy(x.at[half], out.at[me, half], {"z": right})
    to_left = mover.copy(x.at[half], out.at[me, half], {"z": left})
    yield
    to_right.wait_recv()
    on_right = mover.copy(out.at[left, first], out.at[left, first], {"z": right})
    shares = [mover.copy(out.at[left, half], out.at[left, half], sibling())]
    to_left.wait_recv()
    on_left = mover.copy(out.at[right, last], out.at[right, last], {"z": left})
    shares.append(mover.copy(out.at[right, half], out.at[right, half], sibling()))
    yield
    on_right.wait_recv()
    on_left.wait_recv()
    shares.append(mover.copy(out.at[far, half], out.at[far, half], sibling()))
    yield
    for copy in shares:
        copy.wait_recv()


def cut_rows(which, cut):
    base, size = (0, cut) if which == 0 else (cut, BLOCK - cut)
    part = -(-size // 32) * 16
    return pl.ds(base, size), pl.ds(base, part), pl.ds(base + part, size - part)


def plane_gather_steps(mover, axes, x, out, cut=HALF, order=(0, 1), share=False):
    a, b = (lax.axis_index(axis) for axis in axes)
    state = {}
    for which, axis in enumerate(axes):
        rows = cut_rows(which, cut)[0]
        place = (lambda i, r: out.at[i, b, r]) if which == 0 else (lambda i, r: out.at[a, i, r])
        me = (a, b)[which]
        to_right = mover.copy(x.at[rows], place(me, rows), {axis: step(axis, 1)})
        to_left = mover.copy(x.at[rows], place(me, rows), {axis: step(axis, -1)})
        state[which] = (axis, place, to_right, to_left)
    yield
    passed = {}
    for which in order:
        axis, place, to_right, to_left = state[which]
        _, first, last = cut_rows(which, cut)
        left, right = step(axis, -1), step(axis, 1)
        to_right.wait_recv()
        on_right = mover.copy(place(left, first), place(left, first), {axis: right})
        to_left.wait_recv()
        on_left = mover.copy(place(right, last), place(right, last), {axis: left})
        passed[which] = (on_right, on_left)
    yield
    state = {}
    shares = []

    def give(piece):
        if share:
            shares.append(mover.copy(piece, piece, sibling()))

    for which in order:
        axis, other = axes[which], axes[1 - which]
        rows = cut_rows(which, cut)[0]
        if which == 0:
            place = lambda i, lo, n, rows=rows: out.at[pl.ds(lo, n), i, rows]
        else:
            place = lambda i, lo, n, rows=rows: out.at[i, pl.ds(lo, n), rows]
        me = (b, a)[which]
        for copy in passed[which]:
            copy.wait_recv()
        to_right = mover.copy(place(me, 0, 4), place(me, 0, 4), {other: step(other, 1)})
        to_left = mover.copy(place(me, 0, 4), place(me, 0, 4), {other: step(other, -1)})
        give(place(me, 0, 4))
        state[which] = (other, place, to_right, to_left)
        yield
    ends = []
    for which in order:
        other, place, to_right, to_left = state[which]
        left, right = step(other, -1), step(other, 1)
        to_right.wait_recv()
        ends.append(mover.copy(place(left, 0, 2), place(left, 0, 2), {other: right}))
        give(place(left, 0, 4))
        to_left.wait_recv()
        ends.append(mover.copy(place(right, 2, 2), place(right, 2, 2), {other: left}))
        give(place(right, 0, 4))
        yield
    for copy in ends:
        copy.wait_recv()
    for which in order:
        other, place, _, _ = state[which]
        give(place(step(other, 2), 0, 4))
    for copy in shares:
        copy.wait_recv()


def lanes(shape):
    return lax.broadcasted_iota(jnp.int32, shape, len(shape) - 1)


def turn(values, cos, sin):
    return values * cos + pltpu.roll(values, 64, 1) * sin


def whole_rows(blocks, stage, dst):
    for i in range(RING):
        stage[i * OWN : (i + 1) * OWN] = blocks[i].astype(F32)[:OWN]
    dst[...] = stage[...].astype(LOW)


def first_kernel(
    attn_rows,
    feed_rows,
    tokens,
    dy,
    cos_ref,
    sin_ref,
    cos_kv,
    sin_kv,
    feed_full,
    attn_full,
    normed_one,
    dy_all,
    query,
    keyvalue,
    log_total,
    att_slice,
    residual,
    normed_two,
    attended,
    gain_ref,
    send_sem,
    recv_sem,
    local_sem,
    attn_got,
    attn_mine,
    attn_stage,
    feed_got,
    feed_mine,
    feed_stage,
    unit_low,
    unit_all,
    qkv_send,
    qkv_got,
    kv_own,
    scores,
    att_send,
    part,
    other,
    total,
    part_a,
    part_b,
    from_left,
    from_right,
    normed_low,
):
    z, x, y, core = (lax.axis_index(axis) for axis in ("z", "x", "dp", "tensor"))
    left, right, far = (step("z", d) for d in (-1, 1, 2))
    half, _, _, their_half = core_rows()
    plane = ("dp", "x")
    greet(
        [{"z": step("z", d)} for d in (1, 2, 3)] + plane_peers(("dp", "x")) + [sibling()]
    )
    mover = Mover(send_sem, recv_sem)

    attn_swap = exchange_steps(mover, attn_rows, attn_got)
    advance(attn_swap)
    values = tokens[...]
    unit = values * lax.rsqrt(jnp.mean(values * values, axis=-1, keepdims=True) + eps_norm)
    unit_low[...] = unit.astype(LOW)
    unit_gather = gather_steps(mover, unit_low, unit_all)
    advance(unit_gather)
    feed_swap = exchange_steps(mover, feed_rows, feed_got)
    advance(feed_swap)
    unit_all[z] = unit_low[...]
    attn_got[z] = attn_rows[z]
    advance(attn_swap)
    whole_rows(attn_got, attn_stage, attn_mine)
    attn_gather = plane_gather_steps(mover, plane, attn_mine, attn_full)
    advance(attn_gather)
    attn_full[y, x] = attn_mine[...]
    advance(unit_gather)
    advance(attn_gather)
    advance(attn_gather)
    advance(attn_gather)
    feed_got[z] = feed_rows[z]
    advance(unit_gather)
    advance(feed_swap)
    whole_rows(feed_got, feed_stage, feed_mine)
    feed_own = pltpu.make_async_copy(feed_mine, feed_full.at[y, x], local_sem.at[0])
    feed_own.start()
    advance(attn_gather)
    advance(attn_gather)
    feed_gather = plane_gather_steps(mover, plane, feed_mine, feed_full, cut=64, order=(1, 0))
    advance(feed_gather)
    dy_gather = gather_steps(mover, dy, dy_all)
    advance(dy_gather)
    dy_own = pltpu.make_async_copy(dy, dy_all.at[z], local_sem.at[1])
    dy_own.start()
    advance(unit_gather)
    advance(attn_gather)

    scale_cols = attn_full[:, :, :, 640:768].reshape(D, 128)
    pick = (lanes((8, 128)) == 64 + lax.broadcasted_iota(jnp.int32, (8, 128), 0)).astype(LOW)
    gain_ref[...] = 1.0 + dot(pick, scale_cols, (1, 1))
    qkv_weight = attn_full[:, :, :, :384].reshape(D, 384)
    copies = []
    for d in (2, 1, 3, 0):
        block = step("z", d)
        normed = (unit_all[block].astype(F32) * gain_ref[0:1, :]).astype(LOW)
        normed_one[block] = normed
        qkv_send[block] = dot(normed, qkv_weight, (1, 0)).astype(LOW)
        if d:
            copies.append(mover.copy(qkv_send.at[block], qkv_got.at[z], {"z": block}))
    qkv_got[z] = qkv_send[z]
    advance(feed_gather)
    feed_own.wait()
    for copy in copies:
        copy.wait_recv()
    low_lanes = lanes((BLOCK, 128)) < TAIL
    cos, sin = cos_ref[...], sin_ref[...]

    def joined(i, offset):
        one, two = (qkv_got[i + k, :, 256:384].astype(F32) for k in (0, 1))
        if offset == 0:
            return jnp.where(low_lanes, one, pltpu.roll(two, TAIL, 1))
        return jnp.where(low_lanes, pltpu.roll(one, TAIL, 1), two)

    kv_own[:, :128] = turn(joined(0, 1), cos_kv[...], sin_kv[...]).astype(LOW)
    kv_own[:, 128:] = joined(2, 1).astype(LOW)
    kv_mine = keyvalue.at[core]
    kv_gather = plane_gather_steps(mover, ("x", "z"), kv_own, kv_mine, share=True)
    advance(kv_gather)
    keyvalue[core, x, z] = kv_own[...]
    scale = HD ** (-0.5)
    for h in range(4):
        first = qkv_got[h, :, :128].astype(F32)
        query[h, :, :128] = (turn(first, cos, sin) * scale).astype(LOW)
        query[h, :, 128:] = (qkv_got[h, :, 128:256].astype(F32) * scale).astype(LOW)
    query[4, :, :128] = (turn(joined(0, 0), cos, sin) * scale).astype(LOW)
    query[4, :, 128:] = (joined(2, 0) * scale).astype(LOW)
    advance(kv_gather)
    advance(feed_gather)
    advance(kv_gather)
    advance(kv_gather)
    advance(kv_gather)
    advance(kv_gather)
    advance(feed_gather)
    advance(dy_gather)
    advance(kv_gather)

    start = (x * RING + z) * BLOCK
    chunk = RING * BLOCK

    def one_head(h, carry):
        queries = query[h]
        top = jnp.full((BLOCK, 1), masked_fill, F32)
        for k in range(RING):
            rows = keyvalue[0, k].reshape(chunk, HD)
            tile = dot(queries, rows, (1, 1))
            gap = (start - k * chunk) + (
                lax.broadcasted_iota(jnp.int32, tile.shape, 0) - lanes(tile.shape)
            )
            tile = jnp.where((gap >= 0) & (gap < WINDOW), tile, masked_fill)
            scores[:, k * chunk : (k + 1) * chunk] = tile
            top = jnp.maximum(top, jnp.max(tile, axis=-1, keepdims=True))
        sums = jnp.zeros((BLOCK, 1), F32)
        for k in range(RING):
            tile = jnp.exp(scores[:, k * chunk : (k + 1) * chunk] - top)
            scores[:, k * chunk : (k + 1) * chunk] = tile
            sums = sums + jnp.sum(tile, axis=-1, keepdims=True)
        inverse = 1.0 / sums
        result = jnp.zeros((BLOCK, HD), F32)
        for k in range(RING):
            low = (scores[:, k * chunk : (k + 1) * chunk] * inverse).astype(LOW)
            result = result + dot(low, keyvalue[1, k].reshape(chunk, HD), (1, 0))
        attended[h] = result
        log_total[h] = jnp.broadcast_to(top + jnp.log(sums), (BLOCK, 128))
        return carry

    lax.fori_loop(0, 5, one_head, 0)
    for j in range(RING):
        att_send[j, :, :256] = attended[j].astype(LOW)
        tile = attended[4, :, (j // 2) * 128 : (j // 2 + 1) * 128]
        tile = pltpu.roll(tile, TAIL, 1) if j % 2 else tile
        att_send[j, :, 256:] = jnp.where(low_lanes, tile, 0.0).astype(LOW)
    att_swap = exchange_steps(mover, att_send, att_slice)
    advance(att_swap)
    att_slice[z] = att_send[z]
    advance(dy_gather)
    advance(att_swap)

    out_weight = attn_full[:, :, :, 384:].reshape(D, 384)
    blocks = (far, right, left, z)
    shares = []
    for slot, block in enumerate(blocks):
        part[block] = dot(att_slice[block], out_weight, (1, 1)).astype(LOW)
        shares.append(mover.copy(part.at[block, their_half], other.at[slot], sibling()))

    def both(slot):
        return part[blocks[slot], half].astype(F32) + other[slot].astype(F32)

    shares[0].wait_recv()
    total[0] = both(0).astype(LOW)
    far_right = mover.copy(total.at[0, pl.ds(0, PART)], part_a, {"z": right})
    far_left = mover.copy(total.at[0, pl.ds(PART, HALF - PART)], part_b, {"z": left})
    shares[1].wait_recv()
    shares[2].wait_recv()
    far_right.wait_recv()
    summed = both(1)
    total[1, :PART] = (summed[:PART] + part_a[...].astype(F32)).astype(LOW)
    total[1, PART:] = summed[PART:].astype(LOW)
    to_right = mover.copy(total.at[1], from_left, {"z": right})
    far_left.wait_recv()
    summed = both(2)
    total[2, :PART] = summed[:PART].astype(LOW)
    total[2, PART:] = (summed[PART:] + part_b[...].astype(F32)).astype(LOW)
    to_left = mover.copy(total.at[2], from_right, {"z": left})
    shares[3].wait_recv()
    to_right.wait_recv()
    to_left.wait_recv()
    rows = tokens[half, :] + (
        both(3) + from_left[...].astype(F32) + from_right[...].astype(F32)
    )
    residual[half, :] = rows
    res_share = mover.copy(residual.at[half], residual.at[half], sibling())

    def normed_rows(rows):
        unit = rows * lax.rsqrt(jnp.mean(rows * rows, axis=-1, keepdims=True) + eps_norm)
        return (unit * gain_ref[1:2, :]).astype(LOW)

    normed_low[half, :] = normed_rows(rows)
    normed_gather = gather_steps(mover, normed_low, normed_two)
    advance(normed_gather)
    res_share.wait_recv()
    normed_low[their_half, :] = normed_rows(residual[their_half, :])
    normed_two[z] = normed_low[...]
    advance(normed_gather)
    advance(feed_gather)
    advance(normed_gather)
    advance(feed_gather)
    advance(dy_gather)
    advance(normed_gather)
    advance(feed_gather)
    dy_own.wait()
    mover.finish()


def run_first(*operands):
    out = {
        "feed_full": ((RING, RING, BLOCK, 2944), LOW, pl.ANY),
        "attn_full": ((RING, RING, BLOCK, 768), LOW, pltpu.VMEM),
        "normed_one": ((RING, BLOCK, D), LOW, pltpu.VMEM),
        "dy_all": ((RING, BLOCK, D), LOW, pl.ANY),
        "query": ((5, BLOCK, HD), LOW, pltpu.VMEM),
        "keyvalue": ((2, RING, RING, BLOCK, HD), LOW, pltpu.VMEM),
        "log_total": ((5, BLOCK, 128), F32, pltpu.VMEM),
        "att_slice": ((RING, BLOCK, 384), LOW, pltpu.VMEM),
        "residual": ((BLOCK, D), F32, pltpu.VMEM),
        "normed_two": ((RING, BLOCK, D), LOW, pltpu.VMEM),
        "attended": ((5, BLOCK, HD), F32, pltpu.VMEM),
        "gains": ((8, D), F32, pltpu.VMEM),
    }
    spaces = [pltpu.VMEM, pltpu.VMEM, pltpu.VMEM, pl.ANY] + [pltpu.VMEM] * 4
    copies = 120
    results = pl.pallas_call(
        first_kernel,
        out_shape=[jax.ShapeDtypeStruct(shape, kind) for shape, kind, _ in out.values()],
        in_specs=[pl.BlockSpec(memory_space=space) for space in spaces],
        out_specs=[pl.BlockSpec(memory_space=space) for _, _, space in out.values()],
        scratch_shapes=[
            pltpu.SemaphoreType.DMA((copies,)),
            pltpu.SemaphoreType.DMA((copies,)),
            pltpu.SemaphoreType.DMA((2,)),
            pltpu.VMEM((RING, PAD, 768), LOW),
            pltpu.VMEM((BLOCK, 768), LOW),
            pltpu.VMEM((BLOCK, 768), F32),
            pltpu.VMEM((RING, PAD, 2944), LOW),
            pltpu.VMEM((BLOCK, 2944), LOW),
            pltpu.VMEM((BLOCK, 2944), F32),
            pltpu.VMEM((BLOCK, D), LOW),
            pltpu.VMEM((RING, BLOCK, D), LOW),
            pltpu.VMEM((RING, BLOCK, 384), LOW),
            pltpu.VMEM((RING, BLOCK, 384), LOW),
            pltpu.VMEM((BLOCK, HD), LOW),
            pltpu.VMEM((BLOCK, RING * RING * BLOCK), F32),
            pltpu.VMEM((RING, BLOCK, 384), LOW),
            pltpu.VMEM((RING, BLOCK, D), LOW),
            pltpu.VMEM((4, HALF, D), LOW),
            pltpu.VMEM((3, HALF, D), LOW),
            pltpu.VMEM((PART, D), LOW),
            pltpu.VMEM((HALF - PART, D), LOW),
            pltpu.VMEM((HALF, D), LOW),
            pltpu.VMEM((HALF, D), LOW),
            pltpu.VMEM((BLOCK, D), LOW),
        ],
        compiler_params=pltpu.CompilerParams(
            collective_id=1, has_side_effects=True, vmem_limit_bytes=60 * 1024 * 1024
        ),
    )(*operands)
    return dict(zip(out, results, strict=True))


def plane_reduce_steps(mover, axes, g, bufs, res, loads=None):
    far, side, near, far_two, side_two = bufs
    places = [lax.axis_index(axis) for axis in axes]

    def block(which, i, lo, n):
        rows = pl.ds(which * HALF, HALF)
        return g.at[i, pl.ds(lo, n), rows] if which == 0 else g.at[pl.ds(lo, n), i, rows]

    locals_ = []

    def load(src, dst):
        locals_.append(pltpu.make_async_copy(src, dst, loads.at[len(locals_)]))
        locals_[-1].start()
        return locals_[-1]

    first, sides, wanted = [], [], []
    for which, axis in enumerate(axes):
        right, left = step(axis, 1), step(axis, -1)
        far_place = step(axis, 2)
        first.append(
            (
                mover.copy(block(which, far_place, 0, 2), far.at[which, pl.ds(0, 2)], {axis: right}),
                mover.copy(block(which, far_place, 2, 2), far.at[which, pl.ds(2, 2)], {axis: left}),
            )
        )
        if loads is not None:
            wanted.append(
                (
                    load(block(which, right, 0, 2), near.at[which, 0]),
                    load(block(which, left, 2, 2), near.at[which, 1]),
                )
            )
    for which, axis in enumerate(axes):
        right, left = step(axis, 1), step(axis, -1)
        sides.append(
            [
                mover.copy(block(which, right, 2, 2), side.at[which, 0, pl.ds(2, 2)], {axis: right}),
                mover.copy(block(which, left, 0, 2), side.at[which, 1, pl.ds(0, 2)], {axis: left}),
            ]
        )
    yield
    owned = []
    for which, axis in enumerate(axes):
        for k, (d, lo) in enumerate(((1, 0), (-1, 2))):
            first[which][k].wait_recv()
            if loads is not None:
                wanted[which][k].wait()
                term = near[which, k]
            else:
                term = block(which, step(axis, d), lo, 2)[...]
            near[which, k] = (term.astype(F32) + far[which, lo : lo + 2].astype(F32)).astype(LOW)
            sides[which].append(
                mover.copy(near.at[which, k], side.at[which, k, pl.ds(lo, 2)], {axis: step(axis, d)})
            )
        if loads is not None:
            owned.append(load(block(which, places[which], 0, 4), far.at[which]))
    yield

    def summed(which, i):
        if loads is not None:
            term = far[which, i]
        else:
            rows = pl.ds(which * HALF, HALF)
            me = places[which]
            term = (g[me, i, rows] if which == 0 else g[i, me, rows])
        return (
            term.astype(F32) + side[which, 0, i].astype(F32) + side[which, 1, i].astype(F32)
        )

    second = []
    for which, axis in enumerate(axes):
        other = axes[1 - which]
        right, left = {other: step(other, 1)}, {other: step(other, -1)}
        for copy in sides[which]:
            copy.wait_recv()
        if loads is not None:
            owned[which].wait()
        far_two[which, 0] = summed(which, step(other, 2)).astype(LOW)
        upper, lower = pl.ds(0, PART), pl.ds(PART, HALF - PART)
        second.append(
            (
                mover.copy(far_two.at[which, 0, upper], far_two.at[which, 1, upper], right),
                mover.copy(far_two.at[which, 0, lower], far_two.at[which, 1, lower], left),
            )
        )
    yield
    last = []
    for which, axis in enumerate(axes):
        other = axes[1 - which]
        right, left = step(other, 1), step(other, -1)
        total = summed(which, right)
        second[which][0].wait_recv()
        side_two[which, 0, :PART] = (
            total[:PART] + far_two[which, 1, :PART].astype(F32)
        ).astype(LOW)
        side_two[which, 0, PART:] = total[PART:].astype(LOW)
        last.append(mover.copy(side_two.at[which, 0], side_two.at[which, 2], {other: right}))
        total = summed(which, left)
        second[which][1].wait_recv()
        side_two[which, 1, :PART] = total[:PART].astype(LOW)
        side_two[which, 1, PART:] = (
            total[PART:] + far_two[which, 1, PART:].astype(F32)
        ).astype(LOW)
        last.append(mover.copy(side_two.at[which, 1], side_two.at[which, 3], {other: left}))
    yield
    for which, axis in enumerate(axes):
        other = axes[1 - which]
        last[2 * which].wait_recv()
        last[2 * which + 1].wait_recv()
        res[which * HALF : (which + 1) * HALF] = (
            summed(which, lax.axis_index(other))
            + side_two[which, 2].astype(F32)
            + side_two[which, 3].astype(F32)
        )


def plane_reduce_scratch(columns):
    return [
        pltpu.VMEM((2, 4, HALF, columns), LOW),
        pltpu.VMEM((2, 2, 4, HALF, columns), LOW),
        pltpu.VMEM((2, 2, 2, HALF, columns), LOW),
        pltpu.VMEM((2, 2, HALF, columns), LOW),
        pltpu.VMEM((2, 4, HALF, columns), LOW),
        pltpu.VMEM((BLOCK, columns), F32),
    ]


def reduce_steps(mover, part, mine, bufs, out, make=None):
    other, total, part_a, part_b, from_left, from_right = bufs
    _, _, _, their_half = core_rows()
    me, left, right, far = (step("z", d) for d in (0, -1, 1, 2))
    blocks = (far, right, left, me)
    shares = []
    for slot, block in enumerate(blocks):
        if make is not None:
            make(block)
        shares.append(mover.copy(part.at[block, their_half], other.at[slot], sibling()))
    yield

    def both(slot):
        return mine(blocks[slot]).astype(F32) + other[slot].astype(F32)

    shares[0].wait_recv()
    total[0] = both(0).astype(LOW)
    far_right = mover.copy(total.at[0, pl.ds(0, PART)], part_a, {"z": right})
    far_left = mover.copy(total.at[0, pl.ds(PART, HALF - PART)], part_b, {"z": left})
    yield
    shares[1].wait_recv()
    shares[2].wait_recv()
    far_right.wait_recv()
    summed = both(1)
    total[1, :PART] = (summed[:PART] + part_a[...].astype(F32)).astype(LOW)
    total[1, PART:] = summed[PART:].astype(LOW)
    to_right = mover.copy(total.at[1], from_left, {"z": right})
    far_left.wait_recv()
    summed = both(2)
    total[2, :PART] = summed[:PART].astype(LOW)
    total[2, PART:] = (summed[PART:] + part_b[...].astype(F32)).astype(LOW)
    to_left = mover.copy(total.at[2], from_right, {"z": left})
    yield
    shares[3].wait_recv()
    to_right.wait_recv()
    to_left.wait_recv()
    out[...] = both(3) + from_left[...].astype(F32) + from_right[...].astype(F32)


def reduce_scratch():
    return [
        pltpu.VMEM((4, HALF, D), LOW),
        pltpu.VMEM((3, HALF, D), LOW),
        pltpu.VMEM((PART, D), LOW),
        pltpu.VMEM((HALF - PART, D), LOW),
        pltpu.VMEM((HALF, D), LOW),
        pltpu.VMEM((HALF, D), LOW),
    ]


def spread_rows(res, dst):
    for i in range(RING):
        rows = res[i * OWN : (i + 1) * OWN]
        dst[i] = jnp.concatenate([rows, jnp.zeros((PAD - OWN, rows.shape[1]), F32)]).astype(LOW)


def activation(gate, upper, grad):
    square = gate * gate
    tanh = jnp.tanh(GELU_SCALE * gate * (1.0 + GELU_CUBE * square))
    half = 0.5 * (1.0 + tanh)
    gelu = gate * half
    slope = half + 0.5 * gate * (1.0 - tanh * tanh) * GELU_SCALE * (1.0 + 3.0 * GELU_CUBE * square)
    return gelu * upper, grad * upper * slope, grad * gelu


def second_kernel(
    feed_full,
    normed_two,
    dy_all,
    cotangent,
    residual,
    gain_ref,
    grad_rows,
    da_all,
    feed_part,
    gateup_grads,
    down_rows,
    send_sem,
    recv_sem,
    local_sem,
    gateup_weight,
    down_weight,
    hidden,
    dgu,
    norm_part,
    stage,
    grad_half,
    cot_half,
    res_half,
    da_low,
    *bufs,
):
    z = lax.axis_index("z")
    half, _, _, _ = core_rows()
    plane = ("dp", "x")
    gu_width = 2 * (MAIN + TAIL)
    wide = RING * BLOCK
    loads = [
        pltpu.make_async_copy(feed_full.at[:, :, :, pl.ds(0, gu_width)], gateup_weight, local_sem.at[0]),
        pltpu.make_async_copy(
            feed_full.at[:, :, :, pl.ds(gu_width, 1024)], down_weight, local_sem.at[1]
        ),
        pltpu.make_async_copy(cotangent.at[half], cot_half, local_sem.at[2]),
        pltpu.make_async_copy(residual.at[half], res_half, local_sem.at[3]),
    ]
    for load in loads:
        load.start()
    greet(plane_peers(("z",)) + plane_peers(plane) + [sibling()])
    mover = Mover(send_sem, recv_sem)
    for load in loads:
        load.wait()

    def product(rows, weight, lo, n):
        left_side = rows[...].reshape(wide, D)
        return dot(left_side, weight[:, :, :, lo : lo + n].reshape(D, n), (1, 0))

    for lo, n in ((0, 256), (256, 256), (512, 256), (768, 128)):
        value, grad_gate, grad_upper = activation(
            product(normed_two, gateup_weight, lo, n),
            product(normed_two, gateup_weight, MAIN + lo, n),
            product(dy_all, down_weight, lo, n),
        )
        hidden[:, lo : lo + n] = value.astype(LOW)
        dgu[:, lo : lo + n] = grad_gate.astype(LOW)
        dgu[:, MAIN + lo : MAIN + lo + n] = grad_upper.astype(LOW)
    both = product(normed_two, gateup_weight, 2 * MAIN, 2 * TAIL)
    value, grad_gate, grad_upper = activation(
        both, pltpu.roll(both, TAIL, 1), product(dy_all, down_weight, MAIN, 2 * TAIL)
    )
    low_lanes = lanes(both.shape) < TAIL
    hidden[:, MAIN:] = jnp.where(low_lanes, value, 0.0).astype(LOW)
    dgu[:, 2 * MAIN :] = jnp.where(low_lanes, grad_gate, pltpu.roll(grad_upper, TAIL, 1)).astype(LOW)

    for i in range(RING):
        part = dot(dgu[...], gateup_weight[i].reshape(wide, gu_width), (1, 1))
        norm_part[:, :, i * wide : (i + 1) * wide] = part.astype(LOW).reshape(RING, BLOCK, wide)
    norm_sum = reduce_steps(mover, norm_part, lambda i: norm_part[i, half], bufs[:6], grad_half)
    advance(norm_sum)

    for i in range(RING):
        part = dot(hidden[...], down_weight[i].reshape(wide, 1024), (1, 1))
        feed_part[:, :, i * wide : (i + 1) * wide] = part.astype(LOW).reshape(RING, BLOCK, wide)
        if i == 0:
            advance(norm_sum)

    def columns(rows, i):
        return rows[:, :, i * wide : (i + 1) * wide].reshape(wide, wide)

    for i in range(RING):
        grads = dot(columns(dy_all, i), hidden[...], (0, 0))
        down_weight[i] = grads.astype(LOW).reshape(RING, BLOCK, 1024)
        if i == 1:
            advance(norm_sum)
    down_sum = plane_reduce_steps(mover, plane, down_weight, bufs[6:11], bufs[11])
    advance(down_sum)
    saved = []

    def gateup_block(i):
        if saved:
            saved[-1].wait()
        grads = dot(columns(normed_two, i), dgu[...], (0, 0))
        stage[...] = grads.astype(LOW).reshape(RING, BLOCK, gu_width)
        saved.append(pltpu.make_async_copy(stage, gateup_grads.at[i], local_sem.at[4 + i]))
        saved[-1].start()

    gateup_block(0)
    advance(norm_sum)
    rows = res_half[...]
    inverse = lax.rsqrt(jnp.mean(rows * rows, axis=-1, keepdims=True) + eps_norm)
    unit = rows * inverse
    scaled = grad_half[...] * gain_ref[1:2, :]
    grad = cot_half[...] + inverse * (
        scaled - unit * jnp.mean(scaled * unit, axis=-1, keepdims=True)
    )
    grad_rows[...] = grad
    da_low[half, :] = grad.astype(LOW)
    da_share = mover.copy(da_low.at[half], da_low.at[half], sibling())
    da_gather = gather_steps(mover, da_low, da_all)
    advance(da_gather)
    advance(down_sum)
    gateup_block(1)
    da_share.wait_recv()
    da_all[z] = da_low[...]
    advance(da_gather)
    gateup_block(2)
    advance(down_sum)
    advance(da_gather)
    gateup_block(3)
    advance(down_sum)
    advance(da_gather)
    advance(down_sum)
    spread_rows(bufs[11], down_rows)
    saved[-1].wait()
    mover.finish()


def third_kernel(
    feed_part,
    gateup_grads,
    da_all,
    residual,
    attn_full,
    att_slice,
    query,
    keyvalue,
    log_total,
    attended,
    cos_ref,
    sin_ref,
    cos_kv,
    sin_kv,
    grad_out,
    grad_got,
    gateup_rows,
    output,
    send_sem,
    recv_sem,
    local_sem,
    feed_mine,
    out_half,
    datt_send,
    datt_got,
    datt,
    delta,
    ds_all,
    p_all,
    dq,
    kv_pair,
    kv_in,
    grad_kv,
    grad_query,
    grad_send,
    kv_low,
    *bufs,
):
    z, core = lax.axis_index("z"), lax.axis_index("tensor")
    x = lax.axis_index("x")
    half, _, _, their_half = core_rows()
    out_bufs, rows_bufs, rows_res = bufs[:6], bufs[6:11], bufs[11]
    kv_bufs, kv_rows = bufs[12:17], bufs[17]
    feed_load = pltpu.make_async_copy(feed_part.at[:, half], feed_mine, local_sem.at[9])
    feed_load.start()
    greet([{"z": step("z", d)} for d in (1, 2, 3)] + plane_peers(("dp", "x")) + [sibling()])
    mover = Mover(send_sem, recv_sem)
    rows_sum = plane_reduce_steps(
        mover, ("dp", "x"), gateup_grads, rows_bufs, rows_res, loads=local_sem
    )
    advance(rows_sum)
    feed_sum = reduce_steps(mover, feed_part, lambda i: feed_mine[i], out_bufs, out_half)
    out_weight = attn_full[:, :, :, 384:].reshape(D, 384)
    copies = []
    for d in (2, 1, 3, 0):
        block = step("z", d)
        datt_send[block] = dot(da_all[block], out_weight, (1, 0)).astype(LOW)
        if d:
            copies.append(mover.copy(datt_send.at[block], datt_got.at[z], {"z": block}))
    datt_got[z] = datt_send[z]
    advance(feed_sum)
    slices = att_slice[...].reshape(RING * BLOCK, 384)
    wide = RING * BLOCK
    for i in range(RING):
        left_side = da_all[:, :, i * wide : (i + 1) * wide].reshape(wide, wide)
        grad_out[i] = dot(left_side, slices, (0, 0)).astype(LOW).reshape(RING, BLOCK, 384)
    for copy in copies:
        copy.wait_recv()
    feed_load.wait()
    advance(feed_sum)

    low_lanes = lanes((BLOCK, 128)) < TAIL
    for h in range(4):
        datt[h] = datt_got[h, :, :HD]
    for k in range(2):
        one, two = (datt_got[2 * k + i, :, HD:].astype(F32) for i in range(2))
        datt[4, :, k * 128 : (k + 1) * 128] = jnp.where(
            low_lanes, one, pltpu.roll(two, TAIL, 1)
        ).astype(LOW)
    for h in range(5):
        delta[h] = jnp.broadcast_to(
            jnp.sum(datt[h].astype(F32) * attended[h], axis=-1, keepdims=True), (BLOCK, 128)
        )
        dq[h] = jnp.zeros((BLOCK, HD), F32)
    start = (x * RING + z) * BLOCK
    chunk = RING * BLOCK

    def one_chunk(k, carry):
        keys = keyvalue[0, k].reshape(chunk, HD)
        values = keyvalue[1, k].reshape(chunk, HD)
        shape = (BLOCK, chunk)
        gap = (start - k * chunk) + (lax.broadcasted_iota(jnp.int32, shape, 0) - lanes(shape))
        visible = (gap >= 0) & (gap < WINDOW)

        def one_head(h, carry):
            scores = dot(query[h], keys, (1, 1))
            probs = jnp.where(visible, jnp.exp(scores - log_total[h, :, :1]), 0.0)
            grads = dot(datt[h], values, (1, 1))
            low = (probs * (grads - delta[h, :, :1])).astype(LOW)
            ds_all[h] = low
            p_all[h] = probs.astype(LOW)
            dq[h] = dq[h] + dot(low, keys, (1, 0))
            return carry

        lax.fori_loop(0, 5, one_head, 0)
        queries = query[...].reshape(5 * BLOCK, HD)
        outer = datt[...].reshape(5 * BLOCK, HD)
        kv_pair[0, k] = dot(ds_all[...].reshape(5 * BLOCK, chunk), queries, (0, 0)).astype(LOW).reshape(RING, BLOCK, HD)
        kv_pair[1, k] = dot(p_all[...].reshape(5 * BLOCK, chunk), outer, (0, 0)).astype(LOW).reshape(RING, BLOCK, HD)
        return carry

    lax.fori_loop(0, RING, one_chunk, 0)
    kv_swap = mover.copy(kv_pair.at[1 - core], kv_in, sibling())
    advance(feed_sum)
    cos, sin = cos_ref[...], sin_ref[...]
    scale = HD ** (-0.5)
    for h in range(5):
        grad_query[h, :, :128] = turn(dq[h, :, :128] * scale, cos, -sin)
        grad_query[h, :, 128:] = dq[h, :, 128:] * scale
    kv_swap.wait_recv()
    grad_kv[...] = (kv_pair[core].astype(F32) + kv_in[...].astype(F32)).astype(LOW)
    kv_sum = plane_reduce_steps(mover, ("x", "z"), grad_kv, kv_bufs, kv_rows)
    advance(kv_sum)
    advance(rows_sum)
    for h in range(4):
        grad_send[h, :, :HD] = grad_query[h].astype(LOW)
    advance(kv_sum)
    advance(kv_sum)
    advance(kv_sum)
    advance(kv_sum)
    kv_low[:, :128] = turn(kv_rows[:, :128], cos_kv[...], -sin_kv[...])
    kv_low[:, 128:] = kv_rows[:, 128:]
    for j in range(RING):
        place = slice((j // 2) * 128, (j // 2 + 1) * 128)
        one, two = grad_query[4, :, place], kv_low[:, place]
        if j % 2:
            one = pltpu.roll(one, TAIL, 1)
        else:
            two = pltpu.roll(two, TAIL, 1)
        grad_send[j, :, HD:] = jnp.where(low_lanes, one, two).astype(LOW)
    swap = exchange_steps(mover, grad_send, grad_got)
    advance(swap)
    grad_got[z] = grad_send[z]
    advance(feed_sum)
    output[half, :] = residual[half, :] + out_half[...]
    out_share = mover.copy(output.at[half], output.at[half], sibling())
    advance(rows_sum)
    advance(swap)
    advance(rows_sum)
    advance(rows_sum)
    spread_rows(rows_res, gateup_rows)
    out_share.wait_recv()
    mover.finish()


def fourth_kernel(
    grad_got,
    gateup_rows,
    down_rows,
    grad_out,
    attn_full,
    normed_one,
    grad_rows,
    tokens,
    gain_ref,
    grad_tokens,
    gateup_got,
    down_got,
    out_got,
    qkv_got,
    send_sem,
    recv_sem,
    local_sem,
    part,
    grad_half,
    grad_qkv,
    out_send,
    qkv_send,
    *bufs,
):
    z = lax.axis_index("z")
    half, _, _, _ = core_rows()
    plane = ("dp", "x")
    sum_bufs = bufs[:6]
    out_bufs, qkv_bufs = bufs[6:12], bufs[12:18]
    greet([{"z": step("z", d)} for d in (1, 2, 3)] + plane_peers(plane) + [sibling()])
    mover = Mover(send_sem, recv_sem)
    out_sum = plane_reduce_steps(mover, plane, grad_out, out_bufs[:5], out_bufs[5])
    advance(out_sum)
    slices = grad_got[...].reshape(RING * BLOCK, 384)
    wide = RING * BLOCK
    qkv_weight = attn_full[:, :, :, :384].reshape(D, 384)

    def make(block):
        part[block] = dot(grad_got[block], qkv_weight, (1, 1)).astype(LOW)

    norm_sum = reduce_steps(mover, part, lambda i: part[i, half], sum_bufs, grad_half, make)
    advance(norm_sum)
    advance(out_sum)
    for i in range(RING):
        left_side = normed_one[:, :, i * wide : (i + 1) * wide].reshape(wide, wide)
        grad_qkv[i] = dot(left_side, slices, (0, 0)).astype(LOW).reshape(RING, BLOCK, 384)
        if i == 0:
            advance(norm_sum)
    qkv_sum = plane_reduce_steps(mover, plane, grad_qkv, qkv_bufs[:5], qkv_bufs[5])
    advance(qkv_sum)
    advance(norm_sum)
    advance(out_sum)
    gateup_swap = exchange_steps(mover, gateup_rows, gateup_got)
    advance(gateup_swap)
    down_swap = exchange_steps(mover, down_rows, down_got)
    advance(down_swap)
    gateup_got[z] = gateup_rows[z]
    down_got[z] = down_rows[z]
    advance(qkv_sum)
    advance(out_sum)
    advance(out_sum)
    spread_rows(out_bufs[5], out_send)
    out_swap = exchange_steps(mover, out_send, out_got)
    advance(out_swap)
    out_got[z] = out_send[z]
    advance(qkv_sum)
    advance(norm_sum)
    rows = tokens[half, :]
    inverse = lax.rsqrt(jnp.mean(rows * rows, axis=-1, keepdims=True) + eps_norm)
    unit = rows * inverse
    scaled = grad_half[...] * gain_ref[0:1, :]
    grad_tokens[half, :] = grad_rows[...] + inverse * (
        scaled - unit * jnp.mean(scaled * unit, axis=-1, keepdims=True)
    )
    share = mover.copy(grad_tokens.at[half], grad_tokens.at[half], sibling())
    advance(qkv_sum)
    advance(qkv_sum)
    spread_rows(qkv_bufs[5], qkv_send)
    qkv_swap = exchange_steps(mover, qkv_send, qkv_got)
    advance(qkv_swap)
    qkv_got[z] = qkv_send[z]
    for steps in (gateup_swap, down_swap, out_swap, qkv_swap):
        advance(steps)
    share.wait_recv()
    mover.finish()


def call(kernel, ident, copies, out, scratch, operands, spaces, out_spaces=None):
    results = pl.pallas_call(
        kernel,
        out_shape=[jax.ShapeDtypeStruct(shape, kind) for shape, kind in out.values()],
        in_specs=[pl.BlockSpec(memory_space=space) for space in spaces],
        out_specs=[pl.BlockSpec(memory_space=(out_spaces or {}).get(name, pltpu.VMEM)) for name in out],
        scratch_shapes=[
            pltpu.SemaphoreType.DMA((copies,)),
            pltpu.SemaphoreType.DMA((copies,)),
            pltpu.SemaphoreType.DMA((10,)),
            *scratch,
        ],
        compiler_params=pltpu.CompilerParams(
            collective_id=ident, has_side_effects=True, vmem_limit_bytes=60 * 1024 * 1024
        ),
    )(*operands)
    return dict(zip(out, results, strict=True))


def run_second(*operands):
    out = {
        "grad_rows": ((HALF, D), F32),
        "da_all": ((RING, BLOCK, D), LOW),
        "feed_part": ((RING, BLOCK, D), LOW),
        "gateup_grads": ((RING, RING, BLOCK, 2 * (MAIN + TAIL)), LOW),
        "down_rows": ((RING, PAD, 1024), LOW),
    }
    scratch = [
        pltpu.VMEM((RING, RING, BLOCK, 2 * (MAIN + TAIL)), LOW),
        pltpu.VMEM((RING, RING, BLOCK, 1024), LOW),
        pltpu.VMEM((RING * BLOCK, 1024), LOW),
        pltpu.VMEM((RING * BLOCK, 2 * (MAIN + TAIL)), LOW),
        pltpu.VMEM((RING, BLOCK, D), LOW),
        pltpu.VMEM((RING, BLOCK, 2 * (MAIN + TAIL)), LOW),
        pltpu.VMEM((HALF, D), F32),
        pltpu.VMEM((HALF, D), F32),
        pltpu.VMEM((HALF, D), F32),
        pltpu.VMEM((BLOCK, D), LOW),
        *reduce_scratch(),
        *plane_reduce_scratch(1024),
    ]
    spaces = [pl.ANY, pltpu.VMEM, pltpu.VMEM, pl.ANY, pl.ANY, pltpu.VMEM]
    return call(
        second_kernel, 5, 60, out, scratch, operands, spaces, {"gateup_grads": pl.ANY}
    )


def run_third(*operands):
    out = {
        "grad_out": ((RING, RING, BLOCK, 384), LOW),
        "grad_got": ((RING, BLOCK, 384), LOW),
        "gateup_rows": ((RING, PAD, 2 * (MAIN + TAIL)), LOW),
        "output": ((BLOCK, D), F32),
    }
    scratch = [
        pltpu.VMEM((RING, HALF, D), LOW),
        pltpu.VMEM((HALF, D), F32),
        pltpu.VMEM((RING, BLOCK, 384), LOW),
        pltpu.VMEM((RING, BLOCK, 384), LOW),
        pltpu.VMEM((5, BLOCK, HD), LOW),
        pltpu.VMEM((5, BLOCK, 128), F32),
        pltpu.VMEM((5, BLOCK, RING * BLOCK), LOW),
        pltpu.VMEM((5, BLOCK, RING * BLOCK), LOW),
        pltpu.VMEM((5, BLOCK, HD), F32),
        pltpu.VMEM((2, RING, RING, BLOCK, HD), LOW),
        pltpu.VMEM((RING, RING, BLOCK, HD), LOW),
        pltpu.VMEM((RING, RING, BLOCK, HD), LOW),
        pltpu.VMEM((5, BLOCK, HD), F32),
        pltpu.VMEM((RING, BLOCK, 384), LOW),
        pltpu.VMEM((BLOCK, HD), F32),
        *reduce_scratch(),
        *plane_reduce_scratch(2 * (MAIN + TAIL)),
        *plane_reduce_scratch(HD),
    ]
    spaces = [pl.ANY] * 2 + [pltpu.VMEM] * 12
    return call(third_kernel, 2, 100, out, scratch, operands, spaces)


def run_fourth(*operands):
    out = {
        "grad_tokens": ((BLOCK, D), F32),
        "gateup_got": ((RING, PAD, 2 * (MAIN + TAIL)), LOW),
        "down_got": ((RING, PAD, 1024), LOW),
        "out_got": ((RING, PAD, 384), LOW),
        "qkv_got": ((RING, PAD, 384), LOW),
    }
    scratch = [
        pltpu.VMEM((RING, BLOCK, D), LOW),
        pltpu.VMEM((HALF, D), F32),
        pltpu.VMEM((RING, RING, BLOCK, 384), LOW),
        pltpu.VMEM((RING, PAD, 384), LOW),
        pltpu.VMEM((RING, PAD, 384), LOW),
        *reduce_scratch(),
        *plane_reduce_scratch(384),
        *plane_reduce_scratch(384),
    ]
    spaces = [pltpu.VMEM] * 9
    return call(fourth_kernel, 3, 80, out, scratch, operands, spaces)


def adam_update(weight, gradient, first_moment, second_moment, learn_rate, decay_rate):
    first_moment = first_decay * first_moment + (1.0 - first_decay) * gradient
    second_moment = second_decay * second_moment + (1.0 - second_decay) * gradient * gradient
    corrected = (
        first_moment
        / (1.0 - first_decay**STEP)
        / (jnp.sqrt(second_moment / (1.0 - second_decay**STEP)) + adam_eps)
    )
    return (weight - learn_rate * (corrected + decay_rate * weight), first_moment, second_moment)


def out_fan_in(seq_length):
    return max(1, H * HD * 4 // min(WINDOW, seq_length))


def quarters(rows):
    return rows.reshape(OWN, RING, -1).transpose(1, 0, 2)


def head_quarters(rows):
    split = rows.reshape(rows.shape[0], 5, HD)
    last = split[:, 4].reshape(-1, RING, TAIL)
    return jnp.concatenate([split[:, :4], last], axis=2).transpose(1, 0, 2)


def whole_heads(slices):
    slices = slices.transpose(1, 0, 2)
    rows = slices.shape[0]
    return jnp.concatenate(
        [slices[..., :HD].reshape(rows, -1), slices[..., HD:].reshape(rows, -1)], axis=1
    )


def whole(slices):
    return slices.transpose(1, 0, 2).reshape(slices.shape[1], -1)


def pad_to(x, axis, size):
    widths = [(0, 0)] * x.ndim
    widths[axis] = (0, size - x.shape[axis])
    return jnp.pad(x, widths)


def per_device(
    tokens,
    cotangent,
    w_query,
    w_keyvalue,
    w_out,
    w_gateup,
    w_down,
    norm_scales,
    first_query,
    first_keyvalue,
    first_out,
    first_gateup,
    first_down,
    first_scales,
    second_query,
    second_keyvalue,
    second_out,
    second_gateup,
    second_down,
    second_scales,
):
    core = lax.axis_index("tensor")
    seq_index = lax.axis_index("x") * RING + lax.axis_index("z")
    positions = seq_index * BLOCK + jnp.arange(BLOCK, dtype=jnp.int32)
    seq_length = BLOCK * RING * RING

    keyvalue_part = lax.dynamic_index_in_dim(w_keyvalue, core, 1, keepdims=False)
    scale_columns = jnp.broadcast_to(norm_scales.T[None], (RING, OWN, 2))
    attn_rows = jnp.concatenate(
        [head_quarters(w_query), quarters(keyvalue_part), head_quarters(w_out.T), scale_columns],
        axis=2,
    ).astype(LOW)
    attn_rows = pad_to(pad_to(attn_rows, 2, 768), 1, PAD)
    gateup = w_gateup.astype(LOW)
    mains = RING * MAIN
    feed_rows = jnp.concatenate(
        [
            quarters(gateup[:, 0, :mains]),
            quarters(gateup[:, 1, :mains]),
            quarters(gateup[:, 0, mains:]),
            quarters(gateup[:, 1, mains:]),
            quarters(w_down.T[:, :mains].astype(LOW)),
            quarters(w_down.T[:, mains:].astype(LOW)),
        ],
        axis=2,
    )
    feed_rows = pad_to(pad_to(feed_rows, 2, 2944), 1, PAD)
    frequency = 10000.0 ** (-jnp.arange(TAIL, dtype=F32) / TAIL)
    angles = positions.astype(F32)[:, None] * frequency[None, :]
    cos_table = jnp.tile(jnp.cos(angles), (1, 2))
    sin_table = jnp.concatenate([-jnp.sin(angles), jnp.sin(angles)], axis=1)
    cos_kv = jnp.where(core == 0, cos_table, 1.0)
    sin_kv = jnp.where(core == 0, sin_table, 0.0)
    first = run_first(
        attn_rows, feed_rows, tokens, cotangent.astype(LOW), cos_table, sin_table, cos_kv, sin_kv
    )
    second = run_second(
        first["feed_full"],
        first["normed_two"],
        first["dy_all"],
        cotangent,
        first["residual"],
        first["gains"],
    )
    third = run_third(
        second["feed_part"],
        second["gateup_grads"],
        second["da_all"],
        first["residual"],
        first["attn_full"],
        first["att_slice"],
        first["query"],
        first["keyvalue"],
        first["log_total"],
        first["attended"],
        cos_table,
        sin_table,
        cos_kv,
        sin_kv,
    )
    fourth = run_fourth(
        third["grad_got"],
        third["gateup_rows"],
        second["down_rows"],
        third["grad_out"],
        first["attn_full"],
        first["normed_one"],
        second["grad_rows"],
        tokens,
        first["gains"],
    )
    output, grad_tokens = third["output"], fourth["grad_tokens"]

    gateup_shard = fourth["gateup_got"][:, :OWN].astype(F32)
    down_shard = fourth["down_got"][:, :OWN].astype(F32)

    def hidden_units(grads, main, tail):
        return jnp.concatenate(
            [whole(grads[..., main : main + MAIN]), whole(grads[..., tail : tail + TAIL])], axis=1
        )

    gateup_shard = jnp.stack(
        [
            hidden_units(gateup_shard, 0, 2 * MAIN),
            hidden_units(gateup_shard, MAIN, 2 * MAIN + TAIL),
        ],
        axis=1,
    )
    down_shard = hidden_units(down_shard, 0, MAIN).T
    out_shard = whole_heads(fourth["out_got"][:, :OWN, :320].astype(F32)).T
    qkv_shard = fourth["qkv_got"][:, :OWN].astype(F32)
    query_shard = whole_heads(qkv_shard[..., :320])
    kv_half = whole(qkv_shard[..., 320:])
    gain_rows = 1.0 + norm_scales.astype(LOW).astype(F32)

    def with_weight(weight, grads):
        return jnp.sum((weight.astype(LOW).astype(F32) * grads).reshape(OWN, -1), axis=1)

    scale_parts = jnp.stack(
        [
            with_weight(w_query, query_shard) + with_weight(keyvalue_part, kv_half),
            with_weight(w_gateup, gateup_shard),
        ],
        axis=1,
    )
    packed = pad_to(jnp.concatenate([kv_half, pad_to(scale_parts, 1, 128)], axis=1), 0, PAD)
    theirs = swap_cores(packed, 4)[:OWN]
    kv_other = theirs[:, :HD]
    scale_grads = (scale_parts + theirs[:, HD : HD + 2]).T / gain_rows
    keyvalue_shard = jnp.stack(
        [jnp.where(core == 0, kv_half, kv_other), jnp.where(core == 0, kv_other, kv_half)], axis=1
    )

    matrix_rate = 2.0 * D ** (-0.5)
    out_rate = 2.0 * out_fan_in(seq_length) ** (-0.5)
    down_rate = 2.0 * (FF // 2) ** (-0.5)
    triples = [
        adam_update(w_query, query_shard, first_query, second_query, matrix_rate, weight_decay),
        adam_update(
            w_keyvalue, keyvalue_shard, first_keyvalue, second_keyvalue, matrix_rate, weight_decay
        ),
        adam_update(w_out, out_shard, first_out, second_out, out_rate, weight_decay),
        adam_update(w_gateup, gateup_shard, first_gateup, second_gateup, matrix_rate, weight_decay),
        adam_update(w_down, down_shard, first_down, second_down, down_rate, weight_decay),
        adam_update(norm_scales, scale_grads, first_scales, second_scales, gain_rate, 0.0),
    ]
    return (output, grad_tokens, *(triple[i] for i in range(3) for triple in triples))


def solution(mesh):
    split = Mesh(
        mesh.devices.reshape(RING, RING, RING, 2), ("dp", "x", "z", "tensor")
    )
    rows = ("dp", "x", "z")
    matrices = (
        P(rows, "tensor"),
        P(rows, None, None),
        P("tensor", rows),
        P(rows, None, "tensor"),
        P("tensor", rows),
        P(None, rows),
    )
    in_specs = (P(rows, None), P(rows, None), *matrices, *matrices, *matrices)
    out_specs = in_specs
    return jax.shard_map(
        per_device, mesh=split, in_specs=in_specs, out_specs=out_specs, check_vma=False
    )
```

```python
import jax
import jax.numpy as jnp
from jax import lax
from jax.experimental import pallas as pl
from jax.experimental.pallas import tpu as pltpu
from jax.sharding import Mesh
from jax.sharding import PartitionSpec as P

D = 2560
H = 10
HD = 256
FF = 7680
WINDOW = 2048
STEP = 10

eps_norm = 1e-06
masked_fill = -1e30
first_decay = 0.9
second_decay = 0.95
adam_eps = 1e-08
weight_decay = 0.1
gain_rate = 0.2
GELU_SCALE = (2.0 / 3.141592653589793) ** 0.5
GELU_CUBE = 0.044715

MESH = pl.DeviceIdType.MESH
LOW = jnp.bfloat16
F32 = jnp.float32
RING = 4
BLOCK = 160
HALF = BLOCK // 2
PART = 48
OWN = 40
PAD = 48
SPANS = ((0, 48, 32), (48, 32, 16))
MAIN = 896
TAIL = 64


def step(axis, distance):
    return lax.rem(lax.axis_index(axis) + (RING + distance), RING)


def sibling():
    return {"tensor": 1 - lax.axis_index("tensor")}


def greet(peers):
    barrier = pltpu.get_barrier_semaphore()
    for peer in peers:
        pl.semaphore_signal(barrier, inc=1, device_id=peer, device_id_type=MESH)
    pl.semaphore_wait(barrier, len(peers))


def dot(left_side, right_side, contract):
    return lax.dot_general(
        left_side, right_side, ((contract[:1], contract[1:]), ((), ())), preferred_element_type=F32
    )


class Mover:
    def __init__(self, send_sem, recv_sem):
        self.send_sem, self.recv_sem, self.pending = send_sem, recv_sem, []

    def copy(self, src, dst, peer):
        index = len(self.pending)
        one = pltpu.make_async_remote_copy(
            src_ref=src,
            dst_ref=dst,
            send_sem=self.send_sem.at[index],
            recv_sem=self.recv_sem.at[index],
            device_id=peer,
            device_id_type=MESH,
        )
        one.start()
        self.pending.append(one)
        return one

    def finish(self):
        for one in self.pending:
            one.wait_send()


def advance(steps):
    next(steps, None)


def plane_peers(axes):
    return [{axis: step(axis, d)} for axis in axes for d in (-1, 1)]


def swap_kernel(x_ref, o_ref, send_sem, recv_sem):
    greet([sibling()])
    mover = Mover(send_sem, recv_sem)
    mover.copy(x_ref, o_ref, sibling()).wait_recv()
    mover.finish()


def swap_cores(x, ident):
    return pl.pallas_call(
        swap_kernel,
        out_shape=jax.ShapeDtypeStruct(x.shape, x.dtype),
        in_specs=[pl.BlockSpec(memory_space=pltpu.VMEM)],
        out_specs=pl.BlockSpec(memory_space=pltpu.VMEM),
        scratch_shapes=[pltpu.SemaphoreType.DMA((1,)), pltpu.SemaphoreType.DMA((1,))],
        compiler_params=pltpu.CompilerParams(collective_id=ident, has_side_effects=True),
    )(x)


def exchange_steps(mover, src, dst):
    me = lax.axis_index("z")
    copies = [
        mover.copy(src.at[step("z", d)], dst.at[me], {"z": step("z", d)}) for d in (2, 1, 3)
    ]
    yield
    for copy in copies:
        copy.wait_recv()


def core_rows(lo=0, n=HALF, part=PART):
    base = lax.axis_index("tensor") * HALF

    def rows(start, size):
        return pl.ds(pl.multiple_of(start, 16), size)

    return (
        rows(base + lo, n),
        rows(base + lo, part),
        rows(base + (lo + part), n - part),
        rows(HALF - base + lo, n),
    )


def gather_steps(mover, x, out, span=(0, HALF, PART)):
    me, left, right, far = (step("z", d) for d in (0, -1, 1, 2))
    half, first, last, _ = core_rows(*span)
    to_right = mover.copy(x.at[half], out.at[me, half], {"z": right})
    to_left = mover.copy(x.at[half], out.at[me, half], {"z": left})
    yield
    to_right.wait_recv()
    on_right = mover.copy(out.at[left, first], out.at[left, first], {"z": right})
    shares = [mover.copy(out.at[left, half], out.at[left, half], sibling())]
    to_left.wait_recv()
    on_left = mover.copy(out.at[right, last], out.at[right, last], {"z": left})
    shares.append(mover.copy(out.at[right, half], out.at[right, half], sibling()))
    yield
    on_right.wait_recv()
    on_left.wait_recv()
    shares.append(mover.copy(out.at[far, half], out.at[far, half], sibling()))
    yield
    for copy in shares:
        copy.wait_recv()


def cut_rows(which, cut):
    base, size = (0, cut) if which == 0 else (cut, BLOCK - cut)
    part = -(-size // 32) * 16
    return pl.ds(base, size), pl.ds(base, part), pl.ds(base + part, size - part)


def plane_gather_steps(mover, axes, x, out, cut=HALF, order=(0, 1), share=False):
    a, b = (lax.axis_index(axis) for axis in axes)
    state = {}
    for which, axis in enumerate(axes):
        rows = cut_rows(which, cut)[0]
        place = (lambda i, r: out.at[i, b, r]) if which == 0 else (lambda i, r: out.at[a, i, r])
        me = (a, b)[which]
        to_right = mover.copy(x.at[rows], place(me, rows), {axis: step(axis, 1)})
        to_left = mover.copy(x.at[rows], place(me, rows), {axis: step(axis, -1)})
        state[which] = (axis, place, to_right, to_left)
    yield
    passed = {}
    for which in order:
        axis, place, to_right, to_left = state[which]
        _, first, last = cut_rows(which, cut)
        left, right = step(axis, -1), step(axis, 1)
        to_right.wait_recv()
        on_right = mover.copy(place(left, first), place(left, first), {axis: right})
        to_left.wait_recv()
        on_left = mover.copy(place(right, last), place(right, last), {axis: left})
        passed[which] = (on_right, on_left)
    yield
    state = {}
    shares = []

    def give(piece):
        if share:
            shares.append(mover.copy(piece, piece, sibling()))

    for which in order:
        axis, other = axes[which], axes[1 - which]
        rows = cut_rows(which, cut)[0]
        if which == 0:
            place = lambda i, lo, n, rows=rows: out.at[pl.ds(lo, n), i, rows]
        else:
            place = lambda i, lo, n, rows=rows: out.at[i, pl.ds(lo, n), rows]
        me = (b, a)[which]
        for copy in passed[which]:
            copy.wait_recv()
        to_right = mover.copy(place(me, 0, 4), place(me, 0, 4), {other: step(other, 1)})
        to_left = mover.copy(place(me, 0, 4), place(me, 0, 4), {other: step(other, -1)})
        give(place(me, 0, 4))
        state[which] = (other, place, to_right, to_left)
        yield
    ends = []
    for which in order:
        other, place, to_right, to_left = state[which]
        left, right = step(other, -1), step(other, 1)
        to_right.wait_recv()
        ends.append(mover.copy(place(left, 0, 2), place(left, 0, 2), {other: right}))
        give(place(left, 0, 4))
        to_left.wait_recv()
        ends.append(mover.copy(place(right, 2, 2), place(right, 2, 2), {other: left}))
        give(place(right, 0, 4))
        yield
    for copy in ends:
        copy.wait_recv()
    for which in order:
        other, place, _, _ = state[which]
        give(place(step(other, 2), 0, 4))
    for copy in shares:
        copy.wait_recv()


def lanes(shape):
    return lax.broadcasted_iota(jnp.int32, shape, len(shape) - 1)


def turn(values, cos, sin):
    return values * cos + pltpu.roll(values, 64, 1) * sin


def whole_rows(blocks, stage, dst):
    for i in range(RING):
        stage[i * OWN : (i + 1) * OWN] = blocks[i].astype(F32)[:OWN]
    dst[...] = stage[...].astype(LOW)


def first_kernel(
    attn_rows,
    feed_rows,
    tokens,
    dy,
    cos_ref,
    sin_ref,
    cos_kv,
    sin_kv,
    feed_full,
    attn_a,
    attn_b,
    normed_one,
    dy_all,
    query,
    kv_out,
    log_total,
    att_slice,
    residual,
    normed_two,
    attended,
    gain_ref,
    send_sem,
    recv_sem,
    local_sem,
    attn_got,
    mine_a,
    mine_b,
    weight_a,
    weight_b,
    attn_stage,
    feed_got,
    feed_mine,
    feed_stage,
    unit_low,
    unit_all,
    normed,
    qkv_send,
    qkv_got,
    kv_own,
    keyvalue,
    scores,
    att_send,
    part,
    sum_half,
    normed_low,
    *bufs,
):
    z, x, y, core = (lax.axis_index(axis) for axis in ("z", "x", "dp", "tensor"))
    plane = ("dp", "x")
    saves = []

    def save(src, dst):
        saves.append(pltpu.make_async_copy(src, dst, local_sem.at[len(saves)]))
        saves[-1].start()
        return saves[-1]

    greet([{"z": step("z", d)} for d in (1, 2, 3)] + plane_peers(plane) + [sibling()])
    mover = Mover(send_sem, recv_sem)

    attn_swap = exchange_steps(mover, attn_rows, attn_got)
    advance(attn_swap)
    feed_swap = exchange_steps(mover, feed_rows, feed_got)
    advance(feed_swap)
    values = tokens[...]
    unit = values * lax.rsqrt(jnp.mean(values * values, axis=-1, keepdims=True) + eps_norm)
    unit_low[...] = unit.astype(LOW)
    unit_gather = gather_steps(mover, unit_low, unit_all)
    advance(unit_gather)
    attn_got[z] = attn_rows[z]
    advance(attn_swap)
    for i in range(RING):
        attn_stage[i * OWN : (i + 1) * OWN] = attn_got[i].astype(F32)[:OWN]
    mine_a[...] = attn_stage[:, :512].astype(LOW)
    mine_b[...] = attn_stage[:, 512:].astype(LOW)
    a_gather = plane_gather_steps(mover, plane, mine_a, weight_a)
    advance(a_gather)
    weight_a[y, x] = mine_a[...]
    unit_all[z] = unit_low[...]
    advance(a_gather)
    feed_got[z] = feed_rows[z]
    advance(a_gather)
    advance(a_gather)
    advance(feed_swap)
    whole_rows(feed_got, feed_stage, feed_mine)
    feed_own = save(feed_mine, feed_full.at[y, x])
    advance(unit_gather)
    advance(a_gather)
    advance(a_gather)
    feed_gather = plane_gather_steps(mover, plane, feed_mine, feed_full)
    advance(feed_gather)
    advance(unit_gather)
    advance(unit_gather)
    advance(a_gather)
    save(weight_a, attn_a)

    scale_cols = weight_a[:, :, :, 384:].reshape(D, 128)
    pick = (lanes((8, 128)) == TAIL + lax.broadcasted_iota(jnp.int32, (8, 128), 0)).astype(LOW)
    gain_ref[...] = 1.0 + dot(pick, scale_cols, (1, 1))
    qkv_weight = weight_a[:, :, :, :384].reshape(D, 384)
    copies = []
    for d in (2, 1, 3, 0):
        block = step("z", d)
        rows = (unit_all[block].astype(F32) * gain_ref[0:1, :]).astype(LOW)
        normed[block] = rows
        qkv_send[block] = dot(rows, qkv_weight, (1, 0)).astype(LOW)
        if d:
            copies.append(mover.copy(qkv_send.at[block], qkv_got.at[z], {"z": block}))
    save(normed, normed_one)
    qkv_got[z] = qkv_send[z]
    feed_own.wait()
    advance(feed_gather)
    for copy in copies:
        copy.wait_recv()
    low_lanes = lanes((BLOCK, 128)) < TAIL
    cos, sin = cos_ref[...], sin_ref[...]

    def joined(i, offset):
        one, two = (qkv_got[i + k, :, 256:384].astype(F32) for k in (0, 1))
        if offset == 0:
            return jnp.where(low_lanes, one, pltpu.roll(two, TAIL, 1))
        return jnp.where(low_lanes, pltpu.roll(one, TAIL, 1), two)

    kv_own[:, :128] = turn(joined(0, 1), cos_kv[...], sin_kv[...]).astype(LOW)
    kv_own[:, 128:] = joined(2, 1).astype(LOW)
    kv_mine = keyvalue.at[core]
    kv_gather = plane_gather_steps(mover, ("x", "z"), kv_own, kv_mine, share=True)
    advance(kv_gather)
    keyvalue[core, x, z] = kv_own[...]
    scale = HD ** (-0.5)
    for h in range(4):
        first = qkv_got[h, :, :128].astype(F32)
        query[h, :, :128] = (turn(first, cos, sin) * scale).astype(LOW)
        query[h, :, 128:] = (qkv_got[h, :, 128:256].astype(F32) * scale).astype(LOW)
    query[4, :, :128] = (turn(joined(0, 0), cos, sin) * scale).astype(LOW)
    query[4, :, 128:] = (joined(2, 0) * scale).astype(LOW)
    b_gather = plane_gather_steps(mover, plane, mine_b, weight_b)
    advance(b_gather)
    weight_b[y, x] = mine_b[...]
    advance(kv_gather)
    advance(b_gather)
    for _ in range(2):
        advance(kv_gather)
        advance(b_gather)
    for _ in range(2):
        advance(kv_gather)
        advance(b_gather)
    for _ in range(2):
        advance(feed_gather)
    dy_gather = gather_steps(mover, dy, dy_all)
    advance(dy_gather)
    save(dy, dy_all.at[z])
    advance(kv_gather)
    save(keyvalue, kv_out)

    start = (x * RING + z) * BLOCK
    chunk = RING * BLOCK

    def one_head(h, carry):
        queries = query[h]
        top = jnp.full((BLOCK, 1), masked_fill, F32)
        for k in range(RING):
            rows = keyvalue[0, k].reshape(chunk, HD)
            tile = dot(queries, rows, (1, 1))
            gap = (start - k * chunk) + (
                lax.broadcasted_iota(jnp.int32, tile.shape, 0) - lanes(tile.shape)
            )
            tile = jnp.where((gap >= 0) & (gap < WINDOW), tile, masked_fill)
            scores[:, k * chunk : (k + 1) * chunk] = tile
            top = jnp.maximum(top, jnp.max(tile, axis=-1, keepdims=True))
        sums = jnp.zeros((BLOCK, 1), F32)
        for k in range(RING):
            tile = jnp.exp(scores[:, k * chunk : (k + 1) * chunk] - top)
            scores[:, k * chunk : (k + 1) * chunk] = tile
            sums = sums + jnp.sum(tile, axis=-1, keepdims=True)
        inverse = 1.0 / sums
        result = jnp.zeros((BLOCK, HD), F32)
        for k in range(RING):
            low = (scores[:, k * chunk : (k + 1) * chunk] * inverse).astype(LOW)
            result = result + dot(low, keyvalue[1, k].reshape(chunk, HD), (1, 0))
        attended[h] = result
        log_total[h] = jnp.broadcast_to(top + jnp.log(sums), (BLOCK, 128))
        return carry

    lax.fori_loop(0, 5, one_head, 0)
    for j in range(RING):
        att_send[j, :, 128:] = attended[j].astype(LOW)
        tile = attended[4, :, (j // 2) * 128 : (j // 2 + 1) * 128]
        tile = pltpu.roll(tile, TAIL, 1) if j % 2 else tile
        att_send[j, :, :128] = jnp.where(low_lanes, tile, 0.0).astype(LOW)
    att_swap = exchange_steps(mover, att_send, att_slice)
    advance(att_swap)
    att_slice[z] = att_send[z]
    advance(att_swap)

    advance(b_gather)
    save(weight_b, attn_b)

    last_weight = weight_a[:, :, :, 384:].reshape(D, 128)
    main_weight = weight_b[...].reshape(D, HD)

    def make(block):
        rows = dot(att_slice[block, :, :128], last_weight, (1, 1))
        part[block] = (rows + dot(att_slice[block, :, 128:], main_weight, (1, 1))).astype(LOW)

    shares = []
    sharing = share_steps(mover, part, bufs[0], shares, make)
    advance(sharing)
    advance(sharing)
    sums = [
        reduce_steps(mover, own_rows(part), shares[i], bufs, sum_half, span)
        for i, span in enumerate(SPANS)
    ]
    for one in sums:
        advance(one)
    advance(sharing)
    advance(sharing)
    for one in sums:
        advance(one)

    def normed_rows(rows):
        unit = rows * lax.rsqrt(jnp.mean(rows * rows, axis=-1, keepdims=True) + eps_norm)
        return (unit * gain_ref[1:2, :]).astype(LOW)

    gathers, res_shares = [], []
    for one, span in zip(sums, SPANS, strict=True):
        advance(one)
        place = core_rows(*span)[0]
        rows = tokens[place, :] + sum_half[span[0] : span[0] + span[1]]
        residual[place, :] = rows
        normed_low[place, :] = normed_rows(rows)
        gathers.append(gather_steps(mover, normed_low, normed_two, span))
        advance(gathers[-1])
        res_shares.append(mover.copy(residual.at[place], residual.at[place], sibling()))
    advance(dy_gather)
    for copy in res_shares:
        copy.wait_recv()
    theirs = core_rows()[3]
    normed_low[theirs, :] = normed_rows(residual[theirs, :])
    save(normed_low, normed_two.at[z])
    for one in gathers:
        advance(one)
    advance(feed_gather)
    advance(feed_gather)
    for one in gathers:
        advance(one)
    advance(dy_gather)
    for one in gathers:
        advance(one)
    advance(dy_gather)
    advance(feed_gather)
    for one in saves:
        if one is not feed_own:
            one.wait()
    mover.finish()


def run_first(*operands):
    out = {
        "feed_full": ((RING, RING, BLOCK, 2944), LOW),
        "attn_a": ((RING, RING, BLOCK, 512), LOW),
        "attn_b": ((RING, RING, BLOCK, HD), LOW),
        "normed_one": ((RING, BLOCK, D), LOW),
        "dy_all": ((RING, BLOCK, D), LOW),
        "query": ((5, BLOCK, HD), LOW),
        "keyvalue": ((2, RING, RING, BLOCK, HD), LOW),
        "log_total": ((5, BLOCK, 128), F32),
        "att_slice": ((RING, BLOCK, 384), LOW),
        "residual": ((BLOCK, D), F32),
        "normed_two": ((RING, BLOCK, D), LOW),
        "attended": ((5, BLOCK, HD), F32),
        "gains": ((8, D), F32),
    }
    remote = ("feed_full", "attn_a", "attn_b", "normed_one", "dy_all", "keyvalue", "normed_two")
    spaces = [pltpu.VMEM, pltpu.VMEM, pltpu.VMEM, pl.ANY] + [pltpu.VMEM] * 4
    scratch = [
        pltpu.VMEM((RING, PAD, 768), LOW),
        pltpu.VMEM((BLOCK, 512), LOW),
        pltpu.VMEM((BLOCK, HD), LOW),
        pltpu.VMEM((RING, RING, BLOCK, 512), LOW),
        pltpu.VMEM((RING, RING, BLOCK, HD), LOW),
        pltpu.VMEM((BLOCK, 768), F32),
        pltpu.VMEM((RING, PAD, 2944), LOW),
        pltpu.VMEM((BLOCK, 2944), LOW),
        pltpu.VMEM((BLOCK, 2944), F32),
        pltpu.VMEM((BLOCK, D), LOW),
        pltpu.VMEM((RING, BLOCK, D), LOW),
        pltpu.VMEM((RING, BLOCK, D), LOW),
        pltpu.VMEM((RING, BLOCK, 384), LOW),
        pltpu.VMEM((RING, BLOCK, 384), LOW),
        pltpu.VMEM((BLOCK, HD), LOW),
        pltpu.VMEM((2, RING, RING, BLOCK, HD), LOW),
        pltpu.VMEM((BLOCK, RING * RING * BLOCK), F32),
        pltpu.VMEM((RING, BLOCK, 384), LOW),
        pltpu.VMEM((RING, BLOCK, D), LOW),
        pltpu.VMEM((HALF, D), F32),
        pltpu.VMEM((BLOCK, D), LOW),
        *reduce_scratch(),
    ]
    return call(
        first_kernel, 1, 150, out, scratch, operands, spaces, {name: pl.ANY for name in remote}
    )


def plane_reduce_steps(mover, axes, g, bufs, res, loads=None):
    far, side, near, far_two, side_two = bufs
    places = [lax.axis_index(axis) for axis in axes]

    def block(which, i, lo, n):
        rows = pl.ds(which * HALF, HALF)
        return g.at[i, pl.ds(lo, n), rows] if which == 0 else g.at[pl.ds(lo, n), i, rows]

    locals_ = []

    def load(src, dst):
        locals_.append(pltpu.make_async_copy(src, dst, loads.at[len(locals_)]))
        locals_[-1].start()
        return locals_[-1]

    first, sides, wanted = [], [], []
    for which, axis in enumerate(axes):
        right, left = step(axis, 1), step(axis, -1)
        far_place = step(axis, 2)
        first.append(
            (
                mover.copy(block(which, far_place, 0, 2), far.at[which, pl.ds(0, 2)], {axis: right}),
                mover.copy(block(which, far_place, 2, 2), far.at[which, pl.ds(2, 2)], {axis: left}),
            )
        )
        if loads is not None:
            wanted.append(
                (
                    load(block(which, right, 0, 2), near.at[which, 0]),
                    load(block(which, left, 2, 2), near.at[which, 1]),
                )
            )
    for which, axis in enumerate(axes):
        right, left = step(axis, 1), step(axis, -1)
        sides.append(
            [
                mover.copy(block(which, right, 2, 2), side.at[which, 0, pl.ds(2, 2)], {axis: right}),
                mover.copy(block(which, left, 0, 2), side.at[which, 1, pl.ds(0, 2)], {axis: left}),
            ]
        )
    yield
    owned = []
    for which, axis in enumerate(axes):
        for k, (d, lo) in enumerate(((1, 0), (-1, 2))):
            first[which][k].wait_recv()
            if loads is not None:
                wanted[which][k].wait()
                term = near[which, k]
            else:
                term = block(which, step(axis, d), lo, 2)[...]
            near[which, k] = (term.astype(F32) + far[which, lo : lo + 2].astype(F32)).astype(LOW)
            sides[which].append(
                mover.copy(near.at[which, k], side.at[which, k, pl.ds(lo, 2)], {axis: step(axis, d)})
            )
        if loads is not None:
            owned.append(load(block(which, places[which], 0, 4), far.at[which]))
    yield

    def summed(which, i):
        if loads is not None:
            term = far[which, i]
        else:
            rows = pl.ds(which * HALF, HALF)
            me = places[which]
            term = (g[me, i, rows] if which == 0 else g[i, me, rows])
        return (
            term.astype(F32) + side[which, 0, i].astype(F32) + side[which, 1, i].astype(F32)
        )

    second = []
    for which, axis in enumerate(axes):
        other = axes[1 - which]
        right, left = {other: step(other, 1)}, {other: step(other, -1)}
        for copy in sides[which]:
            copy.wait_recv()
        if loads is not None:
            owned[which].wait()
        far_two[which, 0] = summed(which, step(other, 2)).astype(LOW)
        upper, lower = pl.ds(0, PART), pl.ds(PART, HALF - PART)
        second.append(
            (
                mover.copy(far_two.at[which, 0, upper], far_two.at[which, 1, upper], right),
                mover.copy(far_two.at[which, 0, lower], far_two.at[which, 1, lower], left),
            )
        )
    yield
    last = []
    for which, axis in enumerate(axes):
        other = axes[1 - which]
        right, left = step(other, 1), step(other, -1)
        total = summed(which, right)
        second[which][0].wait_recv()
        side_two[which, 0, :PART] = (
            total[:PART] + far_two[which, 1, :PART].astype(F32)
        ).astype(LOW)
        side_two[which, 0, PART:] = total[PART:].astype(LOW)
        last.append(mover.copy(side_two.at[which, 0], side_two.at[which, 2], {other: right}))
        total = summed(which, left)
        second[which][1].wait_recv()
        side_two[which, 1, :PART] = total[:PART].astype(LOW)
        side_two[which, 1, PART:] = (
            total[PART:] + far_two[which, 1, PART:].astype(F32)
        ).astype(LOW)
        last.append(mover.copy(side_two.at[which, 1], side_two.at[which, 3], {other: left}))
    yield
    for which, axis in enumerate(axes):
        other = axes[1 - which]
        last[2 * which].wait_recv()
        last[2 * which + 1].wait_recv()
        res[which * HALF : (which + 1) * HALF] = (
            summed(which, lax.axis_index(other))
            + side_two[which, 2].astype(F32)
            + side_two[which, 3].astype(F32)
        )


def plane_reduce_scratch(columns):
    return [
        pltpu.VMEM((2, 4, HALF, columns), LOW),
        pltpu.VMEM((2, 2, 4, HALF, columns), LOW),
        pltpu.VMEM((2, 2, 2, HALF, columns), LOW),
        pltpu.VMEM((2, 2, HALF, columns), LOW),
        pltpu.VMEM((2, 4, HALF, columns), LOW),
        pltpu.VMEM((BLOCK, columns), F32),
    ]


def share_steps(mover, part, other, shares, make=None, spans=SPANS):
    me, left, right, far = (step("z", d) for d in (0, -1, 1, 2))
    shares.extend([] for _ in spans)
    for slot, block in enumerate((far, right, left, me)):
        if make is not None:
            make(block)
        for copies, (lo, n, first) in zip(shares, spans, strict=True):
            theirs = core_rows(lo, n, first)[3]
            copies.append(
                mover.copy(part.at[block, theirs], other.at[slot, pl.ds(lo, n)], sibling())
            )
        yield


def reduce_steps(mover, mine, shares, bufs, out, span):
    other, total, far_in, from_left, from_right = bufs
    lo, n, part = span
    me, left, right, far = (step("z", d) for d in (0, -1, 1, 2))
    blocks = (far, right, left, me)
    rows, first, last = pl.ds(lo, n), pl.ds(lo, part), pl.ds(lo + part, n - part)

    def both(slot):
        return mine(blocks[slot], span).astype(F32) + other[slot, rows].astype(F32)

    shares[0].wait_recv()
    total[0, rows] = both(0).astype(LOW)
    far_right = mover.copy(total.at[0, first], far_in.at[first], {"z": right})
    far_left = mover.copy(total.at[0, last], far_in.at[last], {"z": left})
    yield
    shares[1].wait_recv()
    summed = both(1)
    far_right.wait_recv()
    total[1, first] = (summed[:part] + far_in[first].astype(F32)).astype(LOW)
    total[1, last] = summed[part:].astype(LOW)
    to_right = mover.copy(total.at[1, rows], from_left.at[rows], {"z": right})
    shares[2].wait_recv()
    summed = both(2)
    far_left.wait_recv()
    total[2, first] = summed[:part].astype(LOW)
    total[2, last] = (summed[part:] + far_in[last].astype(F32)).astype(LOW)
    to_left = mover.copy(total.at[2, rows], from_right.at[rows], {"z": left})
    yield
    shares[3].wait_recv()
    summed = both(3)
    to_right.wait_recv()
    to_left.wait_recv()
    out[rows] = summed + from_left[rows].astype(F32) + from_right[rows].astype(F32)


def own_rows(ref):
    return lambda block, span: ref[block, core_rows(*span)[0]]


def half_rows(ref):
    return lambda block, span: ref[block, pl.ds(span[0], span[1])]


def reduce_scratch():
    return [
        pltpu.VMEM((4, HALF, D), LOW),
        pltpu.VMEM((3, HALF, D), LOW),
        pltpu.VMEM((HALF, D), LOW),
        pltpu.VMEM((HALF, D), LOW),
        pltpu.VMEM((HALF, D), LOW),
    ]


def spread_rows(res, dst):
    for i in range(RING):
        rows = res[i * OWN : (i + 1) * OWN]
        dst[i] = jnp.concatenate([rows, jnp.zeros((PAD - OWN, rows.shape[1]), F32)]).astype(LOW)


def activation(gate, upper, grad):
    square = gate * gate
    tanh = jnp.tanh(GELU_SCALE * gate * (1.0 + GELU_CUBE * square))
    half = 0.5 * (1.0 + tanh)
    gelu = gate * half
    slope = half + 0.5 * gate * (1.0 - tanh * tanh) * GELU_SCALE * (1.0 + 3.0 * GELU_CUBE * square)
    return gelu * upper, grad * upper * slope, grad * gelu


def second_kernel(
    feed_full,
    normed_two,
    dy_all,
    cotangent,
    residual,
    gain_ref,
    grad_rows,
    da_all,
    feed_part,
    gateup_grads,
    down_rows,
    send_sem,
    recv_sem,
    local_sem,
    normed_in,
    dy_in,
    gateup_weight,
    down_weight,
    hidden,
    dgu,
    norm_part,
    stage,
    grad_half,
    cot_half,
    res_half,
    da_low,
    *bufs,
):
    z = lax.axis_index("z")
    half, _, _, _ = core_rows()
    plane = ("dp", "x")
    gu_width = 2 * (MAIN + TAIL)
    wide = RING * BLOCK
    loads = [
        pltpu.make_async_copy(src, dst, local_sem.at[i])
        for i, (src, dst) in enumerate(
            (
                (normed_two, normed_in),
                (feed_full.at[:, :, :, pl.ds(0, gu_width)], gateup_weight),
                (dy_all, dy_in),
                (feed_full.at[:, :, :, pl.ds(gu_width, 1024)], down_weight),
                (cotangent.at[half], cot_half),
                (residual.at[half], res_half),
            )
        )
    ]
    for load in loads:
        load.start()
    greet(plane_peers(("z",)) + plane_peers(plane) + [sibling()])
    mover = Mover(send_sem, recv_sem)
    for load in loads:
        load.wait()

    def product(rows, weight, lo, n):
        left_side = rows[...].reshape(wide, D)
        return dot(left_side, weight[:, :, :, lo : lo + n].reshape(D, n), (1, 0))

    for lo, n in ((0, 256), (256, 256), (512, 256), (768, 128)):
        value, grad_gate, grad_upper = activation(
            product(normed_in, gateup_weight, lo, n),
            product(normed_in, gateup_weight, MAIN + lo, n),
            product(dy_in, down_weight, lo, n),
        )
        hidden[:, lo : lo + n] = value.astype(LOW)
        dgu[:, lo : lo + n] = grad_gate.astype(LOW)
        dgu[:, MAIN + lo : MAIN + lo + n] = grad_upper.astype(LOW)
    both = product(normed_in, gateup_weight, 2 * MAIN, 2 * TAIL)
    value, grad_gate, grad_upper = activation(
        both, pltpu.roll(both, TAIL, 1), product(dy_in, down_weight, MAIN, 2 * TAIL)
    )
    low_lanes = lanes(both.shape) < TAIL
    hidden[:, MAIN:] = jnp.where(low_lanes, value, 0.0).astype(LOW)
    dgu[:, 2 * MAIN :] = jnp.where(low_lanes, grad_gate, pltpu.roll(grad_upper, TAIL, 1)).astype(LOW)

    for i in range(RING):
        part = dot(dgu[...], gateup_weight[i].reshape(wide, gu_width), (1, 1))
        norm_part[:, :, i * wide : (i + 1) * wide] = part.astype(LOW).reshape(RING, BLOCK, wide)
    shares = []
    sharing = share_steps(mover, norm_part, bufs[0], shares)
    for _ in range(RING):
        advance(sharing)
    sums = [
        reduce_steps(mover, own_rows(norm_part), shares[i], bufs[:5], grad_half, span)
        for i, span in enumerate(SPANS)
    ]

    for i in range(RING):
        terms = dot(hidden[...], down_weight[i].reshape(wide, 1024), (1, 1))
        feed_part[:, :, i * wide : (i + 1) * wide] = terms.astype(LOW).reshape(RING, BLOCK, wide)
        if i < 2:
            advance(sums[i])

    def columns(rows, i):
        return rows[:, :, i * wide : (i + 1) * wide].reshape(wide, wide)

    for i in range(RING):
        grads = dot(columns(dy_in, i), hidden[...], (0, 0))
        down_weight[i] = grads.astype(LOW).reshape(RING, BLOCK, 1024)
        if i < 2:
            advance(sums[i])
    down_sum = plane_reduce_steps(mover, plane, down_weight, bufs[5:10], bufs[10])
    advance(down_sum)
    saved = []

    def gateup_block(i):
        if saved:
            saved[-1].wait()
        grads = dot(columns(normed_in, i), dgu[...], (0, 0))
        stage[...] = grads.astype(LOW).reshape(RING, BLOCK, gu_width)
        saved.append(pltpu.make_async_copy(stage, gateup_grads.at[i], local_sem.at[10 + i]))
        saved[-1].start()

    gateup_block(0)
    gathers, da_shares = [], []
    for one, span in zip(sums, SPANS, strict=True):
        advance(one)
        piece = pl.ds(span[0], span[1])
        place = core_rows(*span)[0]
        rows = res_half[piece, :]
        inverse = lax.rsqrt(jnp.mean(rows * rows, axis=-1, keepdims=True) + eps_norm)
        unit = rows * inverse
        scaled = grad_half[piece, :] * gain_ref[1:2, :]
        grad = cot_half[piece, :] + inverse * (
            scaled - unit * jnp.mean(scaled * unit, axis=-1, keepdims=True)
        )
        grad_rows[piece, :] = grad
        da_low[place, :] = grad.astype(LOW)
        gathers.append(gather_steps(mover, da_low, da_all, span))
        advance(gathers[-1])
        da_shares.append(mover.copy(da_low.at[place], da_low.at[place], sibling()))
    advance(down_sum)
    gateup_block(1)
    for copy in da_shares:
        copy.wait_recv()
    da_own = pltpu.make_async_copy(da_low, da_all.at[z], local_sem.at[9])
    da_own.start()
    for one in gathers:
        advance(one)
    gateup_block(2)
    advance(down_sum)
    for one in gathers:
        advance(one)
    gateup_block(3)
    advance(down_sum)
    for one in gathers:
        advance(one)
    advance(down_sum)
    spread_rows(bufs[10], down_rows)
    saved[-1].wait()
    da_own.wait()
    mover.finish()


def third_kernel(
    feed_part,
    gateup_grads,
    da_all,
    residual,
    attn_a,
    attn_b,
    att_slice,
    query,
    kv_hbm,
    log_total,
    attended,
    cos_ref,
    sin_ref,
    cos_kv,
    sin_kv,
    grad_out,
    grad_got,
    gateup_rows,
    output,
    send_sem,
    recv_sem,
    local_sem,
    da_in,
    last_weight,
    main_weight,
    keyvalue,
    feed_mine,
    out_half,
    datt_send,
    datt_got,
    datt,
    delta,
    ds_all,
    p_all,
    dq,
    kv_pair,
    kv_in,
    grad_kv,
    grad_query,
    grad_send,
    kv_low,
    *bufs,
):
    z, core = lax.axis_index("z"), lax.axis_index("tensor")
    x = lax.axis_index("x")
    half = core_rows()[0]
    whole_span = ((0, HALF, PART),)
    out_bufs, rows_bufs, rows_res = bufs[:5], bufs[5:10], bufs[10]
    kv_bufs, kv_rows = bufs[11:16], bufs[16]
    loads = [
        pltpu.make_async_copy(src, dst, local_sem.at[8 + i])
        for i, (src, dst) in enumerate(
            (
                (da_all, da_in),
                (attn_a.at[:, :, :, pl.ds(384, 128)], last_weight),
                (attn_b, main_weight),
                (kv_hbm, keyvalue),
                (feed_part.at[:, half], feed_mine),
            )
        )
    ]
    for load in loads:
        load.start()
    greet([{"z": step("z", d)} for d in (1, 2, 3)] + plane_peers(("dp", "x")) + [sibling()])
    mover = Mover(send_sem, recv_sem)
    rows_sum = plane_reduce_steps(
        mover, ("dp", "x"), gateup_grads, rows_bufs, rows_res, loads=local_sem
    )
    advance(rows_sum)
    for load in loads[:3]:
        load.wait()
    last = last_weight[...].reshape(D, 128)
    main = main_weight[...].reshape(D, HD)
    copies = []
    for d in (2, 1, 3, 0):
        block = step("z", d)
        datt_send[block, :, :128] = dot(da_in[block], last, (1, 0)).astype(LOW)
        datt_send[block, :, 128:] = dot(da_in[block], main, (1, 0)).astype(LOW)
        if d:
            copies.append(mover.copy(datt_send.at[block], datt_got.at[z], {"z": block}))
    datt_got[z] = datt_send[z]
    shares = []
    sharing = share_steps(mover, feed_part, out_bufs[0], shares, spans=whole_span)
    for _ in range(RING):
        advance(sharing)
    feed_sum = reduce_steps(
        mover, half_rows(feed_mine), shares[0], out_bufs, out_half, whole_span[0]
    )
    slices = att_slice[...].reshape(RING * BLOCK, 384)
    wide = RING * BLOCK
    for i in range(RING):
        left_side = da_in[:, :, i * wide : (i + 1) * wide].reshape(wide, wide)
        grad_out[i] = dot(left_side, slices, (0, 0)).astype(LOW).reshape(RING, BLOCK, 384)
    for copy in copies:
        copy.wait_recv()
    for load in loads[3:]:
        load.wait()
    advance(feed_sum)
    advance(rows_sum)

    low_lanes = lanes((BLOCK, 128)) < TAIL
    for h in range(4):
        datt[h] = datt_got[h, :, 128:]
    for k in range(2):
        one, two = (datt_got[2 * k + i, :, :128].astype(F32) for i in range(2))
        datt[4, :, k * 128 : (k + 1) * 128] = jnp.where(
            low_lanes, one, pltpu.roll(two, TAIL, 1)
        ).astype(LOW)
    for h in range(5):
        delta[h] = jnp.broadcast_to(
            jnp.sum(datt[h].astype(F32) * attended[h], axis=-1, keepdims=True), (BLOCK, 128)
        )
        dq[h] = jnp.zeros((BLOCK, HD), F32)
    start = (x * RING + z) * BLOCK
    chunk = RING * BLOCK

    def one_chunk(k, carry):
        keys = keyvalue[0, k].reshape(chunk, HD)
        values = keyvalue[1, k].reshape(chunk, HD)
        shape = (BLOCK, chunk)
        gap = (start - k * chunk) + (lax.broadcasted_iota(jnp.int32, shape, 0) - lanes(shape))
        visible = (gap >= 0) & (gap < WINDOW)

        def one_head(h, carry):
            scores = dot(query[h], keys, (1, 1))
            probs = jnp.where(visible, jnp.exp(scores - log_total[h, :, :1]), 0.0)
            grads = dot(datt[h], values, (1, 1))
            low = (probs * (grads - delta[h, :, :1])).astype(LOW)
            ds_all[h] = low
            p_all[h] = probs.astype(LOW)
            dq[h] = dq[h] + dot(low, keys, (1, 0))
            return carry

        lax.fori_loop(0, 5, one_head, 0)
        queries = query[...].reshape(5 * BLOCK, HD)
        outer = datt[...].reshape(5 * BLOCK, HD)
        kv_pair[0, k] = dot(ds_all[...].reshape(5 * BLOCK, chunk), queries, (0, 0)).astype(LOW).reshape(RING, BLOCK, HD)
        kv_pair[1, k] = dot(p_all[...].reshape(5 * BLOCK, chunk), outer, (0, 0)).astype(LOW).reshape(RING, BLOCK, HD)
        return carry

    lax.fori_loop(0, RING, one_chunk, 0)
    kv_swap = mover.copy(kv_pair.at[1 - core], kv_in, sibling())
    advance(feed_sum)
    cos, sin = cos_ref[...], sin_ref[...]
    scale = HD ** (-0.5)
    for h in range(5):
        grad_query[h, :, :128] = turn(dq[h, :, :128] * scale, cos, -sin)
        grad_query[h, :, 128:] = dq[h, :, 128:] * scale
    kv_swap.wait_recv()
    grad_kv[...] = (kv_pair[core].astype(F32) + kv_in[...].astype(F32)).astype(LOW)
    kv_sum = plane_reduce_steps(mover, ("x", "z"), grad_kv, kv_bufs, kv_rows)
    advance(kv_sum)
    for h in range(4):
        grad_send[h, :, :HD] = grad_query[h].astype(LOW)
    advance(kv_sum)
    advance(kv_sum)
    advance(kv_sum)
    advance(kv_sum)
    kv_low[:, :128] = turn(kv_rows[:, :128], cos_kv[...], -sin_kv[...])
    kv_low[:, 128:] = kv_rows[:, 128:]
    for j in range(RING):
        place = slice((j // 2) * 128, (j // 2 + 1) * 128)
        one, two = grad_query[4, :, place], kv_low[:, place]
        if j % 2:
            one = pltpu.roll(one, TAIL, 1)
        else:
            two = pltpu.roll(two, TAIL, 1)
        grad_send[j, :, HD:] = jnp.where(low_lanes, one, two).astype(LOW)
    swap = exchange_steps(mover, grad_send, grad_got)
    advance(swap)
    grad_got[z] = grad_send[z]
    advance(feed_sum)
    output[half, :] = residual[half, :] + out_half[...]
    out_share = mover.copy(output.at[half], output.at[half], sibling())
    advance(rows_sum)
    advance(swap)
    advance(rows_sum)
    advance(rows_sum)
    spread_rows(rows_res, gateup_rows)
    out_share.wait_recv()
    mover.finish()


def fourth_kernel(
    grad_got,
    gateup_rows,
    down_rows,
    grad_out,
    attn_a,
    normed_hbm,
    grad_rows,
    tokens,
    gain_ref,
    grad_tokens,
    gateup_got,
    down_got,
    out_got,
    qkv_got,
    send_sem,
    recv_sem,
    local_sem,
    qkv_weight,
    normed_one,
    part,
    grad_half,
    grad_qkv,
    out_send,
    qkv_send,
    *bufs,
):
    z = lax.axis_index("z")
    half, _, _, _ = core_rows()
    plane = ("dp", "x")
    sum_bufs = bufs[:5]
    out_bufs, qkv_bufs = bufs[5:11], bufs[11:17]
    loads = [
        pltpu.make_async_copy(attn_a.at[:, :, :, pl.ds(0, 384)], qkv_weight, local_sem.at[0]),
        pltpu.make_async_copy(normed_hbm, normed_one, local_sem.at[1]),
    ]
    for load in loads:
        load.start()
    greet([{"z": step("z", d)} for d in (1, 2, 3)] + plane_peers(plane) + [sibling()])
    mover = Mover(send_sem, recv_sem)
    out_sum = plane_reduce_steps(mover, plane, grad_out, out_bufs[:5], out_bufs[5])
    advance(out_sum)
    slices = grad_got[...].reshape(RING * BLOCK, 384)
    wide = RING * BLOCK
    loads[0].wait()
    weight = qkv_weight[...].reshape(D, 384)

    def make(block):
        part[block] = dot(grad_got[block], weight, (1, 1)).astype(LOW)

    shares = []
    sharing = share_steps(mover, part, sum_bufs[0], shares, make)
    advance(sharing)
    advance(sharing)
    sums = [
        reduce_steps(mover, own_rows(part), shares[i], sum_bufs, grad_half, span)
        for i, span in enumerate(SPANS)
    ]
    for one in sums:
        advance(one)
    advance(sharing)
    advance(sharing)
    advance(out_sum)
    loads[1].wait()
    for i in range(RING):
        left_side = normed_one[:, :, i * wide : (i + 1) * wide].reshape(wide, wide)
        grad_qkv[i] = dot(left_side, slices, (0, 0)).astype(LOW).reshape(RING, BLOCK, 384)
        if i % 2:
            advance(sums[i // 2])
    qkv_sum = plane_reduce_steps(mover, plane, grad_qkv, qkv_bufs[:5], qkv_bufs[5])
    advance(qkv_sum)
    advance(out_sum)
    gateup_swap = exchange_steps(mover, gateup_rows, gateup_got)
    advance(gateup_swap)
    down_swap = exchange_steps(mover, down_rows, down_got)
    advance(down_swap)
    gateup_got[z] = gateup_rows[z]
    down_got[z] = down_rows[z]
    advance(qkv_sum)
    advance(out_sum)
    advance(out_sum)
    spread_rows(out_bufs[5], out_send)
    out_swap = exchange_steps(mover, out_send, out_got)
    advance(out_swap)
    out_got[z] = out_send[z]
    advance(qkv_sum)
    for one in sums:
        advance(one)
    rows = tokens[half, :]
    inverse = lax.rsqrt(jnp.mean(rows * rows, axis=-1, keepdims=True) + eps_norm)
    unit = rows * inverse
    scaled = grad_half[...] * gain_ref[0:1, :]
    grad_tokens[half, :] = grad_rows[...] + inverse * (
        scaled - unit * jnp.mean(scaled * unit, axis=-1, keepdims=True)
    )
    share = mover.copy(grad_tokens.at[half], grad_tokens.at[half], sibling())
    advance(qkv_sum)
    advance(qkv_sum)
    spread_rows(qkv_bufs[5], qkv_send)
    qkv_swap = exchange_steps(mover, qkv_send, qkv_got)
    advance(qkv_swap)
    qkv_got[z] = qkv_send[z]
    for steps in (gateup_swap, down_swap, out_swap, qkv_swap):
        advance(steps)
    share.wait_recv()
    mover.finish()


def call(kernel, ident, copies, out, scratch, operands, spaces, out_spaces=None):
    results = pl.pallas_call(
        kernel,
        out_shape=[jax.ShapeDtypeStruct(shape, kind) for shape, kind in out.values()],
        in_specs=[pl.BlockSpec(memory_space=space) for space in spaces],
        out_specs=[pl.BlockSpec(memory_space=(out_spaces or {}).get(name, pltpu.VMEM)) for name in out],
        scratch_shapes=[
            pltpu.SemaphoreType.DMA((copies,)),
            pltpu.SemaphoreType.DMA((copies,)),
            pltpu.SemaphoreType.DMA((16,)),
            *scratch,
        ],
        compiler_params=pltpu.CompilerParams(
            collective_id=ident, has_side_effects=True, vmem_limit_bytes=60 * 1024 * 1024
        ),
    )(*operands)
    return dict(zip(out, results, strict=True))


def run_second(*operands):
    out = {
        "grad_rows": ((HALF, D), F32),
        "da_all": ((RING, BLOCK, D), LOW),
        "feed_part": ((RING, BLOCK, D), LOW),
        "gateup_grads": ((RING, RING, BLOCK, 2 * (MAIN + TAIL)), LOW),
        "down_rows": ((RING, PAD, 1024), LOW),
    }
    scratch = [
        pltpu.VMEM((RING, BLOCK, D), LOW),
        pltpu.VMEM((RING, BLOCK, D), LOW),
        pltpu.VMEM((RING, RING, BLOCK, 2 * (MAIN + TAIL)), LOW),
        pltpu.VMEM((RING, RING, BLOCK, 1024), LOW),
        pltpu.VMEM((RING * BLOCK, 1024), LOW),
        pltpu.VMEM((RING * BLOCK, 2 * (MAIN + TAIL)), LOW),
        pltpu.VMEM((RING, BLOCK, D), LOW),
        pltpu.VMEM((RING, BLOCK, 2 * (MAIN + TAIL)), LOW),
        pltpu.VMEM((HALF, D), F32),
        pltpu.VMEM((HALF, D), F32),
        pltpu.VMEM((HALF, D), F32),
        pltpu.VMEM((BLOCK, D), LOW),
        *reduce_scratch(),
        *plane_reduce_scratch(1024),
    ]
    spaces = [pl.ANY] * 5 + [pltpu.VMEM]
    return call(
        second_kernel, 5, 80, out, scratch, operands, spaces, {"gateup_grads": pl.ANY, "da_all": pl.ANY}
    )


def run_third(*operands):
    out = {
        "grad_out": ((RING, RING, BLOCK, 384), LOW),
        "grad_got": ((RING, BLOCK, 384), LOW),
        "gateup_rows": ((RING, PAD, 2 * (MAIN + TAIL)), LOW),
        "output": ((BLOCK, D), F32),
    }
    scratch = [
        pltpu.VMEM((RING, BLOCK, D), LOW),
        pltpu.VMEM((RING, RING, BLOCK, 128), LOW),
        pltpu.VMEM((RING, RING, BLOCK, HD), LOW),
        pltpu.VMEM((2, RING, RING, BLOCK, HD), LOW),
        pltpu.VMEM((RING, HALF, D), LOW),
        pltpu.VMEM((HALF, D), F32),
        pltpu.VMEM((RING, BLOCK, 384), LOW),
        pltpu.VMEM((RING, BLOCK, 384), LOW),
        pltpu.VMEM((5, BLOCK, HD), LOW),
        pltpu.VMEM((5, BLOCK, 128), F32),
        pltpu.VMEM((5, BLOCK, RING * BLOCK), LOW),
        pltpu.VMEM((5, BLOCK, RING * BLOCK), LOW),
        pltpu.VMEM((5, BLOCK, HD), F32),
        pltpu.VMEM((2, RING, RING, BLOCK, HD), LOW),
        pltpu.VMEM((RING, RING, BLOCK, HD), LOW),
        pltpu.VMEM((RING, RING, BLOCK, HD), LOW),
        pltpu.VMEM((5, BLOCK, HD), F32),
        pltpu.VMEM((RING, BLOCK, 384), LOW),
        pltpu.VMEM((BLOCK, HD), F32),
        *reduce_scratch(),
        *plane_reduce_scratch(2 * (MAIN + TAIL)),
        *plane_reduce_scratch(HD),
    ]
    spaces = [pl.ANY] * 3 + [pltpu.VMEM] + [pl.ANY] * 2 + [pltpu.VMEM] * 2 + [pl.ANY] + [pltpu.VMEM] * 6
    return call(third_kernel, 2, 100, out, scratch, operands, spaces)


def run_fourth(*operands):
    out = {
        "grad_tokens": ((BLOCK, D), F32),
        "gateup_got": ((RING, PAD, 2 * (MAIN + TAIL)), LOW),
        "down_got": ((RING, PAD, 1024), LOW),
        "out_got": ((RING, PAD, 384), LOW),
        "qkv_got": ((RING, PAD, 384), LOW),
    }
    scratch = [
        pltpu.VMEM((RING, RING, BLOCK, 384), LOW),
        pltpu.VMEM((RING, BLOCK, D), LOW),
        pltpu.VMEM((RING, BLOCK, D), LOW),
        pltpu.VMEM((HALF, D), F32),
        pltpu.VMEM((RING, RING, BLOCK, 384), LOW),
        pltpu.VMEM((RING, PAD, 384), LOW),
        pltpu.VMEM((RING, PAD, 384), LOW),
        *reduce_scratch(),
        *plane_reduce_scratch(384),
        *plane_reduce_scratch(384),
    ]
    spaces = [pltpu.VMEM] * 4 + [pl.ANY] * 2 + [pltpu.VMEM] * 3
    return call(fourth_kernel, 3, 80, out, scratch, operands, spaces)


def adam_update(weight, gradient, first_moment, second_moment, learn_rate, decay_rate):
    first_moment = first_decay * first_moment + (1.0 - first_decay) * gradient
    second_moment = second_decay * second_moment + (1.0 - second_decay) * gradient * gradient
    corrected = (
        first_moment
        / (1.0 - first_decay**STEP)
        / (jnp.sqrt(second_moment / (1.0 - second_decay**STEP)) + adam_eps)
    )
    return (weight - learn_rate * (corrected + decay_rate * weight), first_moment, second_moment)


def out_fan_in(seq_length):
    return max(1, H * HD * 4 // min(WINDOW, seq_length))


def quarters(rows):
    return rows.reshape(OWN, RING, -1).transpose(1, 0, 2)


def head_quarters(rows):
    split = rows.reshape(rows.shape[0], 5, HD)
    last = split[:, 4].reshape(-1, RING, TAIL)
    return jnp.concatenate([split[:, :4], last], axis=2).transpose(1, 0, 2)


def whole_heads(slices):
    slices = slices.transpose(1, 0, 2)
    rows = slices.shape[0]
    return jnp.concatenate(
        [slices[..., :HD].reshape(rows, -1), slices[..., HD:].reshape(rows, -1)], axis=1
    )


def whole(slices):
    return slices.transpose(1, 0, 2).reshape(slices.shape[1], -1)


def pad_to(x, axis, size):
    widths = [(0, 0)] * x.ndim
    widths[axis] = (0, size - x.shape[axis])
    return jnp.pad(x, widths)


def per_device(
    tokens,
    cotangent,
    w_query,
    w_keyvalue,
    w_out,
    w_gateup,
    w_down,
    norm_scales,
    first_query,
    first_keyvalue,
    first_out,
    first_gateup,
    first_down,
    first_scales,
    second_query,
    second_keyvalue,
    second_out,
    second_gateup,
    second_down,
    second_scales,
):
    core = lax.axis_index("tensor")
    seq_index = lax.axis_index("x") * RING + lax.axis_index("z")
    positions = seq_index * BLOCK + jnp.arange(BLOCK, dtype=jnp.int32)
    seq_length = BLOCK * RING * RING

    keyvalue_part = lax.dynamic_index_in_dim(w_keyvalue, core, 1, keepdims=False)
    scale_columns = jnp.broadcast_to(norm_scales.T[None], (RING, OWN, 2))
    out_quarters = head_quarters(w_out.T)
    attn_rows = jnp.concatenate(
        [
            head_quarters(w_query),
            quarters(keyvalue_part),
            out_quarters[..., HD:],
            pad_to(scale_columns, 2, TAIL),
            out_quarters[..., :HD],
        ],
        axis=2,
    ).astype(LOW)
    attn_rows = pad_to(attn_rows, 1, PAD)
    gateup = w_gateup.astype(LOW)
    mains = RING * MAIN
    feed_rows = jnp.concatenate(
        [
            quarters(gateup[:, 0, :mains]),
            quarters(gateup[:, 1, :mains]),
            quarters(gateup[:, 0, mains:]),
            quarters(gateup[:, 1, mains:]),
            quarters(w_down.T[:, :mains].astype(LOW)),
            quarters(w_down.T[:, mains:].astype(LOW)),
        ],
        axis=2,
    )
    feed_rows = pad_to(pad_to(feed_rows, 2, 2944), 1, PAD)
    frequency = 10000.0 ** (-jnp.arange(TAIL, dtype=F32) / TAIL)
    angles = positions.astype(F32)[:, None] * frequency[None, :]
    cos_table = jnp.tile(jnp.cos(angles), (1, 2))
    sin_table = jnp.concatenate([-jnp.sin(angles), jnp.sin(angles)], axis=1)
    cos_kv = jnp.where(core == 0, cos_table, 1.0)
    sin_kv = jnp.where(core == 0, sin_table, 0.0)
    first = run_first(
        attn_rows, feed_rows, tokens, cotangent.astype(LOW), cos_table, sin_table, cos_kv, sin_kv
    )
    second = run_second(
        first["feed_full"],
        first["normed_two"],
        first["dy_all"],
        cotangent,
        first["residual"],
        first["gains"],
    )
    third = run_third(
        second["feed_part"],
        second["gateup_grads"],
        second["da_all"],
        first["residual"],
        first["attn_a"],
        first["attn_b"],
        first["att_slice"],
        first["query"],
        first["keyvalue"],
        first["log_total"],
        first["attended"],
        cos_table,
        sin_table,
        cos_kv,
        sin_kv,
    )
    fourth = run_fourth(
        third["grad_got"],
        third["gateup_rows"],
        second["down_rows"],
        third["grad_out"],
        first["attn_a"],
        first["normed_one"],
        second["grad_rows"],
        tokens,
        first["gains"],
    )
    output, grad_tokens = third["output"], fourth["grad_tokens"]

    gateup_shard = fourth["gateup_got"][:, :OWN].astype(F32)
    down_shard = fourth["down_got"][:, :OWN].astype(F32)

    def hidden_units(grads, main, tail):
        return jnp.concatenate(
            [whole(grads[..., main : main + MAIN]), whole(grads[..., tail : tail + TAIL])], axis=1
        )

    gateup_shard = jnp.stack(
        [
            hidden_units(gateup_shard, 0, 2 * MAIN),
            hidden_units(gateup_shard, MAIN, 2 * MAIN + TAIL),
        ],
        axis=1,
    )
    down_shard = hidden_units(down_shard, 0, MAIN).T
    out_got = fourth["out_got"][:, :OWN].astype(F32)
    out_shard = jnp.concatenate([whole(out_got[..., 128:]), whole(out_got[..., :TAIL])], axis=1).T
    qkv_shard = fourth["qkv_got"][:, :OWN].astype(F32)
    query_shard = whole_heads(qkv_shard[..., :320])
    kv_half = whole(qkv_shard[..., 320:])
    gain_rows = 1.0 + norm_scales.astype(LOW).astype(F32)

    def with_weight(weight, grads):
        return jnp.sum((weight.astype(LOW).astype(F32) * grads).reshape(OWN, -1), axis=1)

    scale_parts = jnp.stack(
        [
            with_weight(w_query, query_shard) + with_weight(keyvalue_part, kv_half),
            with_weight(w_gateup, gateup_shard),
        ],
        axis=1,
    )
    packed = pad_to(jnp.concatenate([kv_half, pad_to(scale_parts, 1, 128)], axis=1), 0, PAD)
    theirs = swap_cores(packed, 4)[:OWN]
    kv_other = theirs[:, :HD]
    scale_grads = (scale_parts + theirs[:, HD : HD + 2]).T / gain_rows
    keyvalue_shard = jnp.stack(
        [jnp.where(core == 0, kv_half, kv_other), jnp.where(core == 0, kv_other, kv_half)], axis=1
    )

    matrix_rate = 2.0 * D ** (-0.5)
    out_rate = 2.0 * out_fan_in(seq_length) ** (-0.5)
    down_rate = 2.0 * (FF // 2) ** (-0.5)
    triples = [
        adam_update(w_query, query_shard, first_query, second_query, matrix_rate, weight_decay),
        adam_update(
            w_keyvalue, keyvalue_shard, first_keyvalue, second_keyvalue, matrix_rate, weight_decay
        ),
        adam_update(w_out, out_shard, first_out, second_out, out_rate, weight_decay),
        adam_update(w_gateup, gateup_shard, first_gateup, second_gateup, matrix_rate, weight_decay),
        adam_update(w_down, down_shard, first_down, second_down, down_rate, weight_decay),
        adam_update(norm_scales, scale_grads, first_scales, second_scales, gain_rate, 0.0),
    ]
    return (output, grad_tokens, *(triple[i] for i in range(3) for triple in triples))


def solution(mesh):
    split = Mesh(
        mesh.devices.reshape(RING, RING, RING, 2), ("dp", "x", "z", "tensor")
    )
    rows = ("dp", "x", "z")
    matrices = (
        P(rows, "tensor"),
        P(rows, None, None),
        P("tensor", rows),
        P(rows, None, "tensor"),
        P("tensor", rows),
        P(None, rows),
    )
    in_specs = (P(rows, None), P(rows, None), *matrices, *matrices, *matrices)
    out_specs = in_specs
    return jax.shard_map(
        per_device, mesh=split, in_specs=in_specs, out_specs=out_specs, check_vma=False
    )
```

```python
import functools

import jax
import jax.numpy as jnp
from jax import lax
from jax.experimental import pallas as pl
from jax.experimental.pallas import tpu as pltpu
from jax.sharding import Mesh
from jax.sharding import PartitionSpec as P

D = 2560
H = 10
HD = 256
FF = 7680
WINDOW = 2048
STEP = 10

eps_norm = 1e-06
masked_fill = -1e30
first_decay = 0.9
second_decay = 0.95
adam_eps = 1e-08
weight_decay = 0.1
gain_rate = 0.2
GELU_SCALE = (2.0 / 3.141592653589793) ** 0.5
GELU_CUBE = 0.044715

MESH = pl.DeviceIdType.MESH
LOW = jnp.bfloat16
F32 = jnp.float32
RING = 4
BLOCK = 160
HALF = BLOCK // 2
PART = 48
OWN = 40
PAD = 48
SPANS = ((0, 48, 32), (48, 32, 16))
MAIN = 896
TAIL = 64


def step(axis, distance):
    return lax.rem(lax.axis_index(axis) + (RING + distance), RING)


def sibling():
    return {"tensor": 1 - lax.axis_index("tensor")}


def greet(peers):
    barrier = pltpu.get_barrier_semaphore()
    for peer in peers:
        pl.semaphore_signal(barrier, inc=1, device_id=peer, device_id_type=MESH)
    pl.semaphore_wait(barrier, len(peers))


def dot(left_side, right_side, contract):
    return lax.dot_general(
        left_side, right_side, ((contract[:1], contract[1:]), ((), ())), preferred_element_type=F32
    )


class Mover:
    def __init__(self, send_sem, recv_sem):
        self.send_sem, self.recv_sem, self.pending = send_sem, recv_sem, []

    def copy(self, src, dst, peer):
        index = len(self.pending)
        one = pltpu.make_async_remote_copy(
            src_ref=src,
            dst_ref=dst,
            send_sem=self.send_sem.at[index],
            recv_sem=self.recv_sem.at[index],
            device_id=peer,
            device_id_type=MESH,
        )
        one.start()
        self.pending.append(one)
        return one

    def finish(self):
        for one in self.pending:
            one.wait_send()


def advance(steps):
    next(steps, None)


def plane_peers(axes):
    return [{axis: step(axis, d)} for axis in axes for d in (-1, 1)]


def exchange_steps(mover, src, dst):
    me = lax.axis_index("z")
    copies = [
        mover.copy(src.at[step("z", d)], dst.at[me], {"z": step("z", d)}) for d in (2, 1, 3)
    ]
    yield
    for copy in copies:
        copy.wait_recv()


def core_rows(lo=0, n=HALF, part=PART):
    base = lax.axis_index("tensor") * HALF

    def rows(start, size):
        return pl.ds(pl.multiple_of(start, 16), size)

    return (
        rows(base + lo, n),
        rows(base + lo, part),
        rows(base + (lo + part), n - part),
        rows(HALF - base + lo, n),
    )


def gather_steps(mover, x, out, span=(0, HALF, PART)):
    me, left, right, far = (step("z", d) for d in (0, -1, 1, 2))
    half, first, last, _ = core_rows(*span)
    to_right = mover.copy(x.at[half], out.at[me, half], {"z": right})
    to_left = mover.copy(x.at[half], out.at[me, half], {"z": left})
    yield
    to_right.wait_recv()
    on_right = mover.copy(out.at[left, first], out.at[left, first], {"z": right})
    shares = [mover.copy(out.at[left, half], out.at[left, half], sibling())]
    to_left.wait_recv()
    on_left = mover.copy(out.at[right, last], out.at[right, last], {"z": left})
    shares.append(mover.copy(out.at[right, half], out.at[right, half], sibling()))
    yield
    on_right.wait_recv()
    on_left.wait_recv()
    shares.append(mover.copy(out.at[far, half], out.at[far, half], sibling()))
    yield
    for copy in shares:
        copy.wait_recv()


def cut_rows(which, cut):
    base, size = (0, cut) if which == 0 else (cut, BLOCK - cut)
    part = -(-size // 32) * 16
    return pl.ds(base, size), pl.ds(base, part), pl.ds(base + part, size - part)


def plane_gather_steps(mover, axes, x, out, cut=HALF, order=(0, 1), share=False):
    a, b = (lax.axis_index(axis) for axis in axes)
    state = {}
    for which, axis in enumerate(axes):
        rows = cut_rows(which, cut)[0]
        place = (lambda i, r: out.at[i, b, r]) if which == 0 else (lambda i, r: out.at[a, i, r])
        me = (a, b)[which]
        to_right = mover.copy(x.at[rows], place(me, rows), {axis: step(axis, 1)})
        to_left = mover.copy(x.at[rows], place(me, rows), {axis: step(axis, -1)})
        state[which] = (axis, place, to_right, to_left)
    yield
    passed = {}
    for which in order:
        axis, place, to_right, to_left = state[which]
        _, first, last = cut_rows(which, cut)
        left, right = step(axis, -1), step(axis, 1)
        to_right.wait_recv()
        on_right = mover.copy(place(left, first), place(left, first), {axis: right})
        to_left.wait_recv()
        on_left = mover.copy(place(right, last), place(right, last), {axis: left})
        passed[which] = (on_right, on_left)
    yield
    state = {}
    shares = []

    def give(piece):
        if share:
            shares.append(mover.copy(piece, piece, sibling()))

    for which in order:
        axis, other = axes[which], axes[1 - which]
        rows = cut_rows(which, cut)[0]
        if which == 0:
            place = lambda i, lo, n, rows=rows: out.at[pl.ds(lo, n), i, rows]
        else:
            place = lambda i, lo, n, rows=rows: out.at[i, pl.ds(lo, n), rows]
        me = (b, a)[which]
        for copy in passed[which]:
            copy.wait_recv()
        to_right = mover.copy(place(me, 0, 4), place(me, 0, 4), {other: step(other, 1)})
        to_left = mover.copy(place(me, 0, 4), place(me, 0, 4), {other: step(other, -1)})
        give(place(me, 0, 4))
        state[which] = (other, place, to_right, to_left)
        yield
    ends = []
    for which in order:
        other, place, to_right, to_left = state[which]
        left, right = step(other, -1), step(other, 1)
        to_right.wait_recv()
        ends.append(mover.copy(place(left, 0, 2), place(left, 0, 2), {other: right}))
        give(place(left, 0, 4))
        to_left.wait_recv()
        ends.append(mover.copy(place(right, 2, 2), place(right, 2, 2), {other: left}))
        give(place(right, 0, 4))
        yield
    for copy in ends:
        copy.wait_recv()
    for which in order:
        other, place, _, _ = state[which]
        give(place(step(other, 2), 0, 4))
    for copy in shares:
        copy.wait_recv()


def lanes(shape):
    return lax.broadcasted_iota(jnp.int32, shape, len(shape) - 1)


def turn(values, cos, sin):
    return values * cos + pltpu.roll(values, 64, 1) * sin


def whole_rows(blocks, stage, dst):
    for i in range(RING):
        stage[i * OWN : (i + 1) * OWN] = blocks[i].astype(F32)[:OWN]
    dst[...] = stage[...].astype(LOW)


def first_kernel(
    attn_rows,
    feed_rows,
    tokens,
    dy,
    cos_ref,
    sin_ref,
    cos_kv,
    sin_kv,
    feed_full,
    attn_a,
    attn_b,
    normed_one,
    dy_all,
    query,
    kv_out,
    log_total,
    att_slice,
    residual,
    normed_two,
    attended,
    gain_ref,
    send_sem,
    recv_sem,
    local_sem,
    attn_got,
    mine_a,
    mine_b,
    weight_a,
    weight_b,
    attn_stage,
    feed_got,
    feed_mine,
    feed_stage,
    unit_low,
    unit_all,
    normed,
    qkv_send,
    qkv_got,
    kv_own,
    keyvalue,
    scores,
    att_send,
    part,
    sum_half,
    normed_low,
    *bufs,
):
    z, x, y, core = (lax.axis_index(axis) for axis in ("z", "x", "dp", "tensor"))
    plane = ("dp", "x")
    saves = []

    def save(src, dst):
        saves.append(pltpu.make_async_copy(src, dst, local_sem.at[len(saves)]))
        saves[-1].start()
        return saves[-1]

    greet([{"z": step("z", d)} for d in (1, 2, 3)] + plane_peers(plane) + [sibling()])
    mover = Mover(send_sem, recv_sem)

    attn_swap = exchange_steps(mover, attn_rows, attn_got)
    advance(attn_swap)
    feed_swap = exchange_steps(mover, feed_rows, feed_got)
    advance(feed_swap)
    values = tokens[...]
    unit = values * lax.rsqrt(jnp.mean(values * values, axis=-1, keepdims=True) + eps_norm)
    unit_low[...] = unit.astype(LOW)
    unit_gather = gather_steps(mover, unit_low, unit_all)
    advance(unit_gather)
    attn_got[z] = attn_rows[z]
    advance(attn_swap)
    for i in range(RING):
        attn_stage[i * OWN : (i + 1) * OWN] = attn_got[i].astype(F32)[:OWN]
    mine_a[...] = attn_stage[:, :512].astype(LOW)
    mine_b[...] = attn_stage[:, 512:].astype(LOW)
    a_gather = plane_gather_steps(mover, plane, mine_a, weight_a)
    advance(a_gather)
    weight_a[y, x] = mine_a[...]
    unit_all[z] = unit_low[...]
    advance(a_gather)
    feed_got[z] = feed_rows[z]
    advance(a_gather)
    advance(a_gather)
    advance(feed_swap)
    whole_rows(feed_got, feed_stage, feed_mine)
    feed_own = save(feed_mine, feed_full.at[y, x])
    advance(unit_gather)
    advance(a_gather)
    advance(a_gather)
    feed_gather = plane_gather_steps(mover, plane, feed_mine, feed_full)
    advance(feed_gather)
    advance(unit_gather)
    advance(unit_gather)
    advance(a_gather)
    save(weight_a, attn_a)

    scale_cols = weight_a[:, :, :, 384:].reshape(D, 128)
    pick = (lanes((8, 128)) == TAIL + lax.broadcasted_iota(jnp.int32, (8, 128), 0)).astype(LOW)
    gain_ref[...] = 1.0 + dot(pick, scale_cols, (1, 1))
    qkv_weight = weight_a[:, :, :, :384].reshape(D, 384)
    copies = []
    for d in (2, 1, 3, 0):
        block = step("z", d)
        rows = (unit_all[block].astype(F32) * gain_ref[0:1, :]).astype(LOW)
        normed[block] = rows
        qkv_send[block] = dot(rows, qkv_weight, (1, 0)).astype(LOW)
        if d:
            copies.append(mover.copy(qkv_send.at[block], qkv_got.at[z], {"z": block}))
    save(normed, normed_one)
    qkv_got[z] = qkv_send[z]
    feed_own.wait()
    advance(feed_gather)
    for copy in copies:
        copy.wait_recv()
    low_lanes = lanes((BLOCK, 128)) < TAIL
    cos, sin = cos_ref[...], sin_ref[...]

    def joined(i, offset):
        one, two = (qkv_got[i + k, :, 256:384].astype(F32) for k in (0, 1))
        if offset == 0:
            return jnp.where(low_lanes, one, pltpu.roll(two, TAIL, 1))
        return jnp.where(low_lanes, pltpu.roll(one, TAIL, 1), two)

    kv_own[:, :128] = turn(joined(0, 1), cos_kv[...], sin_kv[...]).astype(LOW)
    kv_own[:, 128:] = joined(2, 1).astype(LOW)
    kv_mine = keyvalue.at[core]
    kv_gather = plane_gather_steps(mover, ("x", "z"), kv_own, kv_mine, share=True)
    advance(kv_gather)
    keyvalue[core, x, z] = kv_own[...]
    scale = HD ** (-0.5)
    for h in range(4):
        first = qkv_got[h, :, :128].astype(F32)
        query[h, :, :128] = (turn(first, cos, sin) * scale).astype(LOW)
        query[h, :, 128:] = (qkv_got[h, :, 128:256].astype(F32) * scale).astype(LOW)
    query[4, :, :128] = (turn(joined(0, 0), cos, sin) * scale).astype(LOW)
    query[4, :, 128:] = (joined(2, 0) * scale).astype(LOW)
    b_gather = plane_gather_steps(mover, plane, mine_b, weight_b)
    advance(b_gather)
    weight_b[y, x] = mine_b[...]
    advance(kv_gather)
    advance(b_gather)
    for _ in range(2):
        advance(kv_gather)
        advance(b_gather)
    for _ in range(2):
        advance(kv_gather)
        advance(b_gather)
    for _ in range(2):
        advance(feed_gather)
    dy_gather = gather_steps(mover, dy, dy_all)
    advance(dy_gather)
    save(dy, dy_all.at[z])
    advance(kv_gather)
    save(keyvalue, kv_out)

    start = (x * RING + z) * BLOCK
    chunk = RING * BLOCK

    def one_head(h, carry):
        queries = query[h]
        top = jnp.full((BLOCK, 1), masked_fill, F32)
        for k in range(RING):
            rows = keyvalue[0, k].reshape(chunk, HD)
            tile = dot(queries, rows, (1, 1))
            gap = (start - k * chunk) + (
                lax.broadcasted_iota(jnp.int32, tile.shape, 0) - lanes(tile.shape)
            )
            tile = jnp.where((gap >= 0) & (gap < WINDOW), tile, masked_fill)
            scores[:, k * chunk : (k + 1) * chunk] = tile
            top = jnp.maximum(top, jnp.max(tile, axis=-1, keepdims=True))
        sums = jnp.zeros((BLOCK, 1), F32)
        for k in range(RING):
            tile = jnp.exp(scores[:, k * chunk : (k + 1) * chunk] - top)
            scores[:, k * chunk : (k + 1) * chunk] = tile
            sums = sums + jnp.sum(tile, axis=-1, keepdims=True)
        inverse = 1.0 / sums
        result = jnp.zeros((BLOCK, HD), F32)
        for k in range(RING):
            low = (scores[:, k * chunk : (k + 1) * chunk] * inverse).astype(LOW)
            result = result + dot(low, keyvalue[1, k].reshape(chunk, HD), (1, 0))
        attended[h] = result
        log_total[h] = jnp.broadcast_to(top + jnp.log(sums), (BLOCK, 128))
        return carry

    lax.fori_loop(0, 5, one_head, 0)
    for j in range(RING):
        att_send[j, :, 128:] = attended[j].astype(LOW)
        tile = attended[4, :, (j // 2) * 128 : (j // 2 + 1) * 128]
        tile = pltpu.roll(tile, TAIL, 1) if j % 2 else tile
        att_send[j, :, :128] = jnp.where(low_lanes, tile, 0.0).astype(LOW)
    att_swap = exchange_steps(mover, att_send, att_slice)
    advance(att_swap)
    att_slice[z] = att_send[z]
    advance(att_swap)

    advance(b_gather)
    save(weight_b, attn_b)

    last_weight = weight_a[:, :, :, 384:].reshape(D, 128)
    main_weight = weight_b[...].reshape(D, HD)

    def make(block):
        rows = dot(att_slice[block, :, :128], last_weight, (1, 1))
        part[block] = (rows + dot(att_slice[block, :, 128:], main_weight, (1, 1))).astype(LOW)

    shares = []
    sharing = share_steps(mover, part, bufs[0], shares, make)
    advance(sharing)
    advance(sharing)
    sums = [
        reduce_steps(mover, own_rows(part), shares[i], bufs, sum_half, span)
        for i, span in enumerate(SPANS)
    ]
    for one in sums:
        advance(one)
    advance(sharing)
    advance(sharing)
    for one in sums:
        advance(one)

    def normed_rows(rows):
        unit = rows * lax.rsqrt(jnp.mean(rows * rows, axis=-1, keepdims=True) + eps_norm)
        return (unit * gain_ref[1:2, :]).astype(LOW)

    gathers, res_shares = [], []
    for one, span in zip(sums, SPANS, strict=True):
        advance(one)
        place = core_rows(*span)[0]
        rows = tokens[place, :] + sum_half[span[0] : span[0] + span[1]]
        residual[place, :] = rows
        normed_low[place, :] = normed_rows(rows)
        gathers.append(gather_steps(mover, normed_low, normed_two, span))
        advance(gathers[-1])
        res_shares.append(mover.copy(residual.at[place], residual.at[place], sibling()))
    advance(dy_gather)
    for copy in res_shares:
        copy.wait_recv()
    theirs = core_rows()[3]
    normed_low[theirs, :] = normed_rows(residual[theirs, :])
    save(normed_low, normed_two.at[z])
    for one in gathers:
        advance(one)
    advance(feed_gather)
    advance(feed_gather)
    for one in gathers:
        advance(one)
    advance(dy_gather)
    for one in gathers:
        advance(one)
    advance(dy_gather)
    advance(feed_gather)
    for one in saves:
        if one is not feed_own:
            one.wait()
    mover.finish()


def run_first(*operands):
    out = {
        "feed_full": ((RING, RING, BLOCK, 2944), LOW),
        "attn_a": ((RING, RING, BLOCK, 512), LOW),
        "attn_b": ((RING, RING, BLOCK, HD), LOW),
        "normed_one": ((RING, BLOCK, D), LOW),
        "dy_all": ((RING, BLOCK, D), LOW),
        "query": ((5, BLOCK, HD), LOW),
        "keyvalue": ((2, RING, RING, BLOCK, HD), LOW),
        "log_total": ((5, BLOCK, 128), F32),
        "att_slice": ((RING, BLOCK, 384), LOW),
        "residual": ((BLOCK, D), F32),
        "normed_two": ((RING, BLOCK, D), LOW),
        "attended": ((5, BLOCK, HD), F32),
        "gains": ((8, D), F32),
    }
    remote = ("feed_full", "attn_a", "attn_b", "normed_one", "dy_all", "keyvalue", "normed_two")
    spaces = [pltpu.VMEM, pltpu.VMEM, pltpu.VMEM, pl.ANY] + [pltpu.VMEM] * 4
    scratch = [
        pltpu.VMEM((RING, PAD, 768), LOW),
        pltpu.VMEM((BLOCK, 512), LOW),
        pltpu.VMEM((BLOCK, HD), LOW),
        pltpu.VMEM((RING, RING, BLOCK, 512), LOW),
        pltpu.VMEM((RING, RING, BLOCK, HD), LOW),
        pltpu.VMEM((BLOCK, 768), F32),
        pltpu.VMEM((RING, PAD, 2944), LOW),
        pltpu.VMEM((BLOCK, 2944), LOW),
        pltpu.VMEM((BLOCK, 2944), F32),
        pltpu.VMEM((BLOCK, D), LOW),
        pltpu.VMEM((RING, BLOCK, D), LOW),
        pltpu.VMEM((RING, BLOCK, D), LOW),
        pltpu.VMEM((RING, BLOCK, 384), LOW),
        pltpu.VMEM((RING, BLOCK, 384), LOW),
        pltpu.VMEM((BLOCK, HD), LOW),
        pltpu.VMEM((2, RING, RING, BLOCK, HD), LOW),
        pltpu.VMEM((BLOCK, RING * RING * BLOCK), F32),
        pltpu.VMEM((RING, BLOCK, 384), LOW),
        pltpu.VMEM((RING, BLOCK, D), LOW),
        pltpu.VMEM((HALF, D), F32),
        pltpu.VMEM((BLOCK, D), LOW),
        *reduce_scratch(),
    ]
    return call(
        first_kernel, 1, 150, out, scratch, operands, spaces, {name: pl.ANY for name in remote}
    )


def plane_reduce_steps(mover, axes, g, bufs, res, loads=None):
    far, side, near, far_two, side_two = bufs
    places = [lax.axis_index(axis) for axis in axes]

    def block(which, i, lo, n):
        rows = pl.ds(which * HALF, HALF)
        return g.at[i, pl.ds(lo, n), rows] if which == 0 else g.at[pl.ds(lo, n), i, rows]

    locals_ = []

    def load(src, dst):
        locals_.append(pltpu.make_async_copy(src, dst, loads.at[len(locals_)]))
        locals_[-1].start()
        return locals_[-1]

    first, sides, wanted = [], [], []
    for which, axis in enumerate(axes):
        right, left = step(axis, 1), step(axis, -1)
        far_place = step(axis, 2)
        first.append(
            (
                mover.copy(block(which, far_place, 0, 2), far.at[which, pl.ds(0, 2)], {axis: right}),
                mover.copy(block(which, far_place, 2, 2), far.at[which, pl.ds(2, 2)], {axis: left}),
            )
        )
        if loads is not None:
            wanted.append(
                (
                    load(block(which, right, 0, 2), near.at[which, 0]),
                    load(block(which, left, 2, 2), near.at[which, 1]),
                )
            )
    for which, axis in enumerate(axes):
        right, left = step(axis, 1), step(axis, -1)
        sides.append(
            [
                mover.copy(block(which, right, 2, 2), side.at[which, 0, pl.ds(2, 2)], {axis: right}),
                mover.copy(block(which, left, 0, 2), side.at[which, 1, pl.ds(0, 2)], {axis: left}),
            ]
        )
    yield
    owned = []
    for which, axis in enumerate(axes):
        for k, (d, lo) in enumerate(((1, 0), (-1, 2))):
            first[which][k].wait_recv()
            if loads is not None:
                wanted[which][k].wait()
                term = near[which, k]
            else:
                term = block(which, step(axis, d), lo, 2)[...]
            near[which, k] = (term.astype(F32) + far[which, lo : lo + 2].astype(F32)).astype(LOW)
            sides[which].append(
                mover.copy(near.at[which, k], side.at[which, k, pl.ds(lo, 2)], {axis: step(axis, d)})
            )
        if loads is not None:
            owned.append(load(block(which, places[which], 0, 4), far.at[which]))
    yield

    def summed(which, i):
        if loads is not None:
            term = far[which, i]
        else:
            rows = pl.ds(which * HALF, HALF)
            me = places[which]
            term = (g[me, i, rows] if which == 0 else g[i, me, rows])
        return (
            term.astype(F32) + side[which, 0, i].astype(F32) + side[which, 1, i].astype(F32)
        )

    second = []
    for which, axis in enumerate(axes):
        other = axes[1 - which]
        right, left = {other: step(other, 1)}, {other: step(other, -1)}
        for copy in sides[which]:
            copy.wait_recv()
        if loads is not None:
            owned[which].wait()
        far_two[which, 0] = summed(which, step(other, 2)).astype(LOW)
        upper, lower = pl.ds(0, PART), pl.ds(PART, HALF - PART)
        second.append(
            (
                mover.copy(far_two.at[which, 0, upper], far_two.at[which, 1, upper], right),
                mover.copy(far_two.at[which, 0, lower], far_two.at[which, 1, lower], left),
            )
        )
    yield
    last = []
    for which, axis in enumerate(axes):
        other = axes[1 - which]
        right, left = step(other, 1), step(other, -1)
        total = summed(which, right)
        second[which][0].wait_recv()
        side_two[which, 0, :PART] = (
            total[:PART] + far_two[which, 1, :PART].astype(F32)
        ).astype(LOW)
        side_two[which, 0, PART:] = total[PART:].astype(LOW)
        last.append(mover.copy(side_two.at[which, 0], side_two.at[which, 2], {other: right}))
        total = summed(which, left)
        second[which][1].wait_recv()
        side_two[which, 1, :PART] = total[:PART].astype(LOW)
        side_two[which, 1, PART:] = (
            total[PART:] + far_two[which, 1, PART:].astype(F32)
        ).astype(LOW)
        last.append(mover.copy(side_two.at[which, 1], side_two.at[which, 3], {other: left}))
    yield
    for which, axis in enumerate(axes):
        other = axes[1 - which]
        last[2 * which].wait_recv()
        last[2 * which + 1].wait_recv()
        res[which * HALF : (which + 1) * HALF] = (
            summed(which, lax.axis_index(other))
            + side_two[which, 2].astype(F32)
            + side_two[which, 3].astype(F32)
        )


def plane_reduce_scratch(columns):
    return [
        pltpu.VMEM((2, 4, HALF, columns), LOW),
        pltpu.VMEM((2, 2, 4, HALF, columns), LOW),
        pltpu.VMEM((2, 2, 2, HALF, columns), LOW),
        pltpu.VMEM((2, 2, HALF, columns), LOW),
        pltpu.VMEM((2, 4, HALF, columns), LOW),
        pltpu.VMEM((BLOCK, columns), F32),
    ]


def share_steps(mover, part, other, shares, make=None, spans=SPANS):
    me, left, right, far = (step("z", d) for d in (0, -1, 1, 2))
    shares.extend([] for _ in spans)
    for slot, block in enumerate((far, right, left, me)):
        if make is not None:
            make(block)
        for copies, (lo, n, first) in zip(shares, spans, strict=True):
            theirs = core_rows(lo, n, first)[3]
            copies.append(
                mover.copy(part.at[block, theirs], other.at[slot, pl.ds(lo, n)], sibling())
            )
        yield


def reduce_steps(mover, mine, shares, bufs, out, span):
    other, total, far_in, from_left, from_right = bufs
    lo, n, part = span
    me, left, right, far = (step("z", d) for d in (0, -1, 1, 2))
    blocks = (far, right, left, me)
    rows, first, last = pl.ds(lo, n), pl.ds(lo, part), pl.ds(lo + part, n - part)

    def both(slot):
        return mine(blocks[slot], span).astype(F32) + other[slot, rows].astype(F32)

    shares[0].wait_recv()
    total[0, rows] = both(0).astype(LOW)
    far_right = mover.copy(total.at[0, first], far_in.at[first], {"z": right})
    far_left = mover.copy(total.at[0, last], far_in.at[last], {"z": left})
    yield
    shares[1].wait_recv()
    summed = both(1)
    far_right.wait_recv()
    total[1, first] = (summed[:part] + far_in[first].astype(F32)).astype(LOW)
    total[1, last] = summed[part:].astype(LOW)
    to_right = mover.copy(total.at[1, rows], from_left.at[rows], {"z": right})
    shares[2].wait_recv()
    summed = both(2)
    far_left.wait_recv()
    total[2, first] = summed[:part].astype(LOW)
    total[2, last] = (summed[part:] + far_in[last].astype(F32)).astype(LOW)
    to_left = mover.copy(total.at[2, rows], from_right.at[rows], {"z": left})
    yield
    shares[3].wait_recv()
    summed = both(3)
    to_right.wait_recv()
    to_left.wait_recv()
    out[rows] = summed + from_left[rows].astype(F32) + from_right[rows].astype(F32)


def own_rows(ref):
    return lambda block, span: ref[block, core_rows(*span)[0]]


def half_rows(ref):
    return lambda block, span: ref[block, pl.ds(span[0], span[1])]


def reduce_scratch():
    return [
        pltpu.VMEM((4, HALF, D), LOW),
        pltpu.VMEM((3, HALF, D), LOW),
        pltpu.VMEM((HALF, D), LOW),
        pltpu.VMEM((HALF, D), LOW),
        pltpu.VMEM((HALF, D), LOW),
    ]


def spread_rows(res, dst):
    for i in range(RING):
        rows = res[i * OWN : (i + 1) * OWN]
        dst[i] = jnp.concatenate([rows, jnp.zeros((PAD - OWN, rows.shape[1]), F32)]).astype(LOW)


def activation(gate, upper, grad):
    square = gate * gate
    tanh = jnp.tanh(GELU_SCALE * gate * (1.0 + GELU_CUBE * square))
    half = 0.5 * (1.0 + tanh)
    gelu = gate * half
    slope = half + 0.5 * gate * (1.0 - tanh * tanh) * GELU_SCALE * (1.0 + 3.0 * GELU_CUBE * square)
    return gelu * upper, grad * upper * slope, grad * gelu


def second_kernel(
    feed_full,
    normed_two,
    dy_all,
    cotangent,
    residual,
    gain_ref,
    grad_rows,
    da_all,
    feed_part,
    gateup_grads,
    down_rows,
    send_sem,
    recv_sem,
    local_sem,
    normed_in,
    dy_in,
    gateup_weight,
    down_weight,
    hidden,
    dgu,
    norm_part,
    stage,
    grad_half,
    cot_half,
    res_half,
    da_low,
    *bufs,
):
    z = lax.axis_index("z")
    half, _, _, _ = core_rows()
    plane = ("dp", "x")
    gu_width = 2 * (MAIN + TAIL)
    wide = RING * BLOCK
    loads = [
        pltpu.make_async_copy(src, dst, local_sem.at[i])
        for i, (src, dst) in enumerate(
            (
                (normed_two, normed_in),
                (feed_full.at[:, :, :, pl.ds(0, gu_width)], gateup_weight),
                (dy_all, dy_in),
                (feed_full.at[:, :, :, pl.ds(gu_width, 1024)], down_weight),
                (cotangent.at[half], cot_half),
                (residual.at[half], res_half),
            )
        )
    ]
    for load in loads:
        load.start()
    greet(plane_peers(("z",)) + plane_peers(plane) + [sibling()])
    mover = Mover(send_sem, recv_sem)
    for load in loads:
        load.wait()

    def product(rows, weight, lo, n):
        left_side = rows[...].reshape(wide, D)
        return dot(left_side, weight[:, :, :, lo : lo + n].reshape(D, n), (1, 0))

    for lo, n in ((0, 256), (256, 256), (512, 256), (768, 128)):
        value, grad_gate, grad_upper = activation(
            product(normed_in, gateup_weight, lo, n),
            product(normed_in, gateup_weight, MAIN + lo, n),
            product(dy_in, down_weight, lo, n),
        )
        hidden[:, lo : lo + n] = value.astype(LOW)
        dgu[:, lo : lo + n] = grad_gate.astype(LOW)
        dgu[:, MAIN + lo : MAIN + lo + n] = grad_upper.astype(LOW)
    both = product(normed_in, gateup_weight, 2 * MAIN, 2 * TAIL)
    value, grad_gate, grad_upper = activation(
        both, pltpu.roll(both, TAIL, 1), product(dy_in, down_weight, MAIN, 2 * TAIL)
    )
    low_lanes = lanes(both.shape) < TAIL
    hidden[:, MAIN:] = jnp.where(low_lanes, value, 0.0).astype(LOW)
    dgu[:, 2 * MAIN :] = jnp.where(low_lanes, grad_gate, pltpu.roll(grad_upper, TAIL, 1)).astype(LOW)

    for i in range(RING):
        part = dot(dgu[...], gateup_weight[i].reshape(wide, gu_width), (1, 1))
        norm_part[:, :, i * wide : (i + 1) * wide] = part.astype(LOW).reshape(RING, BLOCK, wide)
    shares = []
    sharing = share_steps(mover, norm_part, bufs[0], shares)
    for _ in range(RING):
        advance(sharing)
    sums = [
        reduce_steps(mover, own_rows(norm_part), shares[i], bufs[:5], grad_half, span)
        for i, span in enumerate(SPANS)
    ]

    for i in range(RING):
        terms = dot(hidden[...], down_weight[i].reshape(wide, 1024), (1, 1))
        feed_part[:, :, i * wide : (i + 1) * wide] = terms.astype(LOW).reshape(RING, BLOCK, wide)
        if i < 2:
            advance(sums[i])

    def columns(rows, i):
        return rows[:, :, i * wide : (i + 1) * wide].reshape(wide, wide)

    for i in range(RING):
        grads = dot(columns(dy_in, i), hidden[...], (0, 0))
        down_weight[i] = grads.astype(LOW).reshape(RING, BLOCK, 1024)
        if i < 2:
            advance(sums[i])
    down_sum = plane_reduce_steps(mover, plane, down_weight, bufs[5:10], bufs[10])
    advance(down_sum)
    saved = []

    def gateup_block(i):
        if saved:
            saved[-1].wait()
        grads = dot(columns(normed_in, i), dgu[...], (0, 0))
        stage[...] = grads.astype(LOW).reshape(RING, BLOCK, gu_width)
        saved.append(pltpu.make_async_copy(stage, gateup_grads.at[i], local_sem.at[10 + i]))
        saved[-1].start()

    gateup_block(0)
    gathers, da_shares = [], []
    for one, span in zip(sums, SPANS, strict=True):
        advance(one)
        piece = pl.ds(span[0], span[1])
        place = core_rows(*span)[0]
        rows = res_half[piece, :]
        inverse = lax.rsqrt(jnp.mean(rows * rows, axis=-1, keepdims=True) + eps_norm)
        unit = rows * inverse
        scaled = grad_half[piece, :] * gain_ref[1:2, :]
        grad = cot_half[piece, :] + inverse * (
            scaled - unit * jnp.mean(scaled * unit, axis=-1, keepdims=True)
        )
        grad_rows[piece, :] = grad
        da_low[place, :] = grad.astype(LOW)
        gathers.append(gather_steps(mover, da_low, da_all, span))
        advance(gathers[-1])
        da_shares.append(mover.copy(da_low.at[place], da_low.at[place], sibling()))
    advance(down_sum)
    gateup_block(1)
    for copy in da_shares:
        copy.wait_recv()
    da_own = pltpu.make_async_copy(da_low, da_all.at[z], local_sem.at[9])
    da_own.start()
    for one in gathers:
        advance(one)
    gateup_block(2)
    advance(down_sum)
    for one in gathers:
        advance(one)
    gateup_block(3)
    advance(down_sum)
    for one in gathers:
        advance(one)
    advance(down_sum)
    spread_rows(bufs[10], down_rows)
    saved[-1].wait()
    da_own.wait()
    mover.finish()


def third_kernel(
    feed_part,
    gateup_grads,
    da_all,
    residual,
    attn_a,
    attn_b,
    att_slice,
    query,
    kv_hbm,
    log_total,
    attended,
    cos_ref,
    sin_ref,
    cos_kv,
    sin_kv,
    grad_out,
    grad_got,
    gateup_rows,
    output,
    send_sem,
    recv_sem,
    local_sem,
    da_in,
    last_weight,
    main_weight,
    keyvalue,
    feed_mine,
    out_half,
    datt_send,
    datt_got,
    datt,
    delta,
    ds_all,
    p_all,
    dq,
    kv_pair,
    kv_in,
    grad_kv,
    grad_query,
    grad_send,
    kv_low,
    *bufs,
):
    z, core = lax.axis_index("z"), lax.axis_index("tensor")
    x = lax.axis_index("x")
    half = core_rows()[0]
    whole_span = ((0, HALF, PART),)
    out_bufs, rows_bufs, rows_res = bufs[:5], bufs[5:10], bufs[10]
    kv_bufs, kv_rows = bufs[11:16], bufs[16]
    loads = [
        pltpu.make_async_copy(src, dst, local_sem.at[8 + i])
        for i, (src, dst) in enumerate(
            (
                (da_all, da_in),
                (attn_a.at[:, :, :, pl.ds(384, 128)], last_weight),
                (attn_b, main_weight),
                (kv_hbm, keyvalue),
                (feed_part.at[:, half], feed_mine),
            )
        )
    ]
    for load in loads:
        load.start()
    greet([{"z": step("z", d)} for d in (1, 2, 3)] + plane_peers(("dp", "x")) + [sibling()])
    mover = Mover(send_sem, recv_sem)
    rows_sum = plane_reduce_steps(
        mover, ("dp", "x"), gateup_grads, rows_bufs, rows_res, loads=local_sem
    )
    advance(rows_sum)
    for load in loads[:3]:
        load.wait()
    last = last_weight[...].reshape(D, 128)
    main = main_weight[...].reshape(D, HD)
    copies = []
    for d in (2, 1, 3, 0):
        block = step("z", d)
        datt_send[block, :, :128] = dot(da_in[block], last, (1, 0)).astype(LOW)
        datt_send[block, :, 128:] = dot(da_in[block], main, (1, 0)).astype(LOW)
        if d:
            copies.append(mover.copy(datt_send.at[block], datt_got.at[z], {"z": block}))
    datt_got[z] = datt_send[z]
    shares = []
    sharing = share_steps(mover, feed_part, out_bufs[0], shares, spans=whole_span)
    for _ in range(RING):
        advance(sharing)
    feed_sum = reduce_steps(
        mover, half_rows(feed_mine), shares[0], out_bufs, out_half, whole_span[0]
    )
    slices = att_slice[...].reshape(RING * BLOCK, 384)
    wide = RING * BLOCK
    for i in range(RING):
        left_side = da_in[:, :, i * wide : (i + 1) * wide].reshape(wide, wide)
        grad_out[i] = dot(left_side, slices, (0, 0)).astype(LOW).reshape(RING, BLOCK, 384)
    for copy in copies:
        copy.wait_recv()
    for load in loads[3:]:
        load.wait()
    advance(feed_sum)
    advance(rows_sum)

    low_lanes = lanes((BLOCK, 128)) < TAIL
    for h in range(4):
        datt[h] = datt_got[h, :, 128:]
    for k in range(2):
        one, two = (datt_got[2 * k + i, :, :128].astype(F32) for i in range(2))
        datt[4, :, k * 128 : (k + 1) * 128] = jnp.where(
            low_lanes, one, pltpu.roll(two, TAIL, 1)
        ).astype(LOW)
    for h in range(5):
        delta[h] = jnp.broadcast_to(
            jnp.sum(datt[h].astype(F32) * attended[h], axis=-1, keepdims=True), (BLOCK, 128)
        )
        dq[h] = jnp.zeros((BLOCK, HD), F32)
    start = (x * RING + z) * BLOCK
    chunk = RING * BLOCK

    def one_chunk(k, carry):
        keys = keyvalue[0, k].reshape(chunk, HD)
        values = keyvalue[1, k].reshape(chunk, HD)
        shape = (BLOCK, chunk)
        gap = (start - k * chunk) + (lax.broadcasted_iota(jnp.int32, shape, 0) - lanes(shape))
        visible = (gap >= 0) & (gap < WINDOW)

        def one_head(h, carry):
            scores = dot(query[h], keys, (1, 1))
            probs = jnp.where(visible, jnp.exp(scores - log_total[h, :, :1]), 0.0)
            grads = dot(datt[h], values, (1, 1))
            low = (probs * (grads - delta[h, :, :1])).astype(LOW)
            ds_all[h] = low
            p_all[h] = probs.astype(LOW)
            dq[h] = dq[h] + dot(low, keys, (1, 0))
            return carry

        lax.fori_loop(0, 5, one_head, 0)
        queries = query[...].reshape(5 * BLOCK, HD)
        outer = datt[...].reshape(5 * BLOCK, HD)
        kv_pair[0, k] = dot(ds_all[...].reshape(5 * BLOCK, chunk), queries, (0, 0)).astype(LOW).reshape(RING, BLOCK, HD)
        kv_pair[1, k] = dot(p_all[...].reshape(5 * BLOCK, chunk), outer, (0, 0)).astype(LOW).reshape(RING, BLOCK, HD)
        return carry

    lax.fori_loop(0, RING, one_chunk, 0)
    kv_swap = mover.copy(kv_pair.at[1 - core], kv_in, sibling())
    advance(feed_sum)
    cos, sin = cos_ref[...], sin_ref[...]
    scale = HD ** (-0.5)
    for h in range(5):
        grad_query[h, :, :128] = turn(dq[h, :, :128] * scale, cos, -sin)
        grad_query[h, :, 128:] = dq[h, :, 128:] * scale
    kv_swap.wait_recv()
    grad_kv[...] = (kv_pair[core].astype(F32) + kv_in[...].astype(F32)).astype(LOW)
    kv_sum = plane_reduce_steps(mover, ("x", "z"), grad_kv, kv_bufs, kv_rows)
    advance(kv_sum)
    for h in range(4):
        grad_send[h, :, :HD] = grad_query[h].astype(LOW)
    advance(kv_sum)
    advance(kv_sum)
    advance(kv_sum)
    advance(kv_sum)
    kv_low[:, :128] = turn(kv_rows[:, :128], cos_kv[...], -sin_kv[...])
    kv_low[:, 128:] = kv_rows[:, 128:]
    for j in range(RING):
        place = slice((j // 2) * 128, (j // 2 + 1) * 128)
        one, two = grad_query[4, :, place], kv_low[:, place]
        if j % 2:
            one = pltpu.roll(one, TAIL, 1)
        else:
            two = pltpu.roll(two, TAIL, 1)
        grad_send[j, :, HD:] = jnp.where(low_lanes, one, two).astype(LOW)
    swap = exchange_steps(mover, grad_send, grad_got)
    advance(swap)
    grad_got[z] = grad_send[z]
    advance(feed_sum)
    output[half, :] = residual[half, :] + out_half[...]
    out_share = mover.copy(output.at[half], output.at[half], sibling())
    advance(rows_sum)
    advance(swap)
    advance(rows_sum)
    advance(rows_sum)
    spread_rows(rows_res, gateup_rows)
    out_share.wait_recv()
    mover.finish()


def fourth_kernel(
    grad_got,
    gateup_rows,
    down_rows,
    grad_out,
    attn_a,
    normed_hbm,
    grad_rows,
    tokens,
    gain_ref,
    attn_rows,
    feed_rows,
    grad_tokens,
    gateup_got,
    down_got,
    out_got,
    qkv_got,
    kv_other,
    scale_sums,
    send_sem,
    recv_sem,
    local_sem,
    qkv_weight,
    normed_one,
    part,
    grad_half,
    grad_qkv,
    out_send,
    qkv_send,
    scale_own,
    scale_other,
    *bufs,
):
    z = lax.axis_index("z")
    half, _, _, _ = core_rows()
    plane = ("dp", "x")
    sum_bufs = bufs[:5]
    out_bufs, qkv_bufs = bufs[5:11], bufs[11:17]
    loads = [
        pltpu.make_async_copy(attn_a.at[:, :, :, pl.ds(0, 384)], qkv_weight, local_sem.at[0]),
        pltpu.make_async_copy(normed_hbm, normed_one, local_sem.at[1]),
    ]
    for load in loads:
        load.start()
    greet([{"z": step("z", d)} for d in (1, 2, 3)] + plane_peers(plane) + [sibling()])
    mover = Mover(send_sem, recv_sem)
    out_sum = plane_reduce_steps(mover, plane, grad_out, out_bufs[:5], out_bufs[5])
    advance(out_sum)
    slices = grad_got[...].reshape(RING * BLOCK, 384)
    wide = RING * BLOCK
    loads[0].wait()
    weight = qkv_weight[...].reshape(D, 384)

    def make(block):
        part[block] = dot(grad_got[block], weight, (1, 1)).astype(LOW)

    shares = []
    sharing = share_steps(mover, part, sum_bufs[0], shares, make)
    advance(sharing)
    advance(sharing)
    sums = [
        reduce_steps(mover, own_rows(part), shares[i], sum_bufs, grad_half, span)
        for i, span in enumerate(SPANS)
    ]
    for one in sums:
        advance(one)
    advance(sharing)
    advance(sharing)
    advance(out_sum)
    loads[1].wait()
    for i in range(RING):
        left_side = normed_one[:, :, i * wide : (i + 1) * wide].reshape(wide, wide)
        grad_qkv[i] = dot(left_side, slices, (0, 0)).astype(LOW).reshape(RING, BLOCK, 384)
        if i % 2:
            advance(sums[i // 2])
    qkv_sum = plane_reduce_steps(mover, plane, grad_qkv, qkv_bufs[:5], qkv_bufs[5])
    advance(qkv_sum)
    advance(out_sum)
    gateup_swap = exchange_steps(mover, gateup_rows, gateup_got)
    advance(gateup_swap)
    down_swap = exchange_steps(mover, down_rows, down_got)
    advance(down_swap)
    gateup_got[z] = gateup_rows[z]
    down_got[z] = down_rows[z]
    advance(qkv_sum)
    advance(out_sum)
    advance(out_sum)
    spread_rows(out_bufs[5], out_send)
    out_swap = exchange_steps(mover, out_send, out_got)
    advance(out_swap)
    out_got[z] = out_send[z]
    advance(qkv_sum)
    for one in sums:
        advance(one)
    rows = tokens[half, :]
    inverse = lax.rsqrt(jnp.mean(rows * rows, axis=-1, keepdims=True) + eps_norm)
    unit = rows * inverse
    scaled = grad_half[...] * gain_ref[0:1, :]
    grad_tokens[half, :] = grad_rows[...] + inverse * (
        scaled - unit * jnp.mean(scaled * unit, axis=-1, keepdims=True)
    )
    share = mover.copy(grad_tokens.at[half], grad_tokens.at[half], sibling())
    advance(qkv_sum)
    advance(qkv_sum)
    spread_rows(qkv_bufs[5], qkv_send)
    qkv_swap = exchange_steps(mover, qkv_send, qkv_got)
    advance(qkv_swap)
    qkv_got[z] = qkv_send[z]
    width = gateup_got.shape[2]

    def with_weight(weight, got):
        return sum(
            jnp.sum(weight(j).astype(F32) * got[j].astype(F32), axis=-1, keepdims=True)
            for j in range(RING)
        )

    advance(gateup_swap)
    second = with_weight(lambda j: feed_rows[j, :, :width], gateup_got)
    advance(qkv_swap)
    kv_share = mover.copy(qkv_got.at[:, :, pl.ds(HD, 128)], kv_other, sibling())
    first = with_weight(lambda j: attn_rows[j, :, :384], qkv_got)
    scale_own[...] = jnp.where(lanes((PAD, 128)) == 0, first, second)
    scale_share = mover.copy(scale_own, scale_other, sibling())
    advance(down_swap)
    advance(out_swap)
    share.wait_recv()
    scale_share.wait_recv()
    scale_sums[...] = scale_own[...] + scale_other[...]
    kv_share.wait_recv()
    mover.finish()


def adam_kernel(
    rates,
    gateup_got,
    down_got,
    out_got,
    qkv_got,
    kv_other,
    *refs,
):
    core = lax.axis_index("tensor")
    low_lanes = lanes((OWN, 128)) < TAIL
    old = [refs[3 * i : 3 * i + 3] for i in range(5)]
    new = [refs[15 + 3 * i : 18 + 3 * i] for i in range(5)]

    def rows(got, j, lo, n):
        return got[j, :, lo : lo + n].astype(F32)[:OWN]

    def join(one, two, offset):
        if offset:
            return jnp.where(low_lanes, pltpu.roll(one, TAIL, 1), two)
        return jnp.where(low_lanes, one, pltpu.roll(two, TAIL, 1))

    def tails(got, k, lo, offset=0):
        return join(rows(got, 2 * k, lo, 128), rows(got, 2 * k + 1, lo, 128), offset)

    def update(i, index, gradient):
        results = adam_update(*(ref[index] for ref in old[i][:1]), gradient, *(ref[index] for ref in old[i][1:]), rates[i], weight_decay)
        for ref, value in zip(new[i], results, strict=True):
            ref[index] = value

    every = slice(None)
    for j in range(RING):
        update(0, (every, slice(HD * j, HD * (j + 1))), rows(qkv_got, j, 0, HD))
        update(2, (every, slice(HD * j, HD * (j + 1))), rows(out_got, j, 128, HD))
        place = slice(MAIN * j, MAIN * (j + 1))
        update(4, (every, place), rows(down_got, j, 0, MAIN))
        for g in range(2):
            update(3, (every, g, place), rows(gateup_got, j, MAIN * g, MAIN))
    own, theirs = [], []
    for k in range(2):
        place = slice(4 * HD + 128 * k, 4 * HD + 128 * (k + 1))
        update(0, (every, place), tails(qkv_got, k, HD))
        update(2, (every, place), tails(out_got, k, 0))
        place = slice(RING * MAIN + 128 * k, RING * MAIN + 128 * (k + 1))
        update(4, (every, place), tails(down_got, k, MAIN))
        for g in range(2):
            update(3, (every, g, place), tails(gateup_got, k, 2 * MAIN, g))
        own.append(tails(qkv_got, k, HD, 1))
        theirs.append(tails(kv_other, k, 0, 1))
    for k in range(2):
        place = slice(128 * k, 128 * (k + 1))
        update(1, (every, 0, place), jnp.where(core == 0, own[k], theirs[k]))
        update(1, (every, 1, place), jnp.where(core == 0, theirs[k], own[k]))


def run_adam(rates, grads, matrices):
    flat = [array for triple in matrices for array in triple]
    results = pl.pallas_call(
        functools.partial(adam_kernel, rates),
        out_shape=[jax.ShapeDtypeStruct(array.shape, F32) for array in flat],
        in_specs=[pl.BlockSpec(memory_space=pltpu.VMEM)] * (len(grads) + len(flat)),
        out_specs=[pl.BlockSpec(memory_space=pltpu.VMEM)] * len(flat),
        compiler_params=pltpu.CompilerParams(vmem_limit_bytes=60 * 1024 * 1024),
    )(*grads, *flat)
    return [results[3 * i : 3 * i + 3] for i in range(5)]


def call(kernel, ident, copies, out, scratch, operands, spaces, out_spaces=None):
    results = pl.pallas_call(
        kernel,
        out_shape=[jax.ShapeDtypeStruct(shape, kind) for shape, kind in out.values()],
        in_specs=[pl.BlockSpec(memory_space=space) for space in spaces],
        out_specs=[pl.BlockSpec(memory_space=(out_spaces or {}).get(name, pltpu.VMEM)) for name in out],
        scratch_shapes=[
            pltpu.SemaphoreType.DMA((copies,)),
            pltpu.SemaphoreType.DMA((copies,)),
            pltpu.SemaphoreType.DMA((16,)),
            *scratch,
        ],
        compiler_params=pltpu.CompilerParams(
            collective_id=ident, has_side_effects=True, vmem_limit_bytes=60 * 1024 * 1024
        ),
    )(*operands)
    return dict(zip(out, results, strict=True))


def run_second(*operands):
    out = {
        "grad_rows": ((HALF, D), F32),
        "da_all": ((RING, BLOCK, D), LOW),
        "feed_part": ((RING, BLOCK, D), LOW),
        "gateup_grads": ((RING, RING, BLOCK, 2 * (MAIN + TAIL)), LOW),
        "down_rows": ((RING, PAD, 1024), LOW),
    }
    scratch = [
        pltpu.VMEM((RING, BLOCK, D), LOW),
        pltpu.VMEM((RING, BLOCK, D), LOW),
        pltpu.VMEM((RING, RING, BLOCK, 2 * (MAIN + TAIL)), LOW),
        pltpu.VMEM((RING, RING, BLOCK, 1024), LOW),
        pltpu.VMEM((RING * BLOCK, 1024), LOW),
        pltpu.VMEM((RING * BLOCK, 2 * (MAIN + TAIL)), LOW),
        pltpu.VMEM((RING, BLOCK, D), LOW),
        pltpu.VMEM((RING, BLOCK, 2 * (MAIN + TAIL)), LOW),
        pltpu.VMEM((HALF, D), F32),
        pltpu.VMEM((HALF, D), F32),
        pltpu.VMEM((HALF, D), F32),
        pltpu.VMEM((BLOCK, D), LOW),
        *reduce_scratch(),
        *plane_reduce_scratch(1024),
    ]
    spaces = [pl.ANY] * 5 + [pltpu.VMEM]
    return call(
        second_kernel, 5, 80, out, scratch, operands, spaces, {"gateup_grads": pl.ANY, "da_all": pl.ANY}
    )


def run_third(*operands):
    out = {
        "grad_out": ((RING, RING, BLOCK, 384), LOW),
        "grad_got": ((RING, BLOCK, 384), LOW),
        "gateup_rows": ((RING, PAD, 2 * (MAIN + TAIL)), LOW),
        "output": ((BLOCK, D), F32),
    }
    scratch = [
        pltpu.VMEM((RING, BLOCK, D), LOW),
        pltpu.VMEM((RING, RING, BLOCK, 128), LOW),
        pltpu.VMEM((RING, RING, BLOCK, HD), LOW),
        pltpu.VMEM((2, RING, RING, BLOCK, HD), LOW),
        pltpu.VMEM((RING, HALF, D), LOW),
        pltpu.VMEM((HALF, D), F32),
        pltpu.VMEM((RING, BLOCK, 384), LOW),
        pltpu.VMEM((RING, BLOCK, 384), LOW),
        pltpu.VMEM((5, BLOCK, HD), LOW),
        pltpu.VMEM((5, BLOCK, 128), F32),
        pltpu.VMEM((5, BLOCK, RING * BLOCK), LOW),
        pltpu.VMEM((5, BLOCK, RING * BLOCK), LOW),
        pltpu.VMEM((5, BLOCK, HD), F32),
        pltpu.VMEM((2, RING, RING, BLOCK, HD), LOW),
        pltpu.VMEM((RING, RING, BLOCK, HD), LOW),
        pltpu.VMEM((RING, RING, BLOCK, HD), LOW),
        pltpu.VMEM((5, BLOCK, HD), F32),
        pltpu.VMEM((RING, BLOCK, 384), LOW),
        pltpu.VMEM((BLOCK, HD), F32),
        *reduce_scratch(),
        *plane_reduce_scratch(2 * (MAIN + TAIL)),
        *plane_reduce_scratch(HD),
    ]
    spaces = [pl.ANY] * 3 + [pltpu.VMEM] + [pl.ANY] * 2 + [pltpu.VMEM] * 2 + [pl.ANY] + [pltpu.VMEM] * 6
    return call(third_kernel, 2, 100, out, scratch, operands, spaces)


def run_fourth(*operands):
    out = {
        "grad_tokens": ((BLOCK, D), F32),
        "gateup_got": ((RING, PAD, 2 * (MAIN + TAIL)), LOW),
        "down_got": ((RING, PAD, 1024), LOW),
        "out_got": ((RING, PAD, 384), LOW),
        "qkv_got": ((RING, PAD, 384), LOW),
        "kv_other": ((RING, PAD, 128), LOW),
        "scale_sums": ((PAD, 128), F32),
    }
    scratch = [
        pltpu.VMEM((RING, RING, BLOCK, 384), LOW),
        pltpu.VMEM((RING, BLOCK, D), LOW),
        pltpu.VMEM((RING, BLOCK, D), LOW),
        pltpu.VMEM((HALF, D), F32),
        pltpu.VMEM((RING, RING, BLOCK, 384), LOW),
        pltpu.VMEM((RING, PAD, 384), LOW),
        pltpu.VMEM((RING, PAD, 384), LOW),
        pltpu.VMEM((PAD, 128), F32),
        pltpu.VMEM((PAD, 128), F32),
        *reduce_scratch(),
        *plane_reduce_scratch(384),
        *plane_reduce_scratch(384),
    ]
    spaces = [pltpu.VMEM] * 4 + [pl.ANY] * 2 + [pltpu.VMEM] * 5
    return call(fourth_kernel, 3, 80, out, scratch, operands, spaces)


def adam_update(weight, gradient, first_moment, second_moment, learn_rate, decay_rate):
    first_moment = first_decay * first_moment + (1.0 - first_decay) * gradient
    second_moment = second_decay * second_moment + (1.0 - second_decay) * gradient * gradient
    corrected = (
        first_moment
        / (1.0 - first_decay**STEP)
        / (jnp.sqrt(second_moment / (1.0 - second_decay**STEP)) + adam_eps)
    )
    return (weight - learn_rate * (corrected + decay_rate * weight), first_moment, second_moment)


def out_fan_in(seq_length):
    return max(1, H * HD * 4 // min(WINDOW, seq_length))


def quarters(rows):
    return rows.reshape(OWN, RING, -1).transpose(1, 0, 2)


def head_quarters(rows):
    split = rows.reshape(rows.shape[0], 5, HD)
    last = split[:, 4].reshape(-1, RING, TAIL)
    return jnp.concatenate([split[:, :4], last], axis=2).transpose(1, 0, 2)


def pad_to(x, axis, size):
    widths = [(0, 0)] * x.ndim
    widths[axis] = (0, size - x.shape[axis])
    return jnp.pad(x, widths)


def per_device(
    tokens,
    cotangent,
    w_query,
    w_keyvalue,
    w_out,
    w_gateup,
    w_down,
    norm_scales,
    first_query,
    first_keyvalue,
    first_out,
    first_gateup,
    first_down,
    first_scales,
    second_query,
    second_keyvalue,
    second_out,
    second_gateup,
    second_down,
    second_scales,
):
    core = lax.axis_index("tensor")
    seq_index = lax.axis_index("x") * RING + lax.axis_index("z")
    positions = seq_index * BLOCK + jnp.arange(BLOCK, dtype=jnp.int32)
    seq_length = BLOCK * RING * RING

    keyvalue_part = lax.dynamic_index_in_dim(w_keyvalue, core, 1, keepdims=False)
    scale_columns = jnp.broadcast_to(norm_scales.T[None], (RING, OWN, 2))
    out_quarters = head_quarters(w_out.T)
    attn_rows = jnp.concatenate(
        [
            head_quarters(w_query),
            quarters(keyvalue_part),
            out_quarters[..., HD:],
            pad_to(scale_columns, 2, TAIL),
            out_quarters[..., :HD],
        ],
        axis=2,
    ).astype(LOW)
    attn_rows = pad_to(attn_rows, 1, PAD)
    gateup = w_gateup.astype(LOW)
    mains = RING * MAIN
    feed_rows = jnp.concatenate(
        [
            quarters(gateup[:, 0, :mains]),
            quarters(gateup[:, 1, :mains]),
            quarters(gateup[:, 0, mains:]),
            quarters(gateup[:, 1, mains:]),
            quarters(w_down.T[:, :mains].astype(LOW)),
            quarters(w_down.T[:, mains:].astype(LOW)),
        ],
        axis=2,
    )
    feed_rows = pad_to(pad_to(feed_rows, 2, 2944), 1, PAD)
    frequency = 10000.0 ** (-jnp.arange(TAIL, dtype=F32) / TAIL)
    angles = positions.astype(F32)[:, None] * frequency[None, :]
    cos_table = jnp.tile(jnp.cos(angles), (1, 2))
    sin_table = jnp.concatenate([-jnp.sin(angles), jnp.sin(angles)], axis=1)
    cos_kv = jnp.where(core == 0, cos_table, 1.0)
    sin_kv = jnp.where(core == 0, sin_table, 0.0)
    first = run_first(
        attn_rows, feed_rows, tokens, cotangent.astype(LOW), cos_table, sin_table, cos_kv, sin_kv
    )
    second = run_second(
        first["feed_full"],
        first["normed_two"],
        first["dy_all"],
        cotangent,
        first["residual"],
        first["gains"],
    )
    third = run_third(
        second["feed_part"],
        second["gateup_grads"],
        second["da_all"],
        first["residual"],
        first["attn_a"],
        first["attn_b"],
        first["att_slice"],
        first["query"],
        first["keyvalue"],
        first["log_total"],
        first["attended"],
        cos_table,
        sin_table,
        cos_kv,
        sin_kv,
    )
    fourth = run_fourth(
        third["grad_got"],
        third["gateup_rows"],
        second["down_rows"],
        third["grad_out"],
        first["attn_a"],
        first["normed_one"],
        second["grad_rows"],
        tokens,
        first["gains"],
        attn_rows,
        feed_rows,
    )
    output, grad_tokens = third["output"], fourth["grad_tokens"]

    matrix_rate = 2.0 * D ** (-0.5)
    out_rate = 2.0 * out_fan_in(seq_length) ** (-0.5)
    down_rate = 2.0 * (FF // 2) ** (-0.5)
    triples = run_adam(
        (matrix_rate, matrix_rate, out_rate, matrix_rate, down_rate),
        [fourth[name] for name in ("gateup_got", "down_got", "out_got", "qkv_got", "kv_other")],
        [
            (w_query, first_query, second_query),
            (w_keyvalue, first_keyvalue, second_keyvalue),
            (w_out.T, first_out.T, second_out.T),
            (w_gateup, first_gateup, second_gateup),
            (w_down.T, first_down.T, second_down.T),
        ],
    )
    triples[2] = [array.T for array in triples[2]]
    triples[4] = [array.T for array in triples[4]]
    scale_grads = fourth["scale_sums"][:OWN, :2].T / (1.0 + norm_scales.astype(LOW).astype(F32))
    triples.append(
        adam_update(norm_scales, scale_grads, first_scales, second_scales, gain_rate, 0.0)
    )
    return (output, grad_tokens, *(triple[i] for i in range(3) for triple in triples))


def solution(mesh):
    split = Mesh(
        mesh.devices.reshape(RING, RING, RING, 2), ("dp", "x", "z", "tensor")
    )
    rows = ("dp", "x", "z")
    matrices = (
        P(rows, "tensor"),
        P(rows, None, None),
        P("tensor", rows),
        P(rows, None, "tensor"),
        P("tensor", rows),
        P(None, rows),
    )
    in_specs = (P(rows, None), P(rows, None), *matrices, *matrices, *matrices)
    out_specs = in_specs
    return jax.shard_map(
        per_device, mesh=split, in_specs=in_specs, out_specs=out_specs, check_vma=False
    )
```

```python
import functools

import jax
import jax.numpy as jnp
from jax import lax
from jax.experimental import pallas as pl
from jax.experimental.pallas import tpu as pltpu
from jax.sharding import Mesh
from jax.sharding import PartitionSpec as P

D = 2560
H = 10
HD = 256
FF = 7680
WINDOW = 2048
STEP = 10

eps_norm = 1e-06
masked_fill = -1e30
first_decay = 0.9
second_decay = 0.95
adam_eps = 1e-08
weight_decay = 0.1
gain_rate = 0.2
GELU_SCALE = (2.0 / 3.141592653589793) ** 0.5
GELU_CUBE = 0.044715

MESH = pl.DeviceIdType.MESH
LOW = jnp.bfloat16
F32 = jnp.float32
RING = 4
BLOCK = 160
HALF = BLOCK // 2
PART = 48
OWN = 40
PAD = 48
SPANS = ((0, 48, 32), (48, 32, 16))
MAIN = 896
TAIL = 64


def step(axis, distance):
    return lax.rem(lax.axis_index(axis) + (RING + distance), RING)


def sibling():
    return {"tensor": 1 - lax.axis_index("tensor")}


def greet(peers):
    barrier = pltpu.get_barrier_semaphore()
    for peer in peers:
        pl.semaphore_signal(barrier, inc=1, device_id=peer, device_id_type=MESH)
    pl.semaphore_wait(barrier, len(peers))


def dot(left_side, right_side, contract):
    return lax.dot_general(
        left_side, right_side, ((contract[:1], contract[1:]), ((), ())), preferred_element_type=F32
    )


class Mover:
    def __init__(self, send_sem, recv_sem):
        self.send_sem, self.recv_sem, self.pending = send_sem, recv_sem, []

    def copy(self, src, dst, peer):
        index = len(self.pending)
        one = pltpu.make_async_remote_copy(
            src_ref=src,
            dst_ref=dst,
            send_sem=self.send_sem.at[index],
            recv_sem=self.recv_sem.at[index],
            device_id=peer,
            device_id_type=MESH,
        )
        one.start()
        self.pending.append(one)
        return one

    def finish(self):
        for one in self.pending:
            one.wait_send()


def advance(steps):
    next(steps, None)


def plane_peers(axes):
    return [{axis: step(axis, d)} for axis in axes for d in (-1, 1)]


def exchange_steps(mover, src, dst):
    me = lax.axis_index("z")
    copies = [
        mover.copy(src.at[step("z", d)], dst.at[me], {"z": step("z", d)}) for d in (2, 1, 3)
    ]
    yield
    for copy in copies:
        copy.wait_recv()


def core_rows(lo=0, n=HALF, part=PART):
    base = lax.axis_index("tensor") * HALF

    def rows(start, size):
        return pl.ds(pl.multiple_of(start, 16), size)

    return (
        rows(base + lo, n),
        rows(base + lo, part),
        rows(base + (lo + part), n - part),
        rows(HALF - base + lo, n),
    )


def gather_steps(mover, x, out, span=(0, HALF, PART)):
    me, left, right, far = (step("z", d) for d in (0, -1, 1, 2))
    half, first, last, _ = core_rows(*span)
    to_right = mover.copy(x.at[half], out.at[me, half], {"z": right})
    to_left = mover.copy(x.at[half], out.at[me, half], {"z": left})
    yield
    to_right.wait_recv()
    on_right = mover.copy(out.at[left, first], out.at[left, first], {"z": right})
    shares = [mover.copy(out.at[left, half], out.at[left, half], sibling())]
    to_left.wait_recv()
    on_left = mover.copy(out.at[right, last], out.at[right, last], {"z": left})
    shares.append(mover.copy(out.at[right, half], out.at[right, half], sibling()))
    yield
    on_right.wait_recv()
    on_left.wait_recv()
    shares.append(mover.copy(out.at[far, half], out.at[far, half], sibling()))
    yield
    for copy in shares:
        copy.wait_recv()


def cut_rows(which, cut):
    base, size = (0, cut) if which == 0 else (cut, BLOCK - cut)
    part = -(-size // 32) * 16
    return pl.ds(base, size), pl.ds(base, part), pl.ds(base + part, size - part)


def plane_gather_steps(mover, axes, x, out, cut=HALF, order=(0, 1), share=False):
    a, b = (lax.axis_index(axis) for axis in axes)
    state = {}
    for which, axis in enumerate(axes):
        rows = cut_rows(which, cut)[0]
        place = (lambda i, r: out.at[i, b, r]) if which == 0 else (lambda i, r: out.at[a, i, r])
        me = (a, b)[which]
        to_right = mover.copy(x.at[rows], place(me, rows), {axis: step(axis, 1)})
        to_left = mover.copy(x.at[rows], place(me, rows), {axis: step(axis, -1)})
        state[which] = (axis, place, to_right, to_left)
    yield
    passed = {}
    for which in order:
        axis, place, to_right, to_left = state[which]
        _, first, last = cut_rows(which, cut)
        left, right = step(axis, -1), step(axis, 1)
        to_right.wait_recv()
        on_right = mover.copy(place(left, first), place(left, first), {axis: right})
        to_left.wait_recv()
        on_left = mover.copy(place(right, last), place(right, last), {axis: left})
        passed[which] = (on_right, on_left)
    yield
    state = {}
    shares = []

    def give(piece):
        if share:
            shares.append(mover.copy(piece, piece, sibling()))

    for which in order:
        axis, other = axes[which], axes[1 - which]
        rows = cut_rows(which, cut)[0]
        if which == 0:
            place = lambda i, lo, n, rows=rows: out.at[pl.ds(lo, n), i, rows]
        else:
            place = lambda i, lo, n, rows=rows: out.at[i, pl.ds(lo, n), rows]
        me = (b, a)[which]
        for copy in passed[which]:
            copy.wait_recv()
        to_right = mover.copy(place(me, 0, 4), place(me, 0, 4), {other: step(other, 1)})
        to_left = mover.copy(place(me, 0, 4), place(me, 0, 4), {other: step(other, -1)})
        give(place(me, 0, 4))
        state[which] = (other, place, to_right, to_left)
        yield
    ends = []
    for which in order:
        other, place, to_right, to_left = state[which]
        left, right = step(other, -1), step(other, 1)
        to_right.wait_recv()
        ends.append(mover.copy(place(left, 0, 2), place(left, 0, 2), {other: right}))
        give(place(left, 0, 4))
        to_left.wait_recv()
        ends.append(mover.copy(place(right, 2, 2), place(right, 2, 2), {other: left}))
        give(place(right, 0, 4))
        yield
    for copy in ends:
        copy.wait_recv()
    for which in order:
        other, place, _, _ = state[which]
        give(place(step(other, 2), 0, 4))
    for copy in shares:
        copy.wait_recv()


def lanes(shape):
    return lax.broadcasted_iota(jnp.int32, shape, len(shape) - 1)


def turn(values, cos, sin):
    return values * cos + pltpu.roll(values, 64, 1) * sin


def whole_rows(blocks, stage, dst):
    for i in range(RING):
        stage[i * OWN : (i + 1) * OWN] = blocks[i].astype(F32)[:OWN]
    dst[...] = stage[...].astype(LOW)


def first_kernel(
    w_query,
    w_keyvalue,
    w_out,
    w_gateup,
    w_down,
    scale_columns,
    tokens,
    cotangent,
    cos_ref,
    sin_ref,
    cos_kv,
    sin_kv,
    feed_full,
    attn_a,
    attn_b,
    normed_one,
    dy_all,
    query,
    kv_out,
    log_total,
    att_slice,
    residual,
    normed_two,
    attended,
    gain_ref,
    attn_rows,
    feed_rows,
    send_sem,
    recv_sem,
    local_sem,
    cot_in,
    dy,
    attn_got,
    mine_a,
    mine_b,
    weight_a,
    weight_b,
    attn_stage,
    feed_got,
    feed_mine,
    feed_stage,
    unit_low,
    unit_all,
    normed,
    qkv_send,
    qkv_got,
    kv_own,
    keyvalue,
    scores,
    att_send,
    part,
    sum_half,
    normed_low,
    *bufs,
):
    z, x, y, core = (lax.axis_index(axis) for axis in ("z", "x", "dp", "tensor"))
    plane = ("dp", "x")
    saves = []

    def save(src, dst):
        saves.append(pltpu.make_async_copy(src, dst, local_sem.at[len(saves)]))
        saves[-1].start()
        return saves[-1]

    cot_load = pltpu.make_async_copy(cotangent, cot_in, local_sem.at[15])
    cot_load.start()
    low = lanes((OWN, 128)) < TAIL

    def put(rows, j, lo, values):
        padding = jnp.zeros((PAD - OWN, values.shape[1]), F32)
        rows[j, :, lo : lo + values.shape[1]] = jnp.concatenate([values, padding]).astype(LOW)

    def pair(one, two, odd):
        if odd:
            return jnp.where(low, pltpu.roll(one, TAIL, 1), two)
        return jnp.where(low, one, pltpu.roll(two, TAIL, 1))

    for j in range(RING):
        head = slice(HD * j, HD * (j + 1))
        tile = slice((j // 2) * 128, (j // 2 + 1) * 128)
        last = slice(4 * HD + tile.start, 4 * HD + tile.stop)
        kv_tile = jnp.where(core == 0, w_keyvalue[:, 0, tile], w_keyvalue[:, 1, tile])
        out_tile = pltpu.roll(w_out[:, last], TAIL, 1) if j % 2 else w_out[:, last]
        put(attn_rows, j, 0, w_query[:, head])
        put(attn_rows, j, HD, pair(w_query[:, last], kv_tile, j % 2))
        put(attn_rows, j, 384, jnp.where(low, out_tile, scale_columns[...]))
        put(attn_rows, j, 512, w_out[:, head])
    greet([{"z": step("z", d)} for d in (1, 2, 3)] + plane_peers(plane) + [sibling()])
    mover = Mover(send_sem, recv_sem)

    attn_swap = exchange_steps(mover, attn_rows, attn_got)
    advance(attn_swap)
    for j in range(RING):
        main = slice(MAIN * j, MAIN * (j + 1))
        last = slice(RING * MAIN + (j // 2) * 128, RING * MAIN + (j // 2 + 1) * 128)
        down_tile = pltpu.roll(w_down[:, last], TAIL, 1) if j % 2 else w_down[:, last]
        put(feed_rows, j, 0, w_gateup[:, 0, main])
        put(feed_rows, j, MAIN, w_gateup[:, 1, main])
        put(feed_rows, j, 2 * MAIN, pair(w_gateup[:, 0, last], w_gateup[:, 1, last], j % 2))
        put(feed_rows, j, 2 * (MAIN + TAIL), w_down[:, main])
        put(feed_rows, j, 3 * MAIN + 2 * TAIL, jnp.where(low, down_tile, 0.0))
    feed_swap = exchange_steps(mover, feed_rows, feed_got)
    advance(feed_swap)
    values = tokens[...]
    unit = values * lax.rsqrt(jnp.mean(values * values, axis=-1, keepdims=True) + eps_norm)
    unit_low[...] = unit.astype(LOW)
    unit_gather = gather_steps(mover, unit_low, unit_all)
    advance(unit_gather)
    attn_got[z] = attn_rows[z]
    advance(attn_swap)
    for i in range(RING):
        attn_stage[i * OWN : (i + 1) * OWN] = attn_got[i].astype(F32)[:OWN]
    mine_a[...] = attn_stage[:, :512].astype(LOW)
    mine_b[...] = attn_stage[:, 512:].astype(LOW)
    a_gather = plane_gather_steps(mover, plane, mine_a, weight_a)
    advance(a_gather)
    weight_a[y, x] = mine_a[...]
    unit_all[z] = unit_low[...]
    advance(a_gather)
    feed_got[z] = feed_rows[z]
    advance(a_gather)
    advance(a_gather)
    advance(feed_swap)
    whole_rows(feed_got, feed_stage, feed_mine)
    feed_own = save(feed_mine, feed_full.at[y, x])
    advance(unit_gather)
    advance(a_gather)
    advance(a_gather)
    feed_gather = plane_gather_steps(mover, plane, feed_mine, feed_full)
    advance(feed_gather)
    advance(unit_gather)
    advance(unit_gather)
    advance(a_gather)
    save(weight_a, attn_a)

    scale_cols = weight_a[:, :, :, 384:].reshape(D, 128)
    pick = (lanes((8, 128)) == TAIL + lax.broadcasted_iota(jnp.int32, (8, 128), 0)).astype(LOW)
    gain_ref[...] = 1.0 + dot(pick, scale_cols, (1, 1))
    qkv_weight = weight_a[:, :, :, :384].reshape(D, 384)
    copies = []
    for d in (2, 1, 3, 0):
        block = step("z", d)
        rows = (unit_all[block].astype(F32) * gain_ref[0:1, :]).astype(LOW)
        normed[block] = rows
        qkv_send[block] = dot(rows, qkv_weight, (1, 0)).astype(LOW)
        if d:
            copies.append(mover.copy(qkv_send.at[block], qkv_got.at[z], {"z": block}))
    save(normed, normed_one)
    qkv_got[z] = qkv_send[z]
    feed_own.wait()
    advance(feed_gather)
    for copy in copies:
        copy.wait_recv()
    low_lanes = lanes((BLOCK, 128)) < TAIL
    cos, sin = cos_ref[...], sin_ref[...]

    def joined(i, offset):
        one, two = (qkv_got[i + k, :, 256:384].astype(F32) for k in (0, 1))
        if offset == 0:
            return jnp.where(low_lanes, one, pltpu.roll(two, TAIL, 1))
        return jnp.where(low_lanes, pltpu.roll(one, TAIL, 1), two)

    kv_own[:, :128] = turn(joined(0, 1), cos_kv[...], sin_kv[...]).astype(LOW)
    kv_own[:, 128:] = joined(2, 1).astype(LOW)
    kv_mine = keyvalue.at[core]
    kv_gather = plane_gather_steps(mover, ("x", "z"), kv_own, kv_mine, share=True)
    advance(kv_gather)
    keyvalue[core, x, z] = kv_own[...]
    scale = HD ** (-0.5)
    for h in range(4):
        first = qkv_got[h, :, :128].astype(F32)
        query[h, :, :128] = (turn(first, cos, sin) * scale).astype(LOW)
        query[h, :, 128:] = (qkv_got[h, :, 128:256].astype(F32) * scale).astype(LOW)
    query[4, :, :128] = (turn(joined(0, 0), cos, sin) * scale).astype(LOW)
    query[4, :, 128:] = (joined(2, 0) * scale).astype(LOW)
    b_gather = plane_gather_steps(mover, plane, mine_b, weight_b)
    advance(b_gather)
    weight_b[y, x] = mine_b[...]
    advance(kv_gather)
    advance(b_gather)
    for _ in range(2):
        advance(kv_gather)
        advance(b_gather)
    for _ in range(2):
        advance(kv_gather)
        advance(b_gather)
    for _ in range(2):
        advance(feed_gather)
    cot_load.wait()
    dy[...] = cot_in[...].astype(LOW)
    dy_gather = gather_steps(mover, dy, dy_all)
    advance(dy_gather)
    save(dy, dy_all.at[z])
    advance(kv_gather)
    save(keyvalue, kv_out)

    start = (x * RING + z) * BLOCK
    chunk = RING * BLOCK

    def one_head(h, carry):
        queries = query[h]
        top = jnp.full((BLOCK, 1), masked_fill, F32)
        for k in range(RING):
            rows = keyvalue[0, k].reshape(chunk, HD)
            tile = dot(queries, rows, (1, 1))
            gap = (start - k * chunk) + (
                lax.broadcasted_iota(jnp.int32, tile.shape, 0) - lanes(tile.shape)
            )
            tile = jnp.where((gap >= 0) & (gap < WINDOW), tile, masked_fill)
            scores[:, k * chunk : (k + 1) * chunk] = tile
            top = jnp.maximum(top, jnp.max(tile, axis=-1, keepdims=True))
        sums = jnp.zeros((BLOCK, 1), F32)
        for k in range(RING):
            tile = jnp.exp(scores[:, k * chunk : (k + 1) * chunk] - top)
            scores[:, k * chunk : (k + 1) * chunk] = tile
            sums = sums + jnp.sum(tile, axis=-1, keepdims=True)
        inverse = 1.0 / sums
        result = jnp.zeros((BLOCK, HD), F32)
        for k in range(RING):
            low = (scores[:, k * chunk : (k + 1) * chunk] * inverse).astype(LOW)
            result = result + dot(low, keyvalue[1, k].reshape(chunk, HD), (1, 0))
        attended[h] = result
        log_total[h] = jnp.broadcast_to(top + jnp.log(sums), (BLOCK, 128))
        return carry

    lax.fori_loop(0, 5, one_head, 0)
    for j in range(RING):
        att_send[j, :, 128:] = attended[j].astype(LOW)
        tile = attended[4, :, (j // 2) * 128 : (j // 2 + 1) * 128]
        tile = pltpu.roll(tile, TAIL, 1) if j % 2 else tile
        att_send[j, :, :128] = jnp.where(low_lanes, tile, 0.0).astype(LOW)
    att_swap = exchange_steps(mover, att_send, att_slice)
    advance(att_swap)
    att_slice[z] = att_send[z]
    advance(att_swap)

    advance(b_gather)
    save(weight_b, attn_b)

    last_weight = weight_a[:, :, :, 384:].reshape(D, 128)
    main_weight = weight_b[...].reshape(D, HD)

    def make(block):
        rows = dot(att_slice[block, :, :128], last_weight, (1, 1))
        part[block] = (rows + dot(att_slice[block, :, 128:], main_weight, (1, 1))).astype(LOW)

    shares = []
    sharing = share_steps(mover, part, bufs[0], shares, make)
    advance(sharing)
    advance(sharing)
    sums = [
        reduce_steps(mover, own_rows(part), shares[i], bufs, sum_half, span)
        for i, span in enumerate(SPANS)
    ]
    for one in sums:
        advance(one)
    advance(sharing)
    advance(sharing)
    for one in sums:
        advance(one)

    def normed_rows(rows):
        unit = rows * lax.rsqrt(jnp.mean(rows * rows, axis=-1, keepdims=True) + eps_norm)
        return (unit * gain_ref[1:2, :]).astype(LOW)

    gathers, res_shares = [], []
    for one, span in zip(sums, SPANS, strict=True):
        advance(one)
        place = core_rows(*span)[0]
        rows = tokens[place, :] + sum_half[span[0] : span[0] + span[1]]
        residual[place, :] = rows
        normed_low[place, :] = normed_rows(rows)
        gathers.append(gather_steps(mover, normed_low, normed_two, span))
        advance(gathers[-1])
        res_shares.append(mover.copy(residual.at[place], residual.at[place], sibling()))
    advance(dy_gather)
    for copy in res_shares:
        copy.wait_recv()
    theirs = core_rows()[3]
    normed_low[theirs, :] = normed_rows(residual[theirs, :])
    save(normed_low, normed_two.at[z])
    for one in gathers:
        advance(one)
    advance(feed_gather)
    advance(feed_gather)
    for one in gathers:
        advance(one)
    advance(dy_gather)
    for one in gathers:
        advance(one)
    advance(dy_gather)
    advance(feed_gather)
    for one in saves:
        if one is not feed_own:
            one.wait()
    mover.finish()


def run_first(*operands):
    out = {
        "feed_full": ((RING, RING, BLOCK, 2944), LOW),
        "attn_a": ((RING, RING, BLOCK, 512), LOW),
        "attn_b": ((RING, RING, BLOCK, HD), LOW),
        "normed_one": ((RING, BLOCK, D), LOW),
        "dy_all": ((RING, BLOCK, D), LOW),
        "query": ((5, BLOCK, HD), LOW),
        "keyvalue": ((2, RING, RING, BLOCK, HD), LOW),
        "log_total": ((5, BLOCK, 128), F32),
        "att_slice": ((RING, BLOCK, 384), LOW),
        "residual": ((BLOCK, D), F32),
        "normed_two": ((RING, BLOCK, D), LOW),
        "attended": ((5, BLOCK, HD), F32),
        "gains": ((8, D), F32),
        "attn_rows": ((RING, PAD, 768), LOW),
        "feed_rows": ((RING, PAD, 2944), LOW),
    }
    remote = ("feed_full", "attn_a", "attn_b", "normed_one", "dy_all", "keyvalue", "normed_two")
    spaces = [pltpu.VMEM] * 7 + [pl.ANY] + [pltpu.VMEM] * 4
    scratch = [
        pltpu.VMEM((BLOCK, D), F32),
        pltpu.VMEM((BLOCK, D), LOW),
        pltpu.VMEM((RING, PAD, 768), LOW),
        pltpu.VMEM((BLOCK, 512), LOW),
        pltpu.VMEM((BLOCK, HD), LOW),
        pltpu.VMEM((RING, RING, BLOCK, 512), LOW),
        pltpu.VMEM((RING, RING, BLOCK, HD), LOW),
        pltpu.VMEM((BLOCK, 768), F32),
        pltpu.VMEM((RING, PAD, 2944), LOW),
        pltpu.VMEM((BLOCK, 2944), LOW),
        pltpu.VMEM((BLOCK, 2944), F32),
        pltpu.VMEM((BLOCK, D), LOW),
        pltpu.VMEM((RING, BLOCK, D), LOW),
        pltpu.VMEM((RING, BLOCK, D), LOW),
        pltpu.VMEM((RING, BLOCK, 384), LOW),
        pltpu.VMEM((RING, BLOCK, 384), LOW),
        pltpu.VMEM((BLOCK, HD), LOW),
        pltpu.VMEM((2, RING, RING, BLOCK, HD), LOW),
        pltpu.VMEM((BLOCK, RING * RING * BLOCK), F32),
        pltpu.VMEM((RING, BLOCK, 384), LOW),
        pltpu.VMEM((RING, BLOCK, D), LOW),
        pltpu.VMEM((HALF, D), F32),
        pltpu.VMEM((BLOCK, D), LOW),
        *reduce_scratch(),
    ]
    return call(
        first_kernel, 1, 150, out, scratch, operands, spaces, {name: pl.ANY for name in remote}
    )


def plane_reduce_steps(mover, axes, g, bufs, res, loads=None):
    far, side, near, far_two, side_two = bufs
    places = [lax.axis_index(axis) for axis in axes]

    def block(which, i, lo, n):
        rows = pl.ds(which * HALF, HALF)
        return g.at[i, pl.ds(lo, n), rows] if which == 0 else g.at[pl.ds(lo, n), i, rows]

    locals_ = []

    def load(src, dst):
        locals_.append(pltpu.make_async_copy(src, dst, loads.at[len(locals_)]))
        locals_[-1].start()
        return locals_[-1]

    first, sides, wanted = [], [], []
    for which, axis in enumerate(axes):
        right, left = step(axis, 1), step(axis, -1)
        far_place = step(axis, 2)
        first.append(
            (
                mover.copy(block(which, far_place, 0, 2), far.at[which, pl.ds(0, 2)], {axis: right}),
                mover.copy(block(which, far_place, 2, 2), far.at[which, pl.ds(2, 2)], {axis: left}),
            )
        )
        if loads is not None:
            wanted.append(
                (
                    load(block(which, right, 0, 2), near.at[which, 0]),
                    load(block(which, left, 2, 2), near.at[which, 1]),
                )
            )
    for which, axis in enumerate(axes):
        right, left = step(axis, 1), step(axis, -1)
        sides.append(
            [
                mover.copy(block(which, right, 2, 2), side.at[which, 0, pl.ds(2, 2)], {axis: right}),
                mover.copy(block(which, left, 0, 2), side.at[which, 1, pl.ds(0, 2)], {axis: left}),
            ]
        )
    yield
    owned = []
    for which, axis in enumerate(axes):
        for k, (d, lo) in enumerate(((1, 0), (-1, 2))):
            first[which][k].wait_recv()
            if loads is not None:
                wanted[which][k].wait()
                term = near[which, k]
            else:
                term = block(which, step(axis, d), lo, 2)[...]
            near[which, k] = (term.astype(F32) + far[which, lo : lo + 2].astype(F32)).astype(LOW)
            sides[which].append(
                mover.copy(near.at[which, k], side.at[which, k, pl.ds(lo, 2)], {axis: step(axis, d)})
            )
        if loads is not None:
            owned.append(load(block(which, places[which], 0, 4), far.at[which]))
    yield

    def summed(which, i):
        if loads is not None:
            term = far[which, i]
        else:
            rows = pl.ds(which * HALF, HALF)
            me = places[which]
            term = (g[me, i, rows] if which == 0 else g[i, me, rows])
        return (
            term.astype(F32) + side[which, 0, i].astype(F32) + side[which, 1, i].astype(F32)
        )

    second = []
    for which, axis in enumerate(axes):
        other = axes[1 - which]
        right, left = {other: step(other, 1)}, {other: step(other, -1)}
        for copy in sides[which]:
            copy.wait_recv()
        if loads is not None:
            owned[which].wait()
        far_two[which, 0] = summed(which, step(other, 2)).astype(LOW)
        upper, lower = pl.ds(0, PART), pl.ds(PART, HALF - PART)
        second.append(
            (
                mover.copy(far_two.at[which, 0, upper], far_two.at[which, 1, upper], right),
                mover.copy(far_two.at[which, 0, lower], far_two.at[which, 1, lower], left),
            )
        )
    yield
    last = []
    for which, axis in enumerate(axes):
        other = axes[1 - which]
        right, left = step(other, 1), step(other, -1)
        total = summed(which, right)
        second[which][0].wait_recv()
        side_two[which, 0, :PART] = (
            total[:PART] + far_two[which, 1, :PART].astype(F32)
        ).astype(LOW)
        side_two[which, 0, PART:] = total[PART:].astype(LOW)
        last.append(mover.copy(side_two.at[which, 0], side_two.at[which, 2], {other: right}))
        total = summed(which, left)
        second[which][1].wait_recv()
        side_two[which, 1, :PART] = total[:PART].astype(LOW)
        side_two[which, 1, PART:] = (
            total[PART:] + far_two[which, 1, PART:].astype(F32)
        ).astype(LOW)
        last.append(mover.copy(side_two.at[which, 1], side_two.at[which, 3], {other: left}))
    yield
    for which, axis in enumerate(axes):
        other = axes[1 - which]
        last[2 * which].wait_recv()
        last[2 * which + 1].wait_recv()
        res[which * HALF : (which + 1) * HALF] = (
            summed(which, lax.axis_index(other))
            + side_two[which, 2].astype(F32)
            + side_two[which, 3].astype(F32)
        )


def plane_reduce_scratch(columns):
    return [
        pltpu.VMEM((2, 4, HALF, columns), LOW),
        pltpu.VMEM((2, 2, 4, HALF, columns), LOW),
        pltpu.VMEM((2, 2, 2, HALF, columns), LOW),
        pltpu.VMEM((2, 2, HALF, columns), LOW),
        pltpu.VMEM((2, 4, HALF, columns), LOW),
        pltpu.VMEM((BLOCK, columns), F32),
    ]


def share_steps(mover, part, other, shares, make=None, spans=SPANS):
    me, left, right, far = (step("z", d) for d in (0, -1, 1, 2))
    shares.extend([] for _ in spans)
    for slot, block in enumerate((far, right, left, me)):
        if make is not None:
            make(block)
        for copies, (lo, n, first) in zip(shares, spans, strict=True):
            theirs = core_rows(lo, n, first)[3]
            copies.append(
                mover.copy(part.at[block, theirs], other.at[slot, pl.ds(lo, n)], sibling())
            )
        yield


def reduce_steps(mover, mine, shares, bufs, out, span):
    other, total, far_in, from_left, from_right = bufs
    lo, n, part = span
    me, left, right, far = (step("z", d) for d in (0, -1, 1, 2))
    blocks = (far, right, left, me)
    rows, first, last = pl.ds(lo, n), pl.ds(lo, part), pl.ds(lo + part, n - part)

    def both(slot):
        return mine(blocks[slot], span).astype(F32) + other[slot, rows].astype(F32)

    shares[0].wait_recv()
    total[0, rows] = both(0).astype(LOW)
    far_right = mover.copy(total.at[0, first], far_in.at[first], {"z": right})
    far_left = mover.copy(total.at[0, last], far_in.at[last], {"z": left})
    yield
    shares[1].wait_recv()
    summed = both(1)
    far_right.wait_recv()
    total[1, first] = (summed[:part] + far_in[first].astype(F32)).astype(LOW)
    total[1, last] = summed[part:].astype(LOW)
    to_right = mover.copy(total.at[1, rows], from_left.at[rows], {"z": right})
    shares[2].wait_recv()
    summed = both(2)
    far_left.wait_recv()
    total[2, first] = summed[:part].astype(LOW)
    total[2, last] = (summed[part:] + far_in[last].astype(F32)).astype(LOW)
    to_left = mover.copy(total.at[2, rows], from_right.at[rows], {"z": left})
    yield
    shares[3].wait_recv()
    summed = both(3)
    to_right.wait_recv()
    to_left.wait_recv()
    out[rows] = summed + from_left[rows].astype(F32) + from_right[rows].astype(F32)


def own_rows(ref):
    return lambda block, span: ref[block, core_rows(*span)[0]]


def half_rows(ref):
    return lambda block, span: ref[block, pl.ds(span[0], span[1])]


def reduce_scratch():
    return [
        pltpu.VMEM((4, HALF, D), LOW),
        pltpu.VMEM((3, HALF, D), LOW),
        pltpu.VMEM((HALF, D), LOW),
        pltpu.VMEM((HALF, D), LOW),
        pltpu.VMEM((HALF, D), LOW),
    ]


def spread_rows(res, dst):
    for i in range(RING):
        rows = res[i * OWN : (i + 1) * OWN]
        dst[i] = jnp.concatenate([rows, jnp.zeros((PAD - OWN, rows.shape[1]), F32)]).astype(LOW)


def activation(gate, upper, grad):
    square = gate * gate
    tanh = jnp.tanh(GELU_SCALE * gate * (1.0 + GELU_CUBE * square))
    half = 0.5 * (1.0 + tanh)
    gelu = gate * half
    slope = half + 0.5 * gate * (1.0 - tanh * tanh) * GELU_SCALE * (1.0 + 3.0 * GELU_CUBE * square)
    return gelu * upper, grad * upper * slope, grad * gelu


def second_kernel(
    feed_full,
    normed_two,
    dy_all,
    cotangent,
    residual,
    gain_ref,
    grad_rows,
    da_all,
    feed_part,
    gateup_grads,
    down_rows,
    send_sem,
    recv_sem,
    local_sem,
    normed_in,
    dy_in,
    gateup_weight,
    down_weight,
    hidden,
    dgu,
    norm_part,
    stage,
    grad_half,
    cot_half,
    res_half,
    da_low,
    *bufs,
):
    z = lax.axis_index("z")
    half, _, _, _ = core_rows()
    plane = ("dp", "x")
    gu_width = 2 * (MAIN + TAIL)
    wide = RING * BLOCK
    loads = [
        pltpu.make_async_copy(src, dst, local_sem.at[i])
        for i, (src, dst) in enumerate(
            (
                (normed_two, normed_in),
                (feed_full.at[:, :, :, pl.ds(0, gu_width)], gateup_weight),
                (dy_all, dy_in),
                (feed_full.at[:, :, :, pl.ds(gu_width, 1024)], down_weight),
                (cotangent.at[half], cot_half),
                (residual.at[half], res_half),
            )
        )
    ]
    for load in loads:
        load.start()
    greet(plane_peers(("z",)) + plane_peers(plane) + [sibling()])
    mover = Mover(send_sem, recv_sem)
    for load in loads:
        load.wait()

    def product(rows, weight, lo, n):
        left_side = rows[...].reshape(wide, D)
        return dot(left_side, weight[:, :, :, lo : lo + n].reshape(D, n), (1, 0))

    for lo, n in ((0, 256), (256, 256), (512, 256), (768, 128)):
        value, grad_gate, grad_upper = activation(
            product(normed_in, gateup_weight, lo, n),
            product(normed_in, gateup_weight, MAIN + lo, n),
            product(dy_in, down_weight, lo, n),
        )
        hidden[:, lo : lo + n] = value.astype(LOW)
        dgu[:, lo : lo + n] = grad_gate.astype(LOW)
        dgu[:, MAIN + lo : MAIN + lo + n] = grad_upper.astype(LOW)
    both = product(normed_in, gateup_weight, 2 * MAIN, 2 * TAIL)
    value, grad_gate, grad_upper = activation(
        both, pltpu.roll(both, TAIL, 1), product(dy_in, down_weight, MAIN, 2 * TAIL)
    )
    low_lanes = lanes(both.shape) < TAIL
    hidden[:, MAIN:] = jnp.where(low_lanes, value, 0.0).astype(LOW)
    dgu[:, 2 * MAIN :] = jnp.where(low_lanes, grad_gate, pltpu.roll(grad_upper, TAIL, 1)).astype(LOW)

    for i in range(RING):
        part = dot(dgu[...], gateup_weight[i].reshape(wide, gu_width), (1, 1))
        norm_part[:, :, i * wide : (i + 1) * wide] = part.astype(LOW).reshape(RING, BLOCK, wide)
    shares = []
    sharing = share_steps(mover, norm_part, bufs[0], shares)
    for _ in range(RING):
        advance(sharing)
    sums = [
        reduce_steps(mover, own_rows(norm_part), shares[i], bufs[:5], grad_half, span)
        for i, span in enumerate(SPANS)
    ]

    for i in range(RING):
        terms = dot(hidden[...], down_weight[i].reshape(wide, 1024), (1, 1))
        feed_part[:, :, i * wide : (i + 1) * wide] = terms.astype(LOW).reshape(RING, BLOCK, wide)
        if i < 2:
            advance(sums[i])

    def columns(rows, i):
        return rows[:, :, i * wide : (i + 1) * wide].reshape(wide, wide)

    for i in range(RING):
        grads = dot(columns(dy_in, i), hidden[...], (0, 0))
        down_weight[i] = grads.astype(LOW).reshape(RING, BLOCK, 1024)
        if i < 2:
            advance(sums[i])
    down_sum = plane_reduce_steps(mover, plane, down_weight, bufs[5:10], bufs[10])
    advance(down_sum)
    saved = []

    def gateup_block(i):
        if saved:
            saved[-1].wait()
        grads = dot(columns(normed_in, i), dgu[...], (0, 0))
        stage[...] = grads.astype(LOW).reshape(RING, BLOCK, gu_width)
        saved.append(pltpu.make_async_copy(stage, gateup_grads.at[i], local_sem.at[10 + i]))
        saved[-1].start()

    gateup_block(0)
    gathers, da_shares = [], []
    for one, span in zip(sums, SPANS, strict=True):
        advance(one)
        piece = pl.ds(span[0], span[1])
        place = core_rows(*span)[0]
        rows = res_half[piece, :]
        inverse = lax.rsqrt(jnp.mean(rows * rows, axis=-1, keepdims=True) + eps_norm)
        unit = rows * inverse
        scaled = grad_half[piece, :] * gain_ref[1:2, :]
        grad = cot_half[piece, :] + inverse * (
            scaled - unit * jnp.mean(scaled * unit, axis=-1, keepdims=True)
        )
        grad_rows[piece, :] = grad
        da_low[place, :] = grad.astype(LOW)
        gathers.append(gather_steps(mover, da_low, da_all, span))
        advance(gathers[-1])
        da_shares.append(mover.copy(da_low.at[place], da_low.at[place], sibling()))
    advance(down_sum)
    gateup_block(1)
    for copy in da_shares:
        copy.wait_recv()
    da_own = pltpu.make_async_copy(da_low, da_all.at[z], local_sem.at[9])
    da_own.start()
    for one in gathers:
        advance(one)
    gateup_block(2)
    advance(down_sum)
    for one in gathers:
        advance(one)
    gateup_block(3)
    advance(down_sum)
    for one in gathers:
        advance(one)
    advance(down_sum)
    spread_rows(bufs[10], down_rows)
    saved[-1].wait()
    da_own.wait()
    mover.finish()


def third_kernel(
    feed_part,
    gateup_grads,
    da_all,
    residual,
    attn_a,
    attn_b,
    att_slice,
    query,
    kv_hbm,
    log_total,
    attended,
    cos_ref,
    sin_ref,
    cos_kv,
    sin_kv,
    grad_out,
    grad_got,
    gateup_rows,
    output,
    send_sem,
    recv_sem,
    local_sem,
    da_in,
    last_weight,
    main_weight,
    keyvalue,
    feed_mine,
    out_half,
    datt_send,
    datt_got,
    datt,
    delta,
    ds_all,
    p_all,
    dq,
    kv_pair,
    kv_in,
    grad_kv,
    grad_query,
    grad_send,
    kv_low,
    *bufs,
):
    z, core = lax.axis_index("z"), lax.axis_index("tensor")
    x = lax.axis_index("x")
    half = core_rows()[0]
    whole_span = ((0, HALF, PART),)
    out_bufs, rows_bufs, rows_res = bufs[:5], bufs[5:10], bufs[10]
    kv_bufs, kv_rows = bufs[11:16], bufs[16]
    loads = [
        pltpu.make_async_copy(src, dst, local_sem.at[8 + i])
        for i, (src, dst) in enumerate(
            (
                (da_all, da_in),
                (attn_a.at[:, :, :, pl.ds(384, 128)], last_weight),
                (attn_b, main_weight),
                (kv_hbm, keyvalue),
                (feed_part.at[:, half], feed_mine),
            )
        )
    ]
    for load in loads:
        load.start()
    greet([{"z": step("z", d)} for d in (1, 2, 3)] + plane_peers(("dp", "x")) + [sibling()])
    mover = Mover(send_sem, recv_sem)
    rows_sum = plane_reduce_steps(
        mover, ("dp", "x"), gateup_grads, rows_bufs, rows_res, loads=local_sem
    )
    advance(rows_sum)
    for load in loads[:3]:
        load.wait()
    last = last_weight[...].reshape(D, 128)
    main = main_weight[...].reshape(D, HD)
    copies = []
    for d in (2, 1, 3, 0):
        block = step("z", d)
        datt_send[block, :, :128] = dot(da_in[block], last, (1, 0)).astype(LOW)
        datt_send[block, :, 128:] = dot(da_in[block], main, (1, 0)).astype(LOW)
        if d:
            copies.append(mover.copy(datt_send.at[block], datt_got.at[z], {"z": block}))
    datt_got[z] = datt_send[z]
    shares = []
    sharing = share_steps(mover, feed_part, out_bufs[0], shares, spans=whole_span)
    for _ in range(RING):
        advance(sharing)
    feed_sum = reduce_steps(
        mover, half_rows(feed_mine), shares[0], out_bufs, out_half, whole_span[0]
    )
    slices = att_slice[...].reshape(RING * BLOCK, 384)
    wide = RING * BLOCK
    for i in range(RING):
        left_side = da_in[:, :, i * wide : (i + 1) * wide].reshape(wide, wide)
        grad_out[i] = dot(left_side, slices, (0, 0)).astype(LOW).reshape(RING, BLOCK, 384)
    for copy in copies:
        copy.wait_recv()
    for load in loads[3:]:
        load.wait()
    advance(feed_sum)
    advance(rows_sum)

    low_lanes = lanes((BLOCK, 128)) < TAIL
    for h in range(4):
        datt[h] = datt_got[h, :, 128:]
    for k in range(2):
        one, two = (datt_got[2 * k + i, :, :128].astype(F32) for i in range(2))
        datt[4, :, k * 128 : (k + 1) * 128] = jnp.where(
            low_lanes, one, pltpu.roll(two, TAIL, 1)
        ).astype(LOW)
    for h in range(5):
        delta[h] = jnp.broadcast_to(
            jnp.sum(datt[h].astype(F32) * attended[h], axis=-1, keepdims=True), (BLOCK, 128)
        )
        dq[h] = jnp.zeros((BLOCK, HD), F32)
    start = (x * RING + z) * BLOCK
    chunk = RING * BLOCK

    def one_chunk(k, carry):
        keys = keyvalue[0, k].reshape(chunk, HD)
        values = keyvalue[1, k].reshape(chunk, HD)
        shape = (BLOCK, chunk)
        gap = (start - k * chunk) + (lax.broadcasted_iota(jnp.int32, shape, 0) - lanes(shape))
        visible = (gap >= 0) & (gap < WINDOW)

        def one_head(h, carry):
            scores = dot(query[h], keys, (1, 1))
            probs = jnp.where(visible, jnp.exp(scores - log_total[h, :, :1]), 0.0)
            grads = dot(datt[h], values, (1, 1))
            low = (probs * (grads - delta[h, :, :1])).astype(LOW)
            ds_all[h] = low
            p_all[h] = probs.astype(LOW)
            dq[h] = dq[h] + dot(low, keys, (1, 0))
            return carry

        lax.fori_loop(0, 5, one_head, 0)
        queries = query[...].reshape(5 * BLOCK, HD)
        outer = datt[...].reshape(5 * BLOCK, HD)
        kv_pair[0, k] = dot(ds_all[...].reshape(5 * BLOCK, chunk), queries, (0, 0)).astype(LOW).reshape(RING, BLOCK, HD)
        kv_pair[1, k] = dot(p_all[...].reshape(5 * BLOCK, chunk), outer, (0, 0)).astype(LOW).reshape(RING, BLOCK, HD)
        return carry

    lax.fori_loop(0, RING, one_chunk, 0)
    kv_swap = mover.copy(kv_pair.at[1 - core], kv_in, sibling())
    advance(feed_sum)
    cos, sin = cos_ref[...], sin_ref[...]
    scale = HD ** (-0.5)
    for h in range(5):
        grad_query[h, :, :128] = turn(dq[h, :, :128] * scale, cos, -sin)
        grad_query[h, :, 128:] = dq[h, :, 128:] * scale
    kv_swap.wait_recv()
    grad_kv[...] = (kv_pair[core].astype(F32) + kv_in[...].astype(F32)).astype(LOW)
    kv_sum = plane_reduce_steps(mover, ("x", "z"), grad_kv, kv_bufs, kv_rows)
    advance(kv_sum)
    for h in range(4):
        grad_send[h, :, :HD] = grad_query[h].astype(LOW)
    advance(kv_sum)
    advance(kv_sum)
    advance(kv_sum)
    advance(kv_sum)
    kv_low[:, :128] = turn(kv_rows[:, :128], cos_kv[...], -sin_kv[...])
    kv_low[:, 128:] = kv_rows[:, 128:]
    for j in range(RING):
        place = slice((j // 2) * 128, (j // 2 + 1) * 128)
        one, two = grad_query[4, :, place], kv_low[:, place]
        if j % 2:
            one = pltpu.roll(one, TAIL, 1)
        else:
            two = pltpu.roll(two, TAIL, 1)
        grad_send[j, :, HD:] = jnp.where(low_lanes, one, two).astype(LOW)
    swap = exchange_steps(mover, grad_send, grad_got)
    advance(swap)
    grad_got[z] = grad_send[z]
    advance(feed_sum)
    output[half, :] = residual[half, :] + out_half[...]
    out_share = mover.copy(output.at[half], output.at[half], sibling())
    advance(rows_sum)
    advance(swap)
    advance(rows_sum)
    advance(rows_sum)
    spread_rows(rows_res, gateup_rows)
    out_share.wait_recv()
    mover.finish()


def fourth_kernel(
    grad_got,
    gateup_rows,
    down_rows,
    grad_out,
    attn_a,
    normed_hbm,
    grad_rows,
    tokens,
    gain_ref,
    attn_rows,
    feed_rows,
    grad_tokens,
    gateup_got,
    down_got,
    out_got,
    qkv_got,
    kv_other,
    scale_sums,
    send_sem,
    recv_sem,
    local_sem,
    qkv_weight,
    normed_one,
    part,
    grad_half,
    grad_qkv,
    out_send,
    qkv_send,
    scale_own,
    scale_other,
    *bufs,
):
    z = lax.axis_index("z")
    half, _, _, _ = core_rows()
    plane = ("dp", "x")
    sum_bufs = bufs[:5]
    out_bufs, qkv_bufs = bufs[5:11], bufs[11:17]
    loads = [
        pltpu.make_async_copy(attn_a.at[:, :, :, pl.ds(0, 384)], qkv_weight, local_sem.at[0]),
        pltpu.make_async_copy(normed_hbm, normed_one, local_sem.at[1]),
    ]
    for load in loads:
        load.start()
    greet([{"z": step("z", d)} for d in (1, 2, 3)] + plane_peers(plane) + [sibling()])
    mover = Mover(send_sem, recv_sem)
    out_sum = plane_reduce_steps(mover, plane, grad_out, out_bufs[:5], out_bufs[5])
    advance(out_sum)
    slices = grad_got[...].reshape(RING * BLOCK, 384)
    wide = RING * BLOCK
    loads[0].wait()
    weight = qkv_weight[...].reshape(D, 384)

    def make(block):
        part[block] = dot(grad_got[block], weight, (1, 1)).astype(LOW)

    shares = []
    sharing = share_steps(mover, part, sum_bufs[0], shares, make)
    advance(sharing)
    advance(sharing)
    sums = [
        reduce_steps(mover, own_rows(part), shares[i], sum_bufs, grad_half, span)
        for i, span in enumerate(SPANS)
    ]
    for one in sums:
        advance(one)
    advance(sharing)
    advance(sharing)
    advance(out_sum)
    loads[1].wait()
    for i in range(RING):
        left_side = normed_one[:, :, i * wide : (i + 1) * wide].reshape(wide, wide)
        grad_qkv[i] = dot(left_side, slices, (0, 0)).astype(LOW).reshape(RING, BLOCK, 384)
        if i % 2:
            advance(sums[i // 2])
    qkv_sum = plane_reduce_steps(mover, plane, grad_qkv, qkv_bufs[:5], qkv_bufs[5])
    advance(qkv_sum)
    advance(out_sum)
    gateup_swap = exchange_steps(mover, gateup_rows, gateup_got)
    advance(gateup_swap)
    down_swap = exchange_steps(mover, down_rows, down_got)
    advance(down_swap)
    gateup_got[z] = gateup_rows[z]
    down_got[z] = down_rows[z]
    advance(qkv_sum)
    advance(out_sum)
    advance(out_sum)
    spread_rows(out_bufs[5], out_send)
    out_swap = exchange_steps(mover, out_send, out_got)
    advance(out_swap)
    out_got[z] = out_send[z]
    advance(qkv_sum)
    for one in sums:
        advance(one)
    rows = tokens[half, :]
    inverse = lax.rsqrt(jnp.mean(rows * rows, axis=-1, keepdims=True) + eps_norm)
    unit = rows * inverse
    scaled = grad_half[...] * gain_ref[0:1, :]
    grad_tokens[half, :] = grad_rows[...] + inverse * (
        scaled - unit * jnp.mean(scaled * unit, axis=-1, keepdims=True)
    )
    share = mover.copy(grad_tokens.at[half], grad_tokens.at[half], sibling())
    advance(qkv_sum)
    advance(qkv_sum)
    spread_rows(qkv_bufs[5], qkv_send)
    qkv_swap = exchange_steps(mover, qkv_send, qkv_got)
    advance(qkv_swap)
    qkv_got[z] = qkv_send[z]
    width = gateup_got.shape[2]

    def with_weight(weight, got):
        return sum(
            jnp.sum(weight(j).astype(F32) * got[j].astype(F32), axis=-1, keepdims=True)
            for j in range(RING)
        )

    advance(gateup_swap)
    second = with_weight(lambda j: feed_rows[j, :, :width], gateup_got)
    advance(qkv_swap)
    kv_share = mover.copy(qkv_got.at[:, :, pl.ds(HD, 128)], kv_other, sibling())
    first = with_weight(lambda j: attn_rows[j, :, :384], qkv_got)
    scale_own[...] = jnp.where(lanes((PAD, 128)) == 0, first, second)
    scale_share = mover.copy(scale_own, scale_other, sibling())
    advance(down_swap)
    advance(out_swap)
    share.wait_recv()
    scale_share.wait_recv()
    scale_sums[...] = scale_own[...] + scale_other[...]
    kv_share.wait_recv()
    mover.finish()


def adam_kernel(
    rates,
    gateup_got,
    down_got,
    out_got,
    qkv_got,
    kv_other,
    output_in,
    tokens_in,
    *refs,
):
    core = lax.axis_index("tensor")
    inputs, results = refs[:15], refs[15:30]
    passed = refs[30:32]
    in_bufs, out_bufs = refs[32:47], refs[47:62]
    pass_bufs, in_sem, out_sem = refs[62:64], refs[64], refs[65]
    loads = [
        pltpu.make_async_copy(src, dst, in_sem.at[i])
        for i, (src, dst) in enumerate(
            zip((*inputs, output_in, tokens_in), (*in_bufs, *pass_bufs), strict=True)
        )
    ]
    stores = [
        pltpu.make_async_copy(src, dst, out_sem.at[i])
        for i, (src, dst) in enumerate(
            zip((*out_bufs, *pass_bufs), (*results, *passed), strict=True)
        )
    ]
    order = (3, 4, 0, 2, 1)
    for i in order:
        for one in loads[3 * i : 3 * i + 3]:
            one.start()
    for one in loads[15:]:
        one.start()
    low_lanes = lanes((OWN, 128)) < TAIL
    old = [in_bufs[3 * i : 3 * i + 3] for i in range(5)]
    new = [out_bufs[3 * i : 3 * i + 3] for i in range(5)]

    def rows(got, j, lo, n):
        return got[j, :, lo : lo + n].astype(F32)[:OWN]

    def join(one, two, offset):
        if offset:
            return jnp.where(low_lanes, pltpu.roll(one, TAIL, 1), two)
        return jnp.where(low_lanes, one, pltpu.roll(two, TAIL, 1))

    def tails(got, k, lo, offset=0):
        return join(rows(got, 2 * k, lo, 128), rows(got, 2 * k + 1, lo, 128), offset)

    def update(i, index, gradient):
        results = adam_update(*(ref[index] for ref in old[i][:1]), gradient, *(ref[index] for ref in old[i][1:]), rates[i], weight_decay)
        for ref, value in zip(new[i], results, strict=True):
            ref[index] = value

    every = slice(None)

    def ready(i):
        for one in loads[3 * i : 3 * i + 3]:
            one.wait()

    def done(i):
        for one in stores[3 * i : 3 * i + 3]:
            one.start()

    def main_place(j, width):
        return slice(width * j, width * (j + 1))

    def tail_place(k, width):
        return slice(RING * width + 128 * k, RING * width + 128 * (k + 1))

    ready(3)
    for g in range(2):
        for j in range(RING):
            update(3, (every, g, main_place(j, MAIN)), rows(gateup_got, j, MAIN * g, MAIN))
        for k in range(2):
            update(3, (every, g, tail_place(k, MAIN)), tails(gateup_got, k, 2 * MAIN, g))
    done(3)
    for one, two in zip(loads[15:], stores[15:], strict=True):
        one.wait()
        two.start()
    for i, got, width, main, tail in (
        (4, down_got, MAIN, 0, MAIN),
        (0, qkv_got, HD, 0, HD),
        (2, out_got, HD, 128, 0),
    ):
        ready(i)
        for j in range(RING):
            update(i, (every, main_place(j, width)), rows(got, j, main, width))
        for k in range(2):
            update(i, (every, tail_place(k, width)), tails(got, k, tail))
        done(i)
    ready(1)
    for k in range(2):
        place = slice(128 * k, 128 * (k + 1))
        own, theirs = tails(qkv_got, k, HD, 1), tails(kv_other, k, 0, 1)
        update(1, (every, 0, place), jnp.where(core == 0, own, theirs))
        update(1, (every, 1, place), jnp.where(core == 0, theirs, own))
    done(1)
    for one in stores:
        one.wait()


def run_adam(rates, grads, matrices, passing):
    flat = [array for triple in matrices for array in triple]
    shapes = [jax.ShapeDtypeStruct(array.shape, F32) for array in (*flat, *passing)]
    buffers = [pltpu.VMEM(array.shape, F32) for array in flat]
    results = pl.pallas_call(
        functools.partial(adam_kernel, rates),
        out_shape=shapes,
        in_specs=[pl.BlockSpec(memory_space=pltpu.VMEM)] * len(grads)
        + [pl.BlockSpec(memory_space=pl.ANY)] * len(shapes),
        out_specs=[pl.BlockSpec(memory_space=pl.ANY)] * len(shapes),
        scratch_shapes=[
            *buffers,
            *buffers,
            *(pltpu.VMEM(array.shape, F32) for array in passing),
            pltpu.SemaphoreType.DMA((len(shapes),)),
            pltpu.SemaphoreType.DMA((len(shapes),)),
        ],
        compiler_params=pltpu.CompilerParams(vmem_limit_bytes=60 * 1024 * 1024),
    )(*grads, *passing, *flat)
    return [results[3 * i : 3 * i + 3] for i in range(5)], results[15:]


def call(kernel, ident, copies, out, scratch, operands, spaces, out_spaces=None):
    results = pl.pallas_call(
        kernel,
        out_shape=[jax.ShapeDtypeStruct(shape, kind) for shape, kind in out.values()],
        in_specs=[pl.BlockSpec(memory_space=space) for space in spaces],
        out_specs=[pl.BlockSpec(memory_space=(out_spaces or {}).get(name, pltpu.VMEM)) for name in out],
        scratch_shapes=[
            pltpu.SemaphoreType.DMA((copies,)),
            pltpu.SemaphoreType.DMA((copies,)),
            pltpu.SemaphoreType.DMA((16,)),
            *scratch,
        ],
        compiler_params=pltpu.CompilerParams(
            collective_id=ident, has_side_effects=True, vmem_limit_bytes=60 * 1024 * 1024
        ),
    )(*operands)
    return dict(zip(out, results, strict=True))


def run_second(*operands):
    out = {
        "grad_rows": ((HALF, D), F32),
        "da_all": ((RING, BLOCK, D), LOW),
        "feed_part": ((RING, BLOCK, D), LOW),
        "gateup_grads": ((RING, RING, BLOCK, 2 * (MAIN + TAIL)), LOW),
        "down_rows": ((RING, PAD, 1024), LOW),
    }
    scratch = [
        pltpu.VMEM((RING, BLOCK, D), LOW),
        pltpu.VMEM((RING, BLOCK, D), LOW),
        pltpu.VMEM((RING, RING, BLOCK, 2 * (MAIN + TAIL)), LOW),
        pltpu.VMEM((RING, RING, BLOCK, 1024), LOW),
        pltpu.VMEM((RING * BLOCK, 1024), LOW),
        pltpu.VMEM((RING * BLOCK, 2 * (MAIN + TAIL)), LOW),
        pltpu.VMEM((RING, BLOCK, D), LOW),
        pltpu.VMEM((RING, BLOCK, 2 * (MAIN + TAIL)), LOW),
        pltpu.VMEM((HALF, D), F32),
        pltpu.VMEM((HALF, D), F32),
        pltpu.VMEM((HALF, D), F32),
        pltpu.VMEM((BLOCK, D), LOW),
        *reduce_scratch(),
        *plane_reduce_scratch(1024),
    ]
    spaces = [pl.ANY] * 5 + [pltpu.VMEM]
    return call(
        second_kernel, 5, 80, out, scratch, operands, spaces, {"gateup_grads": pl.ANY, "da_all": pl.ANY}
    )


def run_third(*operands):
    out = {
        "grad_out": ((RING, RING, BLOCK, 384), LOW),
        "grad_got": ((RING, BLOCK, 384), LOW),
        "gateup_rows": ((RING, PAD, 2 * (MAIN + TAIL)), LOW),
        "output": ((BLOCK, D), F32),
    }
    scratch = [
        pltpu.VMEM((RING, BLOCK, D), LOW),
        pltpu.VMEM((RING, RING, BLOCK, 128), LOW),
        pltpu.VMEM((RING, RING, BLOCK, HD), LOW),
        pltpu.VMEM((2, RING, RING, BLOCK, HD), LOW),
        pltpu.VMEM((RING, HALF, D), LOW),
        pltpu.VMEM((HALF, D), F32),
        pltpu.VMEM((RING, BLOCK, 384), LOW),
        pltpu.VMEM((RING, BLOCK, 384), LOW),
        pltpu.VMEM((5, BLOCK, HD), LOW),
        pltpu.VMEM((5, BLOCK, 128), F32),
        pltpu.VMEM((5, BLOCK, RING * BLOCK), LOW),
        pltpu.VMEM((5, BLOCK, RING * BLOCK), LOW),
        pltpu.VMEM((5, BLOCK, HD), F32),
        pltpu.VMEM((2, RING, RING, BLOCK, HD), LOW),
        pltpu.VMEM((RING, RING, BLOCK, HD), LOW),
        pltpu.VMEM((RING, RING, BLOCK, HD), LOW),
        pltpu.VMEM((5, BLOCK, HD), F32),
        pltpu.VMEM((RING, BLOCK, 384), LOW),
        pltpu.VMEM((BLOCK, HD), F32),
        *reduce_scratch(),
        *plane_reduce_scratch(2 * (MAIN + TAIL)),
        *plane_reduce_scratch(HD),
    ]
    spaces = [pl.ANY] * 3 + [pltpu.VMEM] + [pl.ANY] * 2 + [pltpu.VMEM] * 2 + [pl.ANY] + [pltpu.VMEM] * 6
    return call(third_kernel, 2, 100, out, scratch, operands, spaces)


def run_fourth(*operands):
    out = {
        "grad_tokens": ((BLOCK, D), F32),
        "gateup_got": ((RING, PAD, 2 * (MAIN + TAIL)), LOW),
        "down_got": ((RING, PAD, 1024), LOW),
        "out_got": ((RING, PAD, 384), LOW),
        "qkv_got": ((RING, PAD, 384), LOW),
        "kv_other": ((RING, PAD, 128), LOW),
        "scale_sums": ((PAD, 128), F32),
    }
    scratch = [
        pltpu.VMEM((RING, RING, BLOCK, 384), LOW),
        pltpu.VMEM((RING, BLOCK, D), LOW),
        pltpu.VMEM((RING, BLOCK, D), LOW),
        pltpu.VMEM((HALF, D), F32),
        pltpu.VMEM((RING, RING, BLOCK, 384), LOW),
        pltpu.VMEM((RING, PAD, 384), LOW),
        pltpu.VMEM((RING, PAD, 384), LOW),
        pltpu.VMEM((PAD, 128), F32),
        pltpu.VMEM((PAD, 128), F32),
        *reduce_scratch(),
        *plane_reduce_scratch(384),
        *plane_reduce_scratch(384),
    ]
    spaces = [pltpu.VMEM] * 4 + [pl.ANY] * 2 + [pltpu.VMEM] * 5
    return call(fourth_kernel, 3, 80, out, scratch, operands, spaces)


def adam_update(weight, gradient, first_moment, second_moment, learn_rate, decay_rate):
    first_moment = first_decay * first_moment + (1.0 - first_decay) * gradient
    second_moment = second_decay * second_moment + (1.0 - second_decay) * gradient * gradient
    corrected = (
        first_moment
        / (1.0 - first_decay**STEP)
        / (jnp.sqrt(second_moment / (1.0 - second_decay**STEP)) + adam_eps)
    )
    return (weight - learn_rate * (corrected + decay_rate * weight), first_moment, second_moment)


def out_fan_in(seq_length):
    return max(1, H * HD * 4 // min(WINDOW, seq_length))


def per_device(
    tokens,
    cotangent,
    w_query,
    w_keyvalue,
    w_out,
    w_gateup,
    w_down,
    norm_scales,
    first_query,
    first_keyvalue,
    first_out,
    first_gateup,
    first_down,
    first_scales,
    second_query,
    second_keyvalue,
    second_out,
    second_gateup,
    second_down,
    second_scales,
):
    core = lax.axis_index("tensor")
    seq_index = lax.axis_index("x") * RING + lax.axis_index("z")
    positions = seq_index * BLOCK + jnp.arange(BLOCK, dtype=jnp.int32)
    seq_length = BLOCK * RING * RING

    frequency = 10000.0 ** (-jnp.arange(TAIL, dtype=F32) / TAIL)
    angles = positions.astype(F32)[:, None] * frequency[None, :]
    cos_table = jnp.tile(jnp.cos(angles), (1, 2))
    sin_table = jnp.concatenate([-jnp.sin(angles), jnp.sin(angles)], axis=1)
    cos_kv = jnp.where(core == 0, cos_table, 1.0)
    sin_kv = jnp.where(core == 0, sin_table, 0.0)
    first = run_first(
        w_query,
        w_keyvalue,
        w_out.T,
        w_gateup,
        w_down.T,
        jnp.pad(norm_scales.T, ((0, 0), (TAIL, 128 - TAIL - 2))),
        tokens,
        cotangent,
        cos_table,
        sin_table,
        cos_kv,
        sin_kv,
    )
    second = run_second(
        first["feed_full"],
        first["normed_two"],
        first["dy_all"],
        cotangent,
        first["residual"],
        first["gains"],
    )
    third = run_third(
        second["feed_part"],
        second["gateup_grads"],
        second["da_all"],
        first["residual"],
        first["attn_a"],
        first["attn_b"],
        first["att_slice"],
        first["query"],
        first["keyvalue"],
        first["log_total"],
        first["attended"],
        cos_table,
        sin_table,
        cos_kv,
        sin_kv,
    )
    fourth = run_fourth(
        third["grad_got"],
        third["gateup_rows"],
        second["down_rows"],
        third["grad_out"],
        first["attn_a"],
        first["normed_one"],
        second["grad_rows"],
        tokens,
        first["gains"],
        first["attn_rows"],
        first["feed_rows"],
    )
    matrix_rate = 2.0 * D ** (-0.5)
    out_rate = 2.0 * out_fan_in(seq_length) ** (-0.5)
    down_rate = 2.0 * (FF // 2) ** (-0.5)
    triples, (output, grad_tokens) = run_adam(
        (matrix_rate, matrix_rate, out_rate, matrix_rate, down_rate),
        [fourth[name] for name in ("gateup_got", "down_got", "out_got", "qkv_got", "kv_other")],
        [
            (w_query, first_query, second_query),
            (w_keyvalue, first_keyvalue, second_keyvalue),
            (w_out.T, first_out.T, second_out.T),
            (w_gateup, first_gateup, second_gateup),
            (w_down.T, first_down.T, second_down.T),
        ],
        (third["output"], fourth["grad_tokens"]),
    )
    triples[2] = [array.T for array in triples[2]]
    triples[4] = [array.T for array in triples[4]]
    scale_grads = fourth["scale_sums"][:OWN, :2].T / (1.0 + norm_scales.astype(LOW).astype(F32))
    triples.append(
        adam_update(norm_scales, scale_grads, first_scales, second_scales, gain_rate, 0.0)
    )
    return (output, grad_tokens, *(triple[i] for i in range(3) for triple in triples))


def solution(mesh):
    split = Mesh(
        mesh.devices.reshape(RING, RING, RING, 2), ("dp", "x", "z", "tensor")
    )
    rows = ("dp", "x", "z")
    matrices = (
        P(rows, "tensor"),
        P(rows, None, None),
        P("tensor", rows),
        P(rows, None, "tensor"),
        P("tensor", rows),
        P(None, rows),
    )
    in_specs = (P(rows, None), P(rows, None), *matrices, *matrices, *matrices)
    out_specs = in_specs
    return jax.shard_map(
        per_device, mesh=split, in_specs=in_specs, out_specs=out_specs, check_vma=False
    )
```

```python
import functools

import jax
import jax.numpy as jnp
from jax import lax
from jax.experimental import pallas as pl
from jax.experimental.pallas import tpu as pltpu
from jax.sharding import Mesh
from jax.sharding import PartitionSpec as P

D = 2560
H = 10
HD = 256
FF = 7680
WINDOW = 2048
STEP = 10

eps_norm = 1e-06
masked_fill = -1e30
first_decay = 0.9
second_decay = 0.95
adam_eps = 1e-08
weight_decay = 0.1
gain_rate = 0.2
GELU_SCALE = (2.0 / 3.141592653589793) ** 0.5
GELU_CUBE = 0.044715

MESH = pl.DeviceIdType.MESH
LOW = jnp.bfloat16
F32 = jnp.float32
RING = 4
BLOCK = 160
HALF = BLOCK // 2
PART = 48
OWN = 40
PAD = 48
SPANS = ((0, 48, 32), (48, 32, 16))
MAIN = 896
TAIL = 64


def step(axis, distance):
    return lax.rem(lax.axis_index(axis) + (RING + distance), RING)


def sibling():
    return {"tensor": 1 - lax.axis_index("tensor")}


def greet(peers):
    barrier = pltpu.get_barrier_semaphore()
    for peer in peers:
        pl.semaphore_signal(barrier, inc=1, device_id=peer, device_id_type=MESH)
    pl.semaphore_wait(barrier, len(peers))


def dot(left_side, right_side, contract):
    return lax.dot_general(
        left_side, right_side, ((contract[:1], contract[1:]), ((), ())), preferred_element_type=F32
    )


class Mover:
    def __init__(self, send_sem, recv_sem):
        self.send_sem, self.recv_sem, self.pending = send_sem, recv_sem, []

    def copy(self, src, dst, peer):
        index = len(self.pending)
        one = pltpu.make_async_remote_copy(
            src_ref=src,
            dst_ref=dst,
            send_sem=self.send_sem.at[index],
            recv_sem=self.recv_sem.at[index],
            device_id=peer,
            device_id_type=MESH,
        )
        one.start()
        self.pending.append(one)
        return one

    def finish(self):
        for one in self.pending:
            one.wait_send()


def advance(steps):
    next(steps, None)


def plane_peers(axes):
    return [{axis: step(axis, d)} for axis in axes for d in (-1, 1)]


def exchange_steps(mover, src, dst):
    me = lax.axis_index("z")
    copies = [
        mover.copy(src.at[step("z", d)], dst.at[me], {"z": step("z", d)}) for d in (2, 1, 3)
    ]
    yield
    for copy in copies:
        copy.wait_recv()


def core_rows(lo=0, n=HALF, part=PART):
    base = lax.axis_index("tensor") * HALF

    def rows(start, size):
        return pl.ds(pl.multiple_of(start, 16), size)

    return (
        rows(base + lo, n),
        rows(base + lo, part),
        rows(base + (lo + part), n - part),
        rows(HALF - base + lo, n),
    )


def gather_steps(mover, x, out, span=(0, HALF, PART)):
    me, left, right, far = (step("z", d) for d in (0, -1, 1, 2))
    half, first, last, _ = core_rows(*span)
    to_right = mover.copy(x.at[half], out.at[me, half], {"z": right})
    to_left = mover.copy(x.at[half], out.at[me, half], {"z": left})
    yield
    to_right.wait_recv()
    on_right = mover.copy(out.at[left, first], out.at[left, first], {"z": right})
    shares = [mover.copy(out.at[left, half], out.at[left, half], sibling())]
    to_left.wait_recv()
    on_left = mover.copy(out.at[right, last], out.at[right, last], {"z": left})
    shares.append(mover.copy(out.at[right, half], out.at[right, half], sibling()))
    yield
    on_right.wait_recv()
    on_left.wait_recv()
    shares.append(mover.copy(out.at[far, half], out.at[far, half], sibling()))
    yield
    for copy in shares:
        copy.wait_recv()


def cut_rows(which, cut):
    base, size = (0, cut) if which == 0 else (cut, BLOCK - cut)
    part = -(-size // 32) * 16
    return pl.ds(base, size), pl.ds(base, part), pl.ds(base + part, size - part)


def plane_gather_steps(mover, axes, x, out, cut=HALF, order=(0, 1), share=False):
    a, b = (lax.axis_index(axis) for axis in axes)
    state = {}
    for which, axis in enumerate(axes):
        rows = cut_rows(which, cut)[0]
        place = (lambda i, r: out.at[i, b, r]) if which == 0 else (lambda i, r: out.at[a, i, r])
        me = (a, b)[which]
        to_right = mover.copy(x.at[rows], place(me, rows), {axis: step(axis, 1)})
        to_left = mover.copy(x.at[rows], place(me, rows), {axis: step(axis, -1)})
        state[which] = (axis, place, to_right, to_left)
    yield
    passed = {}
    for which in order:
        axis, place, to_right, to_left = state[which]
        _, first, last = cut_rows(which, cut)
        left, right = step(axis, -1), step(axis, 1)
        to_right.wait_recv()
        on_right = mover.copy(place(left, first), place(left, first), {axis: right})
        to_left.wait_recv()
        on_left = mover.copy(place(right, last), place(right, last), {axis: left})
        passed[which] = (on_right, on_left)
    yield
    state = {}
    shares = []

    def give(piece):
        if share:
            shares.append(mover.copy(piece, piece, sibling()))

    for which in order:
        axis, other = axes[which], axes[1 - which]
        rows = cut_rows(which, cut)[0]
        if which == 0:
            place = lambda i, lo, n, rows=rows: out.at[pl.ds(lo, n), i, rows]
        else:
            place = lambda i, lo, n, rows=rows: out.at[i, pl.ds(lo, n), rows]
        me = (b, a)[which]
        for copy in passed[which]:
            copy.wait_recv()
        to_right = mover.copy(place(me, 0, 4), place(me, 0, 4), {other: step(other, 1)})
        to_left = mover.copy(place(me, 0, 4), place(me, 0, 4), {other: step(other, -1)})
        give(place(me, 0, 4))
        state[which] = (other, place, to_right, to_left)
        yield
    ends = []
    for which in order:
        other, place, to_right, to_left = state[which]
        left, right = step(other, -1), step(other, 1)
        to_right.wait_recv()
        ends.append(mover.copy(place(left, 0, 2), place(left, 0, 2), {other: right}))
        give(place(left, 0, 4))
        to_left.wait_recv()
        ends.append(mover.copy(place(right, 2, 2), place(right, 2, 2), {other: left}))
        give(place(right, 0, 4))
        yield
    for copy in ends:
        copy.wait_recv()
    for which in order:
        other, place, _, _ = state[which]
        give(place(step(other, 2), 0, 4))
    for copy in shares:
        copy.wait_recv()


def lanes(shape):
    return lax.broadcasted_iota(jnp.int32, shape, len(shape) - 1)


def turn(values, cos, sin):
    return values * cos + pltpu.roll(values, 64, 1) * sin


def whole_rows(blocks, stage, dst):
    for i in range(RING):
        stage[i * OWN : (i + 1) * OWN] = blocks[i].astype(F32)[:OWN]
    dst[...] = stage[...].astype(LOW)


def first_kernel(
    w_query,
    w_keyvalue,
    w_out,
    w_gateup,
    w_down,
    scale_columns,
    tokens,
    cotangent,
    cos_ref,
    sin_ref,
    cos_kv,
    sin_kv,
    feed_full,
    attn_a,
    attn_b,
    normed_one,
    dy_all,
    query,
    kv_out,
    log_total,
    att_slice,
    residual,
    normed_two,
    attended,
    gain_ref,
    attn_rows,
    feed_rows,
    send_sem,
    recv_sem,
    local_sem,
    cot_in,
    dy,
    attn_got,
    mine_a,
    mine_b,
    weight_a,
    weight_b,
    attn_stage,
    feed_got,
    feed_mine,
    feed_stage,
    unit_low,
    unit_all,
    normed,
    qkv_send,
    qkv_got,
    kv_own,
    keyvalue,
    scores,
    att_send,
    part,
    sum_half,
    normed_low,
    *bufs,
):
    z, x, y, core = (lax.axis_index(axis) for axis in ("z", "x", "dp", "tensor"))
    plane = ("dp", "x")
    saves = []

    def save(src, dst):
        saves.append(pltpu.make_async_copy(src, dst, local_sem.at[len(saves)]))
        saves[-1].start()
        return saves[-1]

    cot_load = pltpu.make_async_copy(cotangent, cot_in, local_sem.at[15])
    cot_load.start()
    low = lanes((OWN, 128)) < TAIL

    def put(rows, j, lo, values):
        padding = jnp.zeros((PAD - OWN, values.shape[1]), F32)
        rows[j, :, lo : lo + values.shape[1]] = jnp.concatenate([values, padding]).astype(LOW)

    def pair(one, two, odd):
        if odd:
            return jnp.where(low, pltpu.roll(one, TAIL, 1), two)
        return jnp.where(low, one, pltpu.roll(two, TAIL, 1))

    for j in range(RING):
        head = slice(HD * j, HD * (j + 1))
        tile = slice((j // 2) * 128, (j // 2 + 1) * 128)
        last = slice(4 * HD + tile.start, 4 * HD + tile.stop)
        kv_tile = jnp.where(core == 0, w_keyvalue[:, 0, tile], w_keyvalue[:, 1, tile])
        out_tile = pltpu.roll(w_out[:, last], TAIL, 1) if j % 2 else w_out[:, last]
        put(attn_rows, j, 0, w_query[:, head])
        put(attn_rows, j, HD, pair(w_query[:, last], kv_tile, j % 2))
        put(attn_rows, j, 384, jnp.where(low, out_tile, scale_columns[...]))
        put(attn_rows, j, 512, w_out[:, head])
    greet([{"z": step("z", d)} for d in (1, 2, 3)] + plane_peers(plane) + [sibling()])
    mover = Mover(send_sem, recv_sem)

    attn_swap = exchange_steps(mover, attn_rows, attn_got)
    advance(attn_swap)
    for j in range(RING):
        main = slice(MAIN * j, MAIN * (j + 1))
        last = slice(RING * MAIN + (j // 2) * 128, RING * MAIN + (j // 2 + 1) * 128)
        down_tile = pltpu.roll(w_down[:, last], TAIL, 1) if j % 2 else w_down[:, last]
        put(feed_rows, j, 0, w_gateup[:, 0, main])
        put(feed_rows, j, MAIN, w_gateup[:, 1, main])
        put(feed_rows, j, 2 * MAIN, pair(w_gateup[:, 0, last], w_gateup[:, 1, last], j % 2))
        put(feed_rows, j, 2 * (MAIN + TAIL), w_down[:, main])
        put(feed_rows, j, 3 * MAIN + 2 * TAIL, jnp.where(low, down_tile, 0.0))
    feed_swap = exchange_steps(mover, feed_rows, feed_got)
    advance(feed_swap)
    values = tokens[...]
    unit = values * lax.rsqrt(jnp.mean(values * values, axis=-1, keepdims=True) + eps_norm)
    unit_low[...] = unit.astype(LOW)
    unit_gather = gather_steps(mover, unit_low, unit_all)
    advance(unit_gather)
    attn_got[z] = attn_rows[z]
    advance(attn_swap)
    for i in range(RING):
        attn_stage[i * OWN : (i + 1) * OWN] = attn_got[i].astype(F32)[:OWN]
    mine_a[...] = attn_stage[:, :512].astype(LOW)
    mine_b[...] = attn_stage[:, 512:].astype(LOW)
    a_gather = plane_gather_steps(mover, plane, mine_a, weight_a)
    advance(a_gather)
    weight_a[y, x] = mine_a[...]
    unit_all[z] = unit_low[...]
    advance(a_gather)
    feed_got[z] = feed_rows[z]
    advance(a_gather)
    advance(a_gather)
    advance(feed_swap)
    whole_rows(feed_got, feed_stage, feed_mine)
    feed_own = save(feed_mine, feed_full.at[y, x])
    advance(unit_gather)
    advance(a_gather)
    advance(a_gather)
    feed_gather = plane_gather_steps(mover, plane, feed_mine, feed_full)
    advance(feed_gather)
    advance(unit_gather)
    advance(unit_gather)
    advance(a_gather)
    save(weight_a, attn_a)

    scale_cols = weight_a[:, :, :, 384:].reshape(D, 128)
    pick = (lanes((8, 128)) == TAIL + lax.broadcasted_iota(jnp.int32, (8, 128), 0)).astype(LOW)
    gain_ref[...] = 1.0 + dot(pick, scale_cols, (1, 1))
    qkv_weight = weight_a[:, :, :, :384].reshape(D, 384)
    copies = []
    for d in (2, 1, 3, 0):
        block = step("z", d)
        rows = (unit_all[block].astype(F32) * gain_ref[0:1, :]).astype(LOW)
        normed[block] = rows
        qkv_send[block] = dot(rows, qkv_weight, (1, 0)).astype(LOW)
        if d:
            copies.append(mover.copy(qkv_send.at[block], qkv_got.at[z], {"z": block}))
    save(normed, normed_one)
    qkv_got[z] = qkv_send[z]
    feed_own.wait()
    advance(feed_gather)
    for copy in copies:
        copy.wait_recv()
    low_lanes = lanes((BLOCK, 128)) < TAIL
    cos, sin = cos_ref[...], sin_ref[...]

    def joined(i, offset):
        one, two = (qkv_got[i + k, :, 256:384].astype(F32) for k in (0, 1))
        if offset == 0:
            return jnp.where(low_lanes, one, pltpu.roll(two, TAIL, 1))
        return jnp.where(low_lanes, pltpu.roll(one, TAIL, 1), two)

    kv_own[:, :128] = turn(joined(0, 1), cos_kv[...], sin_kv[...]).astype(LOW)
    kv_own[:, 128:] = joined(2, 1).astype(LOW)
    kv_mine = keyvalue.at[core]
    kv_gather = plane_gather_steps(mover, ("x", "z"), kv_own, kv_mine, share=True)
    advance(kv_gather)
    keyvalue[core, x, z] = kv_own[...]
    scale = HD ** (-0.5)
    for h in range(4):
        first = qkv_got[h, :, :128].astype(F32)
        query[h, :, :128] = (turn(first, cos, sin) * scale).astype(LOW)
        query[h, :, 128:] = (qkv_got[h, :, 128:256].astype(F32) * scale).astype(LOW)
    query[4, :, :128] = (turn(joined(0, 0), cos, sin) * scale).astype(LOW)
    query[4, :, 128:] = (joined(2, 0) * scale).astype(LOW)
    b_gather = plane_gather_steps(mover, plane, mine_b, weight_b)
    advance(b_gather)
    weight_b[y, x] = mine_b[...]
    advance(kv_gather)
    advance(b_gather)
    for _ in range(2):
        advance(kv_gather)
        advance(b_gather)
    for _ in range(2):
        advance(kv_gather)
        advance(b_gather)
    for _ in range(2):
        advance(feed_gather)
    cot_load.wait()
    dy[...] = cot_in[...].astype(LOW)
    dy_gather = gather_steps(mover, dy, dy_all)
    advance(dy_gather)
    save(dy, dy_all.at[z])
    advance(kv_gather)
    save(keyvalue, kv_out)

    start = (x * RING + z) * BLOCK
    chunk = RING * BLOCK

    def one_head(h, carry):
        queries = query[h]
        top = jnp.full((BLOCK, 1), masked_fill, F32)
        for k in range(RING):
            rows = keyvalue[0, k].reshape(chunk, HD)
            tile = dot(queries, rows, (1, 1))
            gap = (start - k * chunk) + (
                lax.broadcasted_iota(jnp.int32, tile.shape, 0) - lanes(tile.shape)
            )
            tile = jnp.where((gap >= 0) & (gap < WINDOW), tile, masked_fill)
            scores[:, k * chunk : (k + 1) * chunk] = tile
            top = jnp.maximum(top, jnp.max(tile, axis=-1, keepdims=True))
        sums = jnp.zeros((BLOCK, 1), F32)
        for k in range(RING):
            tile = jnp.exp(scores[:, k * chunk : (k + 1) * chunk] - top)
            scores[:, k * chunk : (k + 1) * chunk] = tile
            sums = sums + jnp.sum(tile, axis=-1, keepdims=True)
        inverse = 1.0 / sums
        result = jnp.zeros((BLOCK, HD), F32)
        for k in range(RING):
            low = (scores[:, k * chunk : (k + 1) * chunk] * inverse).astype(LOW)
            result = result + dot(low, keyvalue[1, k].reshape(chunk, HD), (1, 0))
        attended[h] = result
        log_total[h] = jnp.broadcast_to(top + jnp.log(sums), (BLOCK, 128))
        return carry

    lax.fori_loop(0, 5, one_head, 0)
    for j in range(RING):
        att_send[j, :, 128:] = attended[j].astype(LOW)
        tile = attended[4, :, (j // 2) * 128 : (j // 2 + 1) * 128]
        tile = pltpu.roll(tile, TAIL, 1) if j % 2 else tile
        att_send[j, :, :128] = jnp.where(low_lanes, tile, 0.0).astype(LOW)
    att_swap = exchange_steps(mover, att_send, att_slice)
    advance(att_swap)
    att_slice[z] = att_send[z]
    advance(att_swap)

    advance(b_gather)
    save(weight_b, attn_b)

    last_weight = weight_a[:, :, :, 384:].reshape(D, 128)
    main_weight = weight_b[...].reshape(D, HD)

    def make(block):
        rows = dot(att_slice[block, :, :128], last_weight, (1, 1))
        part[block] = (rows + dot(att_slice[block, :, 128:], main_weight, (1, 1))).astype(LOW)

    shares = []
    sharing = share_steps(mover, part, bufs[0], shares, make)
    advance(sharing)
    advance(sharing)
    sums = [
        reduce_steps(mover, own_rows(part), shares[i], bufs, sum_half, span)
        for i, span in enumerate(SPANS)
    ]
    for one in sums:
        advance(one)
    advance(sharing)
    advance(sharing)
    for one in sums:
        advance(one)

    def normed_rows(rows):
        unit = rows * lax.rsqrt(jnp.mean(rows * rows, axis=-1, keepdims=True) + eps_norm)
        return (unit * gain_ref[1:2, :]).astype(LOW)

    gathers, res_shares = [], []
    for one, span in zip(sums, SPANS, strict=True):
        advance(one)
        place = core_rows(*span)[0]
        rows = tokens[place, :] + sum_half[span[0] : span[0] + span[1]]
        residual[place, :] = rows
        normed_low[place, :] = normed_rows(rows)
        gathers.append(gather_steps(mover, normed_low, normed_two, span))
        advance(gathers[-1])
        res_shares.append(mover.copy(residual.at[place], residual.at[place], sibling()))
    advance(dy_gather)
    for copy in res_shares:
        copy.wait_recv()
    theirs = core_rows()[3]
    normed_low[theirs, :] = normed_rows(residual[theirs, :])
    save(normed_low, normed_two.at[z])
    for one in gathers:
        advance(one)
    advance(feed_gather)
    advance(feed_gather)
    for one in gathers:
        advance(one)
    advance(dy_gather)
    for one in gathers:
        advance(one)
    advance(dy_gather)
    advance(feed_gather)
    for one in saves:
        if one is not feed_own:
            one.wait()
    mover.finish()


def run_first(*operands):
    out = {
        "feed_full": ((RING, RING, BLOCK, 2944), LOW),
        "attn_a": ((RING, RING, BLOCK, 512), LOW),
        "attn_b": ((RING, RING, BLOCK, HD), LOW),
        "normed_one": ((RING, BLOCK, D), LOW),
        "dy_all": ((RING, BLOCK, D), LOW),
        "query": ((5, BLOCK, HD), LOW),
        "keyvalue": ((2, RING, RING, BLOCK, HD), LOW),
        "log_total": ((5, BLOCK, 128), F32),
        "att_slice": ((RING, BLOCK, 384), LOW),
        "residual": ((BLOCK, D), F32),
        "normed_two": ((RING, BLOCK, D), LOW),
        "attended": ((5, BLOCK, HD), F32),
        "gains": ((8, D), F32),
        "attn_rows": ((RING, PAD, 768), LOW),
        "feed_rows": ((RING, PAD, 2944), LOW),
    }
    remote = ("feed_full", "attn_a", "attn_b", "normed_one", "dy_all", "keyvalue", "normed_two")
    spaces = [pltpu.VMEM] * 7 + [pl.ANY] + [pltpu.VMEM] * 4
    scratch = [
        pltpu.VMEM((BLOCK, D), F32),
        pltpu.VMEM((BLOCK, D), LOW),
        pltpu.VMEM((RING, PAD, 768), LOW),
        pltpu.VMEM((BLOCK, 512), LOW),
        pltpu.VMEM((BLOCK, HD), LOW),
        pltpu.VMEM((RING, RING, BLOCK, 512), LOW),
        pltpu.VMEM((RING, RING, BLOCK, HD), LOW),
        pltpu.VMEM((BLOCK, 768), F32),
        pltpu.VMEM((RING, PAD, 2944), LOW),
        pltpu.VMEM((BLOCK, 2944), LOW),
        pltpu.VMEM((BLOCK, 2944), F32),
        pltpu.VMEM((BLOCK, D), LOW),
        pltpu.VMEM((RING, BLOCK, D), LOW),
        pltpu.VMEM((RING, BLOCK, D), LOW),
        pltpu.VMEM((RING, BLOCK, 384), LOW),
        pltpu.VMEM((RING, BLOCK, 384), LOW),
        pltpu.VMEM((BLOCK, HD), LOW),
        pltpu.VMEM((2, RING, RING, BLOCK, HD), LOW),
        pltpu.VMEM((BLOCK, RING * RING * BLOCK), F32),
        pltpu.VMEM((RING, BLOCK, 384), LOW),
        pltpu.VMEM((RING, BLOCK, D), LOW),
        pltpu.VMEM((HALF, D), F32),
        pltpu.VMEM((BLOCK, D), LOW),
        *reduce_scratch(),
    ]
    return call(
        first_kernel, 1, 150, out, scratch, operands, spaces, {name: pl.ANY for name in remote}
    )


def plane_reduce_steps(mover, axes, g, bufs, res, loads=None):
    far, side, near, far_two, side_two = bufs
    places = [lax.axis_index(axis) for axis in axes]

    def block(which, i, lo, n):
        rows = pl.ds(which * HALF, HALF)
        return g.at[i, pl.ds(lo, n), rows] if which == 0 else g.at[pl.ds(lo, n), i, rows]

    locals_ = []

    def load(src, dst):
        locals_.append(pltpu.make_async_copy(src, dst, loads.at[len(locals_)]))
        locals_[-1].start()
        return locals_[-1]

    first, sides, wanted = [], [], []
    for which, axis in enumerate(axes):
        right, left = step(axis, 1), step(axis, -1)
        far_place = step(axis, 2)
        first.append(
            (
                mover.copy(block(which, far_place, 0, 2), far.at[which, pl.ds(0, 2)], {axis: right}),
                mover.copy(block(which, far_place, 2, 2), far.at[which, pl.ds(2, 2)], {axis: left}),
            )
        )
        if loads is not None:
            wanted.append(
                (
                    load(block(which, right, 0, 2), near.at[which, 0]),
                    load(block(which, left, 2, 2), near.at[which, 1]),
                )
            )
    for which, axis in enumerate(axes):
        right, left = step(axis, 1), step(axis, -1)
        sides.append(
            [
                mover.copy(block(which, right, 2, 2), side.at[which, 0, pl.ds(2, 2)], {axis: right}),
                mover.copy(block(which, left, 0, 2), side.at[which, 1, pl.ds(0, 2)], {axis: left}),
            ]
        )
    yield
    owned = []
    for which, axis in enumerate(axes):
        for k, (d, lo) in enumerate(((1, 0), (-1, 2))):
            first[which][k].wait_recv()
            if loads is not None:
                wanted[which][k].wait()
                term = near[which, k]
            else:
                term = block(which, step(axis, d), lo, 2)[...]
            near[which, k] = (term.astype(F32) + far[which, lo : lo + 2].astype(F32)).astype(LOW)
            sides[which].append(
                mover.copy(near.at[which, k], side.at[which, k, pl.ds(lo, 2)], {axis: step(axis, d)})
            )
        if loads is not None:
            owned.append(load(block(which, places[which], 0, 4), far.at[which]))
    yield

    def summed(which, i):
        if loads is not None:
            term = far[which, i]
        else:
            rows = pl.ds(which * HALF, HALF)
            me = places[which]
            term = (g[me, i, rows] if which == 0 else g[i, me, rows])
        return (
            term.astype(F32) + side[which, 0, i].astype(F32) + side[which, 1, i].astype(F32)
        )

    second = []
    for which, axis in enumerate(axes):
        other = axes[1 - which]
        right, left = {other: step(other, 1)}, {other: step(other, -1)}
        for copy in sides[which]:
            copy.wait_recv()
        if loads is not None:
            owned[which].wait()
        far_two[which, 0] = summed(which, step(other, 2)).astype(LOW)
        upper, lower = pl.ds(0, PART), pl.ds(PART, HALF - PART)
        second.append(
            (
                mover.copy(far_two.at[which, 0, upper], far_two.at[which, 1, upper], right),
                mover.copy(far_two.at[which, 0, lower], far_two.at[which, 1, lower], left),
            )
        )
    yield
    last = []
    for which, axis in enumerate(axes):
        other = axes[1 - which]
        right, left = step(other, 1), step(other, -1)
        total = summed(which, right)
        second[which][0].wait_recv()
        side_two[which, 0, :PART] = (
            total[:PART] + far_two[which, 1, :PART].astype(F32)
        ).astype(LOW)
        side_two[which, 0, PART:] = total[PART:].astype(LOW)
        last.append(mover.copy(side_two.at[which, 0], side_two.at[which, 2], {other: right}))
        total = summed(which, left)
        second[which][1].wait_recv()
        side_two[which, 1, :PART] = total[:PART].astype(LOW)
        side_two[which, 1, PART:] = (
            total[PART:] + far_two[which, 1, PART:].astype(F32)
        ).astype(LOW)
        last.append(mover.copy(side_two.at[which, 1], side_two.at[which, 3], {other: left}))
    yield
    for which, axis in enumerate(axes):
        other = axes[1 - which]
        last[2 * which].wait_recv()
        last[2 * which + 1].wait_recv()
        res[which * HALF : (which + 1) * HALF] = (
            summed(which, lax.axis_index(other))
            + side_two[which, 2].astype(F32)
            + side_two[which, 3].astype(F32)
        )


def plane_reduce_scratch(columns):
    return [
        pltpu.VMEM((2, 4, HALF, columns), LOW),
        pltpu.VMEM((2, 2, 4, HALF, columns), LOW),
        pltpu.VMEM((2, 2, 2, HALF, columns), LOW),
        pltpu.VMEM((2, 2, HALF, columns), LOW),
        pltpu.VMEM((2, 4, HALF, columns), LOW),
        pltpu.VMEM((BLOCK, columns), F32),
    ]


def share_steps(mover, part, other, shares, make=None, spans=SPANS):
    me, left, right, far = (step("z", d) for d in (0, -1, 1, 2))
    shares.extend([] for _ in spans)
    for slot, block in enumerate((far, right, left, me)):
        if make is not None:
            make(block)
        for copies, (lo, n, first) in zip(shares, spans, strict=True):
            theirs = core_rows(lo, n, first)[3]
            copies.append(
                mover.copy(part.at[block, theirs], other.at[slot, pl.ds(lo, n)], sibling())
            )
        yield


def reduce_steps(mover, mine, shares, bufs, out, span):
    other, total, far_in, from_left, from_right = bufs
    lo, n, part = span
    me, left, right, far = (step("z", d) for d in (0, -1, 1, 2))
    blocks = (far, right, left, me)
    rows, first, last = pl.ds(lo, n), pl.ds(lo, part), pl.ds(lo + part, n - part)

    def both(slot):
        return mine(blocks[slot], span).astype(F32) + other[slot, rows].astype(F32)

    shares[0].wait_recv()
    total[0, rows] = both(0).astype(LOW)
    far_right = mover.copy(total.at[0, first], far_in.at[first], {"z": right})
    far_left = mover.copy(total.at[0, last], far_in.at[last], {"z": left})
    yield
    shares[1].wait_recv()
    summed = both(1)
    far_right.wait_recv()
    total[1, first] = (summed[:part] + far_in[first].astype(F32)).astype(LOW)
    total[1, last] = summed[part:].astype(LOW)
    to_right = mover.copy(total.at[1, rows], from_left.at[rows], {"z": right})
    shares[2].wait_recv()
    summed = both(2)
    far_left.wait_recv()
    total[2, first] = summed[:part].astype(LOW)
    total[2, last] = (summed[part:] + far_in[last].astype(F32)).astype(LOW)
    to_left = mover.copy(total.at[2, rows], from_right.at[rows], {"z": left})
    yield
    shares[3].wait_recv()
    summed = both(3)
    to_right.wait_recv()
    to_left.wait_recv()
    out[rows] = summed + from_left[rows].astype(F32) + from_right[rows].astype(F32)


def own_rows(ref):
    return lambda block, span: ref[block, core_rows(*span)[0]]


def half_rows(ref):
    return lambda block, span: ref[block, pl.ds(span[0], span[1])]


def reduce_scratch():
    return [
        pltpu.VMEM((4, HALF, D), LOW),
        pltpu.VMEM((3, HALF, D), LOW),
        pltpu.VMEM((HALF, D), LOW),
        pltpu.VMEM((HALF, D), LOW),
        pltpu.VMEM((HALF, D), LOW),
    ]


def spread_rows(res, dst):
    for i in range(RING):
        rows = res[i * OWN : (i + 1) * OWN]
        dst[i] = jnp.concatenate([rows, jnp.zeros((PAD - OWN, rows.shape[1]), F32)]).astype(LOW)


def activation(gate, upper, grad):
    square = gate * gate
    tanh = jnp.tanh(GELU_SCALE * gate * (1.0 + GELU_CUBE * square))
    half = 0.5 * (1.0 + tanh)
    gelu = gate * half
    slope = half + 0.5 * gate * (1.0 - tanh * tanh) * GELU_SCALE * (1.0 + 3.0 * GELU_CUBE * square)
    return gelu * upper, grad * upper * slope, grad * gelu


def second_kernel(
    feed_full,
    normed_two,
    dy_all,
    cotangent,
    residual,
    gain_ref,
    grad_rows,
    da_all,
    feed_part,
    gateup_grads,
    down_rows,
    send_sem,
    recv_sem,
    local_sem,
    normed_in,
    dy_in,
    gateup_weight,
    down_weight,
    hidden,
    dgu,
    norm_part,
    stage,
    grad_half,
    cot_half,
    res_half,
    da_low,
    *bufs,
):
    z = lax.axis_index("z")
    half, _, _, _ = core_rows()
    plane = ("dp", "x")
    gu_width = 2 * (MAIN + TAIL)
    wide = RING * BLOCK
    loads = [
        pltpu.make_async_copy(src, dst, local_sem.at[i])
        for i, (src, dst) in enumerate(
            (
                (normed_two, normed_in),
                (feed_full.at[:, :, :, pl.ds(0, gu_width)], gateup_weight),
                (dy_all, dy_in),
                (feed_full.at[:, :, :, pl.ds(gu_width, 1024)], down_weight),
                (cotangent.at[half], cot_half),
                (residual.at[half], res_half),
            )
        )
    ]
    for load in loads:
        load.start()
    greet(plane_peers(("z",)) + plane_peers(plane) + [sibling()])
    mover = Mover(send_sem, recv_sem)
    for load in loads:
        load.wait()

    def product(rows, weight, lo, n):
        left_side = rows[...].reshape(wide, D)
        return dot(left_side, weight[:, :, :, lo : lo + n].reshape(D, n), (1, 0))

    for lo, n in ((0, 256), (256, 256), (512, 256), (768, 128)):
        value, grad_gate, grad_upper = activation(
            product(normed_in, gateup_weight, lo, n),
            product(normed_in, gateup_weight, MAIN + lo, n),
            product(dy_in, down_weight, lo, n),
        )
        hidden[:, lo : lo + n] = value.astype(LOW)
        dgu[:, lo : lo + n] = grad_gate.astype(LOW)
        dgu[:, MAIN + lo : MAIN + lo + n] = grad_upper.astype(LOW)
    both = product(normed_in, gateup_weight, 2 * MAIN, 2 * TAIL)
    value, grad_gate, grad_upper = activation(
        both, pltpu.roll(both, TAIL, 1), product(dy_in, down_weight, MAIN, 2 * TAIL)
    )
    low_lanes = lanes(both.shape) < TAIL
    hidden[:, MAIN:] = jnp.where(low_lanes, value, 0.0).astype(LOW)
    dgu[:, 2 * MAIN :] = jnp.where(low_lanes, grad_gate, pltpu.roll(grad_upper, TAIL, 1)).astype(LOW)

    for i in range(RING):
        part = dot(dgu[...], gateup_weight[i].reshape(wide, gu_width), (1, 1))
        norm_part[:, :, i * wide : (i + 1) * wide] = part.astype(LOW).reshape(RING, BLOCK, wide)
    shares = []
    sharing = share_steps(mover, norm_part, bufs[0], shares)
    for _ in range(RING):
        advance(sharing)
    sums = [
        reduce_steps(mover, own_rows(norm_part), shares[i], bufs[:5], grad_half, span)
        for i, span in enumerate(SPANS)
    ]

    for i in range(RING):
        terms = dot(hidden[...], down_weight[i].reshape(wide, 1024), (1, 1))
        feed_part[:, :, i * wide : (i + 1) * wide] = terms.astype(LOW).reshape(RING, BLOCK, wide)
        if i < 2:
            advance(sums[i])

    def columns(rows, i):
        return rows[:, :, i * wide : (i + 1) * wide].reshape(wide, wide)

    for i in range(RING):
        grads = dot(columns(dy_in, i), hidden[...], (0, 0))
        down_weight[i] = grads.astype(LOW).reshape(RING, BLOCK, 1024)
        if i < 2:
            advance(sums[i])
    down_sum = plane_reduce_steps(mover, plane, down_weight, bufs[5:10], bufs[10])
    advance(down_sum)
    saved = []

    def gateup_block(i):
        if saved:
            saved[-1].wait()
        grads = dot(columns(normed_in, i), dgu[...], (0, 0))
        stage[...] = grads.astype(LOW).reshape(RING, BLOCK, gu_width)
        saved.append(pltpu.make_async_copy(stage, gateup_grads.at[i], local_sem.at[10 + i]))
        saved[-1].start()

    gateup_block(0)
    gathers, da_shares = [], []
    for one, span in zip(sums, SPANS, strict=True):
        advance(one)
        piece = pl.ds(span[0], span[1])
        place = core_rows(*span)[0]
        rows = res_half[piece, :]
        inverse = lax.rsqrt(jnp.mean(rows * rows, axis=-1, keepdims=True) + eps_norm)
        unit = rows * inverse
        scaled = grad_half[piece, :] * gain_ref[1:2, :]
        grad = cot_half[piece, :] + inverse * (
            scaled - unit * jnp.mean(scaled * unit, axis=-1, keepdims=True)
        )
        grad_rows[piece, :] = grad
        da_low[place, :] = grad.astype(LOW)
        gathers.append(gather_steps(mover, da_low, da_all, span))
        advance(gathers[-1])
        da_shares.append(mover.copy(da_low.at[place], da_low.at[place], sibling()))
    advance(down_sum)
    gateup_block(1)
    for copy in da_shares:
        copy.wait_recv()
    da_own = pltpu.make_async_copy(da_low, da_all.at[z], local_sem.at[9])
    da_own.start()
    for one in gathers:
        advance(one)
    gateup_block(2)
    advance(down_sum)
    for one in gathers:
        advance(one)
    gateup_block(3)
    advance(down_sum)
    for one in gathers:
        advance(one)
    advance(down_sum)
    spread_rows(bufs[10], down_rows)
    saved[-1].wait()
    da_own.wait()
    mover.finish()


def third_kernel(
    feed_part,
    gateup_grads,
    da_all,
    residual,
    attn_a,
    attn_b,
    att_slice,
    query,
    kv_hbm,
    log_total,
    attended,
    cos_ref,
    sin_ref,
    cos_kv,
    sin_kv,
    grad_out,
    grad_got,
    gateup_rows,
    output,
    send_sem,
    recv_sem,
    local_sem,
    da_in,
    last_weight,
    main_weight,
    keyvalue,
    feed_mine,
    out_half,
    datt_send,
    datt_got,
    datt,
    delta,
    ds_all,
    p_all,
    dq,
    kv_pair,
    kv_in,
    grad_kv,
    grad_query,
    grad_send,
    kv_low,
    *bufs,
):
    z, core = lax.axis_index("z"), lax.axis_index("tensor")
    x = lax.axis_index("x")
    half = core_rows()[0]
    whole_span = ((0, HALF, PART),)
    out_bufs, rows_bufs, rows_res = bufs[:5], bufs[5:10], bufs[10]
    kv_bufs, kv_rows = bufs[11:16], bufs[16]
    loads = [
        pltpu.make_async_copy(src, dst, local_sem.at[8 + i])
        for i, (src, dst) in enumerate(
            (
                (da_all, da_in),
                (attn_a.at[:, :, :, pl.ds(384, 128)], last_weight),
                (attn_b, main_weight),
                (kv_hbm, keyvalue),
                (feed_part.at[:, half], feed_mine),
            )
        )
    ]
    for load in loads:
        load.start()
    greet([{"z": step("z", d)} for d in (1, 2, 3)] + plane_peers(("dp", "x")) + [sibling()])
    mover = Mover(send_sem, recv_sem)
    rows_sum = plane_reduce_steps(
        mover, ("dp", "x"), gateup_grads, rows_bufs, rows_res, loads=local_sem
    )
    advance(rows_sum)
    for load in loads[:3]:
        load.wait()
    last = last_weight[...].reshape(D, 128)
    main = main_weight[...].reshape(D, HD)
    copies = []
    for d in (2, 1, 3, 0):
        block = step("z", d)
        datt_send[block, :, :128] = dot(da_in[block], last, (1, 0)).astype(LOW)
        datt_send[block, :, 128:] = dot(da_in[block], main, (1, 0)).astype(LOW)
        if d:
            copies.append(mover.copy(datt_send.at[block], datt_got.at[z], {"z": block}))
    datt_got[z] = datt_send[z]
    shares = []
    sharing = share_steps(mover, feed_part, out_bufs[0], shares, spans=whole_span)
    for _ in range(RING):
        advance(sharing)
    feed_sum = reduce_steps(
        mover, half_rows(feed_mine), shares[0], out_bufs, out_half, whole_span[0]
    )
    slices = att_slice[...].reshape(RING * BLOCK, 384)
    wide = RING * BLOCK
    for i in range(RING):
        left_side = da_in[:, :, i * wide : (i + 1) * wide].reshape(wide, wide)
        grad_out[i] = dot(left_side, slices, (0, 0)).astype(LOW).reshape(RING, BLOCK, 384)
    for copy in copies:
        copy.wait_recv()
    for load in loads[3:]:
        load.wait()
    advance(feed_sum)
    advance(rows_sum)

    low_lanes = lanes((BLOCK, 128)) < TAIL
    for h in range(4):
        datt[h] = datt_got[h, :, 128:]
    for k in range(2):
        one, two = (datt_got[2 * k + i, :, :128].astype(F32) for i in range(2))
        datt[4, :, k * 128 : (k + 1) * 128] = jnp.where(
            low_lanes, one, pltpu.roll(two, TAIL, 1)
        ).astype(LOW)
    for h in range(5):
        delta[h] = jnp.broadcast_to(
            jnp.sum(datt[h].astype(F32) * attended[h], axis=-1, keepdims=True), (BLOCK, 128)
        )
        dq[h] = jnp.zeros((BLOCK, HD), F32)
    start = (x * RING + z) * BLOCK
    chunk = RING * BLOCK

    def one_chunk(k, carry):
        keys = keyvalue[0, k].reshape(chunk, HD)
        values = keyvalue[1, k].reshape(chunk, HD)
        shape = (BLOCK, chunk)
        gap = (start - k * chunk) + (lax.broadcasted_iota(jnp.int32, shape, 0) - lanes(shape))
        visible = (gap >= 0) & (gap < WINDOW)

        def one_head(h, carry):
            scores = dot(query[h], keys, (1, 1))
            probs = jnp.where(visible, jnp.exp(scores - log_total[h, :, :1]), 0.0)
            grads = dot(datt[h], values, (1, 1))
            low = (probs * (grads - delta[h, :, :1])).astype(LOW)
            ds_all[h] = low
            p_all[h] = probs.astype(LOW)
            dq[h] = dq[h] + dot(low, keys, (1, 0))
            return carry

        lax.fori_loop(0, 5, one_head, 0)
        queries = query[...].reshape(5 * BLOCK, HD)
        outer = datt[...].reshape(5 * BLOCK, HD)
        kv_pair[0, k] = dot(ds_all[...].reshape(5 * BLOCK, chunk), queries, (0, 0)).astype(LOW).reshape(RING, BLOCK, HD)
        kv_pair[1, k] = dot(p_all[...].reshape(5 * BLOCK, chunk), outer, (0, 0)).astype(LOW).reshape(RING, BLOCK, HD)
        return carry

    lax.fori_loop(0, RING, one_chunk, 0)
    kv_swap = mover.copy(kv_pair.at[1 - core], kv_in, sibling())
    advance(feed_sum)
    cos, sin = cos_ref[...], sin_ref[...]
    scale = HD ** (-0.5)
    for h in range(5):
        grad_query[h, :, :128] = turn(dq[h, :, :128] * scale, cos, -sin)
        grad_query[h, :, 128:] = dq[h, :, 128:] * scale
    kv_swap.wait_recv()
    grad_kv[...] = (kv_pair[core].astype(F32) + kv_in[...].astype(F32)).astype(LOW)
    kv_sum = plane_reduce_steps(mover, ("x", "z"), grad_kv, kv_bufs, kv_rows)
    advance(kv_sum)
    for h in range(4):
        grad_send[h, :, :HD] = grad_query[h].astype(LOW)
    advance(kv_sum)
    advance(kv_sum)
    advance(rows_sum)
    advance(kv_sum)
    advance(kv_sum)
    kv_low[:, :128] = turn(kv_rows[:, :128], cos_kv[...], -sin_kv[...])
    kv_low[:, 128:] = kv_rows[:, 128:]
    for j in range(RING):
        place = slice((j // 2) * 128, (j // 2 + 1) * 128)
        one, two = grad_query[4, :, place], kv_low[:, place]
        if j % 2:
            one = pltpu.roll(one, TAIL, 1)
        else:
            two = pltpu.roll(two, TAIL, 1)
        grad_send[j, :, HD:] = jnp.where(low_lanes, one, two).astype(LOW)
    swap = exchange_steps(mover, grad_send, grad_got)
    advance(swap)
    grad_got[z] = grad_send[z]
    advance(rows_sum)
    advance(feed_sum)
    output[half, :] = residual[half, :] + out_half[...]
    out_share = mover.copy(output.at[half], output.at[half], sibling())
    advance(swap)
    advance(rows_sum)
    spread_rows(rows_res, gateup_rows)
    out_share.wait_recv()
    mover.finish()


def fourth_kernel(
    grad_got,
    gateup_rows,
    down_rows,
    grad_out,
    attn_a,
    normed_hbm,
    grad_rows,
    tokens,
    gain_ref,
    attn_rows,
    feed_rows,
    grad_tokens,
    gateup_got,
    down_got,
    out_got,
    qkv_got,
    kv_other,
    scale_sums,
    send_sem,
    recv_sem,
    local_sem,
    qkv_weight,
    normed_one,
    part,
    grad_half,
    grad_qkv,
    out_send,
    qkv_send,
    scale_own,
    scale_other,
    *bufs,
):
    z = lax.axis_index("z")
    half, _, _, _ = core_rows()
    plane = ("dp", "x")
    sum_bufs = bufs[:5]
    out_bufs, qkv_bufs = bufs[5:11], bufs[11:17]
    loads = [
        pltpu.make_async_copy(attn_a.at[:, :, :, pl.ds(0, 384)], qkv_weight, local_sem.at[0]),
        pltpu.make_async_copy(normed_hbm, normed_one, local_sem.at[1]),
    ]
    for load in loads:
        load.start()
    greet([{"z": step("z", d)} for d in (1, 2, 3)] + plane_peers(plane) + [sibling()])
    mover = Mover(send_sem, recv_sem)
    slices = grad_got[...].reshape(RING * BLOCK, 384)
    wide = RING * BLOCK
    loads[1].wait()
    for i in range(RING):
        left_side = normed_one[:, :, i * wide : (i + 1) * wide].reshape(wide, wide)
        grad_qkv[i] = dot(left_side, slices, (0, 0)).astype(LOW).reshape(RING, BLOCK, 384)
    qkv_sum = plane_reduce_steps(mover, plane, grad_qkv, qkv_bufs[:5], qkv_bufs[5])
    advance(qkv_sum)
    out_sum = plane_reduce_steps(mover, plane, grad_out, out_bufs[:5], out_bufs[5])
    advance(out_sum)
    loads[0].wait()
    weight = qkv_weight[...].reshape(D, 384)

    def make(block):
        part[block] = dot(grad_got[block], weight, (1, 1)).astype(LOW)

    shares = []
    sharing = share_steps(mover, part, sum_bufs[0], shares, make)
    advance(sharing)
    advance(sharing)
    sums = [
        reduce_steps(mover, own_rows(part), shares[i], sum_bufs, grad_half, span)
        for i, span in enumerate(SPANS)
    ]
    for one in sums:
        advance(one)
    advance(sharing)
    advance(sharing)
    advance(qkv_sum)
    for one in sums:
        advance(one)
    advance(out_sum)
    advance(qkv_sum)
    gateup_swap = exchange_steps(mover, gateup_rows, gateup_got)
    advance(gateup_swap)
    down_swap = exchange_steps(mover, down_rows, down_got)
    advance(down_swap)
    gateup_got[z] = gateup_rows[z]
    down_got[z] = down_rows[z]
    advance(out_sum)
    advance(qkv_sum)
    for one in sums:
        advance(one)
    rows = tokens[half, :]
    inverse = lax.rsqrt(jnp.mean(rows * rows, axis=-1, keepdims=True) + eps_norm)
    unit = rows * inverse
    scaled = grad_half[...] * gain_ref[0:1, :]
    grad_tokens[half, :] = grad_rows[...] + inverse * (
        scaled - unit * jnp.mean(scaled * unit, axis=-1, keepdims=True)
    )
    share = mover.copy(grad_tokens.at[half], grad_tokens.at[half], sibling())
    advance(out_sum)
    advance(qkv_sum)
    spread_rows(qkv_bufs[5], qkv_send)
    qkv_swap = exchange_steps(mover, qkv_send, qkv_got)
    advance(qkv_swap)
    qkv_got[z] = qkv_send[z]
    advance(out_sum)
    spread_rows(out_bufs[5], out_send)
    out_swap = exchange_steps(mover, out_send, out_got)
    advance(out_swap)
    out_got[z] = out_send[z]
    width = gateup_got.shape[2]

    def with_weight(weight, got):
        return sum(
            jnp.sum(weight(j).astype(F32) * got[j].astype(F32), axis=-1, keepdims=True)
            for j in range(RING)
        )

    advance(gateup_swap)
    second = with_weight(lambda j: feed_rows[j, :, :width], gateup_got)
    advance(qkv_swap)
    kv_share = mover.copy(qkv_got.at[:, :, pl.ds(HD, 128)], kv_other, sibling())
    first = with_weight(lambda j: attn_rows[j, :, :384], qkv_got)
    scale_own[...] = jnp.where(lanes((PAD, 128)) == 0, first, second)
    scale_share = mover.copy(scale_own, scale_other, sibling())
    advance(down_swap)
    advance(out_swap)
    share.wait_recv()
    scale_share.wait_recv()
    scale_sums[...] = scale_own[...] + scale_other[...]
    kv_share.wait_recv()
    mover.finish()


def adam_kernel(
    rates,
    gateup_got,
    down_got,
    out_got,
    qkv_got,
    kv_other,
    output_in,
    tokens_in,
    *refs,
):
    core = lax.axis_index("tensor")
    inputs, results = refs[:15], refs[15:30]
    passed = refs[30:32]
    in_bufs, out_bufs = refs[32:47], refs[47:62]
    pass_bufs, in_sem, out_sem = refs[62:64], refs[64], refs[65]
    loads = [
        pltpu.make_async_copy(src, dst, in_sem.at[i])
        for i, (src, dst) in enumerate(
            zip((*inputs, output_in, tokens_in), (*in_bufs, *pass_bufs), strict=True)
        )
    ]
    stores = [
        pltpu.make_async_copy(src, dst, out_sem.at[i])
        for i, (src, dst) in enumerate(
            zip((*out_bufs, *pass_bufs), (*results, *passed), strict=True)
        )
    ]
    order = (3, 4, 0, 2, 1)
    for i in order:
        for one in loads[3 * i : 3 * i + 3]:
            one.start()
    for one in loads[15:]:
        one.start()
    low_lanes = lanes((OWN, 128)) < TAIL
    old = [in_bufs[3 * i : 3 * i + 3] for i in range(5)]
    new = [out_bufs[3 * i : 3 * i + 3] for i in range(5)]

    def rows(got, j, lo, n):
        return got[j, :, lo : lo + n].astype(F32)[:OWN]

    def join(one, two, offset):
        if offset:
            return jnp.where(low_lanes, pltpu.roll(one, TAIL, 1), two)
        return jnp.where(low_lanes, one, pltpu.roll(two, TAIL, 1))

    def tails(got, k, lo, offset=0):
        return join(rows(got, 2 * k, lo, 128), rows(got, 2 * k + 1, lo, 128), offset)

    def update(i, index, gradient):
        results = adam_update(*(ref[index] for ref in old[i][:1]), gradient, *(ref[index] for ref in old[i][1:]), rates[i], weight_decay)
        for ref, value in zip(new[i], results, strict=True):
            ref[index] = value

    every = slice(None)

    def ready(i):
        for one in loads[3 * i : 3 * i + 3]:
            one.wait()

    def done(i):
        for one in stores[3 * i : 3 * i + 3]:
            one.start()

    def main_place(j, width):
        return slice(width * j, width * (j + 1))

    def tail_place(k, width):
        return slice(RING * width + 128 * k, RING * width + 128 * (k + 1))

    ready(3)
    for g in range(2):
        for j in range(RING):
            update(3, (every, g, main_place(j, MAIN)), rows(gateup_got, j, MAIN * g, MAIN))
        for k in range(2):
            update(3, (every, g, tail_place(k, MAIN)), tails(gateup_got, k, 2 * MAIN, g))
    done(3)
    for one, two in zip(loads[15:], stores[15:], strict=True):
        one.wait()
        two.start()
    for i, got, width, main, tail in (
        (4, down_got, MAIN, 0, MAIN),
        (0, qkv_got, HD, 0, HD),
        (2, out_got, HD, 128, 0),
    ):
        ready(i)
        for j in range(RING):
            update(i, (every, main_place(j, width)), rows(got, j, main, width))
        for k in range(2):
            update(i, (every, tail_place(k, width)), tails(got, k, tail))
        done(i)
    ready(1)
    for k in range(2):
        place = slice(128 * k, 128 * (k + 1))
        own, theirs = tails(qkv_got, k, HD, 1), tails(kv_other, k, 0, 1)
        update(1, (every, 0, place), jnp.where(core == 0, own, theirs))
        update(1, (every, 1, place), jnp.where(core == 0, theirs, own))
    done(1)
    for one in stores:
        one.wait()


def run_adam(rates, grads, matrices, passing):
    flat = [array for triple in matrices for array in triple]
    shapes = [jax.ShapeDtypeStruct(array.shape, F32) for array in (*flat, *passing)]
    buffers = [pltpu.VMEM(array.shape, F32) for array in flat]
    results = pl.pallas_call(
        functools.partial(adam_kernel, rates),
        out_shape=shapes,
        in_specs=[pl.BlockSpec(memory_space=pltpu.VMEM)] * len(grads)
        + [pl.BlockSpec(memory_space=pl.ANY)] * len(shapes),
        out_specs=[pl.BlockSpec(memory_space=pl.ANY)] * len(shapes),
        scratch_shapes=[
            *buffers,
            *buffers,
            *(pltpu.VMEM(array.shape, F32) for array in passing),
            pltpu.SemaphoreType.DMA((len(shapes),)),
            pltpu.SemaphoreType.DMA((len(shapes),)),
        ],
        compiler_params=pltpu.CompilerParams(vmem_limit_bytes=60 * 1024 * 1024),
    )(*grads, *passing, *flat)
    return [results[3 * i : 3 * i + 3] for i in range(5)], results[15:]


def call(kernel, ident, copies, out, scratch, operands, spaces, out_spaces=None):
    results = pl.pallas_call(
        kernel,
        out_shape=[jax.ShapeDtypeStruct(shape, kind) for shape, kind in out.values()],
        in_specs=[pl.BlockSpec(memory_space=space) for space in spaces],
        out_specs=[pl.BlockSpec(memory_space=(out_spaces or {}).get(name, pltpu.VMEM)) for name in out],
        scratch_shapes=[
            pltpu.SemaphoreType.DMA((copies,)),
            pltpu.SemaphoreType.DMA((copies,)),
            pltpu.SemaphoreType.DMA((16,)),
            *scratch,
        ],
        compiler_params=pltpu.CompilerParams(
            collective_id=ident, has_side_effects=True, vmem_limit_bytes=60 * 1024 * 1024
        ),
    )(*operands)
    return dict(zip(out, results, strict=True))


def run_second(*operands):
    out = {
        "grad_rows": ((HALF, D), F32),
        "da_all": ((RING, BLOCK, D), LOW),
        "feed_part": ((RING, BLOCK, D), LOW),
        "gateup_grads": ((RING, RING, BLOCK, 2 * (MAIN + TAIL)), LOW),
        "down_rows": ((RING, PAD, 1024), LOW),
    }
    scratch = [
        pltpu.VMEM((RING, BLOCK, D), LOW),
        pltpu.VMEM((RING, BLOCK, D), LOW),
        pltpu.VMEM((RING, RING, BLOCK, 2 * (MAIN + TAIL)), LOW),
        pltpu.VMEM((RING, RING, BLOCK, 1024), LOW),
        pltpu.VMEM((RING * BLOCK, 1024), LOW),
        pltpu.VMEM((RING * BLOCK, 2 * (MAIN + TAIL)), LOW),
        pltpu.VMEM((RING, BLOCK, D), LOW),
        pltpu.VMEM((RING, BLOCK, 2 * (MAIN + TAIL)), LOW),
        pltpu.VMEM((HALF, D), F32),
        pltpu.VMEM((HALF, D), F32),
        pltpu.VMEM((HALF, D), F32),
        pltpu.VMEM((BLOCK, D), LOW),
        *reduce_scratch(),
        *plane_reduce_scratch(1024),
    ]
    spaces = [pl.ANY] * 5 + [pltpu.VMEM]
    return call(
        second_kernel, 5, 80, out, scratch, operands, spaces, {"gateup_grads": pl.ANY, "da_all": pl.ANY}
    )


def run_third(*operands):
    out = {
        "grad_out": ((RING, RING, BLOCK, 384), LOW),
        "grad_got": ((RING, BLOCK, 384), LOW),
        "gateup_rows": ((RING, PAD, 2 * (MAIN + TAIL)), LOW),
        "output": ((BLOCK, D), F32),
    }
    scratch = [
        pltpu.VMEM((RING, BLOCK, D), LOW),
        pltpu.VMEM((RING, RING, BLOCK, 128), LOW),
        pltpu.VMEM((RING, RING, BLOCK, HD), LOW),
        pltpu.VMEM((2, RING, RING, BLOCK, HD), LOW),
        pltpu.VMEM((RING, HALF, D), LOW),
        pltpu.VMEM((HALF, D), F32),
        pltpu.VMEM((RING, BLOCK, 384), LOW),
        pltpu.VMEM((RING, BLOCK, 384), LOW),
        pltpu.VMEM((5, BLOCK, HD), LOW),
        pltpu.VMEM((5, BLOCK, 128), F32),
        pltpu.VMEM((5, BLOCK, RING * BLOCK), LOW),
        pltpu.VMEM((5, BLOCK, RING * BLOCK), LOW),
        pltpu.VMEM((5, BLOCK, HD), F32),
        pltpu.VMEM((2, RING, RING, BLOCK, HD), LOW),
        pltpu.VMEM((RING, RING, BLOCK, HD), LOW),
        pltpu.VMEM((RING, RING, BLOCK, HD), LOW),
        pltpu.VMEM((5, BLOCK, HD), F32),
        pltpu.VMEM((RING, BLOCK, 384), LOW),
        pltpu.VMEM((BLOCK, HD), F32),
        *reduce_scratch(),
        *plane_reduce_scratch(2 * (MAIN + TAIL)),
        *plane_reduce_scratch(HD),
    ]
    spaces = [pl.ANY] * 3 + [pltpu.VMEM] + [pl.ANY] * 2 + [pltpu.VMEM] * 2 + [pl.ANY] + [pltpu.VMEM] * 6
    return call(third_kernel, 2, 100, out, scratch, operands, spaces)


def run_fourth(*operands):
    out = {
        "grad_tokens": ((BLOCK, D), F32),
        "gateup_got": ((RING, PAD, 2 * (MAIN + TAIL)), LOW),
        "down_got": ((RING, PAD, 1024), LOW),
        "out_got": ((RING, PAD, 384), LOW),
        "qkv_got": ((RING, PAD, 384), LOW),
        "kv_other": ((RING, PAD, 128), LOW),
        "scale_sums": ((PAD, 128), F32),
    }
    scratch = [
        pltpu.VMEM((RING, RING, BLOCK, 384), LOW),
        pltpu.VMEM((RING, BLOCK, D), LOW),
        pltpu.VMEM((RING, BLOCK, D), LOW),
        pltpu.VMEM((HALF, D), F32),
        pltpu.VMEM((RING, RING, BLOCK, 384), LOW),
        pltpu.VMEM((RING, PAD, 384), LOW),
        pltpu.VMEM((RING, PAD, 384), LOW),
        pltpu.VMEM((PAD, 128), F32),
        pltpu.VMEM((PAD, 128), F32),
        *reduce_scratch(),
        *plane_reduce_scratch(384),
        *plane_reduce_scratch(384),
    ]
    spaces = [pltpu.VMEM] * 4 + [pl.ANY] * 2 + [pltpu.VMEM] * 5
    return call(fourth_kernel, 3, 80, out, scratch, operands, spaces)


def adam_update(weight, gradient, first_moment, second_moment, learn_rate, decay_rate):
    first_moment = first_decay * first_moment + (1.0 - first_decay) * gradient
    second_moment = second_decay * second_moment + (1.0 - second_decay) * gradient * gradient
    corrected = (
        first_moment
        / (1.0 - first_decay**STEP)
        / (jnp.sqrt(second_moment / (1.0 - second_decay**STEP)) + adam_eps)
    )
    return (weight - learn_rate * (corrected + decay_rate * weight), first_moment, second_moment)


def out_fan_in(seq_length):
    return max(1, H * HD * 4 // min(WINDOW, seq_length))


def per_device(
    tokens,
    cotangent,
    w_query,
    w_keyvalue,
    w_out,
    w_gateup,
    w_down,
    norm_scales,
    first_query,
    first_keyvalue,
    first_out,
    first_gateup,
    first_down,
    first_scales,
    second_query,
    second_keyvalue,
    second_out,
    second_gateup,
    second_down,
    second_scales,
):
    core = lax.axis_index("tensor")
    seq_index = lax.axis_index("x") * RING + lax.axis_index("z")
    positions = seq_index * BLOCK + jnp.arange(BLOCK, dtype=jnp.int32)
    seq_length = BLOCK * RING * RING

    frequency = 10000.0 ** (-jnp.arange(TAIL, dtype=F32) / TAIL)
    angles = positions.astype(F32)[:, None] * frequency[None, :]
    cos_table = jnp.tile(jnp.cos(angles), (1, 2))
    sin_table = jnp.concatenate([-jnp.sin(angles), jnp.sin(angles)], axis=1)
    cos_kv = jnp.where(core == 0, cos_table, 1.0)
    sin_kv = jnp.where(core == 0, sin_table, 0.0)
    first = run_first(
        w_query,
        w_keyvalue,
        w_out.T,
        w_gateup,
        w_down.T,
        jnp.pad(norm_scales.T, ((0, 0), (TAIL, 128 - TAIL - 2))),
        tokens,
        cotangent,
        cos_table,
        sin_table,
        cos_kv,
        sin_kv,
    )
    second = run_second(
        first["feed_full"],
        first["normed_two"],
        first["dy_all"],
        cotangent,
        first["residual"],
        first["gains"],
    )
    third = run_third(
        second["feed_part"],
        second["gateup_grads"],
        second["da_all"],
        first["residual"],
        first["attn_a"],
        first["attn_b"],
        first["att_slice"],
        first["query"],
        first["keyvalue"],
        first["log_total"],
        first["attended"],
        cos_table,
        sin_table,
        cos_kv,
        sin_kv,
    )
    fourth = run_fourth(
        third["grad_got"],
        third["gateup_rows"],
        second["down_rows"],
        third["grad_out"],
        first["attn_a"],
        first["normed_one"],
        second["grad_rows"],
        tokens,
        first["gains"],
        first["attn_rows"],
        first["feed_rows"],
    )
    matrix_rate = 2.0 * D ** (-0.5)
    out_rate = 2.0 * out_fan_in(seq_length) ** (-0.5)
    down_rate = 2.0 * (FF // 2) ** (-0.5)
    triples, (output, grad_tokens) = run_adam(
        (matrix_rate, matrix_rate, out_rate, matrix_rate, down_rate),
        [fourth[name] for name in ("gateup_got", "down_got", "out_got", "qkv_got", "kv_other")],
        [
            (w_query, first_query, second_query),
            (w_keyvalue, first_keyvalue, second_keyvalue),
            (w_out.T, first_out.T, second_out.T),
            (w_gateup, first_gateup, second_gateup),
            (w_down.T, first_down.T, second_down.T),
        ],
        (third["output"], fourth["grad_tokens"]),
    )
    triples[2] = [array.T for array in triples[2]]
    triples[4] = [array.T for array in triples[4]]
    scale_grads = fourth["scale_sums"][:OWN, :2].T / (1.0 + norm_scales.astype(LOW).astype(F32))
    triples.append(
        adam_update(norm_scales, scale_grads, first_scales, second_scales, gain_rate, 0.0)
    )
    return (output, grad_tokens, *(triple[i] for i in range(3) for triple in triples))


def solution(mesh):
    split = Mesh(
        mesh.devices.reshape(RING, RING, RING, 2), ("dp", "x", "z", "tensor")
    )
    rows = ("dp", "x", "z")
    matrices = (
        P(rows, "tensor"),
        P(rows, None, None),
        P("tensor", rows),
        P(rows, None, "tensor"),
        P("tensor", rows),
        P(None, rows),
    )
    in_specs = (P(rows, None), P(rows, None), *matrices, *matrices, *matrices)
    out_specs = in_specs
    return jax.shard_map(
        per_device, mesh=split, in_specs=in_specs, out_specs=out_specs, check_vma=False
    )
```

```python
import functools

import jax
import jax.numpy as jnp
from jax import lax
from jax.experimental import pallas as pl
from jax.experimental.pallas import tpu as pltpu
from jax.sharding import Mesh
from jax.sharding import PartitionSpec as P

D = 2560
H = 10
HD = 256
FF = 7680
WINDOW = 2048
STEP = 10

eps_norm = 1e-06
masked_fill = -1e30
first_decay = 0.9
second_decay = 0.95
adam_eps = 1e-08
weight_decay = 0.1
gain_rate = 0.2
GELU_SCALE = (2.0 / 3.141592653589793) ** 0.5
GELU_CUBE = 0.044715

MESH = pl.DeviceIdType.MESH
LOW = jnp.bfloat16
F32 = jnp.float32
RING = 4
BLOCK = 160
HALF = BLOCK // 2
PART = 48
OWN = 40
PAD = 48
SPANS = ((0, 48, 32), (48, 32, 16))
MAIN = 896
TAIL = 64


def step(axis, distance):
    return lax.rem(lax.axis_index(axis) + (RING + distance), RING)


def sibling():
    return {"tensor": 1 - lax.axis_index("tensor")}


def greet(peers):
    barrier = pltpu.get_barrier_semaphore()
    for peer in peers:
        pl.semaphore_signal(barrier, inc=1, device_id=peer, device_id_type=MESH)
    pl.semaphore_wait(barrier, len(peers))


def dot(left_side, right_side, contract):
    return lax.dot_general(
        left_side, right_side, ((contract[:1], contract[1:]), ((), ())), preferred_element_type=F32
    )


class Mover:
    def __init__(self, send_sem, recv_sem):
        self.send_sem, self.recv_sem, self.pending = send_sem, recv_sem, []

    def copy(self, src, dst, peer):
        index = len(self.pending)
        one = pltpu.make_async_remote_copy(
            src_ref=src,
            dst_ref=dst,
            send_sem=self.send_sem.at[index],
            recv_sem=self.recv_sem.at[index],
            device_id=peer,
            device_id_type=MESH,
        )
        one.start()
        self.pending.append(one)
        return one

    def finish(self):
        for one in self.pending:
            one.wait_send()


def advance(steps):
    next(steps, None)


def plane_peers(axes):
    return [{axis: step(axis, d)} for axis in axes for d in (-1, 1)]


def exchange_steps(mover, src, dst):
    me = lax.axis_index("z")
    copies = [
        mover.copy(src.at[step("z", d)], dst.at[me], {"z": step("z", d)}) for d in (2, 1, 3)
    ]
    yield
    for copy in copies:
        copy.wait_recv()


def core_rows(lo=0, n=HALF, part=PART):
    base = lax.axis_index("tensor") * HALF

    def rows(start, size):
        return pl.ds(pl.multiple_of(start, 16), size)

    return (
        rows(base + lo, n),
        rows(base + lo, part),
        rows(base + (lo + part), n - part),
        rows(HALF - base + lo, n),
    )


def gather_steps(mover, x, out, span=(0, HALF, PART)):
    me, left, right, far = (step("z", d) for d in (0, -1, 1, 2))
    half, first, last, _ = core_rows(*span)
    to_right = mover.copy(x.at[half], out.at[me, half], {"z": right})
    to_left = mover.copy(x.at[half], out.at[me, half], {"z": left})
    yield
    to_right.wait_recv()
    on_right = mover.copy(out.at[left, first], out.at[left, first], {"z": right})
    shares = [mover.copy(out.at[left, half], out.at[left, half], sibling())]
    to_left.wait_recv()
    on_left = mover.copy(out.at[right, last], out.at[right, last], {"z": left})
    shares.append(mover.copy(out.at[right, half], out.at[right, half], sibling()))
    yield
    on_right.wait_recv()
    on_left.wait_recv()
    shares.append(mover.copy(out.at[far, half], out.at[far, half], sibling()))
    yield
    for copy in shares:
        copy.wait_recv()


def cut_rows(which, cut):
    base, size = (0, cut) if which == 0 else (cut, BLOCK - cut)
    part = -(-size // 32) * 16
    return pl.ds(base, size), pl.ds(base, part), pl.ds(base + part, size - part)


def plane_gather_steps(mover, axes, x, out, cut=HALF, order=(0, 1), share=False):
    a, b = (lax.axis_index(axis) for axis in axes)
    state = {}
    for which, axis in enumerate(axes):
        rows = cut_rows(which, cut)[0]
        place = (lambda i, r: out.at[i, b, r]) if which == 0 else (lambda i, r: out.at[a, i, r])
        me = (a, b)[which]
        to_right = mover.copy(x.at[rows], place(me, rows), {axis: step(axis, 1)})
        to_left = mover.copy(x.at[rows], place(me, rows), {axis: step(axis, -1)})
        state[which] = (axis, place, to_right, to_left)
    yield
    passed = {}
    for which in order:
        axis, place, to_right, to_left = state[which]
        _, first, last = cut_rows(which, cut)
        left, right = step(axis, -1), step(axis, 1)
        to_right.wait_recv()
        on_right = mover.copy(place(left, first), place(left, first), {axis: right})
        to_left.wait_recv()
        on_left = mover.copy(place(right, last), place(right, last), {axis: left})
        passed[which] = (on_right, on_left)
    yield
    state = {}
    shares = []

    def give(piece):
        if share:
            shares.append(mover.copy(piece, piece, sibling()))

    for which in order:
        axis, other = axes[which], axes[1 - which]
        rows = cut_rows(which, cut)[0]
        if which == 0:
            place = lambda i, lo, n, rows=rows: out.at[pl.ds(lo, n), i, rows]
        else:
            place = lambda i, lo, n, rows=rows: out.at[i, pl.ds(lo, n), rows]
        me = (b, a)[which]
        for copy in passed[which]:
            copy.wait_recv()
        to_right = mover.copy(place(me, 0, 4), place(me, 0, 4), {other: step(other, 1)})
        to_left = mover.copy(place(me, 0, 4), place(me, 0, 4), {other: step(other, -1)})
        give(place(me, 0, 4))
        state[which] = (other, place, to_right, to_left)
        yield
    ends = []
    for which in order:
        other, place, to_right, to_left = state[which]
        left, right = step(other, -1), step(other, 1)
        to_right.wait_recv()
        ends.append(mover.copy(place(left, 0, 2), place(left, 0, 2), {other: right}))
        give(place(left, 0, 4))
        to_left.wait_recv()
        ends.append(mover.copy(place(right, 2, 2), place(right, 2, 2), {other: left}))
        give(place(right, 0, 4))
        yield
    for copy in ends:
        copy.wait_recv()
    for which in order:
        other, place, _, _ = state[which]
        give(place(step(other, 2), 0, 4))
    for copy in shares:
        copy.wait_recv()


def lanes(shape):
    return lax.broadcasted_iota(jnp.int32, shape, len(shape) - 1)


def turn(values, cos, sin):
    return values * cos + pltpu.roll(values, 64, 1) * sin


def whole_rows(blocks, stage, dst):
    for i in range(RING):
        stage[i * OWN : (i + 1) * OWN] = blocks[i].astype(F32)[:OWN]
    dst[...] = stage[...].astype(LOW)


def first_kernel(
    w_query,
    w_keyvalue,
    w_out,
    w_gateup,
    w_down,
    scale_columns,
    tokens,
    cotangent,
    cos_ref,
    sin_ref,
    cos_kv,
    sin_kv,
    feed_full,
    attn_a,
    attn_b,
    normed_one,
    dy_all,
    query,
    kv_out,
    log_total,
    att_slice,
    residual,
    normed_two,
    attended,
    gain_ref,
    attn_rows,
    feed_rows,
    send_sem,
    recv_sem,
    local_sem,
    cot_in,
    dy,
    attn_got,
    mine_a,
    mine_b,
    weight_a,
    weight_b,
    attn_stage,
    feed_got,
    feed_mine,
    feed_stage,
    unit_low,
    unit_all,
    normed,
    qkv_send,
    qkv_got,
    kv_own,
    keyvalue,
    scores,
    att_send,
    part,
    sum_half,
    normed_low,
    *bufs,
):
    z, x, y, core = (lax.axis_index(axis) for axis in ("z", "x", "dp", "tensor"))
    plane = ("dp", "x")
    saves = []

    def save(src, dst):
        saves.append(pltpu.make_async_copy(src, dst, local_sem.at[len(saves)]))
        saves[-1].start()
        return saves[-1]

    cot_load = pltpu.make_async_copy(cotangent, cot_in, local_sem.at[15])
    cot_load.start()
    low = lanes((OWN, 128)) < TAIL

    def put(rows, j, lo, values):
        padding = jnp.zeros((PAD - OWN, values.shape[1]), F32)
        rows[j, :, lo : lo + values.shape[1]] = jnp.concatenate([values, padding]).astype(LOW)

    def pair(one, two, odd):
        if odd:
            return jnp.where(low, pltpu.roll(one, TAIL, 1), two)
        return jnp.where(low, one, pltpu.roll(two, TAIL, 1))

    for j in range(RING):
        head = slice(HD * j, HD * (j + 1))
        tile = slice((j // 2) * 128, (j // 2 + 1) * 128)
        last = slice(4 * HD + tile.start, 4 * HD + tile.stop)
        kv_tile = jnp.where(core == 0, w_keyvalue[:, 0, tile], w_keyvalue[:, 1, tile])
        out_tile = pltpu.roll(w_out[:, last], TAIL, 1) if j % 2 else w_out[:, last]
        put(attn_rows, j, 0, w_query[:, head])
        put(attn_rows, j, HD, pair(w_query[:, last], kv_tile, j % 2))
        put(attn_rows, j, 384, jnp.where(low, out_tile, scale_columns[...]))
        put(attn_rows, j, 512, w_out[:, head])
    greet([{"z": step("z", d)} for d in (1, 2, 3)] + plane_peers(plane) + [sibling()])
    mover = Mover(send_sem, recv_sem)

    attn_swap = exchange_steps(mover, attn_rows, attn_got)
    advance(attn_swap)
    for j in range(RING):
        main = slice(MAIN * j, MAIN * (j + 1))
        last = slice(RING * MAIN + (j // 2) * 128, RING * MAIN + (j // 2 + 1) * 128)
        down_tile = pltpu.roll(w_down[:, last], TAIL, 1) if j % 2 else w_down[:, last]
        put(feed_rows, j, 0, w_gateup[:, 0, main])
        put(feed_rows, j, MAIN, w_gateup[:, 1, main])
        put(feed_rows, j, 2 * MAIN, pair(w_gateup[:, 0, last], w_gateup[:, 1, last], j % 2))
        put(feed_rows, j, 2 * (MAIN + TAIL), w_down[:, main])
        put(feed_rows, j, 3 * MAIN + 2 * TAIL, jnp.where(low, down_tile, 0.0))
    feed_swap = exchange_steps(mover, feed_rows, feed_got)
    advance(feed_swap)
    values = tokens[...]
    unit = values * lax.rsqrt(jnp.mean(values * values, axis=-1, keepdims=True) + eps_norm)
    unit_low[...] = unit.astype(LOW)
    unit_gather = gather_steps(mover, unit_low, unit_all)
    advance(unit_gather)
    attn_got[z] = attn_rows[z]
    advance(attn_swap)
    for i in range(RING):
        attn_stage[i * OWN : (i + 1) * OWN] = attn_got[i].astype(F32)[:OWN]
    mine_a[...] = attn_stage[:, :512].astype(LOW)
    mine_b[...] = attn_stage[:, 512:].astype(LOW)
    a_gather = plane_gather_steps(mover, plane, mine_a, weight_a)
    advance(a_gather)
    weight_a[y, x] = mine_a[...]
    unit_all[z] = unit_low[...]
    advance(a_gather)
    feed_got[z] = feed_rows[z]
    advance(a_gather)
    advance(a_gather)
    advance(feed_swap)
    whole_rows(feed_got, feed_stage, feed_mine)
    feed_own = save(feed_mine, feed_full.at[y, x])
    advance(unit_gather)
    advance(a_gather)
    advance(a_gather)
    feed_gather = plane_gather_steps(mover, plane, feed_mine, feed_full)
    advance(feed_gather)
    advance(unit_gather)
    advance(unit_gather)
    advance(a_gather)
    save(weight_a, attn_a)

    scale_cols = weight_a[:, :, :, 384:].reshape(D, 128)
    pick = (lanes((8, 128)) == TAIL + lax.broadcasted_iota(jnp.int32, (8, 128), 0)).astype(LOW)
    gain_ref[...] = 1.0 + dot(pick, scale_cols, (1, 1))
    qkv_weight = weight_a[:, :, :, :384].reshape(D, 384)
    copies = []
    for d in (2, 1, 3, 0):
        block = step("z", d)
        rows = (unit_all[block].astype(F32) * gain_ref[0:1, :]).astype(LOW)
        normed[block] = rows
        qkv_send[block] = dot(rows, qkv_weight, (1, 0)).astype(LOW)
        if d:
            copies.append(mover.copy(qkv_send.at[block], qkv_got.at[z], {"z": block}))
    save(normed, normed_one)
    qkv_got[z] = qkv_send[z]
    feed_own.wait()
    advance(feed_gather)
    for copy in copies:
        copy.wait_recv()
    low_lanes = lanes((BLOCK, 128)) < TAIL
    cos, sin = cos_ref[...], sin_ref[...]

    def joined(i, offset):
        one, two = (qkv_got[i + k, :, 256:384].astype(F32) for k in (0, 1))
        if offset == 0:
            return jnp.where(low_lanes, one, pltpu.roll(two, TAIL, 1))
        return jnp.where(low_lanes, pltpu.roll(one, TAIL, 1), two)

    kv_own[:, :128] = turn(joined(0, 1), cos_kv[...], sin_kv[...]).astype(LOW)
    kv_own[:, 128:] = joined(2, 1).astype(LOW)
    kv_mine = keyvalue.at[core]
    kv_gather = plane_gather_steps(mover, ("x", "z"), kv_own, kv_mine, share=True)
    advance(kv_gather)
    keyvalue[core, x, z] = kv_own[...]
    scale = HD ** (-0.5)
    for h in range(4):
        first = qkv_got[h, :, :128].astype(F32)
        query[h, :, :128] = (turn(first, cos, sin) * scale).astype(LOW)
        query[h, :, 128:] = (qkv_got[h, :, 128:256].astype(F32) * scale).astype(LOW)
    query[4, :, :128] = (turn(joined(0, 0), cos, sin) * scale).astype(LOW)
    query[4, :, 128:] = (joined(2, 0) * scale).astype(LOW)
    b_gather = plane_gather_steps(mover, plane, mine_b, weight_b)
    advance(b_gather)
    weight_b[y, x] = mine_b[...]
    advance(kv_gather)
    advance(b_gather)
    for _ in range(2):
        advance(kv_gather)
        advance(b_gather)
    for _ in range(2):
        advance(kv_gather)
        advance(b_gather)
    for _ in range(2):
        advance(feed_gather)
    cot_load.wait()
    dy[...] = cot_in[...].astype(LOW)
    dy_gather = gather_steps(mover, dy, dy_all)
    advance(dy_gather)
    save(dy, dy_all.at[z])
    advance(kv_gather)
    save(keyvalue, kv_out)

    start = (x * RING + z) * BLOCK
    chunk = RING * BLOCK

    def one_head(h, carry):
        queries = query[h]
        top = jnp.full((BLOCK, 1), masked_fill, F32)
        for k in range(RING):
            rows = keyvalue[0, k].reshape(chunk, HD)
            tile = dot(queries, rows, (1, 1))
            gap = (start - k * chunk) + (
                lax.broadcasted_iota(jnp.int32, tile.shape, 0) - lanes(tile.shape)
            )
            tile = jnp.where((gap >= 0) & (gap < WINDOW), tile, masked_fill)
            scores[:, k * chunk : (k + 1) * chunk] = tile
            top = jnp.maximum(top, jnp.max(tile, axis=-1, keepdims=True))
        sums = jnp.zeros((BLOCK, 1), F32)
        for k in range(RING):
            tile = jnp.exp(scores[:, k * chunk : (k + 1) * chunk] - top)
            scores[:, k * chunk : (k + 1) * chunk] = tile
            sums = sums + jnp.sum(tile, axis=-1, keepdims=True)
        inverse = 1.0 / sums
        result = jnp.zeros((BLOCK, HD), F32)
        for k in range(RING):
            low = (scores[:, k * chunk : (k + 1) * chunk] * inverse).astype(LOW)
            result = result + dot(low, keyvalue[1, k].reshape(chunk, HD), (1, 0))
        attended[h] = result
        log_total[h] = jnp.broadcast_to(top + jnp.log(sums), (BLOCK, 128))
        return carry

    lax.fori_loop(0, 5, one_head, 0)
    for j in range(RING):
        att_send[j, :, 128:] = attended[j].astype(LOW)
        tile = attended[4, :, (j // 2) * 128 : (j // 2 + 1) * 128]
        tile = pltpu.roll(tile, TAIL, 1) if j % 2 else tile
        att_send[j, :, :128] = jnp.where(low_lanes, tile, 0.0).astype(LOW)
    att_swap = exchange_steps(mover, att_send, att_slice)
    advance(att_swap)
    att_slice[z] = att_send[z]
    advance(att_swap)

    advance(b_gather)
    save(weight_b, attn_b)

    last_weight = weight_a[:, :, :, 384:].reshape(D, 128)
    main_weight = weight_b[...].reshape(D, HD)

    def make(block):
        rows = dot(att_slice[block, :, :128], last_weight, (1, 1))
        part[block] = (rows + dot(att_slice[block, :, 128:], main_weight, (1, 1))).astype(LOW)

    shares = []
    sharing = share_steps(mover, part, bufs[0], shares, make)
    advance(sharing)
    advance(sharing)
    sums = [
        reduce_steps(mover, own_rows(part), shares[i], bufs, sum_half, span)
        for i, span in enumerate(SPANS)
    ]
    for one in sums:
        advance(one)
    advance(sharing)
    advance(sharing)
    for one in sums:
        advance(one)

    def normed_rows(rows):
        unit = rows * lax.rsqrt(jnp.mean(rows * rows, axis=-1, keepdims=True) + eps_norm)
        return (unit * gain_ref[1:2, :]).astype(LOW)

    gathers, res_shares = [], []
    for one, span in zip(sums, SPANS, strict=True):
        advance(one)
        place = core_rows(*span)[0]
        rows = tokens[place, :] + sum_half[span[0] : span[0] + span[1]]
        residual[place, :] = rows
        normed_low[place, :] = normed_rows(rows)
        gathers.append(gather_steps(mover, normed_low, normed_two, span))
        advance(gathers[-1])
        res_shares.append(mover.copy(residual.at[place], residual.at[place], sibling()))
        advance(feed_gather)
    advance(dy_gather)
    for copy in res_shares:
        copy.wait_recv()
    theirs = core_rows()[3]
    normed_low[theirs, :] = normed_rows(residual[theirs, :])
    save(normed_low, normed_two.at[z])
    for one in gathers:
        advance(one)
    for one in gathers:
        advance(one)
    advance(dy_gather)
    for one in gathers:
        advance(one)
    advance(dy_gather)
    advance(feed_gather)
    for one in saves:
        if one is not feed_own:
            one.wait()
    mover.finish()


def run_first(*operands):
    out = {
        "feed_full": ((RING, RING, BLOCK, 2944), LOW),
        "attn_a": ((RING, RING, BLOCK, 512), LOW),
        "attn_b": ((RING, RING, BLOCK, HD), LOW),
        "normed_one": ((RING, BLOCK, D), LOW),
        "dy_all": ((RING, BLOCK, D), LOW),
        "query": ((5, BLOCK, HD), LOW),
        "keyvalue": ((2, RING, RING, BLOCK, HD), LOW),
        "log_total": ((5, BLOCK, 128), F32),
        "att_slice": ((RING, BLOCK, 384), LOW),
        "residual": ((BLOCK, D), F32),
        "normed_two": ((RING, BLOCK, D), LOW),
        "attended": ((5, BLOCK, HD), F32),
        "gains": ((8, D), F32),
        "attn_rows": ((RING, PAD, 768), LOW),
        "feed_rows": ((RING, PAD, 2944), LOW),
    }
    remote = ("feed_full", "attn_a", "attn_b", "normed_one", "dy_all", "keyvalue", "normed_two")
    spaces = [pltpu.VMEM] * 7 + [pl.ANY] + [pltpu.VMEM] * 4
    scratch = [
        pltpu.VMEM((BLOCK, D), F32),
        pltpu.VMEM((BLOCK, D), LOW),
        pltpu.VMEM((RING, PAD, 768), LOW),
        pltpu.VMEM((BLOCK, 512), LOW),
        pltpu.VMEM((BLOCK, HD), LOW),
        pltpu.VMEM((RING, RING, BLOCK, 512), LOW),
        pltpu.VMEM((RING, RING, BLOCK, HD), LOW),
        pltpu.VMEM((BLOCK, 768), F32),
        pltpu.VMEM((RING, PAD, 2944), LOW),
        pltpu.VMEM((BLOCK, 2944), LOW),
        pltpu.VMEM((BLOCK, 2944), F32),
        pltpu.VMEM((BLOCK, D), LOW),
        pltpu.VMEM((RING, BLOCK, D), LOW),
        pltpu.VMEM((RING, BLOCK, D), LOW),
        pltpu.VMEM((RING, BLOCK, 384), LOW),
        pltpu.VMEM((RING, BLOCK, 384), LOW),
        pltpu.VMEM((BLOCK, HD), LOW),
        pltpu.VMEM((2, RING, RING, BLOCK, HD), LOW),
        pltpu.VMEM((BLOCK, RING * RING * BLOCK), F32),
        pltpu.VMEM((RING, BLOCK, 384), LOW),
        pltpu.VMEM((RING, BLOCK, D), LOW),
        pltpu.VMEM((HALF, D), F32),
        pltpu.VMEM((BLOCK, D), LOW),
        *reduce_scratch(),
    ]
    return call(
        first_kernel, 1, 150, out, scratch, operands, spaces, {name: pl.ANY for name in remote}
    )


def plane_reduce_steps(mover, axes, g, bufs, res, loads=None):
    far, side, near, far_two, side_two = bufs
    places = [lax.axis_index(axis) for axis in axes]

    def block(which, i, lo, n):
        rows = pl.ds(which * HALF, HALF)
        return g.at[i, pl.ds(lo, n), rows] if which == 0 else g.at[pl.ds(lo, n), i, rows]

    locals_ = []

    def load(src, dst):
        locals_.append(pltpu.make_async_copy(src, dst, loads.at[len(locals_)]))
        locals_[-1].start()
        return locals_[-1]

    first, sides, wanted = [], [], []
    for which, axis in enumerate(axes):
        right, left = step(axis, 1), step(axis, -1)
        far_place = step(axis, 2)
        first.append(
            (
                mover.copy(block(which, far_place, 0, 2), far.at[which, pl.ds(0, 2)], {axis: right}),
                mover.copy(block(which, far_place, 2, 2), far.at[which, pl.ds(2, 2)], {axis: left}),
            )
        )
        if loads is not None:
            wanted.append(
                (
                    load(block(which, right, 0, 2), near.at[which, 0]),
                    load(block(which, left, 2, 2), near.at[which, 1]),
                )
            )
    for which, axis in enumerate(axes):
        right, left = step(axis, 1), step(axis, -1)
        sides.append(
            [
                mover.copy(block(which, right, 2, 2), side.at[which, 0, pl.ds(2, 2)], {axis: right}),
                mover.copy(block(which, left, 0, 2), side.at[which, 1, pl.ds(0, 2)], {axis: left}),
            ]
        )
    yield
    owned = []
    for which, axis in enumerate(axes):
        for k, (d, lo) in enumerate(((1, 0), (-1, 2))):
            first[which][k].wait_recv()
            if loads is not None:
                wanted[which][k].wait()
                term = near[which, k]
            else:
                term = block(which, step(axis, d), lo, 2)[...]
            near[which, k] = (term.astype(F32) + far[which, lo : lo + 2].astype(F32)).astype(LOW)
            sides[which].append(
                mover.copy(near.at[which, k], side.at[which, k, pl.ds(lo, 2)], {axis: step(axis, d)})
            )
        if loads is not None:
            owned.append(load(block(which, places[which], 0, 4), far.at[which]))
    yield

    def summed(which, i):
        if loads is not None:
            term = far[which, i]
        else:
            rows = pl.ds(which * HALF, HALF)
            me = places[which]
            term = (g[me, i, rows] if which == 0 else g[i, me, rows])
        return (
            term.astype(F32) + side[which, 0, i].astype(F32) + side[which, 1, i].astype(F32)
        )

    second = []
    for which, axis in enumerate(axes):
        other = axes[1 - which]
        right, left = {other: step(other, 1)}, {other: step(other, -1)}
        for copy in sides[which]:
            copy.wait_recv()
        if loads is not None:
            owned[which].wait()
        far_two[which, 0] = summed(which, step(other, 2)).astype(LOW)
        upper, lower = pl.ds(0, PART), pl.ds(PART, HALF - PART)
        second.append(
            (
                mover.copy(far_two.at[which, 0, upper], far_two.at[which, 1, upper], right),
                mover.copy(far_two.at[which, 0, lower], far_two.at[which, 1, lower], left),
            )
        )
    yield
    last = []
    for which, axis in enumerate(axes):
        other = axes[1 - which]
        right, left = step(other, 1), step(other, -1)
        total = summed(which, right)
        second[which][0].wait_recv()
        side_two[which, 0, :PART] = (
            total[:PART] + far_two[which, 1, :PART].astype(F32)
        ).astype(LOW)
        side_two[which, 0, PART:] = total[PART:].astype(LOW)
        last.append(mover.copy(side_two.at[which, 0], side_two.at[which, 2], {other: right}))
        total = summed(which, left)
        second[which][1].wait_recv()
        side_two[which, 1, :PART] = total[:PART].astype(LOW)
        side_two[which, 1, PART:] = (
            total[PART:] + far_two[which, 1, PART:].astype(F32)
        ).astype(LOW)
        last.append(mover.copy(side_two.at[which, 1], side_two.at[which, 3], {other: left}))
    yield
    for which, axis in enumerate(axes):
        other = axes[1 - which]
        last[2 * which].wait_recv()
        last[2 * which + 1].wait_recv()
        res[which * HALF : (which + 1) * HALF] = (
            summed(which, lax.axis_index(other))
            + side_two[which, 2].astype(F32)
            + side_two[which, 3].astype(F32)
        )


def plane_reduce_scratch(columns):
    return [
        pltpu.VMEM((2, 4, HALF, columns), LOW),
        pltpu.VMEM((2, 2, 4, HALF, columns), LOW),
        pltpu.VMEM((2, 2, 2, HALF, columns), LOW),
        pltpu.VMEM((2, 2, HALF, columns), LOW),
        pltpu.VMEM((2, 4, HALF, columns), LOW),
        pltpu.VMEM((BLOCK, columns), F32),
    ]


def share_steps(mover, part, other, shares, make=None, spans=SPANS):
    me, left, right, far = (step("z", d) for d in (0, -1, 1, 2))
    shares.extend([] for _ in spans)
    for slot, block in enumerate((far, right, left, me)):
        if make is not None:
            make(block)
        for copies, (lo, n, first) in zip(shares, spans, strict=True):
            theirs = core_rows(lo, n, first)[3]
            copies.append(
                mover.copy(part.at[block, theirs], other.at[slot, pl.ds(lo, n)], sibling())
            )
        yield


def reduce_steps(mover, mine, shares, bufs, out, span):
    other, total, far_in, from_left, from_right = bufs
    lo, n, part = span
    me, left, right, far = (step("z", d) for d in (0, -1, 1, 2))
    blocks = (far, right, left, me)
    rows, first, last = pl.ds(lo, n), pl.ds(lo, part), pl.ds(lo + part, n - part)

    def both(slot):
        return mine(blocks[slot], span).astype(F32) + other[slot, rows].astype(F32)

    shares[0].wait_recv()
    total[0, rows] = both(0).astype(LOW)
    far_right = mover.copy(total.at[0, first], far_in.at[first], {"z": right})
    far_left = mover.copy(total.at[0, last], far_in.at[last], {"z": left})
    yield
    shares[1].wait_recv()
    summed = both(1)
    far_right.wait_recv()
    total[1, first] = (summed[:part] + far_in[first].astype(F32)).astype(LOW)
    total[1, last] = summed[part:].astype(LOW)
    to_right = mover.copy(total.at[1, rows], from_left.at[rows], {"z": right})
    shares[2].wait_recv()
    summed = both(2)
    far_left.wait_recv()
    total[2, first] = summed[:part].astype(LOW)
    total[2, last] = (summed[part:] + far_in[last].astype(F32)).astype(LOW)
    to_left = mover.copy(total.at[2, rows], from_right.at[rows], {"z": left})
    yield
    shares[3].wait_recv()
    summed = both(3)
    to_right.wait_recv()
    to_left.wait_recv()
    out[rows] = summed + from_left[rows].astype(F32) + from_right[rows].astype(F32)


def own_rows(ref):
    return lambda block, span: ref[block, core_rows(*span)[0]]


def half_rows(ref):
    return lambda block, span: ref[block, pl.ds(span[0], span[1])]


def reduce_scratch():
    return [
        pltpu.VMEM((4, HALF, D), LOW),
        pltpu.VMEM((3, HALF, D), LOW),
        pltpu.VMEM((HALF, D), LOW),
        pltpu.VMEM((HALF, D), LOW),
        pltpu.VMEM((HALF, D), LOW),
    ]


def spread_rows(res, dst):
    for i in range(RING):
        rows = res[i * OWN : (i + 1) * OWN]
        dst[i] = jnp.concatenate([rows, jnp.zeros((PAD - OWN, rows.shape[1]), F32)]).astype(LOW)


def activation(gate, upper, grad):
    square = gate * gate
    tanh = jnp.tanh(GELU_SCALE * gate * (1.0 + GELU_CUBE * square))
    half = 0.5 * (1.0 + tanh)
    gelu = gate * half
    slope = half + 0.5 * gate * (1.0 - tanh * tanh) * GELU_SCALE * (1.0 + 3.0 * GELU_CUBE * square)
    return gelu * upper, grad * upper * slope, grad * gelu


def second_kernel(
    feed_full,
    normed_two,
    dy_all,
    cotangent,
    residual,
    gain_ref,
    grad_rows,
    da_all,
    feed_part,
    gateup_grads,
    down_rows,
    send_sem,
    recv_sem,
    local_sem,
    normed_in,
    dy_in,
    gateup_weight,
    down_weight,
    hidden,
    dgu,
    norm_part,
    stage,
    grad_half,
    cot_half,
    res_half,
    da_low,
    *bufs,
):
    z = lax.axis_index("z")
    half, _, _, _ = core_rows()
    plane = ("dp", "x")
    gu_width = 2 * (MAIN + TAIL)
    wide = RING * BLOCK
    loads = [
        pltpu.make_async_copy(src, dst, local_sem.at[i])
        for i, (src, dst) in enumerate(
            (
                (normed_two, normed_in),
                (feed_full.at[:, :, :, pl.ds(0, gu_width)], gateup_weight),
                (dy_all, dy_in),
                (feed_full.at[:, :, :, pl.ds(gu_width, 1024)], down_weight),
                (cotangent.at[half], cot_half),
                (residual.at[half], res_half),
            )
        )
    ]
    for load in loads:
        load.start()
    greet(plane_peers(("z",)) + plane_peers(plane) + [sibling()])
    mover = Mover(send_sem, recv_sem)
    for load in loads:
        load.wait()

    def product(rows, weight, lo, n):
        left_side = rows[...].reshape(wide, D)
        return dot(left_side, weight[:, :, :, lo : lo + n].reshape(D, n), (1, 0))

    for lo, n in ((0, 256), (256, 256), (512, 256), (768, 128)):
        value, grad_gate, grad_upper = activation(
            product(normed_in, gateup_weight, lo, n),
            product(normed_in, gateup_weight, MAIN + lo, n),
            product(dy_in, down_weight, lo, n),
        )
        hidden[:, lo : lo + n] = value.astype(LOW)
        dgu[:, lo : lo + n] = grad_gate.astype(LOW)
        dgu[:, MAIN + lo : MAIN + lo + n] = grad_upper.astype(LOW)
    both = product(normed_in, gateup_weight, 2 * MAIN, 2 * TAIL)
    value, grad_gate, grad_upper = activation(
        both, pltpu.roll(both, TAIL, 1), product(dy_in, down_weight, MAIN, 2 * TAIL)
    )
    low_lanes = lanes(both.shape) < TAIL
    hidden[:, MAIN:] = jnp.where(low_lanes, value, 0.0).astype(LOW)
    dgu[:, 2 * MAIN :] = jnp.where(low_lanes, grad_gate, pltpu.roll(grad_upper, TAIL, 1)).astype(LOW)

    for i in range(RING):
        part = dot(dgu[...], gateup_weight[i].reshape(wide, gu_width), (1, 1))
        norm_part[:, :, i * wide : (i + 1) * wide] = part.astype(LOW).reshape(RING, BLOCK, wide)
    shares = []
    sharing = share_steps(mover, norm_part, bufs[0], shares)
    for _ in range(RING):
        advance(sharing)
    sums = [
        reduce_steps(mover, own_rows(norm_part), shares[i], bufs[:5], grad_half, span)
        for i, span in enumerate(SPANS)
    ]

    for i in range(RING):
        terms = dot(hidden[...], down_weight[i].reshape(wide, 1024), (1, 1))
        feed_part[:, :, i * wide : (i + 1) * wide] = terms.astype(LOW).reshape(RING, BLOCK, wide)
        if i < 2:
            advance(sums[i])

    def columns(rows, i):
        return rows[:, :, i * wide : (i + 1) * wide].reshape(wide, wide)

    for i in range(RING):
        grads = dot(columns(dy_in, i), hidden[...], (0, 0))
        down_weight[i] = grads.astype(LOW).reshape(RING, BLOCK, 1024)
        if i < 2:
            advance(sums[i])
    down_sum = plane_reduce_steps(mover, plane, down_weight, bufs[5:10], bufs[10])
    advance(down_sum)
    saved = []

    def gateup_block(i):
        if saved:
            saved[-1].wait()
        grads = dot(columns(normed_in, i), dgu[...], (0, 0))
        stage[...] = grads.astype(LOW).reshape(RING, BLOCK, gu_width)
        saved.append(pltpu.make_async_copy(stage, gateup_grads.at[i], local_sem.at[10 + i]))
        saved[-1].start()

    gateup_block(0)
    gathers, da_shares = [], []
    for one, span in zip(sums, SPANS, strict=True):
        advance(one)
        piece = pl.ds(span[0], span[1])
        place = core_rows(*span)[0]
        rows = res_half[piece, :]
        inverse = lax.rsqrt(jnp.mean(rows * rows, axis=-1, keepdims=True) + eps_norm)
        unit = rows * inverse
        scaled = grad_half[piece, :] * gain_ref[1:2, :]
        grad = cot_half[piece, :] + inverse * (
            scaled - unit * jnp.mean(scaled * unit, axis=-1, keepdims=True)
        )
        grad_rows[piece, :] = grad
        da_low[place, :] = grad.astype(LOW)
        gathers.append(gather_steps(mover, da_low, da_all, span))
        advance(gathers[-1])
        da_shares.append(mover.copy(da_low.at[place], da_low.at[place], sibling()))
    advance(down_sum)
    gateup_block(1)
    for copy in da_shares:
        copy.wait_recv()
    da_own = pltpu.make_async_copy(da_low, da_all.at[z], local_sem.at[9])
    da_own.start()
    for one in gathers:
        advance(one)
    gateup_block(2)
    advance(down_sum)
    for one in gathers:
        advance(one)
    gateup_block(3)
    advance(down_sum)
    for one in gathers:
        advance(one)
    advance(down_sum)
    spread_rows(bufs[10], down_rows)
    saved[-1].wait()
    da_own.wait()
    mover.finish()


def third_kernel(
    feed_part,
    gateup_grads,
    da_all,
    residual,
    attn_a,
    attn_b,
    att_slice,
    query,
    kv_hbm,
    log_total,
    attended,
    cos_ref,
    sin_ref,
    cos_kv,
    sin_kv,
    grad_out,
    grad_got,
    gateup_rows,
    output,
    send_sem,
    recv_sem,
    local_sem,
    da_in,
    last_weight,
    main_weight,
    keyvalue,
    feed_mine,
    out_half,
    datt_send,
    datt_got,
    datt,
    delta,
    ds_all,
    p_all,
    dq,
    kv_pair,
    kv_in,
    grad_kv,
    grad_query,
    grad_send,
    kv_low,
    *bufs,
):
    z, core = lax.axis_index("z"), lax.axis_index("tensor")
    x = lax.axis_index("x")
    half = core_rows()[0]
    whole_span = ((0, HALF, PART),)
    out_bufs, rows_bufs, rows_res = bufs[:5], bufs[5:10], bufs[10]
    kv_bufs, kv_rows = bufs[11:16], bufs[16]
    loads = [
        pltpu.make_async_copy(src, dst, local_sem.at[8 + i])
        for i, (src, dst) in enumerate(
            (
                (da_all, da_in),
                (attn_a.at[:, :, :, pl.ds(384, 128)], last_weight),
                (attn_b, main_weight),
                (kv_hbm, keyvalue),
                (feed_part.at[:, half], feed_mine),
            )
        )
    ]
    for load in loads:
        load.start()
    greet([{"z": step("z", d)} for d in (1, 2, 3)] + plane_peers(("dp", "x")) + [sibling()])
    mover = Mover(send_sem, recv_sem)
    rows_sum = plane_reduce_steps(
        mover, ("dp", "x"), gateup_grads, rows_bufs, rows_res, loads=local_sem
    )
    advance(rows_sum)
    for load in loads[:3]:
        load.wait()
    last = last_weight[...].reshape(D, 128)
    main = main_weight[...].reshape(D, HD)
    copies = []
    for d in (2, 1, 3, 0):
        block = step("z", d)
        datt_send[block, :, :128] = dot(da_in[block], last, (1, 0)).astype(LOW)
        datt_send[block, :, 128:] = dot(da_in[block], main, (1, 0)).astype(LOW)
        if d:
            copies.append(mover.copy(datt_send.at[block], datt_got.at[z], {"z": block}))
    datt_got[z] = datt_send[z]
    shares = []
    sharing = share_steps(mover, feed_part, out_bufs[0], shares, spans=whole_span)
    for _ in range(RING):
        advance(sharing)
    feed_sum = reduce_steps(
        mover, half_rows(feed_mine), shares[0], out_bufs, out_half, whole_span[0]
    )
    slices = att_slice[...].reshape(RING * BLOCK, 384)
    wide = RING * BLOCK
    for i in range(RING):
        left_side = da_in[:, :, i * wide : (i + 1) * wide].reshape(wide, wide)
        grad_out[i] = dot(left_side, slices, (0, 0)).astype(LOW).reshape(RING, BLOCK, 384)
    for copy in copies:
        copy.wait_recv()
    for load in loads[3:]:
        load.wait()
    advance(feed_sum)
    advance(rows_sum)

    low_lanes = lanes((BLOCK, 128)) < TAIL
    for h in range(4):
        datt[h] = datt_got[h, :, 128:]
    for k in range(2):
        one, two = (datt_got[2 * k + i, :, :128].astype(F32) for i in range(2))
        datt[4, :, k * 128 : (k + 1) * 128] = jnp.where(
            low_lanes, one, pltpu.roll(two, TAIL, 1)
        ).astype(LOW)
    for h in range(5):
        delta[h] = jnp.broadcast_to(
            jnp.sum(datt[h].astype(F32) * attended[h], axis=-1, keepdims=True), (BLOCK, 128)
        )
        dq[h] = jnp.zeros((BLOCK, HD), F32)
    start = (x * RING + z) * BLOCK
    chunk = RING * BLOCK

    def one_chunk(k, carry):
        keys = keyvalue[0, k].reshape(chunk, HD)
        values = keyvalue[1, k].reshape(chunk, HD)
        shape = (BLOCK, chunk)
        gap = (start - k * chunk) + (lax.broadcasted_iota(jnp.int32, shape, 0) - lanes(shape))
        visible = (gap >= 0) & (gap < WINDOW)

        def one_head(h, carry):
            scores = dot(query[h], keys, (1, 1))
            probs = jnp.where(visible, jnp.exp(scores - log_total[h, :, :1]), 0.0)
            grads = dot(datt[h], values, (1, 1))
            low = (probs * (grads - delta[h, :, :1])).astype(LOW)
            ds_all[h] = low
            p_all[h] = probs.astype(LOW)
            dq[h] = dq[h] + dot(low, keys, (1, 0))
            return carry

        lax.fori_loop(0, 5, one_head, 0)
        queries = query[...].reshape(5 * BLOCK, HD)
        outer = datt[...].reshape(5 * BLOCK, HD)
        kv_pair[0, k] = dot(ds_all[...].reshape(5 * BLOCK, chunk), queries, (0, 0)).astype(LOW).reshape(RING, BLOCK, HD)
        kv_pair[1, k] = dot(p_all[...].reshape(5 * BLOCK, chunk), outer, (0, 0)).astype(LOW).reshape(RING, BLOCK, HD)
        return carry

    lax.fori_loop(0, RING, one_chunk, 0)
    kv_swap = mover.copy(kv_pair.at[1 - core], kv_in, sibling())
    advance(feed_sum)
    cos, sin = cos_ref[...], sin_ref[...]
    scale = HD ** (-0.5)
    for h in range(5):
        grad_query[h, :, :128] = turn(dq[h, :, :128] * scale, cos, -sin)
        grad_query[h, :, 128:] = dq[h, :, 128:] * scale
    kv_swap.wait_recv()
    grad_kv[...] = (kv_pair[core].astype(F32) + kv_in[...].astype(F32)).astype(LOW)
    kv_sum = plane_reduce_steps(mover, ("x", "z"), grad_kv, kv_bufs, kv_rows)
    advance(kv_sum)
    for h in range(4):
        grad_send[h, :, :HD] = grad_query[h].astype(LOW)
    advance(kv_sum)
    advance(kv_sum)
    advance(rows_sum)
    advance(kv_sum)
    advance(kv_sum)
    kv_low[:, :128] = turn(kv_rows[:, :128], cos_kv[...], -sin_kv[...])
    kv_low[:, 128:] = kv_rows[:, 128:]
    for j in range(RING):
        place = slice((j // 2) * 128, (j // 2 + 1) * 128)
        one, two = grad_query[4, :, place], kv_low[:, place]
        if j % 2:
            one = pltpu.roll(one, TAIL, 1)
        else:
            two = pltpu.roll(two, TAIL, 1)
        grad_send[j, :, HD:] = jnp.where(low_lanes, one, two).astype(LOW)
    swap = exchange_steps(mover, grad_send, grad_got)
    advance(swap)
    grad_got[z] = grad_send[z]
    advance(rows_sum)
    advance(feed_sum)
    output[half, :] = residual[half, :] + out_half[...]
    out_share = mover.copy(output.at[half], output.at[half], sibling())
    advance(swap)
    advance(rows_sum)
    spread_rows(rows_res, gateup_rows)
    out_share.wait_recv()
    mover.finish()


def fourth_kernel(
    grad_got,
    gateup_rows,
    down_rows,
    grad_out,
    attn_a,
    normed_hbm,
    grad_rows,
    tokens,
    gain_ref,
    attn_rows,
    feed_rows,
    grad_tokens,
    gateup_got,
    down_got,
    out_got,
    qkv_got,
    kv_other,
    scale_sums,
    send_sem,
    recv_sem,
    local_sem,
    qkv_weight,
    normed_one,
    part,
    grad_half,
    grad_qkv,
    out_send,
    qkv_send,
    scale_own,
    scale_other,
    *bufs,
):
    z = lax.axis_index("z")
    half, _, _, _ = core_rows()
    plane = ("dp", "x")
    sum_bufs = bufs[:5]
    out_bufs, qkv_bufs = bufs[5:11], bufs[11:17]
    loads = [
        pltpu.make_async_copy(attn_a.at[:, :, :, pl.ds(0, 384)], qkv_weight, local_sem.at[0]),
        pltpu.make_async_copy(normed_hbm, normed_one, local_sem.at[1]),
    ]
    for load in loads:
        load.start()
    greet([{"z": step("z", d)} for d in (1, 2, 3)] + plane_peers(plane) + [sibling()])
    mover = Mover(send_sem, recv_sem)
    slices = grad_got[...].reshape(RING * BLOCK, 384)
    wide = RING * BLOCK
    loads[1].wait()
    for i in range(RING):
        left_side = normed_one[:, :, i * wide : (i + 1) * wide].reshape(wide, wide)
        grad_qkv[i] = dot(left_side, slices, (0, 0)).astype(LOW).reshape(RING, BLOCK, 384)
    qkv_sum = plane_reduce_steps(mover, plane, grad_qkv, qkv_bufs[:5], qkv_bufs[5])
    advance(qkv_sum)
    out_sum = plane_reduce_steps(mover, plane, grad_out, out_bufs[:5], out_bufs[5])
    advance(out_sum)
    loads[0].wait()
    weight = qkv_weight[...].reshape(D, 384)

    def make(block):
        part[block] = dot(grad_got[block], weight, (1, 1)).astype(LOW)

    shares = []
    sharing = share_steps(mover, part, sum_bufs[0], shares, make)
    advance(sharing)
    advance(sharing)
    sums = [
        reduce_steps(mover, own_rows(part), shares[i], sum_bufs, grad_half, span)
        for i, span in enumerate(SPANS)
    ]
    for one in sums:
        advance(one)
    advance(sharing)
    advance(sharing)
    advance(qkv_sum)
    for one in sums:
        advance(one)
    advance(out_sum)
    advance(qkv_sum)
    gateup_swap = exchange_steps(mover, gateup_rows, gateup_got)
    advance(gateup_swap)
    down_swap = exchange_steps(mover, down_rows, down_got)
    advance(down_swap)
    gateup_got[z] = gateup_rows[z]
    down_got[z] = down_rows[z]
    advance(out_sum)
    advance(qkv_sum)
    for one in sums:
        advance(one)
    rows = tokens[half, :]
    inverse = lax.rsqrt(jnp.mean(rows * rows, axis=-1, keepdims=True) + eps_norm)
    unit = rows * inverse
    scaled = grad_half[...] * gain_ref[0:1, :]
    grad_tokens[half, :] = grad_rows[...] + inverse * (
        scaled - unit * jnp.mean(scaled * unit, axis=-1, keepdims=True)
    )
    share = mover.copy(grad_tokens.at[half], grad_tokens.at[half], sibling())
    advance(out_sum)
    advance(qkv_sum)
    spread_rows(qkv_bufs[5], qkv_send)
    qkv_swap = exchange_steps(mover, qkv_send, qkv_got)
    advance(qkv_swap)
    qkv_got[z] = qkv_send[z]
    advance(out_sum)
    spread_rows(out_bufs[5], out_send)
    out_swap = exchange_steps(mover, out_send, out_got)
    advance(out_swap)
    out_got[z] = out_send[z]
    width = gateup_got.shape[2]

    def with_weight(weight, got):
        return sum(
            jnp.sum(weight(j).astype(F32) * got[j].astype(F32), axis=-1, keepdims=True)
            for j in range(RING)
        )

    advance(gateup_swap)
    second = with_weight(lambda j: feed_rows[j, :, :width], gateup_got)
    advance(qkv_swap)
    kv_share = mover.copy(qkv_got.at[:, :, pl.ds(HD, 128)], kv_other, sibling())
    first = with_weight(lambda j: attn_rows[j, :, :384], qkv_got)
    scale_own[...] = jnp.where(lanes((PAD, 128)) == 0, first, second)
    scale_share = mover.copy(scale_own, scale_other, sibling())
    advance(down_swap)
    advance(out_swap)
    share.wait_recv()
    scale_share.wait_recv()
    scale_sums[...] = scale_own[...] + scale_other[...]
    kv_share.wait_recv()
    mover.finish()


def adam_kernel(
    rates,
    gateup_got,
    down_got,
    out_got,
    qkv_got,
    kv_other,
    output_in,
    tokens_in,
    *refs,
):
    core = lax.axis_index("tensor")
    inputs, results = refs[:15], refs[15:30]
    passed = refs[30:32]
    in_bufs, out_bufs = refs[32:47], refs[47:62]
    pass_bufs, in_sem, out_sem = refs[62:64], refs[64], refs[65]
    loads = [
        pltpu.make_async_copy(src, dst, in_sem.at[i])
        for i, (src, dst) in enumerate(
            zip((*inputs, output_in, tokens_in), (*in_bufs, *pass_bufs), strict=True)
        )
    ]
    stores = [
        pltpu.make_async_copy(src, dst, out_sem.at[i])
        for i, (src, dst) in enumerate(
            zip((*out_bufs, *pass_bufs), (*results, *passed), strict=True)
        )
    ]
    order = (3, 4, 0, 2, 1)
    for i in order:
        for one in loads[3 * i : 3 * i + 3]:
            one.start()
    for one in loads[15:]:
        one.start()
    low_lanes = lanes((OWN, 128)) < TAIL
    old = [in_bufs[3 * i : 3 * i + 3] for i in range(5)]
    new = [out_bufs[3 * i : 3 * i + 3] for i in range(5)]

    def rows(got, j, lo, n):
        return got[j, :, lo : lo + n].astype(F32)[:OWN]

    def join(one, two, offset):
        if offset:
            return jnp.where(low_lanes, pltpu.roll(one, TAIL, 1), two)
        return jnp.where(low_lanes, one, pltpu.roll(two, TAIL, 1))

    def tails(got, k, lo, offset=0):
        return join(rows(got, 2 * k, lo, 128), rows(got, 2 * k + 1, lo, 128), offset)

    def update(i, index, gradient):
        results = adam_update(*(ref[index] for ref in old[i][:1]), gradient, *(ref[index] for ref in old[i][1:]), rates[i], weight_decay)
        for ref, value in zip(new[i], results, strict=True):
            ref[index] = value

    every = slice(None)

    def ready(i):
        for one in loads[3 * i : 3 * i + 3]:
            one.wait()

    def done(i):
        for one in stores[3 * i : 3 * i + 3]:
            one.start()

    def main_place(j, width):
        return slice(width * j, width * (j + 1))

    def tail_place(k, width):
        return slice(RING * width + 128 * k, RING * width + 128 * (k + 1))

    ready(3)
    for g in range(2):
        for j in range(RING):
            update(3, (every, g, main_place(j, MAIN)), rows(gateup_got, j, MAIN * g, MAIN))
        for k in range(2):
            update(3, (every, g, tail_place(k, MAIN)), tails(gateup_got, k, 2 * MAIN, g))
    done(3)
    for one, two in zip(loads[15:], stores[15:], strict=True):
        one.wait()
        two.start()
    for i, got, width, main, tail in (
        (4, down_got, MAIN, 0, MAIN),
        (0, qkv_got, HD, 0, HD),
        (2, out_got, HD, 128, 0),
    ):
        ready(i)
        for j in range(RING):
            update(i, (every, main_place(j, width)), rows(got, j, main, width))
        for k in range(2):
            update(i, (every, tail_place(k, width)), tails(got, k, tail))
        done(i)
    ready(1)
    for k in range(2):
        place = slice(128 * k, 128 * (k + 1))
        own, theirs = tails(qkv_got, k, HD, 1), tails(kv_other, k, 0, 1)
        update(1, (every, 0, place), jnp.where(core == 0, own, theirs))
        update(1, (every, 1, place), jnp.where(core == 0, theirs, own))
    done(1)
    for one in stores:
        one.wait()


def run_adam(rates, grads, matrices, passing):
    flat = [array for triple in matrices for array in triple]
    shapes = [jax.ShapeDtypeStruct(array.shape, F32) for array in (*flat, *passing)]
    buffers = [pltpu.VMEM(array.shape, F32) for array in flat]
    results = pl.pallas_call(
        functools.partial(adam_kernel, rates),
        out_shape=shapes,
        in_specs=[pl.BlockSpec(memory_space=pltpu.VMEM)] * len(grads)
        + [pl.BlockSpec(memory_space=pl.ANY)] * len(shapes),
        out_specs=[pl.BlockSpec(memory_space=pl.ANY)] * len(shapes),
        scratch_shapes=[
            *buffers,
            *buffers,
            *(pltpu.VMEM(array.shape, F32) for array in passing),
            pltpu.SemaphoreType.DMA((len(shapes),)),
            pltpu.SemaphoreType.DMA((len(shapes),)),
        ],
        compiler_params=pltpu.CompilerParams(vmem_limit_bytes=60 * 1024 * 1024),
    )(*grads, *passing, *flat)
    return [results[3 * i : 3 * i + 3] for i in range(5)], results[15:]


def call(kernel, ident, copies, out, scratch, operands, spaces, out_spaces=None):
    results = pl.pallas_call(
        kernel,
        out_shape=[jax.ShapeDtypeStruct(shape, kind) for shape, kind in out.values()],
        in_specs=[pl.BlockSpec(memory_space=space) for space in spaces],
        out_specs=[pl.BlockSpec(memory_space=(out_spaces or {}).get(name, pltpu.VMEM)) for name in out],
        scratch_shapes=[
            pltpu.SemaphoreType.DMA((copies,)),
            pltpu.SemaphoreType.DMA((copies,)),
            pltpu.SemaphoreType.DMA((16,)),
            *scratch,
        ],
        compiler_params=pltpu.CompilerParams(
            collective_id=ident, has_side_effects=True, vmem_limit_bytes=60 * 1024 * 1024
        ),
    )(*operands)
    return dict(zip(out, results, strict=True))


def run_second(*operands):
    out = {
        "grad_rows": ((HALF, D), F32),
        "da_all": ((RING, BLOCK, D), LOW),
        "feed_part": ((RING, BLOCK, D), LOW),
        "gateup_grads": ((RING, RING, BLOCK, 2 * (MAIN + TAIL)), LOW),
        "down_rows": ((RING, PAD, 1024), LOW),
    }
    scratch = [
        pltpu.VMEM((RING, BLOCK, D), LOW),
        pltpu.VMEM((RING, BLOCK, D), LOW),
        pltpu.VMEM((RING, RING, BLOCK, 2 * (MAIN + TAIL)), LOW),
        pltpu.VMEM((RING, RING, BLOCK, 1024), LOW),
        pltpu.VMEM((RING * BLOCK, 1024), LOW),
        pltpu.VMEM((RING * BLOCK, 2 * (MAIN + TAIL)), LOW),
        pltpu.VMEM((RING, BLOCK, D), LOW),
        pltpu.VMEM((RING, BLOCK, 2 * (MAIN + TAIL)), LOW),
        pltpu.VMEM((HALF, D), F32),
        pltpu.VMEM((HALF, D), F32),
        pltpu.VMEM((HALF, D), F32),
        pltpu.VMEM((BLOCK, D), LOW),
        *reduce_scratch(),
        *plane_reduce_scratch(1024),
    ]
    spaces = [pl.ANY] * 5 + [pltpu.VMEM]
    return call(
        second_kernel, 5, 80, out, scratch, operands, spaces, {"gateup_grads": pl.ANY, "da_all": pl.ANY}
    )


def run_third(*operands):
    out = {
        "grad_out": ((RING, RING, BLOCK, 384), LOW),
        "grad_got": ((RING, BLOCK, 384), LOW),
        "gateup_rows": ((RING, PAD, 2 * (MAIN + TAIL)), LOW),
        "output": ((BLOCK, D), F32),
    }
    scratch = [
        pltpu.VMEM((RING, BLOCK, D), LOW),
        pltpu.VMEM((RING, RING, BLOCK, 128), LOW),
        pltpu.VMEM((RING, RING, BLOCK, HD), LOW),
        pltpu.VMEM((2, RING, RING, BLOCK, HD), LOW),
        pltpu.VMEM((RING, HALF, D), LOW),
        pltpu.VMEM((HALF, D), F32),
        pltpu.VMEM((RING, BLOCK, 384), LOW),
        pltpu.VMEM((RING, BLOCK, 384), LOW),
        pltpu.VMEM((5, BLOCK, HD), LOW),
        pltpu.VMEM((5, BLOCK, 128), F32),
        pltpu.VMEM((5, BLOCK, RING * BLOCK), LOW),
        pltpu.VMEM((5, BLOCK, RING * BLOCK), LOW),
        pltpu.VMEM((5, BLOCK, HD), F32),
        pltpu.VMEM((2, RING, RING, BLOCK, HD), LOW),
        pltpu.VMEM((RING, RING, BLOCK, HD), LOW),
        pltpu.VMEM((RING, RING, BLOCK, HD), LOW),
        pltpu.VMEM((5, BLOCK, HD), F32),
        pltpu.VMEM((RING, BLOCK, 384), LOW),
        pltpu.VMEM((BLOCK, HD), F32),
        *reduce_scratch(),
        *plane_reduce_scratch(2 * (MAIN + TAIL)),
        *plane_reduce_scratch(HD),
    ]
    spaces = [pl.ANY] * 3 + [pltpu.VMEM] + [pl.ANY] * 2 + [pltpu.VMEM] * 2 + [pl.ANY] + [pltpu.VMEM] * 6
    return call(third_kernel, 2, 100, out, scratch, operands, spaces)


def run_fourth(*operands):
    out = {
        "grad_tokens": ((BLOCK, D), F32),
        "gateup_got": ((RING, PAD, 2 * (MAIN + TAIL)), LOW),
        "down_got": ((RING, PAD, 1024), LOW),
        "out_got": ((RING, PAD, 384), LOW),
        "qkv_got": ((RING, PAD, 384), LOW),
        "kv_other": ((RING, PAD, 128), LOW),
        "scale_sums": ((PAD, 128), F32),
    }
    scratch = [
        pltpu.VMEM((RING, RING, BLOCK, 384), LOW),
        pltpu.VMEM((RING, BLOCK, D), LOW),
        pltpu.VMEM((RING, BLOCK, D), LOW),
        pltpu.VMEM((HALF, D), F32),
        pltpu.VMEM((RING, RING, BLOCK, 384), LOW),
        pltpu.VMEM((RING, PAD, 384), LOW),
        pltpu.VMEM((RING, PAD, 384), LOW),
        pltpu.VMEM((PAD, 128), F32),
        pltpu.VMEM((PAD, 128), F32),
        *reduce_scratch(),
        *plane_reduce_scratch(384),
        *plane_reduce_scratch(384),
    ]
    spaces = [pltpu.VMEM] * 4 + [pl.ANY] * 2 + [pltpu.VMEM] * 5
    return call(fourth_kernel, 3, 80, out, scratch, operands, spaces)


def adam_update(weight, gradient, first_moment, second_moment, learn_rate, decay_rate):
    first_moment = first_decay * first_moment + (1.0 - first_decay) * gradient
    second_moment = second_decay * second_moment + (1.0 - second_decay) * gradient * gradient
    corrected = (
        first_moment
        / (1.0 - first_decay**STEP)
        / (jnp.sqrt(second_moment / (1.0 - second_decay**STEP)) + adam_eps)
    )
    return (weight - learn_rate * (corrected + decay_rate * weight), first_moment, second_moment)


def out_fan_in(seq_length):
    return max(1, H * HD * 4 // min(WINDOW, seq_length))


def per_device(
    tokens,
    cotangent,
    w_query,
    w_keyvalue,
    w_out,
    w_gateup,
    w_down,
    norm_scales,
    first_query,
    first_keyvalue,
    first_out,
    first_gateup,
    first_down,
    first_scales,
    second_query,
    second_keyvalue,
    second_out,
    second_gateup,
    second_down,
    second_scales,
):
    core = lax.axis_index("tensor")
    seq_index = lax.axis_index("x") * RING + lax.axis_index("z")
    positions = seq_index * BLOCK + jnp.arange(BLOCK, dtype=jnp.int32)
    seq_length = BLOCK * RING * RING

    frequency = 10000.0 ** (-jnp.arange(TAIL, dtype=F32) / TAIL)
    angles = positions.astype(F32)[:, None] * frequency[None, :]
    cos_table = jnp.tile(jnp.cos(angles), (1, 2))
    sin_table = jnp.concatenate([-jnp.sin(angles), jnp.sin(angles)], axis=1)
    cos_kv = jnp.where(core == 0, cos_table, 1.0)
    sin_kv = jnp.where(core == 0, sin_table, 0.0)
    first = run_first(
        w_query,
        w_keyvalue,
        w_out.T,
        w_gateup,
        w_down.T,
        jnp.pad(norm_scales.T, ((0, 0), (TAIL, 128 - TAIL - 2))),
        tokens,
        cotangent,
        cos_table,
        sin_table,
        cos_kv,
        sin_kv,
    )
    second = run_second(
        first["feed_full"],
        first["normed_two"],
        first["dy_all"],
        cotangent,
        first["residual"],
        first["gains"],
    )
    third = run_third(
        second["feed_part"],
        second["gateup_grads"],
        second["da_all"],
        first["residual"],
        first["attn_a"],
        first["attn_b"],
        first["att_slice"],
        first["query"],
        first["keyvalue"],
        first["log_total"],
        first["attended"],
        cos_table,
        sin_table,
        cos_kv,
        sin_kv,
    )
    fourth = run_fourth(
        third["grad_got"],
        third["gateup_rows"],
        second["down_rows"],
        third["grad_out"],
        first["attn_a"],
        first["normed_one"],
        second["grad_rows"],
        tokens,
        first["gains"],
        first["attn_rows"],
        first["feed_rows"],
    )
    matrix_rate = 2.0 * D ** (-0.5)
    out_rate = 2.0 * out_fan_in(seq_length) ** (-0.5)
    down_rate = 2.0 * (FF // 2) ** (-0.5)
    triples, (output, grad_tokens) = run_adam(
        (matrix_rate, matrix_rate, out_rate, matrix_rate, down_rate),
        [fourth[name] for name in ("gateup_got", "down_got", "out_got", "qkv_got", "kv_other")],
        [
            (w_query, first_query, second_query),
            (w_keyvalue, first_keyvalue, second_keyvalue),
            (w_out.T, first_out.T, second_out.T),
            (w_gateup, first_gateup, second_gateup),
            (w_down.T, first_down.T, second_down.T),
        ],
        (third["output"], fourth["grad_tokens"]),
    )
    triples[2] = [array.T for array in triples[2]]
    triples[4] = [array.T for array in triples[4]]
    scale_grads = fourth["scale_sums"][:OWN, :2].T / (1.0 + norm_scales.astype(LOW).astype(F32))
    triples.append(
        adam_update(norm_scales, scale_grads, first_scales, second_scales, gain_rate, 0.0)
    )
    return (output, grad_tokens, *(triple[i] for i in range(3) for triple in triples))


def solution(mesh):
    split = Mesh(
        mesh.devices.reshape(RING, RING, RING, 2), ("dp", "x", "z", "tensor")
    )
    rows = ("dp", "x", "z")
    matrices = (
        P(rows, "tensor"),
        P(rows, None, None),
        P("tensor", rows),
        P(rows, None, "tensor"),
        P("tensor", rows),
        P(None, rows),
    )
    in_specs = (P(rows, None), P(rows, None), *matrices, *matrices, *matrices)
    out_specs = in_specs
    return jax.shard_map(
        per_device, mesh=split, in_specs=in_specs, out_specs=out_specs, check_vma=False
    )
```
